32 devices in a mesh: dp: 8 (over z, y), mem: 4 (over x, core).
Axes of the slice: x: 2, y: 2, z: 4, core: 2. Of those that a mesh axis runs over, the one named last changes fastest.
Arguments:
- target: bfloat16 [128, 256, 512], P(('dp', 'mem')), may hold values from -6 to 6
- memory: bfloat16 [128, 256, 512], P('dp', 'mem'), may hold values from -6 to 6
- time_steps: int32 [128], P(('dp', 'mem')), may hold values from 0 to 49
- target_len: int32 [128], P(('dp', 'mem')), may hold values from 1 to 256, 20480 in all
- source_len: int32 [128], P('dp'), may hold values from 64 to 256, as said below
- source_off: int32 [128], P('dp'), may hold values from 0 to 192, as said below
- cotangent: bfloat16 [128, 256, 512], P(('dp', 'mem')), may hold values from -6 to 6
- self_query: bfloat16 [512, 512], P('dp', 'mem'), may hold values from -0.25 to 0.25
- self_key: bfloat16 [512, 512], P('dp', 'mem'), may hold values from -0.25 to 0.25
- self_value: bfloat16 [512, 512], P('dp', 'mem'), may hold values from -0.25 to 0.25
- self_out: bfloat16 [512, 512], P('dp', 'mem'), may hold values from -1.5 to 1.5
- cross_query: bfloat16 [512, 512], P('dp', 'mem'), may hold values from -0.25 to 0.25
- cross_key: bfloat16 [512, 512], P('dp', 'mem'), may hold values from -0.25 to 0.25
- cross_value: bfloat16 [512, 512], P('dp', 'mem'), may hold values from -0.25 to 0.25
- cross_out: bfloat16 [512, 512], P('dp', 'mem'), may hold values from -1.5 to 1.5
- feed_in: bfloat16 [512, 2048], P('dp', 'mem'), may hold values from -0.25 to 0.25
- feed_out: bfloat16 [2048, 512], P('dp', 'mem'), may hold values from -0.125 to 0.125
- biases: bfloat16 [7, 512], P(None, 'dp'), may hold values from -4 to 4
- feed_bias: bfloat16 [2048], P('dp'), may hold values from -4 to 4
- norm_gain: bfloat16 [3, 512], P(None, 'dp'), may hold values from 0.5 to 1.5
- norm_shift: bfloat16 [3, 512], P(None, 'dp'), may hold values from -4 to 4
- step_table: bfloat16 [50, 512], P(None, 'dp'), may hold values from -6 to 6
Outputs:
- layer_out: bfloat16 [128, 256, 512], P(('dp', 'mem'))
- grad_target: float32 [128, 256, 512], P(('dp', 'mem'))
- grad_memory: float32 [128, 256, 512], P('dp', 'mem')
- grad_self_query: float32 [512, 512], P('dp', 'mem')
- grad_self_key: float32 [512, 512], P('dp', 'mem')
- grad_self_value: float32 [512, 512], P('dp', 'mem')
- grad_self_out: float32 [512, 512], P('dp', 'mem')
- grad_cross_query: float32 [512, 512], P('dp', 'mem')
- grad_cross_key: float32 [512, 512], P('dp', 'mem')
- grad_cross_value: float32 [512, 512], P('dp', 'mem')
- grad_cross_out: float32 [512, 512], P('dp', 'mem')
- grad_feed_in: float32 [512, 2048], P('dp', 'mem')
- grad_feed_out: float32 [2048, 512], P('dp', 'mem')
- grad_biases: float32 [7, 512], P(None, 'dp')
- grad_feed_bias: float32 [2048], P('dp')
- grad_norm_gain: float32 [3, 512], P(None, 'dp')
- grad_norm_shift: float32 [3, 512], P(None, 'dp')
- grad_step_table: float32 [50, 512], P(None, 'dp')
The draws below stay inside these ranges and needn't reach their ends.
Inputs may be any that keep to these rules, and one draw needn't show every extreme that they name: `target_len`: some target has exactly 256 tokens. `source_len`: among the 16 pairs of each index of dp, one source has exactly 256 tokens and another exactly 64. A source occupies memory positions source_off to source_off + source_len - 1, so source_off + source_len is at most 256.
All inputs are finite; a program needn't handle non-finite values. No bound on the sum of `target_len` on one device may be relied on, other than what follows from the above.
Results may differ from the reference program's by a relative error of at most 0.025.
Values may be sent and summed in bfloat16 or wider, within the bound.
No kernel may reach another device: no remote copies, remote signals or barrier semaphores. Data moves between devices by JAX's collectives and lax.ppermute only.
A program may use at most 192 MiB of HBM per device.

```python
import math
import jax
import jax.numpy as jnp
import numpy as np
from jax import lax

D = 512
HEADS = 8
DH = 64
FF = 2048
T_STEPS = 50
TGT_LEN = 256
SRC_LEN = 256
G = 16
PAIRS = 128


def source_spans(key):
    key_len, key_col, key_off, key_other = jax.random.split(key, 4)
    groups = PAIRS // G
    spans = jax.random.randint(key_len, (PAIRS,), SRC_LEN // 4, SRC_LEN + 1)
    chosen = jax.random.randint(key_col, (groups,), 0, G)
    second = (chosen + 1 + jax.random.randint(key_other, (groups,), 0, G - 1)) % G
    column = jnp.arange(PAIRS) % G
    owner = jnp.repeat(chosen, G)
    other = jnp.repeat(second, G)
    spans = jnp.where(column == owner, SRC_LEN, spans)
    spans = jnp.where(column == other, SRC_LEN // 4, spans)
    raw_draw = jax.random.randint(key_off, (PAIRS,), 0, 1 << 20)
    starts = raw_draw % (SRC_LEN - spans + 1)
    starts = jnp.where(column == other, SRC_LEN - SRC_LEN // 4, starts)
    return (spans.astype(jnp.int32), starts.astype(jnp.int32))


def draw_source_len(key, part):
    spans, starts = source_spans(key)
    return spans


def draw_source_off(key, part):
    spans, starts = source_spans(key)
    return starts


def with_ends(values, stream_key, smallest, high):
    extent = values.shape
    spot = [jax.random.randint(jax.random.fold_in(stream_key, axis), (), 0, extent[axis]) for axis in range(len(extent))]
    values = values.at[tuple(spot)].set(smallest)
    longest = extent.index(max(extent))
    spot[longest] = (spot[longest] + 1) % extent[longest]
    return values.at[tuple(spot)].set(high)


def block_levels(key, extent, cuts, smallest, largest):
    def one(dim, shards_of):
        draws = jax.random.uniform(jax.random.fold_in(jax.random.fold_in(key, 6), dim), (shards_of,), jnp.float32, smallest / len(cuts), largest / len(cuts))
        return jnp.repeat(jnp.exp(draws), extent[dim] // shards_of).reshape((-1,) + (1,) * (len(extent) - dim - 1))

    level = one(*cuts[0])
    for cut in cuts[1:]:
        level = level * one(*cut)
    return level


def profile(number_of, total, most, lean):
    weights = [(1 << 20) // math.isqrt(grade ** lean) + 1 for grade in range(2, number_of + 1)]
    spare, holding = total - most - (number_of - 1), [1] * (number_of - 1)
    while spare > 0:
        free = [i for i in range(number_of - 1) if holding[i] < most]
        mass, budget = sum([weights[i] for i in free]), spare
        for i in free:
            addition = min(most - holding[i], max(1, budget * weights[i] // mass), spare)
            holding[i] = holding[i] + addition
            spare = spare - addition
    return np.array([most] + holding)


def ragged(own_key, count, total, limit, lean):
    if count == 2:
        one = jax.random.randint(own_key, (), max(1, total - limit), min(limit, total - 1) + 1)
        return jnp.stack([one, total - one])
    tallies = jnp.asarray(profile(count, total, limit, lean), jnp.int32)
    twos = (count - 1) // 2
    donor, sink = tallies[1:1 + 2 * twos:2], tallies[2:2 + 2 * twos:2]
    room = jnp.minimum(donor - 1, limit - sink)
    moved = jax.random.randint(jax.random.fold_in(own_key, 1), (twos,), 0, 1 << 20) % (room + 1)
    tallies = tallies.at[1:1 + 2 * twos:2].set(donor - moved).at[2:2 + 2 * twos:2].set(sink + moved)
    return tallies[jax.random.permutation(jax.random.fold_in(own_key, 2), count)]


def scatter_about(stream_key, shape, width, reach, cuts=(), dtype=jnp.bfloat16):
    values = jax.random.normal(stream_key, shape, jnp.float32) * width
    if len(cuts) > 0:
        values = block_levels(stream_key, shape, cuts, -0.22, 0.18) * values
    return jnp.clip(values, min=-reach, max=reach).astype(dtype)


def setup_inputs(seed: int = 0) -> dict:
    streams_of = jax.random.split(jax.random.key(seed), 23)
    target = scatter_about(streams_of[0], (PAIRS, TGT_LEN, D), 1.0, 6.0, ((0, 32),))
    memory = scatter_about(streams_of[1], (PAIRS, SRC_LEN, D), 1.0, 6.0, ((0, 8), (1, 4)))
    time_steps = with_ends(jax.random.randint(streams_of[2], (PAIRS,), 0, T_STEPS), jax.random.fold_in(streams_of[2], 1), 0, T_STEPS - 1).astype(jnp.int32)
    target_len = ragged(streams_of[3], PAIRS, PAIRS * TGT_LEN * 5 // 8, TGT_LEN, 2).astype(jnp.int32)
    source_len = draw_source_len(jax.random.fold_in(streams_of[22], 71), 0)
    source_off = draw_source_off(jax.random.fold_in(streams_of[22], 71), 0)
    cotangent = scatter_about(streams_of[6], (PAIRS, TGT_LEN, D), 1.0, 6.0, ((0, 32),))
    self_query = scatter_about(streams_of[7], (D, D), D ** -0.5, 0.25, ((0, 8), (1, 4)))
    self_key = scatter_about(streams_of[8], (D, D), D ** -0.5, 0.25, ((0, 8), (1, 4)))
    self_value = scatter_about(streams_of[9], (D, D), D ** -0.5, 0.25, ((0, 8), (1, 4)))
    self_out = scatter_about(streams_of[10], (D, D), (8 * D // TGT_LEN) ** -0.5, 1.5, ((0, 8), (1, 4)))
    cross_query = scatter_about(streams_of[11], (D, D), D ** -0.5, 0.25, ((0, 8), (1, 4)))
    cross_key = scatter_about(streams_of[12], (D, D), D ** -0.5, 0.25, ((0, 8), (1, 4)))
    cross_value = scatter_about(streams_of[13], (D, D), D ** -0.5, 0.25, ((0, 8), (1, 4)))
    cross_out = scatter_about(streams_of[14], (D, D), (8 * D // SRC_LEN) ** -0.5, 1.5, ((0, 8), (1, 4)))
    feed_in = scatter_about(streams_of[15], (D, FF), D ** -0.5, 0.25, ((0, 8), (1, 4)))
    feed_out = scatter_about(streams_of[16], (FF, D), FF ** -0.5, 0.125, ((0, 8), (1, 4)))
    biases = scatter_about(streams_of[17], (7, D), 0.3, 4.0, ((1, 8),))
    feed_bias = scatter_about(streams_of[18], (FF,), 0.3, 4.0, ((0, 8),))
    norm_gain = jnp.clip(1.0 + 0.1 * jax.random.normal(streams_of[19], (3, D), jnp.float32), 0.5, 1.5).astype(jnp.bfloat16)
    norm_shift = scatter_about(streams_of[20], (3, D), 0.3, 4.0, ((1, 8),))
    step_table = scatter_about(streams_of[21], (T_STEPS, D), 0.5, 6.0, ((1, 8),))
    return {"target": target, "memory": memory, "time_steps": time_steps, "target_len": target_len, "source_len": source_len, "source_off": source_off, "cotangent": cotangent, "self_query": self_query, "self_key": self_key, "self_value": self_value, "self_out": self_out, "cross_query": cross_query, "cross_key": cross_key, "cross_value": cross_value, "cross_out": cross_out, "feed_in": feed_in, "feed_out": feed_out, "biases": biases, "feed_bias": feed_bias, "norm_gain": norm_gain, "norm_shift": norm_shift, "step_table": step_table}


@jax.custom_vjp
def low(v):
    return lax.optimization_barrier(v.astype(jnp.bfloat16)).astype(jnp.float32)

@jax.custom_vjp
def low_back(v):
    return v

def low_keep(v):
    return (low(v), None)

def low_pass(kept, grad):
    return (grad,)

def back_keep(v):
    return (v, None)

def back_low(kept, grad):
    return (low(grad),)
low.defvjp(low_keep, low_pass)
low_back.defvjp(back_keep, back_low)
norm_epsilon = 1e-05

def matmul(left, right):
    return jnp.dot(left, right, precision=lax.Precision.HIGHEST)

def layer_norm(signal, gain_vec, shift_vec):
    centre = signal - lax.optimization_barrier(jnp.mean(signal, axis=-1, keepdims=True))
    spread = lax.optimization_barrier(jnp.mean(centre * centre, axis=-1, keepdims=True))
    return centre * lax.rsqrt(spread + norm_epsilon) * gain_vec + shift_vec

def attention(queries, key_rows, value_rows, allowed):
    num_seq, num_rows, num_cols = queries.shape
    head_q = queries.reshape(num_seq, num_rows, HEADS, DH)
    head_k = key_rows.reshape(num_seq, key_rows.shape[1], HEADS, DH)
    head_v = value_rows.reshape(num_seq, value_rows.shape[1], HEADS, DH)
    scores = jnp.einsum('bqhd,bkhd->bhqk', head_q, head_k, precision=lax.Precision.HIGHEST) * (1.0 / math.sqrt(DH))
    scores = low_back(scores)
    scores = jnp.where(allowed[:, None, None, :], scores, -1e+30)
    weights = low(jax.nn.softmax(scores, axis=-1))
    mixture = jnp.einsum('bhqk,bkhd->bqhd', weights, head_v, precision=lax.Precision.HIGHEST)
    return low(low_back(mixture.reshape(num_seq, num_rows, num_cols)))

def layer(param_set, target_f, memory_f, time_steps, target_len, source_len, source_off):
    self_query, self_key, self_value, self_out, cross_query, cross_key, cross_value, cross_out, feed_in, feed_out, biases, feed_bias, norm_gain, norm_shift, step_table = param_set
    embedded = target_f + jnp.take(step_table, time_steps, axis=0)[:, None, :]
    normed = low(layer_norm(embedded, norm_gain[0], norm_shift[0]))
    queries = low(low_back(matmul(normed, self_query) + biases[0]))
    key_rows = low(low_back(matmul(normed, self_key)))
    value_rows = low(low_back(matmul(normed, self_value) + biases[1]))
    places = jnp.arange(TGT_LEN)
    allowed = places[None, :] < target_len[:, None]
    mixture = attention(queries, key_rows, value_rows, allowed)
    after_self = embedded + low_back(matmul(mixture, self_out) + biases[2])
    normed = low(layer_norm(after_self, norm_gain[1], norm_shift[1]))
    queries = low(low_back(matmul(normed, cross_query) + biases[3]))
    key_rows = low(low_back(matmul(memory_f, cross_key)))
    value_rows = low(low_back(matmul(memory_f, cross_value) + biases[4]))
    source_pos = jnp.arange(SRC_LEN)[None, :]
    allowed = (source_pos >= source_off[:, None]) & (source_pos < (source_off + source_len)[:, None])
    mixture = attention(queries, key_rows, value_rows, allowed)
    after_cross = after_self + low_back(matmul(mixture, cross_out) + biases[5])
    normed = low(layer_norm(after_cross, norm_gain[2], norm_shift[2]))
    hidden_pre = low_back(matmul(normed, feed_in) + feed_bias)
    active = low(jax.nn.gelu(hidden_pre, approximate=False))
    return after_cross + low_back(matmul(active, feed_out) + biases[6])

def reference(target, memory, time_steps, target_len, source_len, source_off, cotangent, self_query, self_key, self_value, self_out, cross_query, cross_key, cross_value, cross_out, feed_in, feed_out, biases, feed_bias, norm_gain, norm_shift, step_table):
    param_set = tuple((entry.astype(jnp.float32) for entry in (self_query, self_key, self_value, self_out, cross_query, cross_key, cross_value, cross_out, feed_in, feed_out, biases, feed_bias, norm_gain, norm_shift, step_table)))
    groups = PAIRS // G

    def regroup(array):
        return array.reshape((groups, G) + array.shape[1:])

    def one_group(totals, pieces):
        piece_target, piece_memory, piece_steps, piece_tlen, piece_slen, piece_soff, piece_cot = pieces

        def forward(weight_set, target_f, memory_f):
            return layer(weight_set, target_f, memory_f, piece_steps, piece_tlen, piece_slen, piece_soff)
        output, pullback = jax.vjp(forward, param_set, piece_target.astype(jnp.float32), piece_memory.astype(jnp.float32))
        grad_sets, grad_input, grad_source = pullback(piece_cot.astype(jnp.float32))
        totals = jax.tree.map(jnp.add, totals, grad_sets)
        return (totals, (output.astype(jnp.bfloat16), grad_input, grad_source))
    zero_sums = jax.tree.map(jnp.zeros_like, param_set)
    inputs = (regroup(target), regroup(memory), regroup(time_steps), regroup(target_len), regroup(source_len), regroup(source_off), regroup(cotangent))
    totals, (outputs, grad_input, grad_source) = lax.scan(one_group, zero_sums, inputs)
    return (outputs.reshape(PAIRS, TGT_LEN, D), grad_input.reshape(PAIRS, TGT_LEN, D), grad_source.reshape(PAIRS, SRC_LEN, D), totals[0], totals[1], totals[2], totals[3], totals[4], totals[5], totals[6], totals[7], totals[8], totals[9], totals[10], totals[11], totals[12], totals[13], totals[14])
```

```python
import functools
import math

import jax
import jax.numpy as jnp
from jax import lax
from jax.experimental import pallas as pl
from jax.experimental.pallas import tpu as pltpu
from jax.sharding import PartitionSpec as P

HEADS = 8
DH = 64
GROUP = 4
WIDE = GROUP * DH
EPSILON = 1e-05
SCALE = 1.0 / math.sqrt(DH)
BF = jnp.bfloat16
F32 = jnp.float32
VMEM_LIMIT = 60 * 2**20


def contract(left, right, left_dim, right_dim):
    return lax.dot_general(
        left, right, (((left_dim,), (right_dim,)), ((), ())), preferred_element_type=F32
    )


def mul(left, right):
    return contract(left, right, 1, 0)


def mul_nt(left, right):
    return contract(left, right, 1, 1)


def mul_tn(left, right):
    return contract(left, right, 0, 0)


def normalise(signal):
    centre = signal - jnp.mean(signal, axis=-1, keepdims=True)
    inverse = lax.rsqrt(jnp.mean(centre * centre, axis=-1, keepdims=True) + EPSILON)
    return centre * inverse, inverse


def norm_back(grad, scaled, inverse, gain):
    up = grad * gain
    return inverse * (
        up
        - jnp.mean(up, axis=-1, keepdims=True)
        - scaled * jnp.mean(up * scaled, axis=-1, keepdims=True)
    )


def col_sum(array):
    return jnp.sum(array.astype(F32), axis=0, keepdims=True)


def head_of_lane(rows):
    return lax.broadcasted_iota(jnp.int32, (rows, WIDE), 1) // DH


def stacked(block, lane_head):
    zero = jnp.zeros_like(block)
    return jnp.concatenate([jnp.where(lane_head == h, block, zero) for h in range(GROUP)], axis=0)


def unstacked(result, lane_head, rows):
    picked = result[:rows]
    for h in range(1, GROUP):
        picked = jnp.where(lane_head == h, result[h * rows : (h + 1) * rows], picked)
    return picked


def attend_pair(p, bias, q_ref, k_ref, v_ref, w_ref, mix_ref):
    rows = q_ref.shape[1]
    lane_head = head_of_lane(rows)
    for g in range(HEADS // GROUP):
        cols = slice(g * WIDE, (g + 1) * WIDE)
        scores = mul_nt(stacked(q_ref[p, :, cols], lane_head), k_ref[p, :, cols]) + bias
        top = jnp.max(scores, axis=-1, keepdims=True)
        raised = jnp.exp(scores - top)
        total = jnp.sum(raised, axis=-1, keepdims=True)
        weights = (raised * (1.0 / total)).astype(BF)
        w_ref[p, g] = weights
        mixed = mul(weights, v_ref[p, :, cols])
        mix_ref[p, :, cols] = unstacked(mixed, lane_head, rows).astype(BF)


def attend_pair_back(p, q_ref, k_ref, v_ref, w_ref, grad_ref, gq_ref, gk_ref, gv_ref):
    rows = q_ref.shape[1]
    lane_head = head_of_lane(rows)
    for g in range(HEADS // GROUP):
        cols = slice(g * WIDE, (g + 1) * WIDE)
        grads = stacked(grad_ref[p, :, cols], lane_head)
        weights = w_ref[p, g]
        grad_w = mul_nt(grads, v_ref[p, :, cols])
        wide = weights.astype(F32)
        offset = jnp.sum(grad_w * wide, axis=-1, keepdims=True)
        grad_s = (wide * (grad_w - offset)).astype(BF)
        grad_q = unstacked(mul(grad_s, k_ref[p, :, cols]), lane_head, rows)
        gq_ref[p, :, cols] = (grad_q * SCALE).astype(BF)
        gk_ref[p, :, cols] = mul_tn(grad_s, stacked(q_ref[p, :, cols], lane_head)).astype(BF)
        gv_ref[p, :, cols] = mul_tn(weights, grads).astype(BF)


def flat(ref):
    value = ref[...]
    return value.reshape(value.shape[0] * value.shape[1], value.shape[2])


def self_forward_kernel(
    meta, target, table, vecs, wq, wk, wv, wo, in_a, q, k, v, w, mix, after, embedded
):
    pairs, length, width = target.shape
    for p in range(pairs):
        emb = target[p].astype(F32) + table[pl.ds(meta[pairs + p], 1), :]
        embedded[p] = emb
        scaled, unused = normalise(emb)
        in_a[p] = (scaled * vecs[7:8] + vecs[10:11]).astype(BF)
    x = flat(in_a)
    shape = target.shape
    q[...] = ((mul(x, wq[...]) + vecs[0:1]).astype(BF) * SCALE).reshape(shape)
    k[...] = mul(x, wk[...]).astype(BF).reshape(shape)
    v[...] = (mul(x, wv[...]) + vecs[1:2]).astype(BF).reshape(shape)

    def pair(p, carry):
        spot = lax.broadcasted_iota(jnp.int32, (1, length), 1)
        bias = jnp.where(spot < meta[p], 0.0, -1e30)
        attend_pair(p, bias, q, k, v, w, mix)
        return carry

    lax.fori_loop(0, pairs, pair, 0)
    after[...] = embedded[...] + (mul(flat(mix), wo[...]) + vecs[2:3]).reshape(shape)


def cross_forward_kernel(
    meta, after_self, memory, vecs, wq, wk, wv, wo, in_b, q, k, v, w, mix, after
):
    pairs, length, width = after_self.shape
    shape = after_self.shape
    source = memory.shape[1]
    scaled, unused = normalise(flat(after_self))
    x = (scaled * vecs[8:9] + vecs[11:12]).astype(BF)
    in_b[...] = x.reshape(shape)
    q[...] = ((mul(x, wq[...]) + vecs[3:4]).astype(BF) * SCALE).reshape(shape)
    m = flat(memory)
    k[...] = mul(m, wk[...]).astype(BF).reshape(memory.shape)
    v[...] = (mul(m, wv[...]) + vecs[4:5]).astype(BF).reshape(memory.shape)

    def pair(p, carry):
        spot = lax.broadcasted_iota(jnp.int32, (1, source), 1)
        begin = meta[2 * pairs + p]
        end = begin + meta[3 * pairs + p]
        bias = jnp.where((spot >= begin) & (spot < end), 0.0, -1e30)
        attend_pair(p, bias, q, k, v, w, mix)
        return carry

    lax.fori_loop(0, pairs, pair, 0)
    after[...] = after_self[...] + (mul(flat(mix), wo[...]) + vecs[5:6]).reshape(shape)


def gelu_parts(value):
    size = jnp.abs(value) * math.sqrt(0.5)
    t = 1.0 / (1.0 + 0.3275911 * size)
    bell = jnp.exp(-0.5 * value * value)
    tail = (
        t
        * (
            0.5 * 0.254829592
            + t
            * (
                0.5 * -0.284496736
                + t * (0.5 * 1.421413741 + t * (0.5 * -1.453152027 + t * (0.5 * 1.061405429)))
            )
        )
        * bell
    )
    below = jnp.where(value < 0, tail, 1.0 - tail)
    slope = below + value * bell * (1.0 / math.sqrt(2.0 * math.pi))
    return value * below, slope


def feed_kernel(
    after_cross, cot, vecs, feed_bias, wi, wo, layer_out, gres, dwi, dwo, sums, dbias, x_c, out_acc, in_acc
):
    shape = after_cross.shape
    signal = flat(after_cross)
    scaled, inverse = normalise(signal)
    x_c[...] = (scaled * vecs[9:10] + vecs[12:13]).astype(BF)
    hidden = wi.shape[1]
    block = 512
    for j in range(hidden // block):
        cols = slice(j * block, (j + 1) * block)
        c = flat(cot)
        x = x_c[...]
        pre = mul(x, wi[:, cols]) + feed_bias[:, cols]
        value, slope = gelu_parts(pre)
        act = value.astype(BF)
        grad_pre = (mul_nt(c, wo[cols, :]) * slope).astype(BF)
        out_part = mul(act, wo[cols, :])
        in_part = mul_nt(grad_pre, wi[:, cols])
        if j == 0:
            out_acc[...] = out_part
            in_acc[...] = in_part
        else:
            out_acc[...] += out_part
            in_acc[...] += in_part
        dwo[cols, :] = mul_tn(act, c).astype(BF)
        dwi[:, cols] = mul_tn(x, grad_pre).astype(BF)
        dbias[:, cols] = col_sum(grad_pre)
    layer_out[...] = (signal + out_acc[...] + vecs[6:7]).astype(BF).reshape(shape)
    grad = in_acc[...]
    wide_cot = flat(cot).astype(F32)
    sums[0:1] = col_sum(wide_cot)
    sums[1:2] = col_sum(grad * scaled)
    sums[2:3] = col_sum(grad)
    gres[...] = (wide_cot + norm_back(grad, scaled, inverse, vecs[9:10])).reshape(shape)


def cross_back_kernel(
    gres, after_self, in_b, q, k, v, w, mix, memory, vecs, wq, wk, wv, wo,
    gres_out, gmem, dwq, dwk, dwv, dwo, sums, gmix, gq, gk, gv,
):
    shape = gres.shape
    pairs = shape[0]
    grad = flat(gres).astype(BF)
    sums[0:1] = col_sum(grad)
    dwo[...] = mul_tn(flat(mix), grad).astype(BF)
    gmix[...] = mul_nt(grad, wo[...]).astype(BF).reshape(shape)

    def pair(p, carry):
        attend_pair_back(p, q, k, v, w, gmix, gq, gk, gv)
        return carry

    lax.fori_loop(0, pairs, pair, 0)
    gq_f, gk_f, gv_f, m = flat(gq), flat(gk), flat(gv), flat(memory)
    sums[1:2] = col_sum(gq_f)
    sums[2:3] = col_sum(gv_f)
    dwq[...] = mul_tn(flat(in_b), gq_f).astype(BF)
    dwk[...] = mul_tn(m, gk_f).astype(BF)
    dwv[...] = mul_tn(m, gv_f).astype(BF)
    gmem[...] = (mul_nt(gk_f, wk[...]) + mul_nt(gv_f, wv[...])).astype(BF).reshape(memory.shape)
    grad_in = mul_nt(gq_f, wq[...])
    scaled, inverse = normalise(flat(after_self))
    sums[3:4] = col_sum(grad_in * scaled)
    sums[4:5] = col_sum(grad_in)
    gres_out[...] = gres[...] + norm_back(grad_in, scaled, inverse, vecs[8:9]).reshape(shape)


def self_back_kernel(
    meta, gres, target, table, in_a, q, k, v, w, mix, vecs, wq, wk, wv, wo,
    gtarget, dwq, dwk, dwv, dwo, sums, gtable, gmix, gq, gk, gv,
):
    shape = gres.shape
    pairs = shape[0]
    grad = flat(gres).astype(BF)
    sums[0:1] = col_sum(grad)
    dwo[...] = mul_tn(flat(mix), grad).astype(BF)
    gmix[...] = mul_nt(grad, wo[...]).astype(BF).reshape(shape)

    def pair(p, carry):
        attend_pair_back(p, q, k, v, w, gmix, gq, gk, gv)
        return carry

    lax.fori_loop(0, pairs, pair, 0)
    gq_f, gk_f, gv_f, x = flat(gq), flat(gk), flat(gv), flat(in_a)
    sums[1:2] = col_sum(gq_f)
    sums[2:3] = col_sum(gv_f)
    dwq[...] = mul_tn(x, gq_f).astype(BF)
    dwk[...] = mul_tn(x, gk_f).astype(BF)
    dwv[...] = mul_tn(x, gv_f).astype(BF)
    grad_in = (mul_nt(gq_f, wq[...]) + mul_nt(gk_f, wk[...]) + mul_nt(gv_f, wv[...])).reshape(shape)
    gtable[...] = jnp.zeros_like(gtable)
    for p in range(pairs):
        row = pl.ds(meta[pairs + p], 1)
        emb = target[p].astype(F32) + table[row, :]
        scaled, inverse = normalise(emb)
        gain_part = col_sum(grad_in[p] * scaled)
        shift_part = col_sum(grad_in[p])
        if p == 0:
            sums[3:4] = gain_part
            sums[4:5] = shift_part
        else:
            sums[3:4] += gain_part
            sums[4:5] += shift_part
        out = gres[p] + norm_back(grad_in[p], scaled, inverse, vecs[7:8])
        gtarget[p] = out
        gtable[row, :] += col_sum(out)


def call(kernel, outs, scratch, args, smem=0, name=None):
    space = lambda i: pltpu.SMEM if i < smem else pltpu.VMEM
    return pl.pallas_call(
        kernel,
        out_shape=[jax.ShapeDtypeStruct(s, d) for s, d in outs],
        in_specs=[pl.BlockSpec(memory_space=space(i)) for i in range(len(args))],
        out_specs=[pl.BlockSpec(memory_space=pltpu.VMEM)] * len(outs),
        scratch_shapes=[pltpu.VMEM(s, d) for s, d in scratch],
        compiler_params=pltpu.CompilerParams(vmem_limit_bytes=VMEM_LIMIT),
        name=name,
    )(*args)


def self_forward(meta, target, table, vecs, weights):
    shape = target.shape
    pairs, length, width = shape
    w_shape = (pairs, HEADS // GROUP, GROUP * length, length)
    return call(
        self_forward_kernel,
        [(shape, BF)] * 4 + [(w_shape, BF), (shape, BF), (shape, F32)],
        [(shape, F32)],
        [meta, target, table, vecs, *weights],
        1,
        "self_forward",
    )


def cross_forward(meta, after_self, memory, vecs, weights):
    shape = after_self.shape
    pairs, length, width = shape
    w_shape = (pairs, HEADS // GROUP, GROUP * length, memory.shape[1])
    return call(
        cross_forward_kernel,
        [(shape, BF)] * 2 + [(memory.shape, BF)] * 2 + [(w_shape, BF), (shape, BF), (shape, F32)],
        [],
        [meta, after_self, memory, vecs, *weights],
        1,
        "cross_forward",
    )


def feed(after_cross, cot, vecs, feed_bias, wi, wo):
    shape = after_cross.shape
    tokens = shape[0] * shape[1]
    width, hidden = wi.shape
    return call(
        feed_kernel,
        [(shape, BF), (shape, F32), (wi.shape, BF), (wo.shape, BF), ((3, width), F32), ((1, hidden), F32)],
        [((tokens, width), BF), ((tokens, width), F32), ((tokens, width), F32)],
        [after_cross, cot, vecs, feed_bias, wi, wo],
        0,
        "feed",
    )


def cross_back(gres, after_self, kept, memory, vecs, weights):
    shape = gres.shape
    mshape = memory.shape
    square = (shape[2], shape[2])
    return call(
        cross_back_kernel,
        [(shape, F32), (mshape, BF)] + [(square, BF)] * 4 + [((5, shape[2]), F32)],
        [(shape, BF), (shape, BF), (mshape, BF), (mshape, BF)],
        [gres, after_self, *kept, memory, vecs, *weights],
        0,
        "cross_back",
    )


def self_back(meta, gres, target, table, kept, vecs, weights):
    shape = gres.shape
    square = (shape[2], shape[2])
    return call(
        self_back_kernel,
        [(shape, F32)] + [(square, BF)] * 4 + [((5, shape[2]), F32), (table.shape, F32)],
        [(shape, BF)] * 4,
        [meta, gres, target, table, *kept, vecs, *weights],
        1,
        "self_back",
    )


BOTH = ("dp", "mem")


def gather_group(pieces):
    packed = jnp.concatenate([p.reshape(-1, 128) for p in pieces], axis=0)
    rows = [p.size // 128 for p in pieces]
    dp, mem = lax.axis_size("dp"), lax.axis_size("mem")
    every = lax.all_gather(packed, BOTH).reshape(dp, mem, *packed.shape)
    out, at = [], 0
    for piece, count in zip(pieces, rows):
        part = every[:, :, at : at + count].reshape(dp, mem, *piece.shape)
        at += count
        out.append(
            part.transpose(0, 2, 1, 3).reshape(dp * piece.shape[0], mem * piece.shape[1])
        )
    return out


def scatter_group(grads):
    dp, mem = lax.axis_size("dp"), lax.axis_size("mem")
    parts = []
    for g in grads:
        r, c = g.shape[0] // dp, g.shape[1] // mem
        parts.append(
            g.reshape(dp, r, mem, c).transpose(0, 2, 1, 3).reshape(dp * mem, r * c // 128, 128)
        )
    total = lax.psum_scatter(jnp.concatenate(parts, axis=1), BOTH, scatter_dimension=0)
    out, at = [], 0
    for g, part in zip(grads, parts):
        r, c = g.shape[0] // dp, g.shape[1] // mem
        count = part.shape[1]
        out.append(total[at : at + count].reshape(r, c).astype(F32))
        at += count
    return out


def shards(
    target, memory, time_steps, target_len, source_len, source_off, cotangent,
    self_query, self_key, self_value, self_out, cross_query, cross_key, cross_value, cross_out,
    feed_in, feed_out, biases, feed_bias, norm_gain, norm_shift, step_table,
):
    pairs = target.shape[0]
    width = target.shape[2]
    first = lax.axis_index("mem") * pairs
    meta = jnp.concatenate(
        [
            target_len,
            time_steps,
            lax.dynamic_slice_in_dim(source_off, first, pairs),
            lax.dynamic_slice_in_dim(source_len, first, pairs),
        ]
    )
    small = jnp.concatenate([biases, norm_gain, norm_shift, step_table], axis=0)
    small = lax.all_gather(small, "dp", axis=1, tiled=True).astype(F32)
    vecs, table = small[:13], small[13:]
    bias_row = lax.all_gather(feed_bias, "dp", axis=0, tiled=True).astype(F32)[None]
    self_w = gather_group((self_query, self_key, self_value, self_out))
    cross_w = gather_group((cross_query, cross_key, cross_value, cross_out))
    feed_w = gather_group((feed_in, feed_out))
    own_memory = lax.all_to_all(memory, "mem", 0, 1, tiled=True)

    in_a, q_a, k_a, v_a, w_a, mix_a, after_self = self_forward(meta, target, table, vecs, self_w)
    in_b, q_b, k_b, v_b, w_b, mix_b, after_cross = cross_forward(
        meta, after_self, own_memory, vecs, cross_w
    )
    layer_out, gres_c, d_in, d_out, sums_c, d_fbias = feed(
        after_cross, cotangent, vecs, bias_row, *feed_w
    )
    g_feed = scatter_group((d_in, d_out))
    gres_b, gmem, dq_b, dk_b, dv_b, do_b, sums_b = cross_back(
        gres_c, after_self, (in_b, q_b, k_b, v_b, w_b, mix_b), own_memory, vecs, cross_w
    )
    grad_memory = lax.all_to_all(gmem, "mem", 1, 0, tiled=True).astype(F32)
    g_cross = scatter_group((dq_b, dk_b, dv_b, do_b))
    grad_target, dq_a, dk_a, dv_a, do_a, sums_a, gtable = self_back(
        meta, gres_b, target, table, (in_a, q_a, k_a, v_a, w_a, mix_a), vecs, self_w
    )
    g_self = scatter_group((dq_a, dk_a, dv_a, do_a))
    small_grads = jnp.concatenate(
        [
            sums_a[1:2], sums_a[2:3], sums_a[0:1],
            sums_b[1:2], sums_b[2:3], sums_b[0:1],
            sums_c[0:1],
            sums_a[3:4], sums_b[3:4], sums_c[1:2],
            sums_a[4:5], sums_b[4:5], sums_c[2:3],
            gtable,
        ],
        axis=0,
    )
    small_grads = lax.psum(
        lax.psum_scatter(small_grads, "dp", scatter_dimension=1, tiled=True), "mem"
    )
    g_fbias = lax.psum(lax.psum_scatter(d_fbias[0], "dp", scatter_dimension=0, tiled=True), "mem")
    return (
        layer_out, grad_target, grad_memory, *g_self, *g_cross, *g_feed,
        small_grads[:7], g_fbias, small_grads[7:10], small_grads[10:13], small_grads[13:],
    )


def solution(mesh):
    rows = P(BOTH, None, None)
    piece = P("dp", "mem")
    vector = P(None, "dp")
    mem_rows = P("dp", "mem", None)
    return jax.shard_map(
        shards,
        mesh=mesh,
        in_specs=(rows, mem_rows, P(BOTH), P(BOTH), P("dp"), P("dp"), rows)
        + (piece,) * 10
        + (vector, P("dp"), vector, vector, vector),
        out_specs=(rows, rows, mem_rows) + (piece,) * 10 + (vector, P("dp"), vector, vector, vector),
        check_vma=False,
    )
```

```python
import functools
import math

import jax
import jax.numpy as jnp
from jax import lax
from jax.experimental import pallas as pl
from jax.experimental.pallas import tpu as pltpu
from jax.sharding import PartitionSpec as P

HEADS = 8
DH = 64
GROUP = 4
WIDE = GROUP * DH
EPSILON = 1e-05
SCALE = 1.0 / math.sqrt(DH)
BF = jnp.bfloat16
F32 = jnp.float32
VMEM_LIMIT = 60 * 2**20


def contract(left, right, left_dim, right_dim):
    return lax.dot_general(
        left, right, (((left_dim,), (right_dim,)), ((), ())), preferred_element_type=F32
    )


def mul(left, right):
    return contract(left, right, 1, 0)


def mul_nt(left, right):
    return contract(left, right, 1, 1)


def mul_tn(left, right):
    return contract(left, right, 0, 0)


def normalise(signal):
    centre = signal - jnp.mean(signal, axis=-1, keepdims=True)
    inverse = lax.rsqrt(jnp.mean(centre * centre, axis=-1, keepdims=True) + EPSILON)
    return centre * inverse, inverse


def norm_back(grad, scaled, inverse, gain):
    up = grad * gain
    return inverse * (
        up
        - jnp.mean(up, axis=-1, keepdims=True)
        - scaled * jnp.mean(up * scaled, axis=-1, keepdims=True)
    )


def col_sum(array):
    return jnp.sum(array.astype(F32), axis=0, keepdims=True)


def head_of_lane(rows):
    return lax.broadcasted_iota(jnp.int32, (rows, WIDE), 1) // DH


def stacked(block, lane_head):
    zero = jnp.zeros_like(block)
    return jnp.concatenate([jnp.where(lane_head == h, block, zero) for h in range(GROUP)], axis=0)


def unstacked(result, lane_head, rows):
    picked = result[:rows]
    for h in range(1, GROUP):
        picked = jnp.where(lane_head == h, result[h * rows : (h + 1) * rows], picked)
    return picked


def attend_pair(p, bias, q_ref, k_ref, v_ref, w_ref, mix_ref):
    rows = q_ref.shape[1]
    lane_head = head_of_lane(rows)
    for g in range(HEADS // GROUP):
        cols = slice(g * WIDE, (g + 1) * WIDE)
        scores = mul_nt(stacked(q_ref[p, :, cols], lane_head), k_ref[p, :, cols]) + bias
        top = jnp.max(scores, axis=-1, keepdims=True)
        raised = jnp.exp(scores - top)
        total = jnp.sum(raised, axis=-1, keepdims=True)
        weights = (raised * (1.0 / total)).astype(BF)
        w_ref[p, g] = weights
        mixed = mul(weights, v_ref[p, :, cols])
        mix_ref[p, :, cols] = unstacked(mixed, lane_head, rows).astype(BF)


def attend_pair_back(p, q_ref, k_ref, v_ref, w_ref, grad_ref, gq_ref, gk_ref, gv_ref):
    rows = q_ref.shape[1]
    lane_head = head_of_lane(rows)
    for g in range(HEADS // GROUP):
        cols = slice(g * WIDE, (g + 1) * WIDE)
        grads = stacked(grad_ref[p, :, cols], lane_head)
        weights = w_ref[p, g]
        grad_w = mul_nt(grads, v_ref[p, :, cols])
        wide = weights.astype(F32)
        offset = jnp.sum(grad_w * wide, axis=-1, keepdims=True)
        grad_s = (wide * (grad_w - offset)).astype(BF)
        grad_q = unstacked(mul(grad_s, k_ref[p, :, cols]), lane_head, rows)
        gq_ref[p, :, cols] = (grad_q * SCALE).astype(BF)
        gk_ref[p, :, cols] = mul_tn(grad_s, stacked(q_ref[p, :, cols], lane_head)).astype(BF)
        gv_ref[p, :, cols] = mul_tn(weights, grads).astype(BF)


def flat(ref):
    value = ref[...]
    return value.reshape(value.shape[0] * value.shape[1], value.shape[2])


Z, Y, X, CORE = 4, 2, 2, 2
SLOTS = [(y, x, c) for y in range(Y) for x in range(X) for c in range(CORE)]
PIECE = 64
FEED_ROWS = 4 * PIECE + 256
SMALL_ROWS = 48
GAIN, SHIFT, TABLE, HIDDEN = 16, 32, 48, 112
SMALL = 128


def places(meta, slot):
    base = meta.shape[0] - 4
    y, x, c = slot
    return y ^ meta[base + 1], (x ^ meta[base + 2]) * CORE + (c ^ meta[base + 3])


def load_copies(meta, sources, held, sems):
    copies = []
    for i, slot in enumerate(SLOTS):
        row, panel = places(meta, slot)
        copies.append(pltpu.make_async_copy(sources[i], held.at[panel, :, row], sems.at[i]))
    return copies


def store_copies(meta, held, targets, sems):
    copies = []
    for i, slot in enumerate(SLOTS):
        row, panel = places(meta, slot)
        copies.append(pltpu.make_async_copy(held.at[panel, :, row], targets[i], sems.at[i]))
    return copies


def start(copies):
    for copy in copies:
        copy.start()


def wait(copies):
    for copy in copies:
        copy.wait()


def joined(value):
    return value.reshape(-1, value.shape[-1])


def square(held, index):
    span = slice(PIECE * index, PIECE * (index + 1))
    return jnp.concatenate([joined(held[i, :, :, span]) for i in range(X * CORE)], axis=1)


def keep(held, index, value):
    span = slice(PIECE * index, PIECE * (index + 1))
    for i in range(X * CORE):
        part = value[:, i * 128 : (i + 1) * 128].astype(BF)
        held[i, :, :, span] = part.reshape(Z, Y, PIECE, 128)


def self_forward_kernel(meta, target, *refs):
    pieces, refs = refs[:8], refs[8:]
    in_a, q, k, v, w, mix, after, vecs, fbias, embedded, held, sems = refs
    loads = load_copies(meta, pieces, held, sems)
    start(loads)
    pairs, length, width = target.shape
    shape = target.shape
    wait(loads)
    every = [held[0, z, y, 4 * PIECE :].astype(F32) for z in range(Z) for y in range(Y)]
    vecs[...] = jnp.concatenate([one[:HIDDEN, :64] for one in every], axis=1)
    for d, one in enumerate(every):
        for i in range(2):
            fbias[:, d * 256 + i * 128 : d * 256 + (i + 1) * 128] = one[HIDDEN + i : HIDDEN + i + 1]
    for p in range(pairs):
        emb = target[p].astype(F32) + vecs[pl.ds(TABLE + meta[pairs + p], 1), :]
        embedded[p] = emb
        scaled, unused = normalise(emb)
        in_a[p] = (scaled * vecs[GAIN : GAIN + 1] + vecs[SHIFT : SHIFT + 1]).astype(BF)
    x = flat(in_a)
    q[...] = ((mul(x, square(held, 0)) + vecs[0:1]).astype(BF) * SCALE).reshape(shape)
    k[...] = mul(x, square(held, 1)).astype(BF).reshape(shape)
    v[...] = (mul(x, square(held, 2)) + vecs[1:2]).astype(BF).reshape(shape)

    def pair(p, carry):
        spot = lax.broadcasted_iota(jnp.int32, (1, length), 1)
        bias = jnp.where(spot < meta[p], 0.0, -1e30)
        attend_pair(p, bias, q, k, v, w, mix)
        return carry

    lax.fori_loop(0, pairs, pair, 0)
    after[...] = embedded[...] + (mul(flat(mix), square(held, 3)) + vecs[2:3]).reshape(shape)


def cross_forward_kernel(meta, after_self, mem_0, mem_1, mem_2, mem_3, vecs, *refs):
    pieces, refs = refs[:8], refs[8:]
    memory, in_b, q, k, v, w, mix, after, held, sems, mem_sems = refs
    pairs, length, width = after_self.shape
    shape = after_self.shape
    source = memory.shape[1]
    base = meta.shape[0] - 4
    mine = meta[base + 2] * CORE + meta[base + 3]
    part = source // (X * CORE)
    mem_loads = [
        pltpu.make_async_copy(
            one, memory.at[:, pl.ds(pl.multiple_of((mine ^ i) * part, part), part), :], mem_sems.at[i]
        )
        for i, one in enumerate((mem_0, mem_1, mem_2, mem_3))
    ]
    start(mem_loads)
    loads = load_copies(meta, pieces, held, sems)
    start(loads)
    scaled, unused = normalise(flat(after_self))
    x = (scaled * vecs[GAIN + 1 : GAIN + 2] + vecs[SHIFT + 1 : SHIFT + 2]).astype(BF)
    in_b[...] = x.reshape(shape)
    wait(loads)
    q[...] = ((mul(x, square(held, 0)) + vecs[3:4]).astype(BF) * SCALE).reshape(shape)
    wait(mem_loads)
    m = flat(memory)
    k[...] = mul(m, square(held, 1)).astype(BF).reshape(memory.shape)
    v[...] = (mul(m, square(held, 2)) + vecs[4:5]).astype(BF).reshape(memory.shape)

    def pair(p, carry):
        spot = lax.broadcasted_iota(jnp.int32, (1, source), 1)
        begin = meta[2 * pairs + p]
        end = begin + meta[3 * pairs + p]
        bias = jnp.where((spot >= begin) & (spot < end), 0.0, -1e30)
        attend_pair(p, bias, q, k, v, w, mix)
        return carry

    lax.fori_loop(0, pairs, pair, 0)
    after[...] = after_self[...] + (mul(flat(mix), square(held, 3)) + vecs[5:6]).reshape(shape)


def gelu_parts(value):
    size = jnp.abs(value) * math.sqrt(0.5)
    t = 1.0 / (1.0 + 0.3275911 * size)
    bell = jnp.exp(-0.5 * value * value)
    tail = (
        t
        * (
            0.5 * 0.254829592
            + t
            * (
                0.5 * -0.284496736
                + t * (0.5 * 1.421413741 + t * (0.5 * -1.453152027 + t * (0.5 * 1.061405429)))
            )
        )
        * bell
    )
    below = jnp.where(value < 0, tail, 1.0 - tail)
    slope = below + value * bell * (1.0 / math.sqrt(2.0 * math.pi))
    return value * below, slope


def feed_kernel(meta, after_cross, cot, vecs, feed_bias, *refs):
    pieces, refs = refs[:8], refs[8:]
    layer_out, gres, sums, dbias = refs[:4]
    targets, refs = refs[4:12], refs[12:]
    held, kept, x_c, out_acc, in_acc, sems, out_sems = refs
    loads = load_copies(meta, pieces, held, sems)
    start(loads)
    stores = store_copies(meta, kept, targets, out_sems)
    shape = after_cross.shape
    signal = flat(after_cross)
    scaled, inverse = normalise(signal)
    gain = vecs[GAIN + 2 : GAIN + 3]
    x_c[...] = (scaled * gain + vecs[SHIFT + 2 : SHIFT + 3]).astype(BF)
    wait(loads)
    block = 512
    for j in range(4):
        cols = slice(j * block, (j + 1) * block)
        w_in = jnp.concatenate(
            [joined(held[j, :, :, PIECE * i : PIECE * (i + 1)]) for i in range(4)], axis=1
        )
        w_out = jnp.concatenate([joined(held[i, j, :, 4 * PIECE :]) for i in range(4)], axis=1)
        c = flat(cot)
        x = x_c[...]
        pre = mul(x, w_in) + feed_bias[:, cols]
        value, slope = gelu_parts(pre)
        act = value.astype(BF)
        grad_pre = (mul_nt(c, w_out) * slope).astype(BF)
        out_part = mul(act, w_out)
        in_part = mul_nt(grad_pre, w_in)
        if j == 0:
            out_acc[...] = out_part
            in_acc[...] = in_part
        else:
            out_acc[...] += out_part
            in_acc[...] += in_part
        d_out = mul_tn(act, c)
        for i in range(4):
            part = d_out[:, i * 128 : (i + 1) * 128].astype(BF)
            kept[i, j, :, 4 * PIECE :] = part.reshape(Y, 256, 128)
        d_in = mul_tn(x, grad_pre)
        for i in range(4):
            part = d_in[:, i * 128 : (i + 1) * 128].astype(BF)
            kept[j, :, :, PIECE * i : PIECE * (i + 1)] = part.reshape(Z, Y, PIECE, 128)
        dbias[:, cols] = col_sum(grad_pre)
    start(stores)
    layer_out[...] = (signal + out_acc[...] + vecs[6:7]).astype(BF).reshape(shape)
    grad = in_acc[...]
    wide_cot = flat(cot).astype(F32)
    sums[0:1] = col_sum(wide_cot)
    sums[1:2] = col_sum(grad * scaled)
    sums[2:3] = col_sum(grad)
    gres[...] = (wide_cot + norm_back(grad, scaled, inverse, gain)).reshape(shape)
    wait(stores)


def cross_back_kernel(meta, gres, after_self, in_b, q, k, v, w, mix, memory, vecs, *refs):
    pieces, refs = refs[:8], refs[8:]
    gres_out, gmem_0, gmem_1, gmem_2, gmem_3, sums = refs[:6]
    targets, refs = refs[6:14], refs[14:]
    gmix, gq, gk, gv, gmem, held, kept, sems, out_sems, mem_sems = refs
    loads = load_copies(meta, pieces, held, sems)
    start(loads)
    stores = store_copies(meta, kept, targets, out_sems)
    shape = gres.shape
    pairs = shape[0]
    grad = flat(gres).astype(BF)
    sums[0:1] = col_sum(grad)
    keep(kept, 3, mul_tn(flat(mix), grad))
    wait(loads)
    gmix[...] = mul_nt(grad, square(held, 3)).astype(BF).reshape(shape)

    def pair(p, carry):
        attend_pair_back(p, q, k, v, w, gmix, gq, gk, gv)
        return carry

    lax.fori_loop(0, pairs, pair, 0)
    gq_f, gk_f, gv_f, m = flat(gq), flat(gk), flat(gv), flat(memory)
    sums[1:2] = col_sum(gq_f)
    sums[2:3] = col_sum(gv_f)
    keep(kept, 0, mul_tn(flat(in_b), gq_f))
    keep(kept, 1, mul_tn(m, gk_f))
    keep(kept, 2, mul_tn(m, gv_f))
    start(stores)
    grad_m = mul_nt(gk_f, square(held, 1)) + mul_nt(gv_f, square(held, 2))
    gmem[...] = grad_m.astype(BF).reshape(memory.shape)
    base = meta.shape[0] - 4
    mine = meta[base + 2] * CORE + meta[base + 3]
    part = memory.shape[1] // (X * CORE)
    mem_stores = [
        pltpu.make_async_copy(
            gmem.at[:, pl.ds(pl.multiple_of((mine ^ i) * part, part), part), :], one, mem_sems.at[i]
        )
        for i, one in enumerate((gmem_0, gmem_1, gmem_2, gmem_3))
    ]
    start(mem_stores)
    grad_in = mul_nt(gq_f, square(held, 0))
    scaled, inverse = normalise(flat(after_self))
    sums[3:4] = col_sum(grad_in * scaled)
    sums[4:5] = col_sum(grad_in)
    back = norm_back(grad_in, scaled, inverse, vecs[GAIN + 1 : GAIN + 2])
    gres_out[...] = gres[...] + back.reshape(shape)
    wait(stores)
    wait(mem_stores)


def self_back_kernel(meta, gres, target, in_a, q, k, v, w, mix, vecs, sums_b, sums_c, dbias, *refs):
    pieces, refs = refs[:8], refs[8:]
    gtarget, targets, refs = refs[0], refs[1:9], refs[9:]
    gmix, gq, gk, gv, sums, gtable, held, kept, sems, out_sems = refs
    loads = load_copies(meta, pieces, held, sems)
    start(loads)
    stores = store_copies(meta, kept, targets, out_sems)
    shape = gres.shape
    pairs = shape[0]
    grad = flat(gres).astype(BF)
    sums[0:1] = col_sum(grad)
    keep(kept, 3, mul_tn(flat(mix), grad))
    wait(loads)
    gmix[...] = mul_nt(grad, square(held, 3)).astype(BF).reshape(shape)

    def pair(p, carry):
        attend_pair_back(p, q, k, v, w, gmix, gq, gk, gv)
        return carry

    lax.fori_loop(0, pairs, pair, 0)
    gq_f, gk_f, gv_f, x = flat(gq), flat(gk), flat(gv), flat(in_a)
    sums[1:2] = col_sum(gq_f)
    sums[2:3] = col_sum(gv_f)
    grad_in = jnp.zeros((pairs * shape[1], shape[2]), F32)
    for i, one in enumerate((gq_f, gk_f, gv_f)):
        keep(kept, i, mul_tn(x, one))
        grad_in += mul_nt(one, square(held, i))
    grad_in = grad_in.reshape(shape)
    gtable[...] = jnp.zeros_like(gtable)
    for p in range(pairs):
        emb = target[p].astype(F32) + vecs[pl.ds(TABLE + meta[pairs + p], 1), :]
        scaled, inverse = normalise(emb)
        gain_part = col_sum(grad_in[p] * scaled)
        shift_part = col_sum(grad_in[p])
        if p == 0:
            sums[3:4] = gain_part
            sums[4:5] = shift_part
        else:
            sums[3:4] += gain_part
            sums[4:5] += shift_part
        out = gres[p] + norm_back(grad_in[p], scaled, inverse, vecs[GAIN : GAIN + 1])
        gtarget[p] = out
        gtable[pl.ds(meta[pairs + p], 1), :] += col_sum(out)
    rows = [sums[1:2], sums[2:3], sums[0:1], sums_b[1:2], sums_b[2:3], sums_b[0:1], sums_c[0:1]]
    rows += [sums[3:4], sums_b[3:4], sums_c[1:2], sums[4:5], sums_b[4:5], sums_c[2:3]]
    vectors = jnp.concatenate(rows + [jnp.zeros((16 - len(rows), shape[2]), F32)], axis=0)
    steps = gtable.shape[0] // 2
    for d in range(Z * Y):
        lanes = slice(d * 64, (d + 1) * 64)
        top = jnp.concatenate([vectors[:, lanes], jnp.zeros((16, 64), F32)], axis=1)
        low = jnp.concatenate([gtable[:steps, lanes], gtable[steps:, lanes]], axis=1)
        tail = [dbias[:, d * 256 + i * 128 : d * 256 + (i + 1) * 128] for i in range(2)]
        fill = jnp.zeros((SMALL_ROWS - 16 - steps - 2, 128), F32)
        part = jnp.concatenate([top, low, *tail, fill], axis=0).astype(BF)
        for i in range(X * CORE):
            kept[i, d // Y, d % Y, 4 * PIECE :] = part
    start(stores)
    wait(stores)


HBM = pl.ANY
VMEM = pltpu.VMEM
SMEM = pltpu.SMEM


def call(kernel, name, args, spaces, outs, scratch, micros=1):
    cost = pl.CostEstimate(flops=micros * 10**9, bytes_accessed=micros * 3 * 10**6, transcendentals=0)
    return pl.pallas_call(
        kernel,
        out_shape=[jax.ShapeDtypeStruct(s, d) for s, d, unused in outs],
        in_specs=[pl.BlockSpec(memory_space=m) for m in spaces],
        out_specs=[pl.BlockSpec(memory_space=m) for unused, unused2, m in outs],
        scratch_shapes=scratch,
        compiler_params=pltpu.CompilerParams(vmem_limit_bytes=VMEM_LIMIT),
        cost_estimate=cost,
        name=name,
    )(*args)


def held_like(pieces):
    z, rows, lanes = pieces[0].shape
    return VMEM((X * CORE, z, Y, rows, lanes), BF)


def sems(*shape):
    return pltpu.SemaphoreType.DMA(shape)


def self_forward(meta, target, pieces):
    shape = target.shape
    pairs, length, width = shape
    w_shape = (pairs, HEADS // GROUP, GROUP * length, length)
    return call(
        self_forward_kernel,
        "self_forward",
        [meta, target, *pieces],
        [SMEM, VMEM] + [HBM] * 8,
        [(shape, BF, VMEM)] * 4
        + [(w_shape, BF, VMEM), (shape, BF, VMEM), (shape, F32, VMEM)]
        + [((HIDDEN, width), F32, VMEM), ((1, 4 * width), F32, VMEM)],
        [VMEM(shape, F32), held_like(pieces), sems(8)],
        15,
    )


def cross_forward(meta, after_self, mems, vecs, pieces):
    shape = after_self.shape
    pairs, length, width = shape
    source = mems[0].shape[1] * X * CORE
    m_shape = (pairs, source, width)
    w_shape = (pairs, HEADS // GROUP, GROUP * length, source)
    return call(
        cross_forward_kernel,
        "cross_forward",
        [meta, after_self, *mems, vecs, *pieces],
        [SMEM, VMEM] + [HBM] * 4 + [VMEM] + [HBM] * 8,
        [(m_shape, BF, VMEM)] + [(shape, BF, VMEM)] * 2 + [(m_shape, BF, VMEM)] * 2
        + [(w_shape, BF, VMEM), (shape, BF, VMEM), (shape, F32, VMEM)],
        [held_like(pieces), sems(8), sems(4)],
        15,
    )


def feed(meta, after_cross, cot, vecs, feed_bias, pieces):
    shape = after_cross.shape
    tokens, width = shape[0] * shape[1], shape[2]
    return call(
        feed_kernel,
        "feed",
        [meta, after_cross, cot, vecs, feed_bias, *pieces],
        [SMEM] + [VMEM] * 4 + [HBM] * 8,
        [(shape, BF, VMEM), (shape, F32, VMEM), ((3, width), F32, VMEM), (feed_bias.shape, F32, VMEM)]
        + [(pieces[0].shape, BF, HBM)] * 8,
        [held_like(pieces)] * 2
        + [VMEM((tokens, width), BF), VMEM((tokens, width), F32), VMEM((tokens, width), F32)]
        + [sems(8)] * 2,
        26,
    )


def cross_back(meta, gres, after_self, kept, memory, vecs, pieces):
    shape = gres.shape
    mshape = memory.shape
    part = (mshape[0], mshape[1] // (X * CORE), mshape[2])
    return call(
        cross_back_kernel,
        "cross_back",
        [meta, gres, after_self, *kept, memory, vecs, *pieces],
        [SMEM] + [VMEM] * 10 + [HBM] * 8,
        [(shape, F32, VMEM)] + [(part, BF, HBM)] * 4 + [((5, shape[2]), F32, VMEM)]
        + [((Z, 256, 128), BF, HBM)] * 8,
        [VMEM(shape, BF), VMEM(shape, BF)] + [VMEM(mshape, BF)] * 3 + [held_like(pieces)] * 2
        + [sems(8)] * 2 + [sems(4)],
        20,
    )


def self_back(meta, gres, target, kept, vecs, sums_b, sums_c, dbias, pieces, steps):
    shape = gres.shape
    target_shape = (Z, 4 * PIECE + SMALL_ROWS, 128)
    return call(
        self_back_kernel,
        "self_back",
        [meta, gres, target, *kept, vecs, sums_b, sums_c, dbias, *pieces],
        [SMEM] + [VMEM] * 12 + [HBM] * 8,
        [(shape, F32, VMEM)] + [(target_shape, BF, HBM)] * 8,
        [VMEM(shape, BF)] * 4
        + [VMEM((5, shape[2]), F32), VMEM((steps, shape[2]), F32)]
        + [held_like(pieces), VMEM((X * CORE, Z, Y, *target_shape[1:]), BF)]
        + [sems(8)] * 2,
        20,
    )


BOTH = ("dp", "mem")


def swap(array, mask):
    count = lax.axis_size("dp") * lax.axis_size("mem")
    return lax.ppermute(array, BOTH, [(i, i ^ mask) for i in range(count)])


def pack_kernel(*refs):
    squares, (w_in, w_out, biases, f_bias, gain, shift, table) = refs[:8], refs[8:15]
    self_out, cross_out, feed_out, stage = refs[15:]
    for i in range(4):
        self_out[64 * i : 64 * (i + 1)] = squares[i][...]
        cross_out[64 * i : 64 * (i + 1)] = squares[4 + i][...]
        feed_out[64 * i : 64 * (i + 1)] = w_in[:, 128 * i : 128 * (i + 1)]
    feed_out[256:512] = w_out[...]
    stage[...] = jnp.zeros_like(stage)
    stage[0:7, :64] = biases[...].astype(F32)
    stage[GAIN : GAIN + 3, :64] = gain[...].astype(F32)
    stage[SHIFT : SHIFT + 3, :64] = shift[...].astype(F32)
    stage[TABLE : TABLE + table.shape[0], :64] = table[...].astype(F32)
    stage[HIDDEN : HIDDEN + 2] = f_bias[...].astype(F32)
    self_out[256:384] = stage[...].astype(BF)


def assemble_kernel(meta, a, b, c, d, out):
    mine = meta[meta.shape[0] - 4]
    for i, one in enumerate((a, b, c, d)):
        out[mine ^ i] = one[...]


def assemble(meta, parts):
    return call(
        assemble_kernel,
        "assemble",
        [meta, *parts],
        [SMEM] + [VMEM] * 4,
        [((Z, *parts[0].shape), BF, VMEM)],
        [],
    )[0]


def gather_z(meta, packed):
    return assemble(meta, [packed, swap(packed, 8), swap(packed, 16), swap(packed, 24)])


def spread(along_z):
    halves = [along_z, swap(along_z, 2), swap(along_z, 4), swap(along_z, 6)]
    out = []
    for one in halves:
        out += [one, swap(one, 1)]
    return out


def merge_kernel(meta, a, b, c, d, own, s1, s2, s3):
    mine = meta[meta.shape[0] - 4]

    def total(z):
        return (a[z].astype(F32) + b[z].astype(F32)) + (c[z].astype(F32) + d[z].astype(F32))

    own[...] = total(mine)
    s1[...] = total(mine ^ 1).astype(BF)
    s2[...] = total(mine ^ 2).astype(BF)
    s3[...] = total(mine ^ 3).astype(BF)


def final_parts(refs, outs):
    own, a, b, c = refs

    def total(span):
        return (own[span] + a[span].astype(F32)) + (b[span].astype(F32) + c[span].astype(F32))

    at = 0
    for out in outs:
        rows = out.shape[0]
        for i in range(out.shape[1] // 128):
            out[:, 128 * i : 128 * (i + 1)] = total(slice(at, at + rows))
            at += rows
    return total, at


def final_kernel(*refs):
    final_parts(refs[:4], refs[4:])


def final_small_kernel(*refs):
    outs, (biases, f_bias, gain, shift, table) = refs[4:8], refs[8:]
    total, at = final_parts(refs[:4], outs)
    part = total(slice(at, at + SMALL_ROWS))
    biases[...] = part[0:7, :64]
    gain[...] = part[7:10, :64]
    shift[...] = part[10:13, :64]
    half = table.shape[0] // 2
    table[:half] = part[16 : 16 + half, :64]
    table[half:] = part[16 : 16 + half, 64:]
    f_bias[...] = part[16 + half : 18 + half]


def add(left, right):
    return (left.astype(F32) + right.astype(F32)).astype(BF)


def core_sums(slots):
    return [add(slots[i], swap(slots[i + 1], 1)) for i in range(0, 8, 2)]


def chip_sums(meta, pairs):
    near = [pairs[0], swap(pairs[1], 2), swap(pairs[2], 4), swap(pairs[3], 6)]
    z, rows, lanes = near[0].shape
    return call(
        merge_kernel,
        "merge",
        [meta, *near],
        [SMEM] + [VMEM] * 4,
        [((rows, lanes), F32, VMEM)] + [((rows, lanes), BF, VMEM)] * 3,
        [],
    )


def slice_sums(kernel, parts, shapes):
    own, s1, s2, s3 = parts
    return call(
        kernel,
        "final",
        [own, swap(s1, 8), swap(s2, 16), swap(s3, 24)],
        [VMEM] * 4,
        [(s, F32, VMEM) for s in shapes],
        [],
    )


def place_kernel(meta, a, b, c, d, out):
    base = meta.shape[0] - 4
    mine = meta[base + 2] * CORE + meta[base + 3]
    pairs = a.shape[0]
    for i, one in enumerate((a, b, c, d)):
        for p in range(pairs):
            out[(mine ^ i) * pairs + p] = one[p].astype(F32)


def swap_memory(memory, pairs):
    mine = lax.axis_index("mem")
    parts = [lax.dynamic_slice_in_dim(memory, (mine ^ i) * pairs, pairs) for i in range(4)]
    return [parts[0]] + [swap(parts[i], i) for i in range(1, 4)]


def return_memory(meta, parts, shape):
    parts = [parts[0]] + [swap(parts[i], i) for i in range(1, 4)]
    return call(place_kernel, "place", [meta, *parts], [SMEM] + [VMEM] * 4, [(shape, F32, VMEM)], [])[0]


def slots_of(wide):
    rows, cols = wide.shape
    cut = wide.reshape(Z, Y, rows // (Z * Y), X, CORE, cols // (X * CORE))
    return [cut[:, y, :, x, c] for y, x, c in SLOTS]


def wide_of(slots):
    z, rows, cols = slots[0].shape
    cut = jnp.stack(slots).reshape(Y, X, CORE, z, rows, cols)
    return cut.transpose(3, 0, 4, 1, 2, 5).reshape(z * Y * rows, X * CORE * cols)


def gather_any(piece):
    return lax.all_gather(lax.all_gather(piece, "mem", axis=1, tiled=True), "dp", axis=0, tiled=True)


def scatter_any(wide):
    part = lax.psum_scatter(wide.astype(F32), "dp", scatter_dimension=0, tiled=True)
    return lax.psum_scatter(part, "mem", scatter_dimension=1, tiled=True)


def narrow_columns(slots):
    return [jnp.concatenate(jnp.split(one, 4, axis=2), axis=1) for one in slots]


def spread_any(groups, smalls):
    squares_a, squares_b, (w_in, w_out) = groups
    every = [[slots_of(gather_any(one)) for one in group] for group in (squares_a, squares_b)]
    biases, f_bias, gain, shift, table = [
        lax.all_gather(one, "dp", axis=one.ndim - 1, tiled=True) for one in smalls
    ]
    width = biases.shape[1]
    rows = jnp.zeros((HIDDEN, width), BF)
    rows = rows.at[:7].set(biases).at[GAIN : GAIN + 3].set(gain).at[SHIFT : SHIFT + 3].set(shift)
    rows = rows.at[TABLE : TABLE + table.shape[0]].set(table)
    cut = rows.reshape(HIDDEN, Z, Y, 64).transpose(1, 2, 0, 3)
    cut = jnp.concatenate([cut, jnp.zeros_like(cut)], axis=3)
    tail = jnp.pad(f_bias.reshape(Z, Y, 2, 128), ((0, 0), (0, 0), (0, SMALL - HIDDEN - 2), (0, 0)))
    small = jnp.concatenate([cut, tail], axis=2)
    group_a = [
        jnp.concatenate([one[i] for one in every[0][:4]] + [small[:, SLOTS[i][0]]], axis=1) for i in range(8)
    ]
    group_b = [jnp.concatenate([one[i] for one in every[1]], axis=1) for i in range(8)]
    ins = narrow_columns(slots_of(gather_any(w_in)))
    outs = slots_of(gather_any(w_out))
    group_c = [jnp.concatenate([ins[i], outs[i]], axis=1) for i in range(8)]
    return group_a, group_b, group_c


def reduce_any(slots, wide):
    if not wide:
        return [
            scatter_any(wide_of([one[:, 64 * i : 64 * (i + 1)] for one in slots])) for i in range(4)
        ]
    ins = [
        jnp.concatenate([one[:, 64 * j : 64 * (j + 1)] for j in range(4)], axis=2) for one in slots
    ]
    return [scatter_any(wide_of(ins)), scatter_any(wide_of([one[:, 256:512] for one in slots]))]


def reduce_small_any(slots, count):
    parts = [slots[i][:, 4 * PIECE :].astype(F32) for i in (0, 4)]
    part = jnp.stack(parts, axis=1).reshape(Z * Y, SMALL_ROWS, 128)
    vectors = part[:, :13, :64].transpose(1, 0, 2).reshape(13, -1)
    table = part[:, 16 : 16 + count // 2]
    table = jnp.concatenate([table[:, :, :64], table[:, :, 64:]], axis=1)
    rows = jnp.concatenate([vectors, table.transpose(1, 0, 2).reshape(count, -1)], axis=0)
    cut = lax.psum_scatter(lax.psum(rows, "mem"), "dp", scatter_dimension=1, tiled=True)
    f_bias = part[:, 16 + count // 2 : 18 + count // 2].reshape(-1)
    f_bias = lax.psum_scatter(lax.psum(f_bias, "mem"), "dp", scatter_dimension=0, tiled=True)
    return cut[:7], f_bias, cut[7:10], cut[10:13], cut[13:]


def shards(
    target, memory, time_steps, target_len, source_len, source_off, cotangent,
    self_query, self_key, self_value, self_out, cross_query, cross_key, cross_value, cross_out,
    feed_in, feed_out, biases, feed_bias, norm_gain, norm_shift, step_table,
):
    pairs = target.shape[0]
    steps = step_table.shape[0]
    dp, mem = lax.axis_index("dp"), lax.axis_index("mem")
    quick = lax.axis_size("dp") == Z * Y and lax.axis_size("mem") == X * CORE
    here = [dp // 2, dp % 2, mem // 2, mem % 2] if quick else [0, 0, 0, 0]
    meta = jnp.concatenate(
        [
            target_len,
            time_steps,
            lax.dynamic_slice_in_dim(source_off, mem * pairs, pairs),
            lax.dynamic_slice_in_dim(source_len, mem * pairs, pairs),
            jnp.stack([jnp.asarray(i, jnp.int32) for i in here]),
        ]
    )
    squares_a = (self_query, self_key, self_value, self_out)
    squares_b = (cross_query, cross_key, cross_value, cross_out)
    if quick:
        packed = call(
            pack_kernel,
            "pack",
            [*squares_a, *squares_b, feed_in, feed_out, biases, feed_bias.reshape(2, 128)]
            + [norm_gain, norm_shift, step_table],
            [VMEM] * 15,
            [((256 + SMALL, 128), BF, VMEM), ((256, 128), BF, VMEM), ((512, 128), BF, VMEM)],
            [VMEM((SMALL, 128), F32)],
        )
        self_z = gather_z(meta, packed[0])
        self_z, later, own = lax.optimization_barrier((self_z, packed[1:], memory))
        self_w = spread(self_z)
        cross_w, feed_w = [spread(gather_z(meta, one)) for one in later]
        mems = swap_memory(own, pairs)
    else:
        self_w, cross_w, feed_w = spread_any(
            (squares_a, squares_b, (feed_in, feed_out)),
            (biases, feed_bias, norm_gain, norm_shift, step_table),
        )
        own = lax.all_to_all(memory, "mem", 0, 1, tiled=True)
        mems = jnp.split(own, X * CORE, axis=1)

    in_a, q_a, k_a, v_a, w_a, mix_a, after_self, vecs, fbias = self_forward(meta, target, self_w)
    own_memory, in_b, q_b, k_b, v_b, w_b, mix_b, after_cross = cross_forward(
        meta, after_self, mems, vecs, cross_w
    )
    layer_out, gres_c, sums_c, d_fbias, *d_feed = feed(
        meta, after_cross, cotangent, vecs, fbias, feed_w
    )
    back = cross_back(
        meta, gres_c, after_self, (in_b, q_b, k_b, v_b, w_b, mix_b), own_memory, vecs, cross_w
    )
    gres_b, gmem, sums_b, d_cross = back[0], back[1:5], back[5], back[6:]
    if quick:
        u_feed = core_sums(d_feed)
        u_feed, gres_b = lax.optimization_barrier((u_feed, gres_b))
    grad_target, *d_self = self_back(
        meta, gres_b, target, (in_a, q_a, k_a, v_a, w_a, mix_a), vecs, sums_b, sums_c, d_fbias, self_w, steps
    )
    if quick:
        square_shape = self_query.shape
        m_feed = chip_sums(meta, u_feed)
        m_cross = chip_sums(meta, core_sums(d_cross))
        m_self = chip_sums(meta, core_sums(d_self))
        grad_memory = return_memory(meta, gmem, memory.shape)
        g_feed = slice_sums(final_kernel, m_feed, (feed_in.shape, feed_out.shape))
        g_cross = slice_sums(final_kernel, m_cross, (square_shape,) * 4)
        small_shapes = (biases.shape, (2, 128), norm_gain.shape, norm_shift.shape, step_table.shape)
        out = slice_sums(final_small_kernel, m_self, (square_shape,) * 4 + small_shapes)
        g_self, (g_bias, g_fbias, g_gain, g_shift, g_table) = out[:4], out[4:]
        g_fbias = g_fbias.reshape(feed_bias.shape)
    else:
        whole = jnp.concatenate(gmem, axis=1)
        grad_memory = lax.all_to_all(whole, "mem", 1, 0, tiled=True).astype(F32)
        g_feed = reduce_any(d_feed, True)
        g_cross = reduce_any(d_cross, False)
        g_self = reduce_any(d_self, False)
        g_bias, g_fbias, g_gain, g_shift, g_table = reduce_small_any(d_self, steps)
    return (
        layer_out, grad_target, grad_memory, *g_self, *g_cross, *g_feed,
        g_bias, g_fbias, g_gain, g_shift, g_table,
    )


def solution(mesh):
    rows = P(BOTH, None, None)
    piece = P("dp", "mem")
    vector = P(None, "dp")
    mem_rows = P("dp", "mem", None)
    return jax.shard_map(
        shards,
        mesh=mesh,
        in_specs=(rows, mem_rows, P(BOTH), P(BOTH), P("dp"), P("dp"), rows)
        + (piece,) * 10
        + (vector, P("dp"), vector, vector, vector),
        out_specs=(rows, rows, mem_rows) + (piece,) * 10 + (vector, P("dp"), vector, vector, vector),
        check_vma=False,
    )
```

```python
import functools
import math

import jax
import jax.numpy as jnp
from jax import lax
from jax.experimental import pallas as pl
from jax.experimental.pallas import tpu as pltpu
from jax.sharding import PartitionSpec as P

HEADS = 8
DH = 64
GROUP = 4
WIDE = GROUP * DH
EPSILON = 1e-05
SCALE = 1.0 / math.sqrt(DH)
BF = jnp.bfloat16
F32 = jnp.float32
VMEM_LIMIT = 60 * 2**20


def contract(left, right, left_dim, right_dim):
    return lax.dot_general(
        left, right, (((left_dim,), (right_dim,)), ((), ())), preferred_element_type=F32
    )


def mul(left, right):
    return contract(left, right, 1, 0)


def mul_nt(left, right):
    return contract(left, right, 1, 1)


def mul_tn(left, right):
    return contract(left, right, 0, 0)


def normalise(signal):
    centre = signal - jnp.mean(signal, axis=-1, keepdims=True)
    inverse = lax.rsqrt(jnp.mean(centre * centre, axis=-1, keepdims=True) + EPSILON)
    return centre * inverse, inverse


def norm_back(grad, scaled, inverse, gain):
    up = grad * gain
    return inverse * (
        up
        - jnp.mean(up, axis=-1, keepdims=True)
        - scaled * jnp.mean(up * scaled, axis=-1, keepdims=True)
    )


def col_sum(array):
    return jnp.sum(array.astype(F32), axis=0, keepdims=True)


def head_of_lane(rows):
    return lax.broadcasted_iota(jnp.int32, (rows, WIDE), 1) // DH


def stacked(block, lane_head):
    zero = jnp.zeros_like(block)
    return jnp.concatenate([jnp.where(lane_head == h, block, zero) for h in range(GROUP)], axis=0)


def unstacked(result, lane_head, rows):
    picked = result[:rows]
    for h in range(1, GROUP):
        picked = jnp.where(lane_head == h, result[h * rows : (h + 1) * rows], picked)
    return picked


def attend_pair(p, bias, q_ref, k_ref, v_ref, w_ref, mix_ref):
    rows = q_ref.shape[1]
    lane_head = head_of_lane(rows)
    for g in range(HEADS // GROUP):
        cols = slice(g * WIDE, (g + 1) * WIDE)
        scores = mul_nt(stacked(q_ref[p, :, cols], lane_head), k_ref[p, :, cols]) + bias
        top = jnp.max(scores, axis=-1, keepdims=True)
        raised = jnp.exp(scores - top)
        total = jnp.sum(raised, axis=-1, keepdims=True)
        weights = (raised * (1.0 / total)).astype(BF)
        w_ref[p, g] = weights
        mixed = mul(weights, v_ref[p, :, cols])
        mix_ref[p, :, cols] = unstacked(mixed, lane_head, rows).astype(BF)


def attend_pair_back(p, q_ref, k_ref, v_ref, w_ref, grad_ref, gq_ref, gk_ref, gv_ref):
    rows = q_ref.shape[1]
    lane_head = head_of_lane(rows)
    for g in range(HEADS // GROUP):
        cols = slice(g * WIDE, (g + 1) * WIDE)
        grads = stacked(grad_ref[p, :, cols], lane_head)
        weights = w_ref[p, g]
        grad_w = mul_nt(grads, v_ref[p, :, cols])
        wide = weights.astype(F32)
        offset = jnp.sum(grad_w * wide, axis=-1, keepdims=True)
        grad_s = (wide * (grad_w - offset)).astype(BF)
        grad_q = unstacked(mul(grad_s, k_ref[p, :, cols]), lane_head, rows)
        gq_ref[p, :, cols] = (grad_q * SCALE).astype(BF)
        gk_ref[p, :, cols] = mul_tn(grad_s, stacked(q_ref[p, :, cols], lane_head)).astype(BF)
        gv_ref[p, :, cols] = mul_tn(weights, grads).astype(BF)


def flat(ref):
    value = ref[...]
    return value.reshape(value.shape[0] * value.shape[1], value.shape[2])


Z, Y, X, CORE = 4, 2, 2, 2
SLOTS = [(y, x, c) for y in range(Y) for x in range(X) for c in range(CORE)]
PIECE = 64
FEED_ROWS = 4 * PIECE + 256
SMALL_ROWS = 48
SELF_ROWS = 3 * PIECE + SMALL_ROWS
CROSS_ROWS = 5 * PIECE
GAIN, SHIFT, TABLE = 7, 10, 16


def places(meta, slot):
    base = meta.shape[0] - 4
    y, x, c = slot
    return y ^ meta[base + 1], (x ^ meta[base + 2]) * CORE + (c ^ meta[base + 3])


def load_copies(meta, sources, held, sems, first=0):
    copies = []
    rows = held.shape[-2]
    for i, slot in enumerate(SLOTS):
        row, panel = places(meta, slot)
        source = sources[i].at[:, pl.ds(first, rows)]
        copies.append(pltpu.make_async_copy(source, held.at[panel, :, row], sems.at[i]))
    return copies


def store_copies(meta, held, targets, sems):
    copies = []
    for i, slot in enumerate(SLOTS):
        row, panel = places(meta, slot)
        y, x, c = slot
        target = targets[c].at[y * X + x]
        copies.append(pltpu.make_async_copy(held.at[panel, :, row], target, sems.at[i]))
    return copies


def start(copies):
    for copy in copies:
        copy.start()


def wait(copies):
    for copy in copies:
        copy.wait()


def joined(value):
    return value.reshape(-1, value.shape[-1])


def square(held, index):
    span = slice(PIECE * index, PIECE * (index + 1))
    return jnp.concatenate([joined(held[i, :, :, span]) for i in range(X * CORE)], axis=1)


def keep(held, index, value):
    span = slice(PIECE * index, PIECE * (index + 1))
    for i in range(X * CORE):
        part = value[:, i * 128 : (i + 1) * 128].astype(BF)
        held[i, :, :, span] = part.reshape(Z, Y, PIECE, 128)


def self_forward_kernel(meta, target, *refs):
    pieces, refs = refs[:8], refs[8:]
    in_a, q, k, v, w, mix, vecs, fbias, held, sems = refs
    loads = load_copies(meta, pieces, held, sems)
    start(loads)
    pairs, length, width = target.shape
    shape = target.shape
    wait(loads)
    every = [held[0, z, y, 3 * PIECE :].astype(F32) for z in range(Z) for y in range(Y)]
    steps = (vecs.shape[0] - TABLE) // 2
    vecs[:TABLE] = jnp.concatenate([one[:TABLE, :64] for one in every], axis=1)
    for i in range(2):
        part = [one[TABLE : TABLE + steps, 64 * i : 64 * (i + 1)] for one in every]
        vecs[TABLE + i * steps : TABLE + (i + 1) * steps] = jnp.concatenate(part, axis=1)
    for d, one in enumerate(every):
        for i in range(2):
            at = TABLE + steps + i
            fbias[:, d * 256 + i * 128 : d * 256 + (i + 1) * 128] = one[at : at + 1]
    for p in range(pairs):
        emb = target[p].astype(F32) + vecs[pl.ds(TABLE + meta[pairs + p], 1), :]
        scaled, unused = normalise(emb)
        in_a[p] = (scaled * vecs[GAIN : GAIN + 1] + vecs[SHIFT : SHIFT + 1]).astype(BF)
    x = flat(in_a)
    q[...] = ((mul(x, square(held, 0)) + vecs[0:1]).astype(BF) * SCALE).reshape(shape)
    k[...] = mul(x, square(held, 1)).astype(BF).reshape(shape)
    v[...] = (mul(x, square(held, 2)) + vecs[1:2]).astype(BF).reshape(shape)

    def pair(p, carry):
        spot = lax.broadcasted_iota(jnp.int32, (1, length), 1)
        bias = jnp.where(spot < meta[p], 0.0, -1e30)
        attend_pair(p, bias, q, k, v, w, mix)
        return carry

    lax.fori_loop(0, pairs, pair, 0)


def cross_forward_kernel(meta, target, mix_a, mem_0, mem_1, mem_2, mem_3, vecs, *refs):
    pieces, refs = refs[:8], refs[8:]
    memory, after_self, in_b, q, k, v, w, mix, after, held, sems, mem_sems = refs
    pairs, length, width = target.shape
    shape = target.shape
    source = memory.shape[1]
    base = meta.shape[0] - 4
    mine = meta[base + 2] * CORE + meta[base + 3]
    part = source // (X * CORE)
    mem_loads = [
        pltpu.make_async_copy(
            one, memory.at[:, pl.ds(pl.multiple_of((mine ^ i) * part, part), part), :], mem_sems.at[i]
        )
        for i, one in enumerate((mem_0, mem_1, mem_2, mem_3))
    ]
    start(mem_loads)
    loads = load_copies(meta, pieces, held, sems, SELF_ROWS)
    start(loads)
    wait(loads)
    branch = (mul(flat(mix_a), square(held, 0)) + vecs[2:3]).reshape(shape)
    for p in range(pairs):
        row = vecs[pl.ds(TABLE + meta[pairs + p], 1), :]
        after_self[p] = target[p].astype(F32) + row + branch[p]
    scaled, unused = normalise(flat(after_self))
    x = (scaled * vecs[GAIN + 1 : GAIN + 2] + vecs[SHIFT + 1 : SHIFT + 2]).astype(BF)
    in_b[...] = x.reshape(shape)
    q[...] = ((mul(x, square(held, 1)) + vecs[3:4]).astype(BF) * SCALE).reshape(shape)
    wait(mem_loads)
    m = flat(memory)
    k[...] = mul(m, square(held, 2)).astype(BF).reshape(memory.shape)
    v[...] = (mul(m, square(held, 3)) + vecs[4:5]).astype(BF).reshape(memory.shape)

    def pair(p, carry):
        spot = lax.broadcasted_iota(jnp.int32, (1, source), 1)
        begin = meta[2 * pairs + p]
        end = begin + meta[3 * pairs + p]
        bias = jnp.where((spot >= begin) & (spot < end), 0.0, -1e30)
        attend_pair(p, bias, q, k, v, w, mix)
        return carry

    lax.fori_loop(0, pairs, pair, 0)
    after[...] = after_self[...] + (mul(flat(mix), square(held, 4)) + vecs[5:6]).reshape(shape)


def gelu_parts(value):
    size = jnp.abs(value) * math.sqrt(0.5)
    t = 1.0 / (1.0 + 0.3275911 * size)
    bell = jnp.exp(-0.5 * value * value)
    tail = (
        t
        * (
            0.5 * 0.254829592
            + t
            * (
                0.5 * -0.284496736
                + t * (0.5 * 1.421413741 + t * (0.5 * -1.453152027 + t * (0.5 * 1.061405429)))
            )
        )
        * bell
    )
    below = jnp.where(value < 0, tail, 1.0 - tail)
    slope = below + value * bell * (1.0 / math.sqrt(2.0 * math.pi))
    return value * below, slope


def feed_kernel(meta, after_cross, cot, vecs, feed_bias, *refs):
    pieces, refs = refs[:8], refs[8:]
    layer_out, gres, sums, dbias = refs[:4]
    targets, refs = refs[4:6], refs[6:]
    held, kept, x_c, out_acc, in_acc, sems, out_sems = refs
    loads = load_copies(meta, pieces, held, sems)
    start(loads)
    stores = store_copies(meta, kept, targets, out_sems)
    shape = after_cross.shape
    signal = flat(after_cross)
    scaled, inverse = normalise(signal)
    gain = vecs[GAIN + 2 : GAIN + 3]
    x_c[...] = (scaled * gain + vecs[SHIFT + 2 : SHIFT + 3]).astype(BF)
    wait(loads)
    block = 512
    for j in range(4):
        cols = slice(j * block, (j + 1) * block)
        w_in = jnp.concatenate(
            [joined(held[j, :, :, PIECE * i : PIECE * (i + 1)]) for i in range(4)], axis=1
        )
        w_out = jnp.concatenate([joined(held[i, j, :, 4 * PIECE :]) for i in range(4)], axis=1)
        c = flat(cot)
        x = x_c[...]
        pre = mul(x, w_in) + feed_bias[:, cols]
        value, slope = gelu_parts(pre)
        act = value.astype(BF)
        grad_pre = (mul_nt(c, w_out) * slope).astype(BF)
        out_part = mul(act, w_out)
        in_part = mul_nt(grad_pre, w_in)
        if j == 0:
            out_acc[...] = out_part
            in_acc[...] = in_part
        else:
            out_acc[...] += out_part
            in_acc[...] += in_part
        d_out = mul_tn(act, c)
        for i in range(4):
            part = d_out[:, i * 128 : (i + 1) * 128].astype(BF)
            kept[i, j, :, 4 * PIECE :] = part.reshape(Y, 256, 128)
        d_in = mul_tn(x, grad_pre)
        for i in range(4):
            part = d_in[:, i * 128 : (i + 1) * 128].astype(BF)
            kept[j, :, :, PIECE * i : PIECE * (i + 1)] = part.reshape(Z, Y, PIECE, 128)
        dbias[:, cols] = col_sum(grad_pre)
    start(stores)
    layer_out[...] = (signal + out_acc[...] + vecs[6:7]).astype(BF).reshape(shape)
    grad = in_acc[...]
    wide_cot = flat(cot).astype(F32)
    sums[0:1] = col_sum(wide_cot)
    sums[1:2] = col_sum(grad * scaled)
    sums[2:3] = col_sum(grad)
    gres[...] = (wide_cot + norm_back(grad, scaled, inverse, gain)).reshape(shape)
    wait(stores)


def cross_back_kernel(meta, gres, in_b, q, k, v, w, mix, memory, *refs):
    pieces, refs = refs[:8], refs[8:]
    gq, gk, gv, sums = refs[:4]
    targets, refs = refs[4:6], refs[6:]
    gmix, held, kept, sems, out_sems = refs
    loads = load_copies(meta, pieces, held, sems, SELF_ROWS)
    start(loads)
    stores = store_copies(meta, kept, targets, out_sems)
    shape = gres.shape
    grad = flat(gres).astype(BF)
    sums[0:1] = col_sum(grad)
    keep(kept, 3, mul_tn(flat(mix), grad))
    wait(loads)
    gmix[...] = mul_nt(grad, square(held, 4)).astype(BF).reshape(shape)

    def pair(p, carry):
        attend_pair_back(p, q, k, v, w, gmix, gq, gk, gv)
        return carry

    lax.fori_loop(0, shape[0], pair, 0)
    m = flat(memory)
    keep(kept, 0, mul_tn(flat(in_b), flat(gq)))
    keep(kept, 1, mul_tn(m, flat(gk)))
    keep(kept, 2, mul_tn(m, flat(gv)))
    start(stores)
    sums[1:2] = col_sum(flat(gq))
    sums[2:3] = col_sum(flat(gv))
    wait(stores)


def middle_back_kernel(meta, gres, gq, gk, gv, after_self, vecs, *refs):
    pieces, refs = refs[:8], refs[8:]
    gres_out, gmix_a, gmem_0, gmem_1, gmem_2, gmem_3, sums = refs[:7]
    gmem, held, sems, mem_sems = refs[7:]
    loads = load_copies(meta, pieces, held, sems, SELF_ROWS)
    start(loads)
    shape = gres.shape
    scaled, inverse = normalise(flat(after_self))
    wait(loads)
    grad_m = mul_nt(flat(gk), square(held, 2)) + mul_nt(flat(gv), square(held, 3))
    gmem[...] = grad_m.astype(BF).reshape(gmem.shape)
    base = meta.shape[0] - 4
    mine = meta[base + 2] * CORE + meta[base + 3]
    part = gmem.shape[1] // (X * CORE)
    mem_stores = [
        pltpu.make_async_copy(
            gmem.at[:, pl.ds(pl.multiple_of((mine ^ i) * part, part), part), :], one, mem_sems.at[i]
        )
        for i, one in enumerate((gmem_0, gmem_1, gmem_2, gmem_3))
    ]
    start(mem_stores)
    grad_in = mul_nt(flat(gq), square(held, 1))
    sums[0:1] = col_sum(grad_in * scaled)
    sums[1:2] = col_sum(grad_in)
    total = flat(gres) + norm_back(grad_in, scaled, inverse, vecs[GAIN + 1 : GAIN + 2])
    gres_out[...] = total.reshape(shape)
    grad_a = total.astype(BF)
    sums[2:3] = col_sum(grad_a)
    gmix_a[...] = mul_nt(grad_a, square(held, 0)).astype(BF).reshape(shape)
    wait(mem_stores)


def self_back_kernel(meta, gres, gmix, in_a, q, k, v, w, mix, *refs):
    gq, gk, gv, sums = refs[:4]
    targets, refs = refs[4:6], refs[6:]
    kept, out_sems = refs
    stores = store_copies(meta, kept, targets, out_sems)

    def pair(p, carry):
        attend_pair_back(p, q, k, v, w, gmix, gq, gk, gv)
        return carry

    lax.fori_loop(0, gmix.shape[0], pair, 0)
    x = flat(in_a)
    for i, one in enumerate((gq, gk, gv)):
        keep(kept, i, mul_tn(x, flat(one)))
    keep(kept, 3, mul_tn(flat(mix), flat(gres).astype(BF)))
    start(stores)
    sums[0:1] = col_sum(flat(gq))
    sums[1:2] = col_sum(flat(gv))
    wait(stores)


def last_back_kernel(meta, gres, gq, gk, gv, target, vecs, sums_a, sums_m, sums_b, sums_c, dbias, *refs):
    pieces, refs = refs[:8], refs[8:]
    gtarget, own, other, gtable, held, small, sums, sems, out_sems = refs
    loads = load_copies(meta, pieces, held, sems)
    start(loads)
    stores = store_copies(meta, small, (own, other), out_sems)
    shape = gres.shape
    pairs = shape[0]
    wait(loads)
    grad_in = (
        mul_nt(flat(gq), square(held, 0))
        + mul_nt(flat(gk), square(held, 1))
        + mul_nt(flat(gv), square(held, 2))
    ).reshape(shape)
    gtable[...] = jnp.zeros_like(gtable)
    for p in range(pairs):
        emb = target[p].astype(F32) + vecs[pl.ds(TABLE + meta[pairs + p], 1), :]
        scaled, inverse = normalise(emb)
        gain_part = col_sum(grad_in[p] * scaled)
        shift_part = col_sum(grad_in[p])
        if p == 0:
            sums[0:1] = gain_part
            sums[1:2] = shift_part
        else:
            sums[0:1] += gain_part
            sums[1:2] += shift_part
        out = gres[p] + norm_back(grad_in[p], scaled, inverse, vecs[GAIN : GAIN + 1])
        gtarget[p] = out
        gtable[pl.ds(meta[pairs + p], 1), :] += col_sum(out)
    rows = [sums_a[0:1], sums_a[1:2], sums_m[2:3], sums_b[1:2], sums_b[2:3], sums_b[0:1], sums_c[0:1]]
    rows += [sums[0:1], sums_m[0:1], sums_c[1:2], sums[1:2], sums_m[1:2], sums_c[2:3]]
    vectors = jnp.concatenate(rows + [jnp.zeros((TABLE - len(rows), shape[2]), F32)], axis=0)
    steps = gtable.shape[0] // 2
    for d in range(Z * Y):
        lanes = slice(d * 64, (d + 1) * 64)
        top = jnp.concatenate([vectors[:, lanes], jnp.zeros((TABLE, 64), F32)], axis=1)
        low = jnp.concatenate([gtable[:steps, lanes], gtable[steps:, lanes]], axis=1)
        tail = [dbias[:, d * 256 + i * 128 : d * 256 + (i + 1) * 128] for i in range(2)]
        fill = jnp.zeros((SMALL_ROWS - TABLE - steps - 2, 128), F32)
        part = jnp.concatenate([top, low, *tail, fill], axis=0).astype(BF)
        for i in range(X * CORE):
            small[i, d // Y, d % Y] = part
    start(stores)
    wait(stores)


HBM = pl.ANY
VMEM = pltpu.VMEM
SMEM = pltpu.SMEM


def call(kernel, name, args, spaces, outs, scratch, micros=1):
    cost = pl.CostEstimate(flops=micros * 10**9, bytes_accessed=micros * 3 * 10**6, transcendentals=0)
    return pl.pallas_call(
        kernel,
        out_shape=[jax.ShapeDtypeStruct(s, d) for s, d, unused in outs],
        in_specs=[pl.BlockSpec(memory_space=m) for m in spaces],
        out_specs=[pl.BlockSpec(memory_space=m) for unused, unused2, m in outs],
        scratch_shapes=scratch,
        compiler_params=pltpu.CompilerParams(vmem_limit_bytes=VMEM_LIMIT),
        cost_estimate=cost,
        name=name,
    )(*args)


def held_like(rows):
    return VMEM((X * CORE, Z, Y, rows, 128), BF)


def kept_like(slots):
    return VMEM((X * CORE, slots[1], Y, *slots[2:]), BF)


def sems(*shape):
    return pltpu.SemaphoreType.DMA(shape)


def weights_shape(shape, source):
    return (shape[0], HEADS // GROUP, GROUP * shape[1], source)


def slot_shape(count, extra=0):
    return (Y * X, Z, count * PIECE + extra, 128)


def self_forward(meta, target, pieces, steps):
    shape = target.shape
    return call(
        self_forward_kernel,
        "self_forward",
        [meta, target, *pieces],
        [SMEM, VMEM] + [HBM] * 8,
        [(shape, BF, VMEM)] * 4
        + [(weights_shape(shape, shape[1]), BF, VMEM), (shape, BF, VMEM)]
        + [((TABLE + steps, shape[2]), F32, VMEM), ((1, 4 * shape[2]), F32, VMEM)],
        [held_like(SELF_ROWS), sems(8)],
        14,
    )


def cross_forward(meta, target, mix_a, mems, vecs, pieces):
    shape = target.shape
    source = mems[0].shape[1] * X * CORE
    m_shape = (shape[0], source, shape[2])
    return call(
        cross_forward_kernel,
        "cross_forward",
        [meta, target, mix_a, *mems, vecs, *pieces],
        [SMEM] + [VMEM] * 2 + [HBM] * 4 + [VMEM] + [HBM] * 8,
        [(m_shape, BF, VMEM), (shape, F32, VMEM)] + [(shape, BF, VMEM)] * 2 + [(m_shape, BF, VMEM)] * 2
        + [(weights_shape(shape, source), BF, VMEM), (shape, BF, VMEM), (shape, F32, VMEM)],
        [held_like(CROSS_ROWS), sems(8), sems(4)],
        30,
    )


def feed(meta, after_cross, cot, vecs, feed_bias, pieces):
    shape = after_cross.shape
    tokens, width = shape[0] * shape[1], shape[2]
    return call(
        feed_kernel,
        "feed",
        [meta, after_cross, cot, vecs, feed_bias, *pieces],
        [SMEM] + [VMEM] * 4 + [HBM] * 8,
        [(shape, BF, VMEM), (shape, F32, VMEM), ((3, width), F32, VMEM), (feed_bias.shape, F32, VMEM)]
        + [(slot_shape(4, 256), BF, HBM)] * 2,
        [held_like(FEED_ROWS)] * 2
        + [VMEM((tokens, width), BF), VMEM((tokens, width), F32), VMEM((tokens, width), F32)]
        + [sems(8)] * 2,
        26,
    )


def cross_back(meta, gres, kept, memory, pieces):
    shape = gres.shape
    mshape = memory.shape
    return call(
        cross_back_kernel,
        "cross_back",
        [meta, gres, *kept, memory, *pieces],
        [SMEM] + [VMEM] * 8 + [HBM] * 8,
        [(shape, BF, VMEM), (mshape, BF, VMEM), (mshape, BF, VMEM), ((3, shape[2]), F32, VMEM)]
        + [(slot_shape(4), BF, HBM)] * 2,
        [VMEM(shape, BF), held_like(CROSS_ROWS), kept_like(slot_shape(4))] + [sems(8)] * 2,
        15,
    )


def middle_back(meta, gres, grads, after_self, vecs, pieces):
    shape = gres.shape
    mshape = grads[1].shape
    part = (mshape[0], mshape[1] // (X * CORE), mshape[2])
    return call(
        middle_back_kernel,
        "middle_back",
        [meta, gres, *grads, after_self, vecs, *pieces],
        [SMEM] + [VMEM] * 6 + [HBM] * 8,
        [(shape, F32, VMEM), (shape, BF, VMEM)] + [(part, BF, HBM)] * 4 + [((3, shape[2]), F32, VMEM)],
        [VMEM(mshape, BF), held_like(CROSS_ROWS), sems(8), sems(4)],
        8,
    )


def self_back(meta, gres, gmix, kept):
    shape = gmix.shape
    return call(
        self_back_kernel,
        "self_back",
        [meta, gres, gmix, *kept],
        [SMEM] + [VMEM] * 8,
        [(shape, BF, VMEM)] * 3 + [((2, shape[2]), F32, VMEM)] + [(slot_shape(4), BF, HBM)] * 2,
        [kept_like(slot_shape(4)), sems(8)],
        15,
    )


def last_back(meta, gres, grads, target, vecs, sums, dbias, pieces, steps):
    shape = gres.shape
    small = (Y * X, Z, SMALL_ROWS, 128)
    return call(
        last_back_kernel,
        "last_back",
        [meta, gres, *grads, target, vecs, *sums, dbias, *pieces],
        [SMEM] + [VMEM] * 11 + [HBM] * 8,
        [(shape, F32, VMEM)] + [(small, BF, HBM)] * 2,
        [VMEM((steps, shape[2]), F32), held_like(3 * PIECE), kept_like(small), VMEM((2, shape[2]), F32)]
        + [sems(8)] * 2,
        8,
    )


BOTH = ("dp", "mem")


def swap(array, mask):
    count = lax.axis_size("dp") * lax.axis_size("mem")
    return lax.ppermute(array, BOTH, [(i, i ^ mask) for i in range(count)])


def pack_kernel(*refs):
    squares, (w_in, w_out, biases, f_bias, gain, shift, table) = refs[:8], refs[8:15]
    square_out, feed_out, stage = refs[15:]
    for i, ref in enumerate(squares):
        if i < 3:
            square_out[PIECE * i : PIECE * (i + 1)] = ref[...]
        else:
            square_out[SELF_ROWS + PIECE * (i - 3) : SELF_ROWS + PIECE * (i - 2)] = ref[...]
    for i in range(4):
        feed_out[PIECE * i : PIECE * (i + 1)] = w_in[:, 128 * i : 128 * (i + 1)]
    feed_out[4 * PIECE :] = w_out[...]
    stage[...] = jnp.zeros_like(stage)
    stage[0:7, :64] = biases[...].astype(F32)
    stage[GAIN : GAIN + 3, :64] = gain[...].astype(F32)
    stage[SHIFT : SHIFT + 3, :64] = shift[...].astype(F32)
    rows = table[...].astype(F32)
    half = rows.shape[0] // 2
    stage[TABLE : TABLE + half] = jnp.concatenate([rows[:half], rows[half:]], axis=1)
    stage[TABLE + half : TABLE + half + 2] = f_bias[...].astype(F32)
    square_out[3 * PIECE : SELF_ROWS] = stage[...].astype(BF)


def assemble_kernel(meta, a, b, c, d, out):
    mine = meta[meta.shape[0] - 4]
    for i, one in enumerate((a, b, c, d)):
        out[mine ^ i] = one[...]


def assemble(meta, parts):
    return call(
        assemble_kernel,
        "assemble",
        [meta, *parts],
        [SMEM] + [VMEM] * 4,
        [((Z, *parts[0].shape), BF, VMEM)],
        [],
    )[0]


fence = lax.optimization_barrier


def swap_z(packed):
    return [packed, swap(packed, 8), swap(packed, 16), swap(packed, 24)]


def spread_near(along_z):
    return [along_z, swap(along_z, 2), swap(along_z, 4), swap(along_z, 6)]


def spread_core(near):
    out = []
    for one in near:
        out += [one, swap(one, 1)]
    return out


def merge_kernel(meta, a, b, c, d, own, s1, s2, s3):
    mine = meta[meta.shape[0] - 4]

    def total(z):
        return (a[z].astype(F32) + b[z].astype(F32)) + (c[z].astype(F32) + d[z].astype(F32))

    own[...] = total(mine)
    s1[...] = total(mine ^ 1).astype(BF)
    s2[...] = total(mine ^ 2).astype(BF)
    s3[...] = total(mine ^ 3).astype(BF)


def final_parts(refs, outs):
    own, a, b, c = refs

    def total(span):
        return (own[span] + a[span].astype(F32)) + (b[span].astype(F32) + c[span].astype(F32))

    at = 0
    for out in outs:
        rows = out.shape[0]
        for i in range(out.shape[1] // 128):
            out[:, 128 * i : 128 * (i + 1)] = total(slice(at, at + rows))
            at += rows
    return total, at


def final_kernel(*refs):
    final_parts(refs[:4], refs[4:])


def final_small_kernel(*refs):
    outs, (biases, f_bias, gain, shift, table) = refs[4:8], refs[8:]
    total, at = final_parts(refs[:4], outs)
    part = total(slice(at, at + SMALL_ROWS))
    biases[...] = part[0:7, :64]
    gain[...] = part[GAIN : GAIN + 3, :64]
    shift[...] = part[SHIFT : SHIFT + 3, :64]
    half = table.shape[0] // 2
    table[:half] = part[TABLE : TABLE + half, :64]
    table[half:] = part[TABLE : TABLE + half, 64:]
    f_bias[...] = part[TABLE + half : TABLE + half + 2]


def add(left, right):
    return (left.astype(F32) + right.astype(F32)).astype(BF)


def core_sums(own, other):
    return [add(own[i], other[i]) for i in range(Y * X)]


def join_kernel(own, other, small_own, small_other, *outs):
    rows = own.shape[2]
    for i, out in enumerate(outs):
        out[:, :rows] = add(own[i], other[i])
        out[:, rows:] = add(small_own[i], small_other[i])


def core_sums_joined(own, other, more_own, more_other):
    unused, z, rows, lanes = own.shape
    out = (z, rows + more_own.shape[2], lanes)
    return call(
        join_kernel,
        "join",
        [own, other, more_own, more_other],
        [VMEM] * 4,
        [(out, BF, VMEM)] * (Y * X),
        [],
    )


def near_parts(pairs):
    return [pairs[0], swap(pairs[1], 2), swap(pairs[2], 4), swap(pairs[3], 6)]


def chip_sums(meta, near):
    unused, rows, lanes = near[0].shape
    return call(
        merge_kernel,
        "merge",
        [meta, *near],
        [SMEM] + [VMEM] * 4,
        [((rows, lanes), F32, VMEM)] + [((rows, lanes), BF, VMEM)] * 3,
        [],
    )


def sent_z(parts):
    own, s1, s2, s3 = parts
    return [own, swap(s1, 8), swap(s2, 16), swap(s3, 24)]


def slice_sums(kernel, parts, shapes):
    return call(
        kernel,
        "final",
        parts,
        [VMEM] * 4,
        [(s, F32, VMEM) for s in shapes],
        [],
    )


def place_kernel(meta, a, b, c, d, out):
    base = meta.shape[0] - 4
    mine = meta[base + 2] * CORE + meta[base + 3]
    pairs = a.shape[0]
    for i, one in enumerate((a, b, c, d)):
        for p in range(pairs):
            out[(mine ^ i) * pairs + p] = one[p].astype(F32)


def swap_memory(memory, pairs):
    mine = lax.axis_index("mem")
    parts = [lax.dynamic_slice_in_dim(memory, (mine ^ i) * pairs, pairs) for i in range(4)]
    return parts


def return_memory(meta, parts, shape):
    return call(place_kernel, "place", [meta, *parts], [SMEM] + [VMEM] * 4, [(shape, F32, VMEM)], [])[0]


def slots_of(wide):
    rows, cols = wide.shape
    cut = wide.reshape(Z, Y, rows // (Z * Y), X, CORE, cols // (X * CORE))
    return [cut[:, y, :, x, c] for y, x, c in SLOTS]


def wide_of(slots):
    z, rows, cols = slots[0].shape
    cut = jnp.stack(slots).reshape(Y, X, CORE, z, rows, cols)
    return cut.transpose(3, 0, 4, 1, 2, 5).reshape(z * Y * rows, X * CORE * cols)


def gather_any(piece):
    return lax.all_gather(lax.all_gather(piece, "mem", axis=1, tiled=True), "dp", axis=0, tiled=True)


def scatter_any(wide):
    part = lax.psum_scatter(wide.astype(F32), "dp", scatter_dimension=0, tiled=True)
    return lax.psum_scatter(part, "mem", scatter_dimension=1, tiled=True)


def narrow_columns(slots):
    return [jnp.concatenate(jnp.split(one, 4, axis=2), axis=1) for one in slots]


def small_pieces(biases, f_bias, gain, shift, table):
    vectors = jnp.concatenate([biases, gain, shift], axis=0)
    vectors = jnp.pad(vectors, ((0, TABLE - vectors.shape[0]), (0, 0)))
    half = table.shape[0] // 2

    def cut(rows):
        return rows.reshape(rows.shape[0], Z, Y, 64).transpose(1, 2, 0, 3)

    top = jnp.pad(cut(vectors), ((0, 0),) * 3 + ((0, 64),))
    low = jnp.concatenate([cut(table[:half]), cut(table[half:])], axis=3)
    whole = jnp.concatenate([top, low, f_bias.reshape(Z, Y, 2, 128)], axis=2)
    return jnp.pad(whole, ((0, 0), (0, 0), (0, SMALL_ROWS - whole.shape[2]), (0, 0)))


def spread_any(squares, w_in, w_out, smalls):
    wide = [slots_of(gather_any(one)) for one in squares]
    small = small_pieces(*[lax.all_gather(one, "dp", axis=one.ndim - 1, tiled=True) for one in smalls])
    ins = narrow_columns(slots_of(gather_any(w_in)))
    outs = slots_of(gather_any(w_out))
    square_w, feed_w = [], []
    for i, (y, unused, unused2) in enumerate(SLOTS):
        parts = [one[i] for one in wide]
        square_w.append(jnp.concatenate([*parts[:3], small[:, y], *parts[3:]], axis=1))
        feed_w.append(jnp.concatenate([ins[i], outs[i]], axis=1))
    return square_w, feed_w


def by_slot(halves):
    return [halves[c][y * X + x] for y, x, c in SLOTS]


def reduce_squares_any(halves, count):
    slots = by_slot(halves)
    return [
        scatter_any(wide_of([one[:, PIECE * i : PIECE * (i + 1)] for one in slots]))
        for i in range(count)
    ]


def reduce_feed_any(halves):
    slots = by_slot(halves)
    ins = [
        jnp.concatenate([one[:, PIECE * j : PIECE * (j + 1)] for j in range(4)], axis=2)
        for one in slots
    ]
    return [scatter_any(wide_of(ins)), scatter_any(wide_of([one[:, 4 * PIECE :] for one in slots]))]


def reduce_small_any(halves, count):
    parts = [halves[0][y * X].astype(F32) for y in range(Y)]
    part = jnp.stack(parts, axis=1).reshape(Z * Y, SMALL_ROWS, 128)
    vectors = part[:, :13, :64].transpose(1, 0, 2).reshape(13, -1)
    half = count // 2
    table = part[:, TABLE : TABLE + half]
    table = jnp.concatenate([table[:, :, :64], table[:, :, 64:]], axis=1)
    rows = jnp.concatenate([vectors, table.transpose(1, 0, 2).reshape(count, -1)], axis=0)
    cut = lax.psum_scatter(lax.psum(rows, "mem"), "dp", scatter_dimension=1, tiled=True)
    f_bias = part[:, TABLE + half : TABLE + half + 2].reshape(-1)
    f_bias = lax.psum_scatter(lax.psum(f_bias, "mem"), "dp", scatter_dimension=0, tiled=True)
    return cut[:7], f_bias, cut[7:10], cut[10:13], cut[13:]


def shards(
    target, memory, time_steps, target_len, source_len, source_off, cotangent,
    self_query, self_key, self_value, self_out, cross_query, cross_key, cross_value, cross_out,
    feed_in, feed_out, biases, feed_bias, norm_gain, norm_shift, step_table,
):
    pairs = target.shape[0]
    steps = step_table.shape[0]
    dp, mem = lax.axis_index("dp"), lax.axis_index("mem")
    quick = lax.axis_size("dp") == Z * Y and lax.axis_size("mem") == X * CORE
    here = [dp // 2, dp % 2, mem // 2, mem % 2] if quick else [0, 0, 0, 0]
    meta = jnp.concatenate(
        [
            target_len,
            time_steps,
            lax.dynamic_slice_in_dim(source_off, mem * pairs, pairs),
            lax.dynamic_slice_in_dim(source_len, mem * pairs, pairs),
            jnp.stack([jnp.asarray(i, jnp.int32) for i in here]),
        ]
    )
    squares = (self_query, self_key, self_value, self_out, cross_query, cross_key, cross_value, cross_out)
    if quick:
        packed = call(
            pack_kernel,
            "pack",
            [*squares, feed_in, feed_out, biases, feed_bias.reshape(2, 128)]
            + [norm_gain, norm_shift, step_table],
            [VMEM] * 15,
            [((i, 128), BF, VMEM) for i in (SELF_ROWS + CROSS_ROWS, FEED_ROWS)],
            [VMEM((SMALL_ROWS, 128), F32)],
        )
        packed, memory = fence((packed, memory))
        square_p, feed_p = packed
        mems = swap_memory(memory, pairs)
        square_z = swap_z(square_p)
        mems = [mems[0], mems[1], swap(mems[2], 2), swap(mems[3], 3)]
        square_z, mems, feed_p = fence((square_z, mems, feed_p))
        square_near = spread_near(assemble(meta, square_z))
        feed_z = swap_z(feed_p)
        mems[1] = swap(mems[1], 1)
        square_near, feed_z, mems = fence((square_near, feed_z, mems))
        square_w = spread_core(square_near)
        feed_z = assemble(meta, feed_z)
        square_w, feed_z = fence((square_w, feed_z))
        feed_near = spread_near(feed_z)
    else:
        square_w, feed_w = spread_any(
            squares, feed_in, feed_out, (biases, feed_bias, norm_gain, norm_shift, step_table)
        )
        own = lax.all_to_all(memory, "mem", 0, 1, tiled=True)
        mems = jnp.split(own, X * CORE, axis=1)

    in_a, q_a, k_a, v_a, w_a, mix_a, vecs, fbias = self_forward(meta, target, square_w, steps)
    own_memory, after_self, in_b, q_b, k_b, v_b, w_b, mix_b, after_cross = cross_forward(
        meta, target, mix_a, mems, vecs, square_w
    )
    if quick:
        feed_near, after_cross = fence((feed_near, after_cross))
        feed_w = spread_core(feed_near)
    layer_out, gres_c, sums_c, d_fbias, *d_feed = feed(
        meta, after_cross, cotangent, vecs, fbias, feed_w
    )
    if quick:
        d_feed, gres_c = fence((d_feed, gres_c))
        d_feed[1] = swap(d_feed[1], 1)
    gq_b, gk_b, gv_b, sums_b, *d_cross = cross_back(
        meta, gres_c, (in_b, q_b, k_b, v_b, w_b, mix_b), own_memory, square_w
    )
    if quick:
        d_feed, gq_b, d_cross = fence((d_feed, gq_b, d_cross))
        u_first = core_sums_joined(*d_feed, d_cross[0], swap(d_cross[1], 1))
        u_first, gq_b = fence((u_first, gq_b))
        n_first = near_parts(u_first)
    gres_b, gmix_a, *gmem, sums_m = middle_back(
        meta, gres_c, (gq_b, gk_b, gv_b), after_self, vecs, square_w
    )
    gq_a, gk_a, gv_a, sums_a, *d_self = self_back(meta, gres_b, gmix_a, (in_a, q_a, k_a, v_a, w_a, mix_a))
    if quick:
        n_first, gmem, gq_a, d_self = fence((n_first, gmem, gq_a, d_self))
        m_first = chip_sums(meta, n_first)
        m_first, gmem, gq_a, d_self = fence((m_first, gmem, gq_a, d_self))
        m_first = sent_z(m_first)
        gmem = [gmem[0], gmem[1], swap(gmem[2], 2), swap(gmem[3], 3)]
    grad_target, *d_small = last_back(
        meta, gres_b, (gq_a, gk_a, gv_a), target, vecs, (sums_a, sums_m, sums_b, sums_c), d_fbias, square_w, steps
    )
    if quick:
        one = self_query.shape
        m_first, gmem, d_self, d_small = fence((m_first, gmem, d_self, d_small))
        u_self = core_sums_joined(d_self[0], swap(d_self[1], 1), d_small[0], swap(d_small[1], 1))
        gmem[1] = swap(gmem[1], 1)
        u_self, gmem, m_first = fence((u_self, gmem, m_first))
        n_self = near_parts(u_self)
        g_feed_in, g_feed_out, *g_cross = slice_sums(
            final_kernel, m_first, (feed_in.shape, feed_out.shape) + (one,) * 4
        )
        grad_memory = return_memory(meta, gmem, memory.shape)
        n_self, g_feed_in, grad_memory = fence((n_self, g_feed_in, grad_memory))
        m_self = sent_z(chip_sums(meta, n_self))
        small_shapes = (biases.shape, (2, 128), norm_gain.shape, norm_shift.shape, step_table.shape)
        out = slice_sums(final_small_kernel, m_self, (one,) * 4 + small_shapes)
        g_self, (g_bias, g_fbias, g_gain, g_shift, g_table) = out[:4], out[4:]
        g_feed = [g_feed_in, g_feed_out]
        g_fbias = g_fbias.reshape(feed_bias.shape)
    else:
        whole = jnp.concatenate(gmem, axis=1)
        grad_memory = lax.all_to_all(whole, "mem", 1, 0, tiled=True).astype(F32)
        g_feed = reduce_feed_any(d_feed)
        g_cross = reduce_squares_any(d_cross, 4)
        g_self = reduce_squares_any(d_self, 4)
        g_bias, g_fbias, g_gain, g_shift, g_table = reduce_small_any(d_small, steps)
    return (
        layer_out, grad_target, grad_memory, *g_self, *g_cross, *g_feed,
        g_bias, g_fbias, g_gain, g_shift, g_table,
    )


def solution(mesh):
    rows = P(BOTH, None, None)
    piece = P("dp", "mem")
    vector = P(None, "dp")
    mem_rows = P("dp", "mem", None)
    return jax.shard_map(
        shards,
        mesh=mesh,
        in_specs=(rows, mem_rows, P(BOTH), P(BOTH), P("dp"), P("dp"), rows)
        + (piece,) * 10
        + (vector, P("dp"), vector, vector, vector),
        out_specs=(rows, rows, mem_rows) + (piece,) * 10 + (vector, P("dp"), vector, vector, vector),
        check_vma=False,
    )
```

```python
import functools
import math

import jax
import jax.numpy as jnp
from jax import lax
from jax.experimental import pallas as pl
from jax.experimental.pallas import tpu as pltpu
from jax.sharding import PartitionSpec as P

HEADS = 8
DH = 64
GROUP = 4
WIDE = GROUP * DH
EPSILON = 1e-05
SCALE = 1.0 / math.sqrt(DH)
BF = jnp.bfloat16
F32 = jnp.float32
VMEM_LIMIT = 40 * 2**20


def contract(left, right, left_dim, right_dim):
    return lax.dot_general(
        left, right, (((left_dim,), (right_dim,)), ((), ())), preferred_element_type=F32
    )


def mul(left, right):
    return contract(left, right, 1, 0)


def mul_nt(left, right):
    return contract(left, right, 1, 1)


def mul_tn(left, right):
    return contract(left, right, 0, 0)


def normalise(signal):
    centre = signal - jnp.mean(signal, axis=-1, keepdims=True)
    inverse = lax.rsqrt(jnp.mean(centre * centre, axis=-1, keepdims=True) + EPSILON)
    return centre * inverse, inverse


def norm_back(grad, scaled, inverse, gain):
    up = grad * gain
    return inverse * (
        up
        - jnp.mean(up, axis=-1, keepdims=True)
        - scaled * jnp.mean(up * scaled, axis=-1, keepdims=True)
    )


def col_sum(array):
    return jnp.sum(array.astype(F32), axis=0, keepdims=True)


def head_of_lane(rows):
    return lax.broadcasted_iota(jnp.int32, (rows, WIDE), 1) // DH


def stacked(block, lane_head):
    zero = jnp.zeros_like(block)
    return jnp.concatenate([jnp.where(lane_head == h, block, zero) for h in range(GROUP)], axis=0)


def unstacked(result, lane_head, rows):
    picked = result[:rows]
    for h in range(1, GROUP):
        picked = jnp.where(lane_head == h, result[h * rows : (h + 1) * rows], picked)
    return picked


def attend_pair(p, bias, q_ref, k_ref, v_ref, w_ref, mix_ref):
    rows = q_ref.shape[1]
    lane_head = head_of_lane(rows)
    for g in range(HEADS // GROUP):
        cols = slice(g * WIDE, (g + 1) * WIDE)
        scores = mul_nt(stacked(q_ref[p, :, cols], lane_head), k_ref[p, :, cols]) + bias
        top = jnp.max(scores, axis=-1, keepdims=True)
        raised = jnp.exp(scores - top)
        total = jnp.sum(raised, axis=-1, keepdims=True)
        weights = (raised * (1.0 / total)).astype(BF)
        w_ref[p, g] = weights
        mixed = mul(weights, v_ref[p, :, cols])
        mix_ref[p, :, cols] = unstacked(mixed, lane_head, rows).astype(BF)


def attend_pair_back(p, q_ref, k_ref, v_ref, w_ref, grad_ref, gq_ref, gk_ref, gv_ref):
    rows = q_ref.shape[1]
    lane_head = head_of_lane(rows)
    for g in range(HEADS // GROUP):
        cols = slice(g * WIDE, (g + 1) * WIDE)
        grads = stacked(grad_ref[p, :, cols], lane_head)
        weights = w_ref[p, g]
        grad_w = mul_nt(grads, v_ref[p, :, cols])
        wide = weights.astype(F32)
        offset = jnp.sum(grad_w * wide, axis=-1, keepdims=True)
        grad_s = (wide * (grad_w - offset)).astype(BF)
        grad_q = unstacked(mul(grad_s, k_ref[p, :, cols]), lane_head, rows)
        gq_ref[p, :, cols] = (grad_q * SCALE).astype(BF)
        gk_ref[p, :, cols] = mul_tn(grad_s, stacked(q_ref[p, :, cols], lane_head)).astype(BF)
        gv_ref[p, :, cols] = mul_tn(weights, grads).astype(BF)


def flat(ref):
    value = ref[...]
    return value.reshape(value.shape[0] * value.shape[1], value.shape[2])


Z, Y, X, CORE = 4, 2, 2, 2
SLOTS = [(y, x, c) for y in range(Y) for x in range(X) for c in range(CORE)]
PIECE = 64
FEED_ROWS = 4 * PIECE + 256
SMALL_ROWS = 48
SELF_ROWS = 3 * PIECE + SMALL_ROWS
CROSS_ROWS = 5 * PIECE
GAIN, SHIFT, TABLE = 7, 10, 16


def places(meta, slot):
    base = meta.shape[0] - 4
    y, x, c = slot
    return y ^ meta[base + 1], (x ^ meta[base + 2]) * CORE + (c ^ meta[base + 3])


def load_copies(meta, sources, held, sems, first=0):
    copies = []
    rows = held.shape[-2]
    for i, slot in enumerate(SLOTS):
        row, panel = places(meta, slot)
        source = sources[i].at[:, pl.ds(first, rows)]
        copies.append(pltpu.make_async_copy(source, held.at[panel, :, row], sems.at[i]))
    return copies


def store_copies(meta, held, targets, sems):
    copies = []
    for i, slot in enumerate(SLOTS):
        row, panel = places(meta, slot)
        y, x, c = slot
        target = targets[c].at[y * X + x]
        copies.append(pltpu.make_async_copy(held.at[panel, :, row], target, sems.at[i]))
    return copies


def start(copies):
    for copy in copies:
        copy.start()


def wait(copies):
    for copy in copies:
        copy.wait()


def moves(sources, targets, sems):
    return [pltpu.make_async_copy(a, b, sems.at[i]) for i, (a, b) in enumerate(zip(sources, targets))]


def joined(value):
    return value.reshape(-1, value.shape[-1])


def square(held, index):
    span = slice(PIECE * index, PIECE * (index + 1))
    return jnp.concatenate([joined(held[i, :, :, span]) for i in range(X * CORE)], axis=1)


def keep(held, index, value):
    span = slice(PIECE * index, PIECE * (index + 1))
    for i in range(X * CORE):
        part = value[:, i * 128 : (i + 1) * 128].astype(BF)
        held[i, :, :, span] = part.reshape(Z, Y, PIECE, 128)


def self_forward_kernel(meta, target, *refs):
    pieces, refs = refs[:8], refs[8:]
    far, (mix, vecs, fbias), refs = refs[:6], refs[6:9], refs[9:]
    in_a, q, k, v, w, held, sems, far_sems, w_sems = refs
    copies = moves((in_a, q, k, v, mix), (*far[:4], far[5]), far_sems)
    loads = load_copies(meta, pieces, held, sems)
    start(loads)
    pairs, length, width = target.shape
    shape = target.shape
    wait(loads)
    every = [held[0, z, y, 3 * PIECE :].astype(F32) for z in range(Z) for y in range(Y)]
    steps = (vecs.shape[0] - TABLE) // 2
    vecs[:TABLE] = jnp.concatenate([one[:TABLE, :64] for one in every], axis=1)
    for i in range(2):
        part = [one[TABLE : TABLE + steps, 64 * i : 64 * (i + 1)] for one in every]
        vecs[TABLE + i * steps : TABLE + (i + 1) * steps] = jnp.concatenate(part, axis=1)
    for d, one in enumerate(every):
        for i in range(2):
            at = TABLE + steps + i
            fbias[:, d * 256 + i * 128 : d * 256 + (i + 1) * 128] = one[at : at + 1]
    for p in range(pairs):
        emb = target[p].astype(F32) + vecs[pl.ds(TABLE + meta[pairs + p], 1), :]
        scaled, unused = normalise(emb)
        in_a[p] = (scaled * vecs[GAIN : GAIN + 1] + vecs[SHIFT : SHIFT + 1]).astype(BF)
    copies[0].start()
    x = flat(in_a)
    q[...] = ((mul(x, square(held, 0)) + vecs[0:1]).astype(BF) * SCALE).reshape(shape)
    k[...] = mul(x, square(held, 1)).astype(BF).reshape(shape)
    v[...] = (mul(x, square(held, 2)) + vecs[1:2]).astype(BF).reshape(shape)
    start(copies[1:4])

    def pair(p, carry):
        spot = lax.broadcasted_iota(jnp.int32, (1, length), 1)
        bias = jnp.where(spot < meta[p], 0.0, -1e30)
        attend_pair(p, bias, q, k, v, w, mix)
        pltpu.make_async_copy(w.at[p], far[4].at[p], w_sems.at[p]).start()
        return carry

    lax.fori_loop(0, pairs, pair, 0)
    copies[4].start()
    wait(copies)
    for p in range(pairs):
        pltpu.make_async_copy(w.at[p], far[4].at[p], w_sems.at[p]).wait()


def cross_forward_kernel(meta, target, mix_a, mem_0, mem_1, mem_2, mem_3, vecs, *refs):
    pieces, refs = refs[:8], refs[8:]
    far, after, refs = refs[:8], refs[8], refs[9:]
    memory, after_self, in_b, q, k, v, mix, w, held, sems, mem_sems, far_sems, w_sems = refs
    copies = moves((memory, after_self, in_b, q, k, v, mix), (*far[:6], far[7]), far_sems)
    pairs, length, width = target.shape
    shape = target.shape
    source = memory.shape[1]
    base = meta.shape[0] - 4
    mine = meta[base + 2] * CORE + meta[base + 3]
    part = source // (X * CORE)
    mem_loads = [
        pltpu.make_async_copy(
            one, memory.at[:, pl.ds(pl.multiple_of((mine ^ i) * part, part), part), :], mem_sems.at[i]
        )
        for i, one in enumerate((mem_0, mem_1, mem_2, mem_3))
    ]
    start(mem_loads)
    loads = load_copies(meta, pieces, held, sems, SELF_ROWS)
    start(loads)
    wait(loads)
    branch = (mul(flat(mix_a), square(held, 0)) + vecs[2:3]).reshape(shape)
    for p in range(pairs):
        row = vecs[pl.ds(TABLE + meta[pairs + p], 1), :]
        after_self[p] = target[p].astype(F32) + row + branch[p]
    scaled, unused = normalise(flat(after_self))
    x = (scaled * vecs[GAIN + 1 : GAIN + 2] + vecs[SHIFT + 1 : SHIFT + 2]).astype(BF)
    in_b[...] = x.reshape(shape)
    q[...] = ((mul(x, square(held, 1)) + vecs[3:4]).astype(BF) * SCALE).reshape(shape)
    start(copies[1:4])
    wait(mem_loads)
    copies[0].start()
    m = flat(memory)
    k[...] = mul(m, square(held, 2)).astype(BF).reshape(memory.shape)
    v[...] = (mul(m, square(held, 3)) + vecs[4:5]).astype(BF).reshape(memory.shape)
    start(copies[4:6])

    def pair(p, carry):
        spot = lax.broadcasted_iota(jnp.int32, (1, source), 1)
        begin = meta[2 * pairs + p]
        end = begin + meta[3 * pairs + p]
        bias = jnp.where((spot >= begin) & (spot < end), 0.0, -1e30)
        attend_pair(p, bias, q, k, v, w, mix)
        pltpu.make_async_copy(w.at[p], far[6].at[p], w_sems.at[p]).start()
        return carry

    lax.fori_loop(0, pairs, pair, 0)
    copies[6].start()
    after[...] = after_self[...] + (mul(flat(mix), square(held, 4)) + vecs[5:6]).reshape(shape)
    wait(copies)
    for p in range(pairs):
        pltpu.make_async_copy(w.at[p], far[6].at[p], w_sems.at[p]).wait()


def gelu_parts(value):
    size = jnp.abs(value) * math.sqrt(0.5)
    t = 1.0 / (1.0 + 0.3275911 * size)
    bell = jnp.exp(-0.5 * value * value)
    tail = (
        t
        * (
            0.5 * 0.254829592
            + t
            * (
                0.5 * -0.284496736
                + t * (0.5 * 1.421413741 + t * (0.5 * -1.453152027 + t * (0.5 * 1.061405429)))
            )
        )
        * bell
    )
    below = jnp.where(value < 0, tail, 1.0 - tail)
    slope = below + value * bell * (1.0 / math.sqrt(2.0 * math.pi))
    return value * below, slope


def feed_kernel(meta, after_cross, cot, vecs, feed_bias, *refs):
    pieces, refs = refs[:8], refs[8:]
    far_out, gres, sums, dbias = refs[:4]
    targets, refs = refs[4:6], refs[6:]
    held, kept, x_c, out_acc, in_acc, layer_out, sems, out_sems, far_sems = refs
    copies = moves((layer_out,), (far_out,), far_sems)
    loads = load_copies(meta, pieces, held, sems)
    start(loads)
    stores = store_copies(meta, kept, targets, out_sems)
    shape = after_cross.shape
    signal = flat(after_cross)
    scaled, inverse = normalise(signal)
    gain = vecs[GAIN + 2 : GAIN + 3]
    x_c[...] = (scaled * gain + vecs[SHIFT + 2 : SHIFT + 3]).astype(BF)
    wait(loads)
    block = 512
    for j in range(4):
        cols = slice(j * block, (j + 1) * block)
        w_in = jnp.concatenate(
            [joined(held[j, :, :, PIECE * i : PIECE * (i + 1)]) for i in range(4)], axis=1
        )
        w_out = jnp.concatenate([joined(held[i, j, :, 4 * PIECE :]) for i in range(4)], axis=1)
        c = flat(cot)
        x = x_c[...]
        pre = mul(x, w_in) + feed_bias[:, cols]
        value, slope = gelu_parts(pre)
        act = value.astype(BF)
        grad_pre = (mul_nt(c, w_out) * slope).astype(BF)
        out_part = mul(act, w_out)
        in_part = mul_nt(grad_pre, w_in)
        if j == 0:
            out_acc[...] = out_part
            in_acc[...] = in_part
        else:
            out_acc[...] += out_part
            in_acc[...] += in_part
        d_out = mul_tn(act, c)
        for i in range(4):
            part = d_out[:, i * 128 : (i + 1) * 128].astype(BF)
            kept[i, j, :, 4 * PIECE :] = part.reshape(Y, 256, 128)
        d_in = mul_tn(x, grad_pre)
        for i in range(4):
            part = d_in[:, i * 128 : (i + 1) * 128].astype(BF)
            kept[j, :, :, PIECE * i : PIECE * (i + 1)] = part.reshape(Z, Y, PIECE, 128)
        dbias[:, cols] = col_sum(grad_pre)
    start(stores)
    layer_out[...] = (signal + out_acc[...] + vecs[6:7]).astype(BF).reshape(shape)
    start(copies)
    grad = in_acc[...]
    wide_cot = flat(cot).astype(F32)
    sums[0:1] = col_sum(wide_cot)
    sums[1:2] = col_sum(grad * scaled)
    sums[2:3] = col_sum(grad)
    gres[...] = (wide_cot + norm_back(grad, scaled, inverse, gain)).reshape(shape)
    wait(stores)
    wait(copies)


def cross_back_kernel(meta, gres, far_in, far_q, far_k, far_v, far_w, far_mix, far_memory, *refs):
    pieces, refs = refs[:8], refs[8:]
    gq, gk, gv, sums = refs[:4]
    targets, refs = refs[4:6], refs[6:]
    gmix, held, kept, mix, q, k, v, in_b, memory, w, sems, out_sems, far_sems, w_sems = refs
    copies = moves(
        (far_mix, far_q, far_k, far_v, far_in, far_memory), (mix, q, k, v, in_b, memory), far_sems
    )
    loads = load_copies(meta, pieces, held, sems, SELF_ROWS)
    copies[0].start()
    start(loads)
    start(copies[1:4])
    w_copies = moves([far_w.at[p] for p in range(w.shape[0])], [w.at[p] for p in range(w.shape[0])], w_sems)
    start(w_copies)
    start(copies[4:])
    stores = store_copies(meta, kept, targets, out_sems)
    shape = gres.shape
    grad = flat(gres).astype(BF)
    sums[0:1] = col_sum(grad)
    copies[0].wait()
    keep(kept, 3, mul_tn(flat(mix), grad))
    wait(loads)
    gmix[...] = mul_nt(grad, square(held, 4)).astype(BF).reshape(shape)
    wait(copies[1:4])

    def pair(p, carry):
        pltpu.make_async_copy(far_w.at[p], w.at[p], w_sems.at[p]).wait()
        attend_pair_back(p, q, k, v, w, gmix, gq, gk, gv)
        return carry

    lax.fori_loop(0, shape[0], pair, 0)
    wait(copies[4:])
    m = flat(memory)
    keep(kept, 0, mul_tn(flat(in_b), flat(gq)))
    keep(kept, 1, mul_tn(m, flat(gk)))
    keep(kept, 2, mul_tn(m, flat(gv)))
    start(stores)
    sums[1:2] = col_sum(flat(gq))
    sums[2:3] = col_sum(flat(gv))
    wait(stores)


def middle_back_kernel(meta, gres, gq, gk, gv, far_after, vecs, *refs):
    pieces, refs = refs[:8], refs[8:]
    gres_out, gmix_a, gmem_0, gmem_1, gmem_2, gmem_3, sums = refs[:7]
    gmem, held, after_self, sems, mem_sems, far_sems = refs[7:]
    loads = load_copies(meta, pieces, held, sems, SELF_ROWS)
    start(loads)
    copies = moves((far_after,), (after_self,), far_sems)
    start(copies)
    shape = gres.shape
    wait(loads)
    grad_m = mul_nt(flat(gk), square(held, 2)) + mul_nt(flat(gv), square(held, 3))
    gmem[...] = grad_m.astype(BF).reshape(gmem.shape)
    base = meta.shape[0] - 4
    mine = meta[base + 2] * CORE + meta[base + 3]
    part = gmem.shape[1] // (X * CORE)
    mem_stores = [
        pltpu.make_async_copy(
            gmem.at[:, pl.ds(pl.multiple_of((mine ^ i) * part, part), part), :], one, mem_sems.at[i]
        )
        for i, one in enumerate((gmem_0, gmem_1, gmem_2, gmem_3))
    ]
    start(mem_stores)
    grad_in = mul_nt(flat(gq), square(held, 1))
    wait(copies)
    scaled, inverse = normalise(flat(after_self))
    sums[0:1] = col_sum(grad_in * scaled)
    sums[1:2] = col_sum(grad_in)
    total = flat(gres) + norm_back(grad_in, scaled, inverse, vecs[GAIN + 1 : GAIN + 2])
    gres_out[...] = total.reshape(shape)
    grad_a = total.astype(BF)
    sums[2:3] = col_sum(grad_a)
    gmix_a[...] = mul_nt(grad_a, square(held, 0)).astype(BF).reshape(shape)
    wait(mem_stores)


def self_back_kernel(meta, gres, gmix, far_in, far_q, far_k, far_v, far_w, far_mix, *refs):
    gq, gk, gv, sums = refs[:4]
    targets, refs = refs[4:6], refs[6:]
    kept, mix, q, k, v, in_a, w, out_sems, far_sems, w_sems = refs
    stores = store_copies(meta, kept, targets, out_sems)
    copies = moves((far_mix, far_q, far_k, far_v, far_in), (mix, q, k, v, in_a), far_sems)
    w_copies = moves([far_w.at[p] for p in range(w.shape[0])], [w.at[p] for p in range(w.shape[0])], w_sems)
    start(copies[:4])
    start(w_copies)
    copies[4].start()
    copies[0].wait()
    keep(kept, 3, mul_tn(flat(mix), flat(gres).astype(BF)))
    wait(copies[1:4])

    def pair(p, carry):
        pltpu.make_async_copy(far_w.at[p], w.at[p], w_sems.at[p]).wait()
        attend_pair_back(p, q, k, v, w, gmix, gq, gk, gv)
        return carry

    lax.fori_loop(0, gmix.shape[0], pair, 0)
    copies[4].wait()
    x = flat(in_a)
    for i, one in enumerate((gq, gk, gv)):
        keep(kept, i, mul_tn(x, flat(one)))
    start(stores)
    sums[0:1] = col_sum(flat(gq))
    sums[1:2] = col_sum(flat(gv))
    wait(stores)


def last_back_kernel(meta, gres, gq, gk, gv, target, vecs, sums_a, sums_m, sums_b, sums_c, dbias, *refs):
    pieces, refs = refs[:8], refs[8:]
    far_target, own, other, gtable, held, small, sums, gtarget, sems, out_sems, far_sems = refs
    loads = load_copies(meta, pieces, held, sems)
    start(loads)
    stores = store_copies(meta, small, (own, other), out_sems)
    shape = gres.shape
    pairs = shape[0]
    wait(loads)
    grad_in = (
        mul_nt(flat(gq), square(held, 0))
        + mul_nt(flat(gk), square(held, 1))
        + mul_nt(flat(gv), square(held, 2))
    ).reshape(shape)
    gtable[...] = jnp.zeros_like(gtable)
    for p in range(pairs):
        emb = target[p].astype(F32) + vecs[pl.ds(TABLE + meta[pairs + p], 1), :]
        scaled, inverse = normalise(emb)
        gain_part = col_sum(grad_in[p] * scaled)
        shift_part = col_sum(grad_in[p])
        if p == 0:
            sums[0:1] = gain_part
            sums[1:2] = shift_part
        else:
            sums[0:1] += gain_part
            sums[1:2] += shift_part
        out = gres[p] + norm_back(grad_in[p], scaled, inverse, vecs[GAIN : GAIN + 1])
        gtarget[p] = out
        copies = moves([gtarget.at[p]], [far_target.at[p]], far_sems.at[pl.ds(p, 1)])
        start(copies)
        gtable[pl.ds(meta[pairs + p], 1), :] += col_sum(out)
    rows = [sums_a[0:1], sums_a[1:2], sums_m[2:3], sums_b[1:2], sums_b[2:3], sums_b[0:1], sums_c[0:1]]
    rows += [sums[0:1], sums_m[0:1], sums_c[1:2], sums[1:2], sums_m[1:2], sums_c[2:3]]
    vectors = jnp.concatenate(rows + [jnp.zeros((TABLE - len(rows), shape[2]), F32)], axis=0)
    steps = gtable.shape[0] // 2
    for d in range(Z * Y):
        lanes = slice(d * 64, (d + 1) * 64)
        top = jnp.concatenate([vectors[:, lanes], jnp.zeros((TABLE, 64), F32)], axis=1)
        low = jnp.concatenate([gtable[:steps, lanes], gtable[steps:, lanes]], axis=1)
        tail = [dbias[:, d * 256 + i * 128 : d * 256 + (i + 1) * 128] for i in range(2)]
        fill = jnp.zeros((SMALL_ROWS - TABLE - steps - 2, 128), F32)
        part = jnp.concatenate([top, low, *tail, fill], axis=0).astype(BF)
        for i in range(X * CORE):
            small[i, d // Y, d % Y] = part
    start(stores)
    wait(stores)
    for p in range(pairs):
        wait(moves([gtarget.at[p]], [far_target.at[p]], far_sems.at[pl.ds(p, 1)]))


HBM = pl.ANY
FAR = pltpu.HBM
VMEM = pltpu.VMEM
SMEM = pltpu.SMEM


def call(kernel, name, args, spaces, outs, scratch, micros=1, limit=VMEM_LIMIT):
    cost = pl.CostEstimate(flops=micros * 10**9, bytes_accessed=micros * 3 * 10**6, transcendentals=0)
    return pl.pallas_call(
        kernel,
        out_shape=[FAR(s, d) if m is FAR else jax.ShapeDtypeStruct(s, d) for s, d, m in outs],
        in_specs=[pl.BlockSpec(memory_space=m) for m in spaces],
        out_specs=[pl.BlockSpec(memory_space=m) for unused, unused2, m in outs],
        scratch_shapes=scratch,
        compiler_params=pltpu.CompilerParams(vmem_limit_bytes=limit),
        cost_estimate=cost,
        name=name,
    )(*[pltpu.with_memory_space_constraint(a, m) if m is FAR else a for a, m in zip(args, spaces)])


def held_like(rows):
    return VMEM((X * CORE, Z, Y, rows, 128), BF)


def kept_like(slots):
    return VMEM((X * CORE, slots[1], Y, *slots[2:]), BF)


def sems(*shape):
    return pltpu.SemaphoreType.DMA(shape)


def weights_shape(shape, source):
    return (shape[0], HEADS // GROUP, GROUP * shape[1], source)


def slot_shape(count, extra=0):
    return (Y * X, Z, count * PIECE + extra, 128)


def self_forward(meta, target, pieces, steps):
    shape = target.shape
    return call(
        self_forward_kernel,
        "self_forward",
        [meta, target, *pieces],
        [SMEM, VMEM] + [FAR] * 8,
        [(shape, BF, FAR)] * 4
        + [(weights_shape(shape, shape[1]), BF, FAR), (shape, BF, FAR), (shape, BF, VMEM)]
        + [((TABLE + steps, shape[2]), F32, VMEM), ((1, 4 * shape[2]), F32, VMEM)],
        [VMEM(shape, BF)] * 4
        + [VMEM(weights_shape(shape, shape[1]), BF), held_like(SELF_ROWS), sems(8), sems(5), sems(shape[0])],
        14,
    )


def cross_forward(meta, target, mix_a, mems, vecs, pieces):
    shape = target.shape
    source = mems[0].shape[1] * X * CORE
    m_shape = (shape[0], source, shape[2])
    return call(
        cross_forward_kernel,
        "cross_forward",
        [meta, target, mix_a, *mems, vecs, *pieces],
        [SMEM] + [VMEM] * 2 + [HBM] * 4 + [VMEM] + [FAR] * 8,
        [(m_shape, BF, FAR), (shape, F32, FAR)] + [(shape, BF, FAR)] * 2 + [(m_shape, BF, FAR)] * 2
        + [(weights_shape(shape, source), BF, FAR), (shape, BF, FAR), (shape, F32, VMEM)],
        [VMEM(m_shape, BF), VMEM(shape, F32), VMEM(shape, BF), VMEM(shape, BF), VMEM(m_shape, BF)]
        + [VMEM(m_shape, BF), VMEM(shape, BF), VMEM(weights_shape(shape, source), BF)]
        + [held_like(CROSS_ROWS), sems(8), sems(4), sems(7), sems(shape[0])],
        30,
    )


def feed(meta, after_cross, cot, vecs, feed_bias, pieces):
    shape = after_cross.shape
    tokens, width = shape[0] * shape[1], shape[2]
    return call(
        feed_kernel,
        "feed",
        [meta, after_cross, cot, vecs, feed_bias, *pieces],
        [SMEM] + [VMEM] * 4 + [FAR] * 8,
        [(shape, BF, FAR), (shape, F32, VMEM), ((3, width), F32, VMEM), (feed_bias.shape, F32, VMEM)]
        + [(slot_shape(4, 256), BF, HBM)] * 2,
        [held_like(FEED_ROWS)] * 2
        + [VMEM((tokens, width), BF), VMEM((tokens, width), F32), VMEM((tokens, width), F32)]
        + [VMEM(shape, BF)]
        + [sems(8)] * 2 + [sems(1)],
        26,
    )


def cross_back(meta, gres, kept, memory, pieces):
    shape = gres.shape
    mshape = memory.shape
    return call(
        cross_back_kernel,
        "cross_back",
        [meta, gres, *kept, memory, *pieces],
        [SMEM, VMEM] + [FAR] * 7 + [FAR] * 8,
        [(shape, BF, VMEM), (mshape, BF, VMEM), (mshape, BF, VMEM), ((3, shape[2]), F32, VMEM)]
        + [(slot_shape(4), BF, HBM)] * 2,
        [VMEM(shape, BF), held_like(CROSS_ROWS), kept_like(slot_shape(4)), VMEM(shape, BF), VMEM(shape, BF)]
        + [VMEM(mshape, BF), VMEM(mshape, BF), VMEM(shape, BF), VMEM(mshape, BF), VMEM(kept[4].shape, BF)]
        + [sems(8)] * 2 + [sems(6), sems(shape[0])],
        15,
    )


def middle_back(meta, gres, grads, after_self, vecs, pieces):
    shape = gres.shape
    mshape = grads[1].shape
    part = (mshape[0], mshape[1] // (X * CORE), mshape[2])
    return call(
        middle_back_kernel,
        "middle_back",
        [meta, gres, *grads, after_self, vecs, *pieces],
        [SMEM] + [VMEM] * 4 + [FAR, VMEM] + [FAR] * 8,
        [(shape, F32, VMEM), (shape, BF, VMEM)] + [(part, BF, HBM)] * 4 + [((3, shape[2]), F32, VMEM)],
        [VMEM(mshape, BF), held_like(CROSS_ROWS), VMEM(shape, F32), sems(8), sems(4), sems(1)],
        8,
    )


def self_back(meta, gres, gmix, kept):
    shape = gmix.shape
    return call(
        self_back_kernel,
        "self_back",
        [meta, gres, gmix, *kept],
        [SMEM] + [VMEM] * 2 + [FAR] * 6,
        [(shape, BF, VMEM)] * 3 + [((2, shape[2]), F32, VMEM)] + [(slot_shape(4), BF, HBM)] * 2,
        [kept_like(slot_shape(4))] + [VMEM(shape, BF)] * 5 + [VMEM(kept[4].shape, BF)]
        + [sems(8), sems(5), sems(shape[0])],
        15,
    )


def last_back(meta, gres, grads, target, vecs, sums, dbias, pieces, steps):
    shape = gres.shape
    small = (Y * X, Z, SMALL_ROWS, 128)
    return call(
        last_back_kernel,
        "last_back",
        [meta, gres, *grads, target, vecs, *sums, dbias, *pieces],
        [SMEM] + [VMEM] * 11 + [FAR] * 8,
        [(shape, F32, FAR)] + [(small, BF, HBM)] * 2,
        [VMEM((steps, shape[2]), F32), held_like(3 * PIECE), kept_like(small), VMEM((2, shape[2]), F32)]
        + [VMEM(shape, F32)] + [sems(8)] * 2 + [sems(shape[0])],
        8,
    )


BOTH = ("dp", "mem")


def swap(array, mask):
    count = lax.axis_size("dp") * lax.axis_size("mem")
    return lax.ppermute(array, BOTH, [(i, i ^ mask) for i in range(count)])


def pack_kernel(*refs):
    squares, (w_in, w_out, biases, f_bias, gain, shift, table) = refs[:8], refs[8:15]
    square_out, feed_out, stage = refs[15:]
    for i, ref in enumerate(squares):
        if i < 3:
            square_out[PIECE * i : PIECE * (i + 1)] = ref[...]
        else:
            square_out[SELF_ROWS + PIECE * (i - 3) : SELF_ROWS + PIECE * (i - 2)] = ref[...]
    for i in range(4):
        feed_out[PIECE * i : PIECE * (i + 1)] = w_in[:, 128 * i : 128 * (i + 1)]
    feed_out[4 * PIECE :] = w_out[...]
    stage[...] = jnp.zeros_like(stage)
    stage[0:7, :64] = biases[...].astype(F32)
    stage[GAIN : GAIN + 3, :64] = gain[...].astype(F32)
    stage[SHIFT : SHIFT + 3, :64] = shift[...].astype(F32)
    rows = table[...].astype(F32)
    half = rows.shape[0] // 2
    stage[TABLE : TABLE + half] = jnp.concatenate([rows[:half], rows[half:]], axis=1)
    stage[TABLE + half : TABLE + half + 2] = f_bias[...].astype(F32)
    square_out[3 * PIECE : SELF_ROWS] = stage[...].astype(BF)


def assemble_kernel(meta, a, b, c, d, out):
    mine = meta[meta.shape[0] - 4]
    for i, one in enumerate((a, b, c, d)):
        out[mine ^ i] = one[...]


def assemble(meta, parts):
    return call(
        assemble_kernel,
        "assemble",
        [meta, *parts],
        [SMEM] + [VMEM] * 4,
        [((Z, *parts[0].shape), BF, VMEM)],
        [],
    )[0]


fence = lax.optimization_barrier


def swap_z(packed):
    return [packed, swap(packed, 8), swap(packed, 16), swap(packed, 24)]


def spread_near(along_z):
    return [along_z, swap(along_z, 2), swap(along_z, 4), swap(along_z, 6)]


def spread_core(near):
    out = []
    for one in near:
        out += [one, swap(one, 1)]
    return out


def merge_kernel(meta, a, b, c, d, own, s1, s2, s3):
    mine = meta[meta.shape[0] - 4]

    def total(z):
        return (a[z].astype(F32) + b[z].astype(F32)) + (c[z].astype(F32) + d[z].astype(F32))

    own[...] = total(mine)
    s1[...] = total(mine ^ 1).astype(BF)
    s2[...] = total(mine ^ 2).astype(BF)
    s3[...] = total(mine ^ 3).astype(BF)


def final_parts(refs, outs):
    own, a, b, c = refs

    def total(span):
        return (own[span] + a[span].astype(F32)) + (b[span].astype(F32) + c[span].astype(F32))

    at = 0
    for out in outs:
        rows = out.shape[0]
        for i in range(out.shape[1] // 128):
            out[:, 128 * i : 128 * (i + 1)] = total(slice(at, at + rows))
            at += rows
    return total, at


def final_kernel(*refs):
    final_parts(refs[:4], refs[4:])


def final_small_kernel(*refs):
    outs, (biases, f_bias, gain, shift, table) = refs[4:8], refs[8:]
    total, at = final_parts(refs[:4], outs)
    part = total(slice(at, at + SMALL_ROWS))
    biases[...] = part[0:7, :64]
    gain[...] = part[GAIN : GAIN + 3, :64]
    shift[...] = part[SHIFT : SHIFT + 3, :64]
    half = table.shape[0] // 2
    table[:half] = part[TABLE : TABLE + half, :64]
    table[half:] = part[TABLE : TABLE + half, 64:]
    f_bias[...] = part[TABLE + half : TABLE + half + 2]


def add(left, right):
    return (left.astype(F32) + right.astype(F32)).astype(BF)


def core_sums(own, other):
    return [add(own[i], other[i]) for i in range(Y * X)]


def join_kernel(own, other, small_own, small_other, *outs):
    rows = own.shape[2]
    for i, out in enumerate(outs):
        out[:, :rows] = add(own[i], other[i])
        out[:, rows:] = add(small_own[i], small_other[i])


def core_sums_joined(own, other, more_own, more_other):
    unused, z, rows, lanes = own.shape
    out = (z, rows + more_own.shape[2], lanes)
    return call(
        join_kernel,
        "join",
        [own, other, more_own, more_other],
        [VMEM] * 4,
        [(out, BF, VMEM)] * (Y * X),
        [],
    )


def near_parts(pairs):
    return [pairs[0], swap(pairs[1], 2), swap(pairs[2], 4), swap(pairs[3], 6)]


def chip_sums(meta, near):
    unused, rows, lanes = near[0].shape
    return call(
        merge_kernel,
        "merge",
        [meta, *near],
        [SMEM] + [VMEM] * 4,
        [((rows, lanes), F32, VMEM)] + [((rows, lanes), BF, VMEM)] * 3,
        [],
    )


def sent_z(parts):
    own, s1, s2, s3 = parts
    return [own, swap(s1, 8), swap(s2, 16), swap(s3, 24)]


def slice_sums(kernel, parts, shapes):
    return call(
        kernel,
        "final",
        parts,
        [VMEM] * 4,
        [(s, F32, VMEM) for s in shapes],
        [],
    )


def place_kernel(meta, a, b, c, d, out):
    base = meta.shape[0] - 4
    mine = meta[base + 2] * CORE + meta[base + 3]
    pairs = a.shape[0]
    for i, one in enumerate((a, b, c, d)):
        for p in range(pairs):
            out[(mine ^ i) * pairs + p] = one[p].astype(F32)


def swap_memory(memory, pairs):
    mine = lax.axis_index("mem")
    parts = [lax.dynamic_slice_in_dim(memory, (mine ^ i) * pairs, pairs) for i in range(4)]
    return parts


def return_memory(meta, parts, shape):
    return call(place_kernel, "place", [meta, *parts], [SMEM] + [VMEM] * 4, [(shape, F32, VMEM)], [])[0]


def slots_of(wide):
    rows, cols = wide.shape
    cut = wide.reshape(Z, Y, rows // (Z * Y), X, CORE, cols // (X * CORE))
    return [cut[:, y, :, x, c] for y, x, c in SLOTS]


def wide_of(slots):
    z, rows, cols = slots[0].shape
    cut = jnp.stack(slots).reshape(Y, X, CORE, z, rows, cols)
    return cut.transpose(3, 0, 4, 1, 2, 5).reshape(z * Y * rows, X * CORE * cols)


def gather_any(piece):
    return lax.all_gather(lax.all_gather(piece, "mem", axis=1, tiled=True), "dp", axis=0, tiled=True)


def scatter_any(wide):
    part = lax.psum_scatter(wide.astype(F32), "dp", scatter_dimension=0, tiled=True)
    return lax.psum_scatter(part, "mem", scatter_dimension=1, tiled=True)


def narrow_columns(slots):
    return [jnp.concatenate(jnp.split(one, 4, axis=2), axis=1) for one in slots]


def small_pieces(biases, f_bias, gain, shift, table):
    vectors = jnp.concatenate([biases, gain, shift], axis=0)
    vectors = jnp.pad(vectors, ((0, TABLE - vectors.shape[0]), (0, 0)))
    half = table.shape[0] // 2

    def cut(rows):
        return rows.reshape(rows.shape[0], Z, Y, 64).transpose(1, 2, 0, 3)

    top = jnp.pad(cut(vectors), ((0, 0),) * 3 + ((0, 64),))
    low = jnp.concatenate([cut(table[:half]), cut(table[half:])], axis=3)
    whole = jnp.concatenate([top, low, f_bias.reshape(Z, Y, 2, 128)], axis=2)
    return jnp.pad(whole, ((0, 0), (0, 0), (0, SMALL_ROWS - whole.shape[2]), (0, 0)))


def spread_any(squares, w_in, w_out, smalls):
    wide = [slots_of(gather_any(one)) for one in squares]
    small = small_pieces(*[lax.all_gather(one, "dp", axis=one.ndim - 1, tiled=True) for one in smalls])
    ins = narrow_columns(slots_of(gather_any(w_in)))
    outs = slots_of(gather_any(w_out))
    square_w, feed_w = [], []
    for i, (y, unused, unused2) in enumerate(SLOTS):
        parts = [one[i] for one in wide]
        square_w.append(jnp.concatenate([*parts[:3], small[:, y], *parts[3:]], axis=1))
        feed_w.append(jnp.concatenate([ins[i], outs[i]], axis=1))
    return square_w, feed_w


def by_slot(halves):
    return [halves[c][y * X + x] for y, x, c in SLOTS]


def reduce_squares_any(halves, count):
    slots = by_slot(halves)
    return [
        scatter_any(wide_of([one[:, PIECE * i : PIECE * (i + 1)] for one in slots]))
        for i in range(count)
    ]


def reduce_feed_any(halves):
    slots = by_slot(halves)
    ins = [
        jnp.concatenate([one[:, PIECE * j : PIECE * (j + 1)] for j in range(4)], axis=2)
        for one in slots
    ]
    return [scatter_any(wide_of(ins)), scatter_any(wide_of([one[:, 4 * PIECE :] for one in slots]))]


def reduce_small_any(halves, count):
    parts = [halves[0][y * X].astype(F32) for y in range(Y)]
    part = jnp.stack(parts, axis=1).reshape(Z * Y, SMALL_ROWS, 128)
    vectors = part[:, :13, :64].transpose(1, 0, 2).reshape(13, -1)
    half = count // 2
    table = part[:, TABLE : TABLE + half]
    table = jnp.concatenate([table[:, :, :64], table[:, :, 64:]], axis=1)
    rows = jnp.concatenate([vectors, table.transpose(1, 0, 2).reshape(count, -1)], axis=0)
    cut = lax.psum_scatter(lax.psum(rows, "mem"), "dp", scatter_dimension=1, tiled=True)
    f_bias = part[:, TABLE + half : TABLE + half + 2].reshape(-1)
    f_bias = lax.psum_scatter(lax.psum(f_bias, "mem"), "dp", scatter_dimension=0, tiled=True)
    return cut[:7], f_bias, cut[7:10], cut[10:13], cut[13:]


def shards(
    target, memory, time_steps, target_len, source_len, source_off, cotangent,
    self_query, self_key, self_value, self_out, cross_query, cross_key, cross_value, cross_out,
    feed_in, feed_out, biases, feed_bias, norm_gain, norm_shift, step_table,
):
    pairs = target.shape[0]
    steps = step_table.shape[0]
    dp, mem = lax.axis_index("dp"), lax.axis_index("mem")
    quick = lax.axis_size("dp") == Z * Y and lax.axis_size("mem") == X * CORE
    here = [dp // 2, dp % 2, mem // 2, mem % 2] if quick else [0, 0, 0, 0]
    meta = jnp.concatenate(
        [
            target_len,
            time_steps,
            lax.dynamic_slice_in_dim(source_off, mem * pairs, pairs),
            lax.dynamic_slice_in_dim(source_len, mem * pairs, pairs),
            jnp.stack([jnp.asarray(i, jnp.int32) for i in here]),
        ]
    )
    squares = (self_query, self_key, self_value, self_out, cross_query, cross_key, cross_value, cross_out)
    if quick:
        packed = call(
            pack_kernel,
            "pack",
            [*squares, feed_in, feed_out, biases, feed_bias.reshape(2, 128)]
            + [norm_gain, norm_shift, step_table],
            [VMEM] * 15,
            [((i, 128), BF, VMEM) for i in (SELF_ROWS + CROSS_ROWS, FEED_ROWS)],
            [VMEM((SMALL_ROWS, 128), F32)],
            1,
            60 * 2**20,
        )
        packed, memory = fence((packed, memory))
        square_p, feed_p = packed
        mems = swap_memory(memory, pairs)
        square_z = swap_z(square_p)
        mems = [mems[0], mems[1], swap(mems[2], 2), swap(mems[3], 3)]
        square_z, mems, feed_p = fence((square_z, mems, feed_p))
        square_near = spread_near(assemble(meta, square_z))
        feed_z = swap_z(feed_p)
        mems[1] = swap(mems[1], 1)
        square_near, feed_z, mems = fence((square_near, feed_z, mems))
        square_w = spread_core(square_near)
        feed_z = assemble(meta, feed_z)
        square_w, feed_z = fence((square_w, feed_z))
        feed_near = spread_near(feed_z)
    else:
        square_w, feed_w = spread_any(
            squares, feed_in, feed_out, (biases, feed_bias, norm_gain, norm_shift, step_table)
        )
        own = lax.all_to_all(memory, "mem", 0, 1, tiled=True)
        mems = jnp.split(own, X * CORE, axis=1)

    in_a, q_a, k_a, v_a, w_a, mix_a, near_mix, vecs, fbias = self_forward(meta, target, square_w, steps)
    own_memory, after_self, in_b, q_b, k_b, v_b, w_b, mix_b, after_cross = cross_forward(
        meta, target, near_mix, mems, vecs, square_w
    )
    if quick:
        feed_near, after_cross = fence((feed_near, after_cross))
        feed_w = spread_core(feed_near)
    layer_out, gres_c, sums_c, d_fbias, *d_feed = feed(
        meta, after_cross, cotangent, vecs, fbias, feed_w
    )
    if quick:
        d_feed, gres_c = fence((d_feed, gres_c))
        d_feed[1] = swap(d_feed[1], 1)
    gq_b, gk_b, gv_b, sums_b, *d_cross = cross_back(
        meta, gres_c, (in_b, q_b, k_b, v_b, w_b, mix_b), own_memory, square_w
    )
    if quick:
        d_feed, gq_b, d_cross = fence((d_feed, gq_b, d_cross))
        u_first = core_sums_joined(*d_feed, d_cross[0], swap(d_cross[1], 1))
        u_first, gq_b = fence((u_first, gq_b))
        n_first = near_parts(u_first)
    gres_b, gmix_a, *gmem, sums_m = middle_back(
        meta, gres_c, (gq_b, gk_b, gv_b), after_self, vecs, square_w
    )
    gq_a, gk_a, gv_a, sums_a, *d_self = self_back(meta, gres_b, gmix_a, (in_a, q_a, k_a, v_a, w_a, mix_a))
    if quick:
        n_first, gmem, gq_a, d_self = fence((n_first, gmem, gq_a, d_self))
        m_first = chip_sums(meta, n_first)
        m_first, gmem, gq_a, d_self = fence((m_first, gmem, gq_a, d_self))
        m_first = sent_z(m_first)
        gmem = [gmem[0], gmem[1], swap(gmem[2], 2), swap(gmem[3], 3)]
    grad_target, *d_small = last_back(
        meta, gres_b, (gq_a, gk_a, gv_a), target, vecs, (sums_a, sums_m, sums_b, sums_c), d_fbias, square_w, steps
    )
    if quick:
        one = self_query.shape
        m_first, gmem, d_self, d_small = fence((m_first, gmem, d_self, d_small))
        u_self = core_sums_joined(d_self[0], swap(d_self[1], 1), d_small[0], swap(d_small[1], 1))
        gmem[1] = swap(gmem[1], 1)
        u_self, gmem, m_first = fence((u_self, gmem, m_first))
        n_self = near_parts(u_self)
        g_feed_in, g_feed_out, *g_cross = slice_sums(
            final_kernel, m_first, (feed_in.shape, feed_out.shape) + (one,) * 4
        )
        grad_memory = return_memory(meta, gmem, memory.shape)
        n_self, g_feed_in, grad_memory = fence((n_self, g_feed_in, grad_memory))
        m_self = sent_z(chip_sums(meta, n_self))
        small_shapes = (biases.shape, (2, 128), norm_gain.shape, norm_shift.shape, step_table.shape)
        out = slice_sums(final_small_kernel, m_self, (one,) * 4 + small_shapes)
        g_self, (g_bias, g_fbias, g_gain, g_shift, g_table) = out[:4], out[4:]
        g_feed = [g_feed_in, g_feed_out]
        g_fbias = g_fbias.reshape(feed_bias.shape)
    else:
        whole = jnp.concatenate(gmem, axis=1)
        grad_memory = lax.all_to_all(whole, "mem", 1, 0, tiled=True).astype(F32)
        g_feed = reduce_feed_any(d_feed)
        g_cross = reduce_squares_any(d_cross, 4)
        g_self = reduce_squares_any(d_self, 4)
        g_bias, g_fbias, g_gain, g_shift, g_table = reduce_small_any(d_small, steps)
    return (
        layer_out, grad_target, grad_memory, *g_self, *g_cross, *g_feed,
        g_bias, g_fbias, g_gain, g_shift, g_table,
    )


def solution(mesh):
    rows = P(BOTH, None, None)
    piece = P("dp", "mem")
    vector = P(None, "dp")
    mem_rows = P("dp", "mem", None)
    return jax.shard_map(
        shards,
        mesh=mesh,
        in_specs=(rows, mem_rows, P(BOTH), P(BOTH), P("dp"), P("dp"), rows)
        + (piece,) * 10
        + (vector, P("dp"), vector, vector, vector),
        out_specs=(rows, rows, mem_rows) + (piece,) * 10 + (vector, P("dp"), vector, vector, vector),
        check_vma=False,
    )
```

```python
import functools
import math

import jax
import jax.numpy as jnp
from jax import lax
from jax.experimental import pallas as pl
from jax.experimental.pallas import tpu as pltpu
from jax.sharding import PartitionSpec as P

HEADS = 8
DH = 64
GROUP = 4
WIDE = GROUP * DH
EPSILON = 1e-05
SCALE = 1.0 / math.sqrt(DH)
BF = jnp.bfloat16
F32 = jnp.float32
VMEM_LIMIT = 40 * 2**20


def contract(left, right, left_dim, right_dim):
    return lax.dot_general(
        left, right, (((left_dim,), (right_dim,)), ((), ())), preferred_element_type=F32
    )


def mul(left, right):
    return contract(left, right, 1, 0)


def mul_nt(left, right):
    return contract(left, right, 1, 1)


def mul_tn(left, right):
    return contract(left, right, 0, 0)


def normalise(signal):
    centre = signal - jnp.mean(signal, axis=-1, keepdims=True)
    inverse = lax.rsqrt(jnp.mean(centre * centre, axis=-1, keepdims=True) + EPSILON)
    return centre * inverse, inverse


def norm_back(grad, scaled, inverse, gain):
    up = grad * gain
    return inverse * (
        up
        - jnp.mean(up, axis=-1, keepdims=True)
        - scaled * jnp.mean(up * scaled, axis=-1, keepdims=True)
    )


def col_sum(array):
    return jnp.sum(array.astype(F32), axis=0, keepdims=True)


def head_of_lane(rows):
    return lax.broadcasted_iota(jnp.int32, (rows, WIDE), 1) // DH


def stacked(block, lane_head):
    zero = jnp.zeros_like(block)
    return jnp.concatenate([jnp.where(lane_head == h, block, zero) for h in range(GROUP)], axis=0)


def unstacked(result, lane_head, rows):
    picked = result[:rows]
    for h in range(1, GROUP):
        picked = jnp.where(lane_head == h, result[h * rows : (h + 1) * rows], picked)
    return picked


def blocks(pairs):
    return [(p, g, slice(g * WIDE, (g + 1) * WIDE)) for p in range(pairs) for g in range(HEADS // GROUP)]


def attend(bias_of, q_ref, k_ref, v_ref, w_ref, mix_ref, done):
    pairs, rows, unused = q_ref.shape
    lane_head = head_of_lane(rows)
    every = blocks(pairs)

    def scores_of(p, g, cols):
        return mul_nt(stacked(q_ref[p, :, cols], lane_head), k_ref[p, :, cols])

    ahead = scores_of(*every[0])
    for i, (p, g, cols) in enumerate(every):
        scores = ahead + bias_of(p)
        if i + 1 < len(every):
            ahead = scores_of(*every[i + 1])
        top = jnp.max(scores, axis=-1, keepdims=True)
        raised = jnp.exp(scores - top)
        total = jnp.sum(raised, axis=-1, keepdims=True)
        weights = (raised * (1.0 / total)).astype(BF)
        w_ref[p, g] = weights
        mixed = mul(weights, v_ref[p, :, cols])
        mix_ref[p, :, cols] = unstacked(mixed, lane_head, rows).astype(BF)
        if g == HEADS // GROUP - 1:
            done(p)


def attend_back(ready, q_ref, k_ref, v_ref, w_ref, grad_ref, gq_ref, gk_ref, gv_ref):
    pairs, rows, unused = q_ref.shape
    lane_head = head_of_lane(rows)
    every = blocks(pairs)

    def weight_grads(p, g, cols):
        grads = stacked(grad_ref[p, :, cols], lane_head)
        return grads, mul_nt(grads, v_ref[p, :, cols])

    ahead = weight_grads(*every[0])
    for i, (p, g, cols) in enumerate(every):
        grads, grad_w = ahead
        if i + 1 < len(every):
            ahead = weight_grads(*every[i + 1])
        if g == 0:
            ready(p)
        weights = w_ref[p, g]
        wide = weights.astype(F32)
        offset = jnp.sum(grad_w * wide, axis=-1, keepdims=True)
        grad_s = (wide * (grad_w - offset)).astype(BF)
        grad_q = unstacked(mul(grad_s, k_ref[p, :, cols]), lane_head, rows)
        gq_ref[p, :, cols] = (grad_q * SCALE).astype(BF)
        gk_ref[p, :, cols] = mul_tn(grad_s, stacked(q_ref[p, :, cols], lane_head)).astype(BF)
        gv_ref[p, :, cols] = mul_tn(weights, grads).astype(BF)


def flat(ref):
    value = ref[...]
    return value.reshape(value.shape[0] * value.shape[1], value.shape[2])


Z, Y, X, CORE = 4, 2, 2, 2
SLOTS = [(y, x, c) for y in range(Y) for x in range(X) for c in range(CORE)]
PIECE = 64
FEED_ROWS = 4 * PIECE + 256
SMALL_ROWS = 48
SELF_ROWS = 3 * PIECE + SMALL_ROWS
CROSS_ROWS = 5 * PIECE
GAIN, SHIFT, TABLE = 7, 10, 16


def places(meta, slot):
    base = meta.shape[0] - 4
    y, x, c = slot
    return y ^ meta[base + 1], (x ^ meta[base + 2]) * CORE + (c ^ meta[base + 3])


def load_copies(meta, sources, held, sems, first=0):
    copies = []
    rows = held.shape[-2]
    for i, slot in enumerate(SLOTS):
        row, panel = places(meta, slot)
        source = sources[i].at[:, pl.ds(first, rows)]
        copies.append(pltpu.make_async_copy(source, held.at[panel, :, row], sems.at[i]))
    return copies


def store_copies(meta, held, targets, sems, first=0):
    copies = []
    rows = targets[0].shape[2]
    for i, slot in enumerate(SLOTS):
        row, panel = places(meta, slot)
        y, x, c = slot
        target = targets[c].at[y * X + x]
        source = held.at[panel, :, row, pl.ds(first, rows)]
        copies.append(pltpu.make_async_copy(source, target, sems.at[i]))
    return copies


def start(copies):
    for copy in copies:
        copy.start()


def wait(copies):
    for copy in copies:
        copy.wait()


def moves(sources, targets, sems):
    return [pltpu.make_async_copy(a, b, sems.at[i]) for i, (a, b) in enumerate(zip(sources, targets))]


def joined(value):
    return value.reshape(-1, value.shape[-1])


def square(held, index):
    span = slice(PIECE * index, PIECE * (index + 1))
    return jnp.concatenate([joined(held[i, :, :, span]) for i in range(X * CORE)], axis=1)


def keep(held, index, value):
    span = slice(PIECE * index, PIECE * (index + 1))
    for i in range(X * CORE):
        part = value[:, i * 128 : (i + 1) * 128].astype(BF)
        held[i, :, :, span] = part.reshape(Z, Y, PIECE, 128)


def self_forward_kernel(meta, target, *refs):
    pieces, refs = refs[:8], refs[8:]
    far, (mix, vecs, fbias), refs = refs[:6], refs[6:9], refs[9:]
    in_a, q, k, v, w, held, sems, far_sems, w_sems = refs
    copies = moves((in_a, q, k, v, mix), (*far[:4], far[5]), far_sems)
    loads = load_copies(meta, pieces, held, sems)
    start(loads)
    pairs, length, width = target.shape
    shape = target.shape
    wait(loads)
    every = [held[0, z, y, 3 * PIECE :].astype(F32) for z in range(Z) for y in range(Y)]
    steps = (vecs.shape[0] - TABLE) // 2
    vecs[:TABLE] = jnp.concatenate([one[:TABLE, :64] for one in every], axis=1)
    for i in range(2):
        part = [one[TABLE : TABLE + steps, 64 * i : 64 * (i + 1)] for one in every]
        vecs[TABLE + i * steps : TABLE + (i + 1) * steps] = jnp.concatenate(part, axis=1)
    for d, one in enumerate(every):
        for i in range(2):
            at = TABLE + steps + i
            fbias[:, d * 256 + i * 128 : d * 256 + (i + 1) * 128] = one[at : at + 1]
    for p in range(pairs):
        emb = target[p].astype(F32) + vecs[pl.ds(TABLE + meta[pairs + p], 1), :]
        scaled, unused = normalise(emb)
        in_a[p] = (scaled * vecs[GAIN : GAIN + 1] + vecs[SHIFT : SHIFT + 1]).astype(BF)
    copies[0].start()
    x = flat(in_a)
    q[...] = ((mul(x, square(held, 0)) + vecs[0:1]).astype(BF) * SCALE).reshape(shape)
    k[...] = mul(x, square(held, 1)).astype(BF).reshape(shape)
    v[...] = (mul(x, square(held, 2)) + vecs[1:2]).astype(BF).reshape(shape)
    start(copies[1:4])

    w_copies = moves([w.at[p] for p in range(pairs)], [far[4].at[p] for p in range(pairs)], w_sems)

    def bias_of(p):
        spot = lax.broadcasted_iota(jnp.int32, (1, length), 1)
        return jnp.where(spot < meta[p], 0.0, -1e30)

    attend(bias_of, q, k, v, w, mix, lambda p: w_copies[p].start())
    copies[4].start()
    wait(copies)
    wait(w_copies)


def cross_forward_kernel(meta, target, mix_a, mem_0, mem_1, mem_2, mem_3, vecs, *refs):
    pieces, refs = refs[:8], refs[8:]
    far, after, refs = refs[:8], refs[8], refs[9:]
    memory, after_self, in_b, q, k, v, mix, w, held, sems, mem_sems, far_sems, w_sems = refs
    copies = moves((memory, after_self, in_b, q, k, v, mix), (*far[:6], far[7]), far_sems)
    pairs, length, width = target.shape
    shape = target.shape
    source = memory.shape[1]
    base = meta.shape[0] - 4
    mine = meta[base + 2] * CORE + meta[base + 3]
    part = source // (X * CORE)
    mem_loads = [
        pltpu.make_async_copy(
            one, memory.at[:, pl.ds(pl.multiple_of((mine ^ i) * part, part), part), :], mem_sems.at[i]
        )
        for i, one in enumerate((mem_0, mem_1, mem_2, mem_3))
    ]
    start(mem_loads)
    loads = load_copies(meta, pieces, held, sems, SELF_ROWS)
    start(loads)
    wait(loads)
    branch = (mul(flat(mix_a), square(held, 0)) + vecs[2:3]).reshape(shape)
    for p in range(pairs):
        row = vecs[pl.ds(TABLE + meta[pairs + p], 1), :]
        after_self[p] = target[p].astype(F32) + row + branch[p]
    scaled, unused = normalise(flat(after_self))
    x = (scaled * vecs[GAIN + 1 : GAIN + 2] + vecs[SHIFT + 1 : SHIFT + 2]).astype(BF)
    in_b[...] = x.reshape(shape)
    q[...] = ((mul(x, square(held, 1)) + vecs[3:4]).astype(BF) * SCALE).reshape(shape)
    start(copies[1:4])
    wait(mem_loads)
    copies[0].start()
    m = flat(memory)
    k[...] = mul(m, square(held, 2)).astype(BF).reshape(memory.shape)
    v[...] = (mul(m, square(held, 3)) + vecs[4:5]).astype(BF).reshape(memory.shape)
    start(copies[4:6])

    w_copies = moves([w.at[p] for p in range(pairs)], [far[6].at[p] for p in range(pairs)], w_sems)

    def bias_of(p):
        spot = lax.broadcasted_iota(jnp.int32, (1, source), 1)
        begin = meta[2 * pairs + p]
        end = begin + meta[3 * pairs + p]
        return jnp.where((spot >= begin) & (spot < end), 0.0, -1e30)

    attend(bias_of, q, k, v, w, mix, lambda p: w_copies[p].start())
    copies[6].start()
    after[...] = after_self[...] + (mul(flat(mix), square(held, 4)) + vecs[5:6]).reshape(shape)
    wait(copies)
    wait(w_copies)


def gelu_parts(value):
    size = jnp.abs(value) * math.sqrt(0.5)
    t = 1.0 / (1.0 + 0.3275911 * size)
    bell = jnp.exp(-0.5 * value * value)
    tail = (
        t
        * (
            0.5 * 0.254829592
            + t
            * (
                0.5 * -0.284496736
                + t * (0.5 * 1.421413741 + t * (0.5 * -1.453152027 + t * (0.5 * 1.061405429)))
            )
        )
        * bell
    )
    below = jnp.where(value < 0, tail, 1.0 - tail)
    slope = below + value * bell * (1.0 / math.sqrt(2.0 * math.pi))
    return value * below, slope


def feed_kernel(meta, after_cross, cot, vecs, feed_bias, *refs):
    pieces, refs = refs[:8], refs[8:]
    far_out, gres, sums, dbias = refs[:4]
    targets, refs = refs[4:8], refs[8:]
    held, kept, x_c, act, grad_pre, layer_out, sems, out_sems, far_sems = refs
    copies = moves((layer_out,), (far_out,), far_sems)
    loads = load_copies(meta, pieces, held, sems)
    start(loads)
    stores = store_copies(meta, kept, targets[:2], out_sems.at[0])
    stores += store_copies(meta, kept, targets[2:], out_sems.at[1], 4 * PIECE)
    shape = after_cross.shape
    signal = flat(after_cross)
    scaled, inverse = normalise(signal)
    gain = vecs[GAIN + 2 : GAIN + 3]
    x_c[...] = (scaled * gain + vecs[SHIFT + 2 : SHIFT + 3]).astype(BF)
    wait(loads)
    c = flat(cot)
    x = x_c[...]
    w_in = [
        jnp.concatenate([joined(held[j, :, :, PIECE * i : PIECE * (i + 1)]) for i in range(4)], axis=1)
        for j in range(4)
    ]
    w_out = [jnp.concatenate([joined(held[i, j, :, 4 * PIECE :]) for i in range(4)], axis=1) for j in range(4)]
    w_in = jnp.concatenate(w_in, axis=1)
    w_out = jnp.concatenate(w_out, axis=0)
    block = 256
    count = w_in.shape[1] // block

    def first(j):
        cols = slice(j * block, (j + 1) * block)
        return mul(x, w_in[:, cols]), mul_nt(c, w_out[cols])

    ready = [first(j) for j in range(1)]
    for j in range(count):
        cols = slice(j * block, (j + 1) * block)
        if j + 1 < count:
            ready.append(first(j + 1))
        pre, grad_act = ready[j]
        value, slope = gelu_parts(pre + feed_bias[:, cols])
        act[:, cols] = value.astype(BF)
        grad = (grad_act * slope).astype(BF)
        grad_pre[:, cols] = grad
        dbias[:, cols] = col_sum(grad)
    for j in range(4):
        cols = slice(j * 512, (j + 1) * 512)
        d_out = mul_tn(act[:, cols], c)
        for i in range(4):
            part = d_out[:, i * 128 : (i + 1) * 128].astype(BF)
            kept[i, j, :, 4 * PIECE :] = part.reshape(Y, 256, 128)
        d_in = mul_tn(x, grad_pre[:, cols])
        for i in range(4):
            part = d_in[:, i * 128 : (i + 1) * 128].astype(BF)
            kept[j, :, :, PIECE * i : PIECE * (i + 1)] = part.reshape(Z, Y, PIECE, 128)
    start(stores)
    layer_out[...] = (signal + mul(act[...], w_out) + vecs[6:7]).astype(BF).reshape(shape)
    start(copies)
    grad = mul_nt(grad_pre[...], w_in)
    wide_cot = flat(cot).astype(F32)
    sums[0:1] = col_sum(wide_cot)
    sums[1:2] = col_sum(grad * scaled)
    sums[2:3] = col_sum(grad)
    gres[...] = (wide_cot + norm_back(grad, scaled, inverse, gain)).reshape(shape)
    wait(stores)
    wait(copies)


def cross_back_kernel(meta, gres, far_in, far_q, far_k, far_v, far_w, far_mix, far_memory, *refs):
    pieces, refs = refs[:8], refs[8:]
    gq, gk, gv, sums = refs[:4]
    targets, refs = refs[4:6], refs[6:]
    gmix, held, kept, mix, q, k, v, in_b, memory, w, sems, out_sems, far_sems, w_sems = refs
    copies = moves(
        (far_mix, far_q, far_k, far_v, far_in, far_memory), (mix, q, k, v, in_b, memory), far_sems
    )
    loads = load_copies(meta, pieces, held, sems, SELF_ROWS)
    copies[0].start()
    start(loads)
    start(copies[1:4])
    w_copies = moves([far_w.at[p] for p in range(w.shape[0])], [w.at[p] for p in range(w.shape[0])], w_sems)
    start(w_copies)
    start(copies[4:])
    stores = store_copies(meta, kept, targets, out_sems)
    shape = gres.shape
    grad = flat(gres).astype(BF)
    sums[0:1] = col_sum(grad)
    copies[0].wait()
    keep(kept, 3, mul_tn(flat(mix), grad))
    wait(loads)
    gmix[...] = mul_nt(grad, square(held, 4)).astype(BF).reshape(shape)
    wait(copies[1:4])

    attend_back(lambda p: w_copies[p].wait(), q, k, v, w, gmix, gq, gk, gv)
    wait(copies[4:])
    m = flat(memory)
    keep(kept, 0, mul_tn(flat(in_b), flat(gq)))
    keep(kept, 1, mul_tn(m, flat(gk)))
    keep(kept, 2, mul_tn(m, flat(gv)))
    start(stores)
    sums[1:2] = col_sum(flat(gq))
    sums[2:3] = col_sum(flat(gv))
    wait(stores)


def lower_back_kernel(
    meta, gres, grad_q, grad_k, grad_v, far_after, far_mix, far_in, far_q, far_k, far_v, far_w, vecs, *refs
):
    pieces, refs = refs[:8], refs[8:]
    gres_out, gq, gk, gv, gmem_0, gmem_1, gmem_2, gmem_3, sums = refs[:9]
    targets, refs = refs[9:11], refs[11:]
    gmem, held, after_self, gmix, kept, mix, q, k, v, in_a, w = refs[:11]
    load_sems, mem_sems, far_sems, out_sems, w_sems = refs[11:]
    loads = load_copies(meta, pieces, held, load_sems, SELF_ROWS)
    start(loads)
    copies = moves(
        (far_after, far_mix, far_q, far_k, far_v, far_in), (after_self, mix, q, k, v, in_a), far_sems
    )
    start(copies[:5])
    w_copies = moves([far_w.at[p] for p in range(w.shape[0])], [w.at[p] for p in range(w.shape[0])], w_sems)
    start(w_copies)
    copies[5].start()
    stores = store_copies(meta, kept, targets, out_sems)
    shape = gres.shape
    wait(loads)
    grad_m = mul_nt(flat(grad_k), square(held, 2)) + mul_nt(flat(grad_v), square(held, 3))
    gmem[...] = grad_m.astype(BF).reshape(gmem.shape)
    base = meta.shape[0] - 4
    mine = meta[base + 2] * CORE + meta[base + 3]
    part = gmem.shape[1] // (X * CORE)
    mem_stores = [
        pltpu.make_async_copy(
            gmem.at[:, pl.ds(pl.multiple_of((mine ^ i) * part, part), part), :], one, mem_sems.at[i]
        )
        for i, one in enumerate((gmem_0, gmem_1, gmem_2, gmem_3))
    ]
    start(mem_stores)
    grad_in = mul_nt(flat(grad_q), square(held, 1))
    copies[0].wait()
    scaled, inverse = normalise(flat(after_self))
    sums[0:1] = col_sum(grad_in * scaled)
    sums[1:2] = col_sum(grad_in)
    total = flat(gres) + norm_back(grad_in, scaled, inverse, vecs[GAIN + 1 : GAIN + 2])
    gres_out[...] = total.reshape(shape)
    grad_a = total.astype(BF)
    sums[2:3] = col_sum(grad_a)
    gmix[...] = mul_nt(grad_a, square(held, 0)).astype(BF).reshape(shape)
    copies[1].wait()
    keep(kept, 3, mul_tn(flat(mix), grad_a))
    wait(copies[2:5])

    attend_back(lambda p: w_copies[p].wait(), q, k, v, w, gmix, gq, gk, gv)
    copies[5].wait()
    x = flat(in_a)
    for i, one in enumerate((gq, gk, gv)):
        keep(kept, i, mul_tn(x, flat(one)))
    start(stores)
    sums[3:4] = col_sum(flat(gq))
    sums[4:5] = col_sum(flat(gv))
    wait(mem_stores)
    wait(stores)


def last_back_kernel(meta, gres, gq, gk, gv, target, vecs, sums_a, sums_b, sums_c, dbias, *refs):
    pieces, refs = refs[:8], refs[8:]
    far_target, own, other, gtable, held, small, sums, gtarget, sems, out_sems, far_sems = refs
    loads = load_copies(meta, pieces, held, sems)
    start(loads)
    stores = store_copies(meta, small, (own, other), out_sems)
    shape = gres.shape
    pairs = shape[0]
    wait(loads)
    grad_in = (
        mul_nt(flat(gq), square(held, 0))
        + mul_nt(flat(gk), square(held, 1))
        + mul_nt(flat(gv), square(held, 2))
    ).reshape(shape)
    gtable[...] = jnp.zeros_like(gtable)
    for p in range(pairs):
        emb = target[p].astype(F32) + vecs[pl.ds(TABLE + meta[pairs + p], 1), :]
        scaled, inverse = normalise(emb)
        gain_part = col_sum(grad_in[p] * scaled)
        shift_part = col_sum(grad_in[p])
        if p == 0:
            sums[0:1] = gain_part
            sums[1:2] = shift_part
        else:
            sums[0:1] += gain_part
            sums[1:2] += shift_part
        out = gres[p] + norm_back(grad_in[p], scaled, inverse, vecs[GAIN : GAIN + 1])
        gtarget[p] = out
        copies = moves([gtarget.at[p]], [far_target.at[p]], far_sems.at[pl.ds(p, 1)])
        start(copies)
        gtable[pl.ds(meta[pairs + p], 1), :] += col_sum(out)
    rows = [sums_a[3:4], sums_a[4:5], sums_a[2:3], sums_b[1:2], sums_b[2:3], sums_b[0:1], sums_c[0:1]]
    rows += [sums[0:1], sums_a[0:1], sums_c[1:2], sums[1:2], sums_a[1:2], sums_c[2:3]]
    vectors = jnp.concatenate(rows + [jnp.zeros((TABLE - len(rows), shape[2]), F32)], axis=0)
    steps = gtable.shape[0] // 2
    for d in range(Z * Y):
        lanes = slice(d * 64, (d + 1) * 64)
        top = jnp.concatenate([vectors[:, lanes], jnp.zeros((TABLE, 64), F32)], axis=1)
        low = jnp.concatenate([gtable[:steps, lanes], gtable[steps:, lanes]], axis=1)
        tail = [dbias[:, d * 256 + i * 128 : d * 256 + (i + 1) * 128] for i in range(2)]
        fill = jnp.zeros((SMALL_ROWS - TABLE - steps - 2, 128), F32)
        part = jnp.concatenate([top, low, *tail, fill], axis=0).astype(BF)
        for i in range(X * CORE):
            small[i, d // Y, d % Y] = part
    start(stores)
    wait(stores)
    for p in range(pairs):
        wait(moves([gtarget.at[p]], [far_target.at[p]], far_sems.at[pl.ds(p, 1)]))


HBM = pl.ANY
FAR = pltpu.HBM
VMEM = pltpu.VMEM
SMEM = pltpu.SMEM


def call(kernel, name, args, spaces, outs, scratch, micros=1, limit=VMEM_LIMIT):
    cost = pl.CostEstimate(flops=int(micros * 10**9), bytes_accessed=int(micros * 3 * 10**6), transcendentals=0)
    function = pl.pallas_call(
        kernel,
        out_shape=[FAR(s, d) if m is FAR else jax.ShapeDtypeStruct(s, d) for s, d, m in outs],
        in_specs=[pl.BlockSpec(memory_space=m) for m in spaces],
        out_specs=[pl.BlockSpec(memory_space=m) for unused, unused2, m in outs],
        scratch_shapes=scratch,
        compiler_params=pltpu.CompilerParams(vmem_limit_bytes=limit),
        cost_estimate=cost,
        name=name,
    )
    return list(function(*[pltpu.with_memory_space_constraint(a, m) if m is FAR else a for a, m in zip(args, spaces)]))


def held_like(rows):
    return VMEM((X * CORE, Z, Y, rows, 128), BF)


def kept_like(slots):
    return VMEM((X * CORE, slots[1], Y, *slots[2:]), BF)


def sems(*shape):
    return pltpu.SemaphoreType.DMA(shape)


def weights_shape(shape, source):
    return (shape[0], HEADS // GROUP, GROUP * shape[1], source)


def slot_shape(count, extra=0):
    return (Y * X, Z, count * PIECE + extra, 128)


def self_forward(meta, target, pieces, steps):
    shape = target.shape
    return call(
        self_forward_kernel,
        "self_forward",
        [meta, target, *pieces],
        [SMEM, VMEM] + [FAR] * 8,
        [(shape, BF, FAR)] * 4
        + [(weights_shape(shape, shape[1]), BF, FAR), (shape, BF, FAR), (shape, BF, VMEM)]
        + [((TABLE + steps, shape[2]), F32, VMEM), ((1, 4 * shape[2]), F32, VMEM)],
        [VMEM(shape, BF)] * 4
        + [VMEM(weights_shape(shape, shape[1]), BF), held_like(SELF_ROWS), sems(8), sems(5), sems(shape[0])],
        0.1,
    )


def cross_forward(meta, target, mix_a, mems, vecs, pieces):
    shape = target.shape
    source = mems[0].shape[1] * X * CORE
    m_shape = (shape[0], source, shape[2])
    return call(
        cross_forward_kernel,
        "cross_forward",
        [meta, target, mix_a, *mems, vecs, *pieces],
        [SMEM] + [VMEM] * 2 + [HBM] * 4 + [VMEM] + [FAR] * 8,
        [(m_shape, BF, FAR), (shape, F32, FAR)] + [(shape, BF, FAR)] * 2 + [(m_shape, BF, FAR)] * 2
        + [(weights_shape(shape, source), BF, FAR), (shape, BF, FAR), (shape, F32, VMEM)],
        [VMEM(m_shape, BF), VMEM(shape, F32), VMEM(shape, BF), VMEM(shape, BF), VMEM(m_shape, BF)]
        + [VMEM(m_shape, BF), VMEM(shape, BF), VMEM(weights_shape(shape, source), BF)]
        + [held_like(CROSS_ROWS), sems(8), sems(4), sems(7), sems(shape[0])],
        0.1,
    )


def feed(meta, after_cross, cot, vecs, feed_bias, pieces):
    shape = after_cross.shape
    tokens, width = shape[0] * shape[1], shape[2]
    return call(
        feed_kernel,
        "feed",
        [meta, after_cross, cot, vecs, feed_bias, *pieces],
        [SMEM] + [VMEM] * 4 + [FAR] * 8,
        [(shape, BF, FAR), (shape, F32, VMEM), ((3, width), F32, VMEM), (feed_bias.shape, F32, VMEM)]
        + [(slot_shape(4), BF, HBM)] * 4,
        [held_like(FEED_ROWS)] * 2
        + [VMEM((tokens, width), BF)] + [VMEM((tokens, feed_bias.shape[1]), BF)] * 2
        + [VMEM(shape, BF)]
        + [sems(8), sems(2, 8), sems(1)],
        26,
    )


def cross_back(meta, gres, kept, memory, pieces):
    shape = gres.shape
    mshape = memory.shape
    return call(
        cross_back_kernel,
        "cross_back",
        [meta, gres, *kept, memory, *pieces],
        [SMEM, VMEM] + [FAR] * 7 + [FAR] * 8,
        [(shape, BF, VMEM), (mshape, BF, VMEM), (mshape, BF, VMEM), ((3, shape[2]), F32, VMEM)]
        + [(slot_shape(4), BF, HBM)] * 2,
        [VMEM(shape, BF), held_like(CROSS_ROWS), kept_like(slot_shape(4)), VMEM(shape, BF), VMEM(shape, BF)]
        + [VMEM(mshape, BF), VMEM(mshape, BF), VMEM(shape, BF), VMEM(mshape, BF), VMEM(kept[4].shape, BF)]
        + [sems(8)] * 2 + [sems(6), sems(shape[0])],
        15,
    )


def lower_back(meta, gres, grads, after_self, mix_a, kept, vecs, pieces):
    shape = gres.shape
    mshape = grads[1].shape
    part = (mshape[0], mshape[1] // (X * CORE), mshape[2])
    return call(
        lower_back_kernel,
        "lower_back",
        [meta, gres, *grads, after_self, mix_a, *kept, vecs, *pieces],
        [SMEM] + [VMEM] * 4 + [FAR] * 7 + [VMEM] + [FAR] * 8,
        [(shape, F32, VMEM)] + [(shape, BF, VMEM)] * 3 + [(part, BF, HBM)] * 4 + [((5, shape[2]), F32, VMEM)]
        + [(slot_shape(4), BF, HBM)] * 2,
        [VMEM(mshape, BF), held_like(CROSS_ROWS), VMEM(shape, F32), VMEM(shape, BF), kept_like(slot_shape(4))]
        + [VMEM(shape, BF)] * 5 + [VMEM(kept[4].shape, BF)]
        + [sems(8), sems(4), sems(6), sems(8), sems(shape[0])],
        20,
    )


def last_back(meta, gres, grads, target, vecs, sums, dbias, pieces, steps):
    shape = gres.shape
    small = (Y * X, Z, SMALL_ROWS, 128)
    return call(
        last_back_kernel,
        "last_back",
        [meta, gres, *grads, target, vecs, *sums, dbias, *pieces],
        [SMEM] + [VMEM] * 10 + [FAR] * 8,
        [(shape, F32, FAR)] + [(small, BF, HBM)] * 2,
        [VMEM((steps, shape[2]), F32), held_like(3 * PIECE), kept_like(small), VMEM((2, shape[2]), F32)]
        + [VMEM(shape, F32)] + [sems(8)] * 2 + [sems(shape[0])],
        8,
    )


BOTH = ("dp", "mem")


def swap(array, mask):
    count = lax.axis_size("dp") * lax.axis_size("mem")
    return lax.ppermute(array, BOTH, [(i, i ^ mask) for i in range(count)])


def pack_kernel(*refs):
    squares, (w_in, w_out, biases, f_bias, gain, shift, table) = refs[:8], refs[8:15]
    square_out, feed_out, stage = refs[15:]
    for i, ref in enumerate(squares):
        if i < 3:
            square_out[PIECE * i : PIECE * (i + 1)] = ref[...]
        else:
            square_out[SELF_ROWS + PIECE * (i - 3) : SELF_ROWS + PIECE * (i - 2)] = ref[...]
    for i in range(4):
        feed_out[PIECE * i : PIECE * (i + 1)] = w_in[:, 128 * i : 128 * (i + 1)]
    feed_out[4 * PIECE :] = w_out[...]
    stage[...] = jnp.zeros_like(stage)
    stage[0:7, :64] = biases[...].astype(F32)
    stage[GAIN : GAIN + 3, :64] = gain[...].astype(F32)
    stage[SHIFT : SHIFT + 3, :64] = shift[...].astype(F32)
    rows = table[...].astype(F32)
    half = rows.shape[0] // 2
    stage[TABLE : TABLE + half] = jnp.concatenate([rows[:half], rows[half:]], axis=1)
    stage[TABLE + half : TABLE + half + 2] = f_bias[...].astype(F32)
    square_out[3 * PIECE : SELF_ROWS] = stage[...].astype(BF)


def pair_kernel(meta, mine, other, out):
    low = meta[meta.shape[0] - 4] % 2
    out[low] = mine[...]
    out[1 - low] = other[...]


def quad_kernel(meta, mine, other, out):
    high = meta[meta.shape[0] - 4] // 2
    for i in range(2):
        out[2 * high + i] = mine[i]
        out[2 * (1 - high) + i] = other[i]


def quarter_kernel(meta, a, b, c, d, out):
    mine = meta[meta.shape[0] - 4]
    for i, one in enumerate((a, b, c, d)):
        out[mine ^ i] = one[...]


def sent_z(parts):
    return [parts[0], swap(parts[1], 8), swap(parts[2], 16), swap(parts[3], 24)]


def z_all(meta, parts):
    return call(
        quarter_kernel,
        "quarter",
        [meta, *parts],
        [SMEM] + [VMEM] * 4,
        [((Z, *parts[0].shape), BF, VMEM)],
        [],
    )[0]


def z_pair(meta, packed):
    return call(
        pair_kernel,
        "pair",
        [meta, packed, swap(packed, 8)],
        [SMEM, VMEM, VMEM],
        [((2, *packed.shape), BF, VMEM)],
        [],
    )[0]


def z_quad(meta, pair, other):
    return call(
        quad_kernel,
        "quad",
        [meta, pair, other],
        [SMEM, VMEM, VMEM],
        [((Z, *pair.shape[1:]), BF, VMEM)],
        [],
    )[0]


fence = lax.optimization_barrier


def spread_near(along_z):
    return [along_z, swap(along_z, 2), swap(along_z, 4), swap(along_z, 6)]


def spread_core(near):
    out = []
    for one in near:
        out += [one, swap(one, 1)]
    return out


def merge_kernel(meta, a, b, c, d, own, sent):
    mine = meta[meta.shape[0] - 4]

    def total(z):
        return (a[z].astype(F32) + b[z].astype(F32)) + (c[z].astype(F32) + d[z].astype(F32))

    for i in range(2):
        own[i] = total(mine ^ i)
        sent[i] = total(mine ^ (2 + i)).astype(BF)


def halve_kernel(pair, other, own, sent):
    own[...] = pair[0] + other[0].astype(F32)
    sent[...] = (pair[1] + other[1].astype(F32)).astype(BF)


def final_parts(refs, outs):
    def total(span):
        value = refs[0][span]
        for ref in refs[1:]:
            value = value + ref[span].astype(F32)
        return value

    at = 0
    for out in outs:
        rows = out.shape[0]
        for i in range(out.shape[1] // 128):
            out[:, 128 * i : 128 * (i + 1)] = total(slice(at, at + rows))
            at += rows
    return total, at


def final_kernel(*refs):
    final_parts(refs[:2], refs[2:])


def final_small_kernel(*refs):
    outs, (biases, f_bias, gain, shift, table) = refs[4:8], refs[8:]
    total, at = final_parts(refs[:4], outs)
    part = total(slice(at, at + SMALL_ROWS))
    biases[...] = part[0:7, :64]
    gain[...] = part[GAIN : GAIN + 3, :64]
    shift[...] = part[SHIFT : SHIFT + 3, :64]
    half = table.shape[0] // 2
    table[:half] = part[TABLE : TABLE + half, :64]
    table[half:] = part[TABLE : TABLE + half, 64:]
    f_bias[...] = part[TABLE + half : TABLE + half + 2]


def add(left, right):
    return (left.astype(F32) + right.astype(F32)).astype(BF)


def core_sums(own, other):
    return [add(own[i], other[i]) for i in range(Y * X)]


def join_kernel(own, other, small_own, small_other, *outs):
    rows = own.shape[2]
    for i, out in enumerate(outs):
        out[:, :rows] = add(own[i], other[i])
        out[:, rows:] = add(small_own[i], small_other[i])


def core_sums_joined(own, other, more_own, more_other):
    unused, z, rows, lanes = own.shape
    out = (z, rows + more_own.shape[2], lanes)
    return call(
        join_kernel,
        "join",
        [own, other, more_own, more_other],
        [VMEM] * 4,
        [(out, BF, VMEM)] * (Y * X),
        [],
    )


def near_parts(pairs):
    return [pairs[0], swap(pairs[1], 2), swap(pairs[2], 4), swap(pairs[3], 6)]


def chip_sums(meta, near):
    unused, rows, lanes = near[0].shape
    return call(
        merge_kernel,
        "merge",
        [meta, *near],
        [SMEM] + [VMEM] * 4,
        [((2, rows, lanes), F32, VMEM), ((2, rows, lanes), BF, VMEM)],
        [],
    )


def halved(pair, other):
    rows, lanes = pair.shape[1:]
    return call(
        halve_kernel, "halve", [pair, other], [VMEM] * 2, [((rows, lanes), F32, VMEM), ((rows, lanes), BF, VMEM)], []
    )


def merge_joined_kernel(meta, *refs):
    parts, small, outs = refs[:4], refs[4:8], refs[8:]
    mine = meta[meta.shape[0] - 4]
    rows = parts[0].shape[1]

    def total(refs, z):
        a, b, c, d = [ref[z].astype(F32) for ref in refs]
        return (a + b) + (c + d)

    for i, out in enumerate(outs):
        out[:rows] = total(parts, mine ^ i).astype(out.dtype)
        out[rows:] = total(small, mine ^ i).astype(out.dtype)


def chip_sums_joined(meta, near, small):
    unused, rows, lanes = near[0].shape
    out = (rows + small[0].shape[1], lanes)
    return call(
        merge_joined_kernel,
        "merge_joined",
        [meta, *near, *small],
        [SMEM] + [VMEM] * 8,
        [(out, F32, VMEM)] + [(out, BF, VMEM)] * 3,
        [],
    )


def slice_sums(kernel, parts, shapes):
    return call(kernel, "final", parts, [VMEM] * len(parts), [(s, F32, VMEM) for s in shapes], [])


def place_kernel(meta, a, b, c, d, out):
    base = meta.shape[0] - 4
    mine = meta[base + 2] * CORE + meta[base + 3]
    pairs = a.shape[0]
    for i, one in enumerate((a, b, c, d)):
        for p in range(pairs):
            out[(mine ^ i) * pairs + p] = one[p].astype(F32)


def swap_memory(memory, pairs):
    mine = lax.axis_index("mem")
    parts = [lax.dynamic_slice_in_dim(memory, (mine ^ i) * pairs, pairs) for i in range(4)]
    return parts


def return_memory(meta, parts, shape):
    return call(place_kernel, "place", [meta, *parts], [SMEM] + [VMEM] * 4, [(shape, F32, VMEM)], [])[0]


def slots_of(wide):
    rows, cols = wide.shape
    cut = wide.reshape(Z, Y, rows // (Z * Y), X, CORE, cols // (X * CORE))
    return [cut[:, y, :, x, c] for y, x, c in SLOTS]


def wide_of(slots):
    z, rows, cols = slots[0].shape
    cut = jnp.stack(slots).reshape(Y, X, CORE, z, rows, cols)
    return cut.transpose(3, 0, 4, 1, 2, 5).reshape(z * Y * rows, X * CORE * cols)


def gather_any(piece):
    return lax.all_gather(lax.all_gather(piece, "mem", axis=1, tiled=True), "dp", axis=0, tiled=True)


def scatter_any(wide):
    part = lax.psum_scatter(wide.astype(F32), "dp", scatter_dimension=0, tiled=True)
    return lax.psum_scatter(part, "mem", scatter_dimension=1, tiled=True)


def narrow_columns(slots):
    return [jnp.concatenate(jnp.split(one, 4, axis=2), axis=1) for one in slots]


def small_pieces(biases, f_bias, gain, shift, table):
    vectors = jnp.concatenate([biases, gain, shift], axis=0)
    vectors = jnp.pad(vectors, ((0, TABLE - vectors.shape[0]), (0, 0)))
    half = table.shape[0] // 2

    def cut(rows):
        return rows.reshape(rows.shape[0], Z, Y, 64).transpose(1, 2, 0, 3)

    top = jnp.pad(cut(vectors), ((0, 0),) * 3 + ((0, 64),))
    low = jnp.concatenate([cut(table[:half]), cut(table[half:])], axis=3)
    whole = jnp.concatenate([top, low, f_bias.reshape(Z, Y, 2, 128)], axis=2)
    return jnp.pad(whole, ((0, 0), (0, 0), (0, SMALL_ROWS - whole.shape[2]), (0, 0)))


def spread_any(squares, w_in, w_out, smalls):
    wide = [slots_of(gather_any(one)) for one in squares]
    small = small_pieces(*[lax.all_gather(one, "dp", axis=one.ndim - 1, tiled=True) for one in smalls])
    ins = narrow_columns(slots_of(gather_any(w_in)))
    outs = slots_of(gather_any(w_out))
    square_w, feed_w = [], []
    for i, (y, unused, unused2) in enumerate(SLOTS):
        parts = [one[i] for one in wide]
        square_w.append(jnp.concatenate([*parts[:3], small[:, y], *parts[3:]], axis=1))
        feed_w.append(jnp.concatenate([ins[i], outs[i]], axis=1))
    return square_w, feed_w


def by_slot(halves):
    return [halves[c][y * X + x] for y, x, c in SLOTS]


def reduce_squares_any(halves, count):
    slots = by_slot(halves)
    return [
        scatter_any(wide_of([one[:, PIECE * i : PIECE * (i + 1)] for one in slots]))
        for i in range(count)
    ]


def reduce_feed_any(d_in, d_out):
    slots = by_slot(d_in)
    ins = [
        jnp.concatenate([one[:, PIECE * j : PIECE * (j + 1)] for j in range(4)], axis=2)
        for one in slots
    ]
    return [scatter_any(wide_of(ins)), scatter_any(wide_of(by_slot(d_out)))]


def reduce_small_any(halves, count):
    parts = [halves[0][y * X].astype(F32) for y in range(Y)]
    part = jnp.stack(parts, axis=1).reshape(Z * Y, SMALL_ROWS, 128)
    vectors = part[:, :13, :64].transpose(1, 0, 2).reshape(13, -1)
    half = count // 2
    table = part[:, TABLE : TABLE + half]
    table = jnp.concatenate([table[:, :, :64], table[:, :, 64:]], axis=1)
    rows = jnp.concatenate([vectors, table.transpose(1, 0, 2).reshape(count, -1)], axis=0)
    cut = lax.psum_scatter(lax.psum(rows, "mem"), "dp", scatter_dimension=1, tiled=True)
    f_bias = part[:, TABLE + half : TABLE + half + 2].reshape(-1)
    f_bias = lax.psum_scatter(lax.psum(f_bias, "mem"), "dp", scatter_dimension=0, tiled=True)
    return cut[:7], f_bias, cut[7:10], cut[10:13], cut[13:]


def shards(
    target, memory, time_steps, target_len, source_len, source_off, cotangent,
    self_query, self_key, self_value, self_out, cross_query, cross_key, cross_value, cross_out,
    feed_in, feed_out, biases, feed_bias, norm_gain, norm_shift, step_table,
):
    pairs = target.shape[0]
    steps = step_table.shape[0]
    dp, mem = lax.axis_index("dp"), lax.axis_index("mem")
    quick = lax.axis_size("dp") == Z * Y and lax.axis_size("mem") == X * CORE
    here = [dp // 2, dp % 2, mem // 2, mem % 2] if quick else [0, 0, 0, 0]
    meta = jnp.concatenate(
        [
            target_len,
            time_steps,
            lax.dynamic_slice_in_dim(source_off, mem * pairs, pairs),
            lax.dynamic_slice_in_dim(source_len, mem * pairs, pairs),
            jnp.stack([jnp.asarray(i, jnp.int32) for i in here]),
        ]
    )
    squares = (self_query, self_key, self_value, self_out, cross_query, cross_key, cross_value, cross_out)
    if quick:
        packed = call(
            pack_kernel,
            "pack",
            [*squares, feed_in, feed_out, biases, feed_bias.reshape(2, 128)]
            + [norm_gain, norm_shift, step_table],
            [VMEM] * 15,
            [((i, 128), BF, VMEM) for i in (SELF_ROWS + CROSS_ROWS, FEED_ROWS)],
            [VMEM((SMALL_ROWS, 128), F32)],
            1,
            60 * 2**20,
        )
        packed, memory = fence((packed, memory))
        square_p, feed_p = packed
        mems = swap_memory(memory, pairs)
        mems[2], mems[3] = swap(mems[2], 2), swap(mems[3], 3)
        square_z = sent_z([square_p] * 4)
        square_z, mems, feed_p = fence((square_z, mems, feed_p))
        square_near = spread_near(z_all(meta, square_z))
        feed_z = z_pair(meta, feed_p)
        feed_z = (feed_z, swap(feed_z, 16))
        mems[1] = swap(mems[1], 1)
        feed_z = z_quad(meta, *feed_z)
        square_near, feed_z, mems = fence((square_near, feed_z, mems))
        square_w = spread_core(square_near)
        feed_near = spread_near(feed_z)
    else:
        square_w, feed_w = spread_any(
            squares, feed_in, feed_out, (biases, feed_bias, norm_gain, norm_shift, step_table)
        )
        own = lax.all_to_all(memory, "mem", 0, 1, tiled=True)
        mems = jnp.split(own, X * CORE, axis=1)

    in_a, q_a, k_a, v_a, w_a, mix_a, near_mix, vecs, fbias = self_forward(meta, target, square_w, steps)
    own_memory, after_self, in_b, q_b, k_b, v_b, w_b, mix_b, after_cross = cross_forward(
        meta, target, near_mix, mems, vecs, square_w
    )
    if quick:
        feed_near, after_cross = fence((feed_near, after_cross))
        feed_w = spread_core(feed_near)
    layer_out, gres_c, sums_c, d_fbias, *d_feed = feed(
        meta, after_cross, cotangent, vecs, fbias, feed_w
    )
    if quick:
        d_feed, gres_c = fence((d_feed, gres_c))
        u_in = core_sums(d_feed[0], swap(d_feed[1], 1))
        d_feed[3] = swap(d_feed[3], 1)
        u_in, gres_c = fence((u_in, gres_c))
        n_in = near_parts(u_in)
    gq_b, gk_b, gv_b, sums_b, *d_cross = cross_back(
        meta, gres_c, (in_b, q_b, k_b, v_b, w_b, mix_b), own_memory, square_w
    )
    if quick:
        n_in, d_feed, gq_b, d_cross = fence((n_in, d_feed, gq_b, d_cross))
        m_in = chip_sums(meta, n_in)
        u_out = core_sums_joined(*d_feed[2:], d_cross[0], swap(d_cross[1], 1))
        m_in, u_out, gq_b = fence((m_in, u_out, gq_b))
        m_in[1] = swap(m_in[1], 16)
        n_out = near_parts(u_out)
    gres_b, gq_a, gk_a, gv_a, *gmem, sums_a, d_first, d_second = lower_back(
        meta, gres_c, (gq_b, gk_b, gv_b), after_self, mix_a, (in_a, q_a, k_a, v_a, w_a), vecs, square_w
    )
    d_self = [d_first, d_second]
    if quick:
        m_in, n_out, gmem, gq_a, d_self = fence((m_in, n_out, gmem, gq_a, d_self))
        m_in = halved(*m_in)
        m_out = chip_sums(meta, n_out)
        u_self = core_sums(d_self[0], swap(d_self[1], 1))
        m_in, m_out, u_self, gmem, gq_a = fence((m_in, m_out, u_self, gmem, gq_a))
        m_in[1] = swap(m_in[1], 8)
        m_out[1] = swap(m_out[1], 16)
        n_self = near_parts(u_self)
    grad_target, *d_small = last_back(
        meta, gres_b, (gq_a, gk_a, gv_a), target, vecs, (sums_a, sums_b, sums_c), d_fbias, square_w, steps
    )
    if quick:
        one = self_query.shape
        m_in, m_out, n_self, d_small, gmem = fence((m_in, m_out, n_self, d_small, gmem))
        u_small = core_sums(d_small[0], swap(d_small[1], 1))
        m_out = halved(*m_out)
        u_small, m_out, gmem = fence((u_small, m_out, gmem))
        n_small = near_parts(u_small)
        m_out[1] = swap(m_out[1], 8)
        gmem[2] = swap(gmem[2], 2)
        n_small, m_out, gmem = fence((n_small, m_out, gmem))
        m_self = sent_z(chip_sums_joined(meta, n_self, n_small))
        gmem[3], gmem[1] = swap(gmem[3], 3), swap(gmem[1], 1)
        g_in = slice_sums(final_kernel, m_in, (feed_in.shape,))
        g_out, *g_cross = slice_sums(final_kernel, m_out, (feed_out.shape,) + (one,) * 4)
        grad_memory = return_memory(meta, gmem, memory.shape)
        small_shapes = (biases.shape, (2, 128), norm_gain.shape, norm_shift.shape, step_table.shape)
        m_self, grad_memory = fence((m_self, grad_memory))
        out = slice_sums(final_small_kernel, m_self, (one,) * 4 + small_shapes)
        g_self, (g_bias, g_fbias, g_gain, g_shift, g_table) = out[:4], out[4:]
        g_feed = [*g_in, g_out]
        g_fbias = g_fbias.reshape(feed_bias.shape)
    else:
        whole = jnp.concatenate(gmem, axis=1)
        grad_memory = lax.all_to_all(whole, "mem", 1, 0, tiled=True).astype(F32)
        g_feed = reduce_feed_any(d_feed[:2], d_feed[2:])
        g_cross = reduce_squares_any(d_cross, 4)
        g_self = reduce_squares_any(d_self, 4)
        g_bias, g_fbias, g_gain, g_shift, g_table = reduce_small_any(d_small, steps)
    return (
        layer_out, grad_target, grad_memory, *g_self, *g_cross, *g_feed,
        g_bias, g_fbias, g_gain, g_shift, g_table,
    )


def solution(mesh):
    rows = P(BOTH, None, None)
    piece = P("dp", "mem")
    vector = P(None, "dp")
    mem_rows = P("dp", "mem", None)
    return jax.shard_map(
        shards,
        mesh=mesh,
        in_specs=(rows, mem_rows, P(BOTH), P(BOTH), P("dp"), P("dp"), rows)
        + (piece,) * 10
        + (vector, P("dp"), vector, vector, vector),
        out_specs=(rows, rows, mem_rows) + (piece,) * 10 + (vector, P("dp"), vector, vector, vector),
        check_vma=False,
    )
```

```python
import functools
import math

import jax
import jax.numpy as jnp
from jax import lax
from jax.experimental import pallas as pl
from jax.experimental.pallas import tpu as pltpu
from jax.sharding import PartitionSpec as P

HEADS = 8
DH = 64
GROUP = 4
WIDE = GROUP * DH
EPSILON = 1e-05
SCALE = 1.0 / math.sqrt(DH)
BF = jnp.bfloat16
F32 = jnp.float32
VMEM_LIMIT = 30 * 2**20


def contract(left, right, left_dim, right_dim):
    return lax.dot_general(
        left, right, (((left_dim,), (right_dim,)), ((), ())), preferred_element_type=F32
    )


def mul(left, right):
    return contract(left, right, 1, 0)


def mul_nt(left, right):
    return contract(left, right, 1, 1)


def mul_tn(left, right):
    return contract(left, right, 0, 0)


def normalise(signal):
    centre = signal - jnp.mean(signal, axis=-1, keepdims=True)
    inverse = lax.rsqrt(jnp.mean(centre * centre, axis=-1, keepdims=True) + EPSILON)
    return centre * inverse, inverse


def norm_back(grad, scaled, inverse, gain):
    up = grad * gain
    return inverse * (
        up
        - jnp.mean(up, axis=-1, keepdims=True)
        - scaled * jnp.mean(up * scaled, axis=-1, keepdims=True)
    )


def col_sum(array):
    return jnp.sum(array.astype(F32), axis=0, keepdims=True)


def head_of_lane(rows):
    return lax.broadcasted_iota(jnp.int32, (rows, WIDE), 1) // DH


def stacked(block, lane_head):
    zero = jnp.zeros_like(block)
    return jnp.concatenate([jnp.where(lane_head == h, block, zero) for h in range(GROUP)], axis=0)


def unstacked(result, lane_head, rows):
    picked = result[:rows]
    for h in range(1, GROUP):
        picked = jnp.where(lane_head == h, result[h * rows : (h + 1) * rows], picked)
    return picked


def blocks(pairs):
    return [(p, g, slice(g * WIDE, (g + 1) * WIDE)) for p in range(pairs) for g in range(HEADS // GROUP)]


INPUT, QUERY, KEY, VALUE, MIXED, MEMORY = range(6)


def attend(before, bias_of, kept, w_ref, after):
    pairs, unused, rows, unused2 = kept.shape
    lane_head = head_of_lane(rows)
    every = blocks(pairs)

    def scores_of(p, g, cols):
        return mul_nt(stacked(kept[p, QUERY, :, cols], lane_head), kept[p, KEY, :, cols])

    before(0)
    ahead = scores_of(*every[0])
    for i, (p, g, cols) in enumerate(every):
        scores = ahead + bias_of(p)
        if g == 0 and p + 1 < pairs:
            before(p + 1)
        if i + 1 < len(every):
            ahead = scores_of(*every[i + 1])
        top = jnp.max(scores, axis=-1, keepdims=True)
        raised = jnp.exp(scores - top)
        total = jnp.sum(raised, axis=-1, keepdims=True)
        weights = (raised * (1.0 / total)).astype(BF)
        w_ref[p, g] = weights
        mixed = mul(weights, kept[p, VALUE, :, cols])
        kept[p, MIXED, :, cols] = unstacked(mixed, lane_head, rows).astype(BF)
        if g == HEADS // GROUP - 1:
            after(p)


def attend_back(before, ready, kept, w_ref, grad_ref, gq_ref, gk_ref, gv_ref, after):
    pairs, unused, rows, unused2 = kept.shape
    lane_head = head_of_lane(rows)
    every = blocks(pairs)

    def weight_grads(p, g, cols):
        if g == 0:
            ready(p)
        grads = stacked(grad_ref[p, :, cols], lane_head)
        return grads, mul_nt(grads, kept[p, VALUE, :, cols])

    before(0)
    ahead = weight_grads(*every[0])
    for i, (p, g, cols) in enumerate(every):
        grads, grad_w = ahead
        if g == 0 and p + 1 < pairs:
            before(p + 1)
        if i + 1 < len(every):
            ahead = weight_grads(*every[i + 1])
        weights = w_ref[p, g]
        wide = weights.astype(F32)
        offset = jnp.sum(grad_w * wide, axis=-1, keepdims=True)
        grad_s = (wide * (grad_w - offset)).astype(BF)
        grad_q = unstacked(mul(grad_s, kept[p, KEY, :, cols]), lane_head, rows)
        gq_ref[p, :, cols] = (grad_q * SCALE).astype(BF)
        gk_ref[p, :, cols] = mul_tn(grad_s, stacked(kept[p, QUERY, :, cols], lane_head)).astype(BF)
        gv_ref[p, :, cols] = mul_tn(weights, grads).astype(BF)
        if g == HEADS // GROUP - 1:
            after(p)


def flat(ref):
    value = ref[...]
    return value.reshape(value.shape[0] * value.shape[1], value.shape[2])


Z, Y, X, CORE = 4, 2, 2, 2
SLOTS = [(y, x, c) for y in range(Y) for x in range(X) for c in range(CORE)]
PIECE = 64
FEED_ROWS = 4 * PIECE + 256
SMALL_ROWS = 48
SELF_ROWS = 3 * PIECE + SMALL_ROWS
CROSS_ROWS = 5 * PIECE
GAIN, SHIFT, TABLE = 7, 10, 16


def places(meta, slot):
    base = meta.shape[0] - 4
    y, x, c = slot
    return y ^ meta[base + 1], (x ^ meta[base + 2]) * CORE + (c ^ meta[base + 3])


def load_copies(meta, sources, held, sems, first=0):
    copies = []
    rows = held.shape[-2]
    for i, slot in enumerate(SLOTS):
        row, panel = places(meta, slot)
        source = sources[i].at[:, pl.ds(first, rows)]
        copies.append(pltpu.make_async_copy(source, held.at[panel, :, row], sems.at[i]))
    return copies


def store_copies(meta, held, targets, sems, first=0):
    copies = []
    rows = targets[0].shape[2]
    for i, slot in enumerate(SLOTS):
        row, panel = places(meta, slot)
        y, x, c = slot
        target = targets[c].at[y * X + x]
        source = held.at[panel, :, row, pl.ds(first, rows)]
        copies.append(pltpu.make_async_copy(source, target, sems.at[i]))
    return copies


def start(copies):
    for copy in copies:
        copy.start()


def wait(copies):
    for copy in copies:
        copy.wait()


def moves(sources, targets, sems):
    return [pltpu.make_async_copy(a, b, sems.at[i]) for i, (a, b) in enumerate(zip(sources, targets))]


def joined(value):
    return value.reshape(-1, value.shape[-1])


def square(held, index):
    span = slice(PIECE * index, PIECE * (index + 1))
    return jnp.concatenate([joined(held[i, :, :, span]) for i in range(X * CORE)], axis=1)


def keep(held, index, value):
    span = slice(PIECE * index, PIECE * (index + 1))
    for i in range(X * CORE):
        part = value[:, i * 128 : (i + 1) * 128].astype(BF)
        held[i, :, :, span] = part.reshape(Z, Y, PIECE, 128)


def all_rows(kept, index):
    value = kept[:, index]
    return value.reshape(value.shape[0] * value.shape[1], value.shape[2])


def each(source, target, sems):
    count = source.shape[0]
    return moves([source.at[p] for p in range(count)], [target.at[p] for p in range(count)], sems)


def self_forward_kernel(meta, target, *refs):
    pieces, refs = refs[:8], refs[8:]
    far, far_w, near_mix, vecs, fbias, held, held_cross = refs[:7]
    kept, w, small, sems, cross_sems, small_sems, far_sems, w_sems = refs[7:]
    base = meta.shape[0] - 4
    small_loads = [
        pltpu.make_async_copy(
            pieces[y * X * CORE].at[:, pl.ds(3 * PIECE, SMALL_ROWS)], small.at[:, y ^ meta[base + 1]], small_sems.at[y]
        )
        for y in range(Y)
    ]
    start(small_loads)
    loads = load_copies(meta, pieces, held, sems)
    start(loads)
    cross_loads = load_copies(meta, pieces, held_cross, cross_sems, SELF_ROWS)
    start(cross_loads)
    copies, w_copies = each(kept, far, far_sems), each(w, far_w, w_sems)
    pairs, length, width = target.shape
    wait(small_loads)
    every = [small[z, y].astype(F32) for z in range(Z) for y in range(Y)]
    steps = (vecs.shape[0] - TABLE) // 2
    vecs[:TABLE] = jnp.concatenate([one[:TABLE, :64] for one in every], axis=1)
    for i in range(2):
        part = [one[TABLE : TABLE + steps, 64 * i : 64 * (i + 1)] for one in every]
        vecs[TABLE + i * steps : TABLE + (i + 1) * steps] = jnp.concatenate(part, axis=1)
    for d, one in enumerate(every):
        for i in range(2):
            at = TABLE + steps + i
            fbias[:, d * 256 + i * 128 : d * 256 + (i + 1) * 128] = one[at : at + 1]

    def before(p):
        emb = target[p].astype(F32) + vecs[pl.ds(TABLE + meta[pairs + p], 1), :]
        scaled, unused = normalise(emb)
        x = (scaled * vecs[GAIN : GAIN + 1] + vecs[SHIFT : SHIFT + 1]).astype(BF)
        kept[p, INPUT] = x
        if p == 0:
            wait(loads)
        kept[p, QUERY] = (mul(x, square(held, 0)) + vecs[0:1]).astype(BF) * SCALE
        kept[p, KEY] = mul(x, square(held, 1)).astype(BF)
        kept[p, VALUE] = (mul(x, square(held, 2)) + vecs[1:2]).astype(BF)

    def bias_of(p):
        spot = lax.broadcasted_iota(jnp.int32, (1, length), 1)
        return jnp.where(spot < meta[p], 0.0, -1e30)

    def after(p):
        near_mix[p] = kept[p, MIXED]
        copies[p].start()
        w_copies[p].start()

    attend(before, bias_of, kept, w, after)
    wait(cross_loads)
    wait(copies)
    wait(w_copies)


def cross_forward_kernel(meta, target, mix_a, mem_0, mem_1, mem_2, mem_3, vecs, held, *refs):
    far, far_w, far_after, after_cross = refs[:4]
    kept, w, after_self, mem_sems, far_sems, w_sems, after_sems = refs[4:]
    pairs, length, width = target.shape
    source = kept.shape[2]
    base = meta.shape[0] - 4
    mine = meta[base + 2] * CORE + meta[base + 3]
    part = source // (X * CORE)
    mem_loads = [
        pltpu.make_async_copy(
            one,
            kept.at[:, MEMORY, pl.ds(pl.multiple_of((mine ^ i) * part, part), part), :],
            mem_sems.at[i],
        )
        for i, one in enumerate((mem_0, mem_1, mem_2, mem_3))
    ]
    start(mem_loads)
    copies, w_copies = each(kept, far, far_sems), each(w, far_w, w_sems)
    after_copies = each(after_self, far_after, after_sems)

    def before(p):
        row = vecs[pl.ds(TABLE + meta[pairs + p], 1), :]
        total = target[p].astype(F32) + row + mul(mix_a[p], square(held, 0)) + vecs[2:3]
        after_self[p] = total
        after_copies[p].start()
        scaled, unused = normalise(total)
        x = (scaled * vecs[GAIN + 1 : GAIN + 2] + vecs[SHIFT + 1 : SHIFT + 2]).astype(BF)
        kept[p, INPUT] = x
        kept[p, QUERY] = (mul(x, square(held, 1)) + vecs[3:4]).astype(BF) * SCALE
        if p == 0:
            wait(mem_loads)
        m = kept[p, MEMORY]
        kept[p, KEY] = mul(m, square(held, 2)).astype(BF)
        kept[p, VALUE] = (mul(m, square(held, 3)) + vecs[4:5]).astype(BF)

    def bias_of(p):
        spot = lax.broadcasted_iota(jnp.int32, (1, source), 1)
        begin = meta[2 * pairs + p]
        end = begin + meta[3 * pairs + p]
        return jnp.where((spot >= begin) & (spot < end), 0.0, -1e30)

    def after(p):
        copies[p].start()
        w_copies[p].start()
        after_cross[p] = after_self[p] + mul(kept[p, MIXED], square(held, 4)) + vecs[5:6]

    attend(before, bias_of, kept, w, after)
    wait(after_copies)
    wait(copies)
    wait(w_copies)


def gelu_parts(value):
    size = jnp.abs(value) * math.sqrt(0.5)
    t = 1.0 / (1.0 + 0.3275911 * size)
    bell = jnp.exp(-0.5 * value * value)
    tail = (
        t
        * (
            0.5 * 0.254829592
            + t
            * (
                0.5 * -0.284496736
                + t * (0.5 * 1.421413741 + t * (0.5 * -1.453152027 + t * (0.5 * 1.061405429)))
            )
        )
        * bell
    )
    below = jnp.where(value < 0, tail, 1.0 - tail)
    slope = below + value * bell * (1.0 / math.sqrt(2.0 * math.pi))
    return value * below, slope


def feed_kernel(meta, after_cross, cot, vecs, feed_bias, *refs):
    pieces, refs = refs[:8], refs[8:]
    far_out, gres, sums, dbias = refs[:4]
    targets, refs = refs[4:6], refs[6:]
    held, kept, x_c, act, grad_pre, layer_out, sems, out_sems, far_sems = refs
    copies = moves((layer_out,), (far_out,), far_sems)
    loads = load_copies(meta, pieces, held, sems)
    start(loads)
    stores = store_copies(meta, kept, targets, out_sems)
    shape = after_cross.shape
    signal = flat(after_cross)
    scaled, inverse = normalise(signal)
    gain = vecs[GAIN + 2 : GAIN + 3]
    x_c[...] = (scaled * gain + vecs[SHIFT + 2 : SHIFT + 3]).astype(BF)
    wait(loads)
    c = flat(cot)
    x = x_c[...]
    w_in = [
        jnp.concatenate([joined(held[j, :, :, PIECE * i : PIECE * (i + 1)]) for i in range(4)], axis=1)
        for j in range(4)
    ]
    w_out = [jnp.concatenate([joined(held[i, j, :, 4 * PIECE :]) for i in range(4)], axis=1) for j in range(4)]
    w_in = jnp.concatenate(w_in, axis=1)
    w_out = jnp.concatenate(w_out, axis=0)
    block = 256
    count = w_in.shape[1] // block

    def first(j):
        cols = slice(j * block, (j + 1) * block)
        return mul(x, w_in[:, cols]), mul_nt(c, w_out[cols])

    ready = [first(j) for j in range(1)]
    for j in range(count):
        cols = slice(j * block, (j + 1) * block)
        if j + 1 < count:
            ready.append(first(j + 1))
        pre, grad_act = ready[j]
        value, slope = gelu_parts(pre + feed_bias[:, cols])
        act[:, cols] = value.astype(BF)
        grad = (grad_act * slope).astype(BF)
        grad_pre[:, cols] = grad
        dbias[:, cols] = col_sum(grad)
    for j in range(4):
        cols = slice(j * 512, (j + 1) * 512)
        d_out = mul_tn(act[:, cols], c)
        for i in range(4):
            part = d_out[:, i * 128 : (i + 1) * 128].astype(BF)
            kept[i, j, :, 4 * PIECE :] = part.reshape(Y, 256, 128)
        d_in = mul_tn(x, grad_pre[:, cols])
        for i in range(4):
            part = d_in[:, i * 128 : (i + 1) * 128].astype(BF)
            kept[j, :, :, PIECE * i : PIECE * (i + 1)] = part.reshape(Z, Y, PIECE, 128)
    start(stores)
    layer_out[...] = (signal + mul(act[...], w_out) + vecs[6:7]).astype(BF).reshape(shape)
    start(copies)
    grad = mul_nt(grad_pre[...], w_in)
    wide_cot = flat(cot).astype(F32)
    sums[0:1] = col_sum(wide_cot)
    sums[1:2] = col_sum(grad * scaled)
    sums[2:3] = col_sum(grad)
    gres[...] = (wide_cot + norm_back(grad, scaled, inverse, gain)).reshape(shape)
    wait(stores)
    wait(copies)


def cross_back_kernel(meta, gres, far, far_w, held, *refs):
    gq, gk, gv, sums = refs[:4]
    targets, (kept, w, gmix, grads, out_sems, far_sems, w_sems) = refs[4:6], refs[6:]
    copies, w_copies = each(far, kept, far_sems), each(far_w, w, w_sems)
    for one, two in zip(copies, w_copies):
        one.start()
        two.start()
    stores = store_copies(meta, grads, targets, out_sems)

    def before(p):
        gmix[p] = mul_nt(gres[p].astype(BF), square(held, 4)).astype(BF)

    def ready(p):
        copies[p].wait()
        w_copies[p].wait()

    attend_back(before, ready, kept, w, gmix, gq, gk, gv, lambda p: None)
    grad = flat(gres).astype(BF)
    m = all_rows(kept, MEMORY)
    keep(grads, 3, mul_tn(all_rows(kept, MIXED), grad))
    keep(grads, 0, mul_tn(all_rows(kept, INPUT), flat(gq)))
    keep(grads, 1, mul_tn(m, flat(gk)))
    keep(grads, 2, mul_tn(m, flat(gv)))
    start(stores)
    sums[0:1] = col_sum(grad)
    sums[1:2] = col_sum(flat(gq))
    sums[2:3] = col_sum(flat(gv))
    wait(stores)


def lower_back_kernel(
    meta, gres, grad_q, grad_k, grad_v, far_after, far, far_w, target, vecs, sums_b, sums_c, dbias, held, held_a, *refs
):
    far_target, gmem_0, gmem_1, gmem_2, gmem_3 = refs[:5]
    targets, refs = refs[5:7], refs[7:]
    kept, w, after_self, gres_a, gmix, gmem, gq, gk, gv, gtarget, gtable, grads = refs[:12]
    mem_sems, far_sems, w_sems, after_sems, target_sems, out_sems = refs[12:]
    copies, w_copies = each(far, kept, far_sems), each(far_w, w, w_sems)
    after_copies = each(far_after, after_self, after_sems)
    for group in zip(after_copies, copies, w_copies):
        start(group)
    target_copies = each(gtarget, far_target, target_sems)
    stores = store_copies(meta, grads, targets, out_sems)
    base = meta.shape[0] - 4
    mine = meta[base + 2] * CORE + meta[base + 3]
    part = gmem.shape[1] // (X * CORE)
    mem_stores = [
        pltpu.make_async_copy(
            gmem.at[:, pl.ds(pl.multiple_of((mine ^ i) * part, part), part), :], one, mem_sems.at[i]
        )
        for i, one in enumerate((gmem_0, gmem_1, gmem_2, gmem_3))
    ]
    pairs, length, width = gres.shape
    totals = [0.0] * 5
    gtable[...] = jnp.zeros_like(gtable)

    def count(first, *parts):
        for i, one in enumerate(parts):
            totals[first + i] = totals[first + i] + col_sum(one)

    def before(p):
        grad_m = mul_nt(grad_k[p], square(held, 2)) + mul_nt(grad_v[p], square(held, 3))
        gmem[p] = grad_m.astype(BF)
        grad_in = mul_nt(grad_q[p], square(held, 1))
        after_copies[p].wait()
        scaled, inverse = normalise(after_self[p])
        total = gres[p] + norm_back(grad_in, scaled, inverse, vecs[GAIN + 1 : GAIN + 2])
        gres_a[p] = total
        grad_a = total.astype(BF)
        gmix[p] = mul_nt(grad_a, square(held, 0)).astype(BF)
        count(0, grad_in * scaled, grad_in, grad_a)
        if p + 1 == pairs:
            start(mem_stores)

    def ready(p):
        copies[p].wait()
        w_copies[p].wait()

    def after(p):
        grad_in = (
            mul_nt(gq[p], square(held_a, 0)) + mul_nt(gk[p], square(held_a, 1)) + mul_nt(gv[p], square(held_a, 2))
        )
        row = pl.ds(TABLE + meta[pairs + p], 1)
        scaled, inverse = normalise(target[p].astype(F32) + vecs[row, :])
        count(3, grad_in * scaled, grad_in)
        total = gres_a[p] + norm_back(grad_in, scaled, inverse, vecs[GAIN : GAIN + 1])
        gtarget[p] = total
        target_copies[p].start()
        gtable[pl.ds(meta[pairs + p], 1), :] += col_sum(total)

    attend_back(before, ready, kept, w, gmix, gq, gk, gv, after)
    x = all_rows(kept, INPUT)
    keep(grads, 3, mul_tn(all_rows(kept, MIXED), flat(gres_a).astype(BF)))
    for i, one in enumerate((gq, gk, gv)):
        keep(grads, i, mul_tn(x, flat(one)))
    rows = [col_sum(flat(gq)), col_sum(flat(gv)), totals[2], sums_b[1:2], sums_b[2:3], sums_b[0:1], sums_c[0:1]]
    rows += [totals[3], totals[0], sums_c[1:2], totals[4], totals[1], sums_c[2:3]]
    vectors = jnp.concatenate(rows + [jnp.zeros((TABLE - len(rows), width), F32)], axis=0)
    steps = gtable.shape[0] // 2
    for d in range(Z * Y):
        lanes = slice(d * 64, (d + 1) * 64)
        top = jnp.concatenate([vectors[:, lanes], jnp.zeros((TABLE, 64), F32)], axis=1)
        low = jnp.concatenate([gtable[:steps, lanes], gtable[steps:, lanes]], axis=1)
        tail = [dbias[:, d * 256 + i * 128 : d * 256 + (i + 1) * 128] for i in range(2)]
        fill = jnp.zeros((SMALL_ROWS - TABLE - steps - 2, 128), F32)
        small = jnp.concatenate([top, low, *tail, fill], axis=0).astype(BF)
        for i in range(X * CORE):
            grads[i, d // Y, d % Y, 4 * PIECE :] = small
    start(stores)
    wait(mem_stores)
    wait(target_copies)
    wait(stores)


HBM = pl.ANY
FAR = pltpu.HBM
VMEM = pltpu.VMEM
SMEM = pltpu.SMEM


def call(kernel, name, args, spaces, outs, scratch, micros=1, limit=VMEM_LIMIT):
    cost = pl.CostEstimate(flops=int(micros * 10**9), bytes_accessed=int(micros * 3 * 10**6), transcendentals=0)
    function = pl.pallas_call(
        kernel,
        out_shape=[FAR(s, d) if m is FAR else jax.ShapeDtypeStruct(s, d) for s, d, m in outs],
        in_specs=[pl.BlockSpec(memory_space=m) for m in spaces],
        out_specs=[pl.BlockSpec(memory_space=m) for unused, unused2, m in outs],
        scratch_shapes=scratch,
        compiler_params=pltpu.CompilerParams(vmem_limit_bytes=limit),
        cost_estimate=cost,
        name=name,
    )
    return list(function(*[pltpu.with_memory_space_constraint(a, m) if m is FAR else a for a, m in zip(args, spaces)]))


def held_shape(rows):
    return (X * CORE, Z, Y, rows, 128)


def held_like(rows):
    return VMEM(held_shape(rows), BF)


def kept_like(slots):
    return VMEM((X * CORE, slots[1], Y, *slots[2:]), BF)


def sems(*shape):
    return pltpu.SemaphoreType.DMA(shape)


def weights_shape(shape, source):
    return (shape[0], HEADS // GROUP, GROUP * shape[1], source)


def slot_shape(count, extra=0):
    return (Y * X, Z, count * PIECE + extra, 128)


def kept_shape(shape, count):
    return (shape[0], count, *shape[1:])


def self_forward(meta, target, pieces, steps):
    shape = target.shape
    kept, w_shape = kept_shape(shape, MIXED + 1), weights_shape(shape, shape[1])
    return call(
        self_forward_kernel,
        "self_forward",
        [meta, target, *pieces],
        [SMEM, VMEM] + [FAR] * 8,
        [(kept, BF, FAR), (w_shape, BF, FAR), (shape, BF, VMEM)]
        + [((TABLE + steps, shape[2]), F32, VMEM), ((1, 4 * shape[2]), F32, VMEM)]
        + [(held_shape(3 * PIECE), BF, VMEM), (held_shape(CROSS_ROWS), BF, VMEM)],
        [VMEM(kept, BF), VMEM(w_shape, BF), VMEM((Z, Y, SMALL_ROWS, 128), BF)]
        + [sems(8), sems(8), sems(2), sems(shape[0]), sems(shape[0])],
        0.1,
    )


def cross_forward(meta, target, mix_a, mems, vecs, held):
    shape = target.shape
    kept, w_shape = kept_shape(shape, MEMORY + 1), weights_shape(shape, shape[1])
    return call(
        cross_forward_kernel,
        "cross_forward",
        [meta, target, mix_a, *mems, vecs, held],
        [SMEM] + [VMEM] * 2 + [HBM] * 4 + [VMEM] * 2,
        [(kept, BF, FAR), (w_shape, BF, FAR), (shape, F32, FAR), (shape, F32, VMEM)],
        [VMEM(kept, BF), VMEM(w_shape, BF), VMEM(shape, F32)] + [sems(4)] + [sems(shape[0])] * 3,
        0.1,
    )


def feed(meta, after_cross, cot, vecs, feed_bias, pieces):
    shape = after_cross.shape
    tokens, width = shape[0] * shape[1], shape[2]
    return call(
        feed_kernel,
        "feed",
        [meta, after_cross, cot, vecs, feed_bias, *pieces],
        [SMEM] + [VMEM] * 4 + [FAR] * 8,
        [(shape, BF, FAR), (shape, F32, VMEM), ((3, width), F32, VMEM), (feed_bias.shape, F32, VMEM)]
        + [(slot_shape(4, 256), BF, HBM)] * 2,
        [held_like(FEED_ROWS)] * 2
        + [VMEM((tokens, width), BF)] + [VMEM((tokens, feed_bias.shape[1]), BF)] * 2
        + [VMEM(shape, BF)]
        + [sems(8), sems(8), sems(1)],
        26,
        36 * 2**20,
    )


def cross_back(meta, gres, far, far_w, held):
    shape = gres.shape
    return call(
        cross_back_kernel,
        "cross_back",
        [meta, gres, far, far_w, held],
        [SMEM, VMEM, FAR, FAR, VMEM],
        [(shape, BF, VMEM)] * 3 + [((3, shape[2]), F32, VMEM)] + [(slot_shape(4), BF, HBM)] * 2,
        [VMEM(far.shape, BF), VMEM(far_w.shape, BF), VMEM(shape, BF), kept_like(slot_shape(4))]
        + [sems(8), sems(shape[0]), sems(shape[0])],
        15,
    )


def lower_back(meta, gres, grads, after_self, far, far_w, target, vecs, sums, dbias, held, held_a, steps):
    shape = gres.shape
    part = (shape[0], shape[1] // (X * CORE), shape[2])
    slots = slot_shape(4, SMALL_ROWS)
    return call(
        lower_back_kernel,
        "lower_back",
        [meta, gres, *grads, after_self, far, far_w, target, vecs, *sums, dbias, held, held_a],
        [SMEM] + [VMEM] * 4 + [FAR] * 3 + [VMEM] * 7,
        [(shape, F32, FAR)] + [(part, BF, HBM)] * 4 + [(slots, BF, HBM)] * 2,
        [VMEM(far.shape, BF), VMEM(far_w.shape, BF), VMEM(shape, F32), VMEM(shape, F32)]
        + [VMEM(shape, BF)] * 5 + [VMEM(shape, F32), VMEM((steps, shape[2]), F32), kept_like(slots)]
        + [sems(4)] + [sems(shape[0])] * 4 + [sems(8)],
        20,
        38 * 2**20,
    )


BOTH = ("dp", "mem")


def swap(array, mask):
    count = lax.axis_size("dp") * lax.axis_size("mem")
    return lax.ppermute(array, BOTH, [(i, i ^ mask) for i in range(count)])


def pack_kernel(*refs):
    squares, (w_in, w_out, biases, f_bias, gain, shift, table) = refs[:8], refs[8:15]
    square_out, feed_out, stage = refs[15:]
    for i, ref in enumerate(squares):
        if i < 3:
            square_out[PIECE * i : PIECE * (i + 1)] = ref[...]
        else:
            square_out[SELF_ROWS + PIECE * (i - 3) : SELF_ROWS + PIECE * (i - 2)] = ref[...]
    for i in range(4):
        feed_out[PIECE * i : PIECE * (i + 1)] = w_in[:, 128 * i : 128 * (i + 1)]
    feed_out[4 * PIECE :] = w_out[...]
    stage[...] = jnp.zeros_like(stage)
    stage[0:7, :64] = biases[...].astype(F32)
    stage[GAIN : GAIN + 3, :64] = gain[...].astype(F32)
    stage[SHIFT : SHIFT + 3, :64] = shift[...].astype(F32)
    rows = table[...].astype(F32)
    half = rows.shape[0] // 2
    stage[TABLE : TABLE + half] = jnp.concatenate([rows[:half], rows[half:]], axis=1)
    stage[TABLE + half : TABLE + half + 2] = f_bias[...].astype(F32)
    square_out[3 * PIECE : SELF_ROWS] = stage[...].astype(BF)


def pair_kernel(meta, mine, other, out):
    low = meta[meta.shape[0] - 4] % 2
    out[low] = mine[...]
    out[1 - low] = other[...]


def quad_kernel(meta, mine, other, out):
    high = meta[meta.shape[0] - 4] // 2
    for i in range(2):
        out[2 * high + i] = mine[i]
        out[2 * (1 - high) + i] = other[i]


def quarter_kernel(meta, a, b, c, d, out):
    mine = meta[meta.shape[0] - 4]
    for i, one in enumerate((a, b, c, d)):
        out[mine ^ i] = one[...]


def sent_z(parts):
    return [parts[0], swap(parts[1], 8), swap(parts[2], 16), swap(parts[3], 24)]


def z_all(meta, parts):
    return call(
        quarter_kernel,
        "quarter",
        [meta, *parts],
        [SMEM] + [VMEM] * 4,
        [((Z, *parts[0].shape), BF, VMEM)],
        [],
    )[0]


def z_pair(meta, packed):
    return call(
        pair_kernel,
        "pair",
        [meta, packed, swap(packed, 8)],
        [SMEM, VMEM, VMEM],
        [((2, *packed.shape), BF, VMEM)],
        [],
    )[0]


def z_quad(meta, pair, other):
    return call(
        quad_kernel,
        "quad",
        [meta, pair, other],
        [SMEM, VMEM, VMEM],
        [((Z, *pair.shape[1:]), BF, VMEM)],
        [],
    )[0]


fence = lax.optimization_barrier


def spread_near(along_z):
    return [along_z, swap(along_z, 2), swap(along_z, 4), swap(along_z, 6)]


def spread_core(near):
    out = []
    for one in near:
        out += [one, swap(one, 1)]
    return out


def merge_kernel(meta, a, b, c, d, own, sent):
    mine = meta[meta.shape[0] - 4]

    def total(z):
        return (a[z].astype(F32) + b[z].astype(F32)) + (c[z].astype(F32) + d[z].astype(F32))

    for i in range(2):
        own[i] = total(mine ^ i)
        sent[i] = total(mine ^ (2 + i)).astype(BF)


def halve_kernel(pair, other, own, sent):
    own[...] = pair[0] + other[0].astype(F32)
    sent[...] = (pair[1] + other[1].astype(F32)).astype(BF)


def final_parts(refs, outs):
    def total(span):
        value = refs[0][span]
        for ref in refs[1:]:
            value = value + ref[span].astype(F32)
        return value

    at = 0
    for out in outs:
        rows = out.shape[0]
        for i in range(out.shape[1] // 128):
            out[:, 128 * i : 128 * (i + 1)] = total(slice(at, at + rows))
            at += rows
    return total, at


def final_kernel(*refs):
    final_parts(refs[:2], refs[2:])


def final_small_kernel(*refs):
    outs, (biases, f_bias, gain, shift, table) = refs[4:12], refs[12:]
    total, at = final_parts(refs[:4], outs)
    part = total(slice(at, at + SMALL_ROWS))
    biases[...] = part[0:7, :64]
    gain[...] = part[GAIN : GAIN + 3, :64]
    shift[...] = part[SHIFT : SHIFT + 3, :64]
    half = table.shape[0] // 2
    table[:half] = part[TABLE : TABLE + half, :64]
    table[half:] = part[TABLE : TABLE + half, 64:]
    f_bias[...] = part[TABLE + half : TABLE + half + 2]


def add(left, right):
    return (left.astype(F32) + right.astype(F32)).astype(BF)


def core_sums(own, other):
    return [add(own[i], other[i]) for i in range(Y * X)]


def join_kernel(*refs):
    parts, outs = refs[: -Y * X], refs[-Y * X :]
    at = 0
    for own, other in zip(parts[::2], parts[1::2]):
        rows = own.shape[2]
        for i, out in enumerate(outs):
            out[:, at : at + rows] = add(own[i], other[i])
        at += rows


def core_sums_joined(*parts):
    rows = sum(one.shape[2] for one in parts[::2])
    return call(
        join_kernel,
        "join",
        list(parts),
        [VMEM] * len(parts),
        [((Z, rows, 128), BF, VMEM)] * (Y * X),
        [],
    )


def near_parts(pairs):
    return [pairs[0], swap(pairs[1], 2), swap(pairs[2], 4), swap(pairs[3], 6)]


def chip_sums(meta, near):
    unused, rows, lanes = near[0].shape
    return call(
        merge_kernel,
        "merge",
        [meta, *near],
        [SMEM] + [VMEM] * 4,
        [((2, rows, lanes), F32, VMEM), ((2, rows, lanes), BF, VMEM)],
        [],
    )


def halved(pair, other):
    rows, lanes = pair.shape[1:]
    return call(
        halve_kernel, "halve", [pair, other], [VMEM] * 2, [((rows, lanes), F32, VMEM), ((rows, lanes), BF, VMEM)], []
    )


def merge_all_kernel(meta, a, b, c, d, *outs):
    mine = meta[meta.shape[0] - 4]
    for i, out in enumerate(outs):
        z = mine ^ i
        value = (a[z].astype(F32) + b[z].astype(F32)) + (c[z].astype(F32) + d[z].astype(F32))
        out[...] = value.astype(out.dtype)


def chip_sums_all(meta, near):
    unused, rows, lanes = near[0].shape
    return call(
        merge_all_kernel,
        "merge_all",
        [meta, *near],
        [SMEM] + [VMEM] * 4,
        [((rows, lanes), F32, VMEM)] + [((rows, lanes), BF, VMEM)] * 3,
        [],
    )


def slice_sums(kernel, parts, shapes):
    return call(kernel, "final", parts, [VMEM] * len(parts), [(s, F32, VMEM) for s in shapes], [])


def place_kernel(meta, a, b, c, d, out):
    base = meta.shape[0] - 4
    mine = meta[base + 2] * CORE + meta[base + 3]
    pairs = a.shape[0]
    for i, one in enumerate((a, b, c, d)):
        for p in range(pairs):
            out[(mine ^ i) * pairs + p] = one[p].astype(F32)


def swap_memory(memory, pairs):
    mine = lax.axis_index("mem")
    parts = [lax.dynamic_slice_in_dim(memory, (mine ^ i) * pairs, pairs) for i in range(4)]
    return parts


def return_memory(meta, parts, shape):
    return call(place_kernel, "place", [meta, *parts], [SMEM] + [VMEM] * 4, [(shape, F32, VMEM)], [])[0]


def slots_of(wide):
    rows, cols = wide.shape
    cut = wide.reshape(Z, Y, rows // (Z * Y), X, CORE, cols // (X * CORE))
    return [cut[:, y, :, x, c] for y, x, c in SLOTS]


def wide_of(slots):
    z, rows, cols = slots[0].shape
    cut = jnp.stack(slots).reshape(Y, X, CORE, z, rows, cols)
    return cut.transpose(3, 0, 4, 1, 2, 5).reshape(z * Y * rows, X * CORE * cols)


def gather_any(piece):
    return lax.all_gather(lax.all_gather(piece, "mem", axis=1, tiled=True), "dp", axis=0, tiled=True)


def scatter_any(wide):
    part = lax.psum_scatter(wide.astype(F32), "dp", scatter_dimension=0, tiled=True)
    return lax.psum_scatter(part, "mem", scatter_dimension=1, tiled=True)


def narrow_columns(slots):
    return [jnp.concatenate(jnp.split(one, 4, axis=2), axis=1) for one in slots]


def small_pieces(biases, f_bias, gain, shift, table):
    vectors = jnp.concatenate([biases, gain, shift], axis=0)
    vectors = jnp.pad(vectors, ((0, TABLE - vectors.shape[0]), (0, 0)))
    half = table.shape[0] // 2

    def cut(rows):
        return rows.reshape(rows.shape[0], Z, Y, 64).transpose(1, 2, 0, 3)

    top = jnp.pad(cut(vectors), ((0, 0),) * 3 + ((0, 64),))
    low = jnp.concatenate([cut(table[:half]), cut(table[half:])], axis=3)
    whole = jnp.concatenate([top, low, f_bias.reshape(Z, Y, 2, 128)], axis=2)
    return jnp.pad(whole, ((0, 0), (0, 0), (0, SMALL_ROWS - whole.shape[2]), (0, 0)))


def spread_any(squares, w_in, w_out, smalls):
    wide = [slots_of(gather_any(one)) for one in squares]
    small = small_pieces(*[lax.all_gather(one, "dp", axis=one.ndim - 1, tiled=True) for one in smalls])
    ins = narrow_columns(slots_of(gather_any(w_in)))
    outs = slots_of(gather_any(w_out))
    square_w, feed_w = [], []
    for i, (y, unused, unused2) in enumerate(SLOTS):
        parts = [one[i] for one in wide]
        square_w.append(jnp.concatenate([*parts[:3], small[:, y], *parts[3:]], axis=1))
        feed_w.append(jnp.concatenate([ins[i], outs[i]], axis=1))
    return square_w, feed_w


def by_slot(halves):
    return [halves[c][y * X + x] for y, x, c in SLOTS]


def reduce_squares_any(halves, count):
    slots = by_slot(halves)
    return [
        scatter_any(wide_of([one[:, PIECE * i : PIECE * (i + 1)] for one in slots]))
        for i in range(count)
    ]


def reduce_feed_any(halves):
    slots = by_slot(halves)
    ins = [
        jnp.concatenate([one[:, PIECE * j : PIECE * (j + 1)] for j in range(4)], axis=2)
        for one in slots
    ]
    return [scatter_any(wide_of(ins)), scatter_any(wide_of([one[:, 4 * PIECE :] for one in slots]))]


def reduce_small_any(halves, count):
    parts = [halves[0][y * X][:, 4 * PIECE :].astype(F32) for y in range(Y)]
    part = jnp.stack(parts, axis=1).reshape(Z * Y, SMALL_ROWS, 128)
    vectors = part[:, :13, :64].transpose(1, 0, 2).reshape(13, -1)
    half = count // 2
    table = part[:, TABLE : TABLE + half]
    table = jnp.concatenate([table[:, :, :64], table[:, :, 64:]], axis=1)
    rows = jnp.concatenate([vectors, table.transpose(1, 0, 2).reshape(count, -1)], axis=0)
    cut = lax.psum_scatter(lax.psum(rows, "mem"), "dp", scatter_dimension=1, tiled=True)
    f_bias = part[:, TABLE + half : TABLE + half + 2].reshape(-1)
    f_bias = lax.psum_scatter(lax.psum(f_bias, "mem"), "dp", scatter_dimension=0, tiled=True)
    return cut[:7], f_bias, cut[7:10], cut[10:13], cut[13:]


def shards(
    target, memory, time_steps, target_len, source_len, source_off, cotangent,
    self_query, self_key, self_value, self_out, cross_query, cross_key, cross_value, cross_out,
    feed_in, feed_out, biases, feed_bias, norm_gain, norm_shift, step_table,
):
    pairs = target.shape[0]
    steps = step_table.shape[0]
    dp, mem = lax.axis_index("dp"), lax.axis_index("mem")
    quick = lax.axis_size("dp") == Z * Y and lax.axis_size("mem") == X * CORE
    here = [dp // 2, dp % 2, mem // 2, mem % 2] if quick else [0, 0, 0, 0]
    meta = jnp.concatenate(
        [
            target_len,
            time_steps,
            lax.dynamic_slice_in_dim(source_off, mem * pairs, pairs),
            lax.dynamic_slice_in_dim(source_len, mem * pairs, pairs),
            jnp.stack([jnp.asarray(i, jnp.int32) for i in here]),
        ]
    )
    squares = (self_query, self_key, self_value, self_out, cross_query, cross_key, cross_value, cross_out)
    if quick:
        packed = call(
            pack_kernel,
            "pack",
            [*squares, feed_in, feed_out, biases, feed_bias.reshape(2, 128)]
            + [norm_gain, norm_shift, step_table],
            [VMEM] * 15,
            [((i, 128), BF, VMEM) for i in (SELF_ROWS + CROSS_ROWS, FEED_ROWS)],
            [VMEM((SMALL_ROWS, 128), F32)],
            1,
            60 * 2**20,
        )
        packed, memory = fence((packed, memory))
        square_p, feed_p = packed
        mems = swap_memory(memory, pairs)
        mems[2], mems[3] = swap(mems[2], 2), swap(mems[3], 3)
        square_z = sent_z([square_p] * 4)
        square_z, mems, feed_p = fence((square_z, mems, feed_p))
        square_near = spread_near(z_all(meta, square_z))
        feed_z = z_pair(meta, feed_p)
        feed_z = (feed_z, swap(feed_z, 16))
        mems[1] = swap(mems[1], 1)
        feed_z = z_quad(meta, *feed_z)
        square_near, feed_z, mems = fence((square_near, feed_z, mems))
        square_w = spread_core(square_near)
        feed_near = spread_near(feed_z)
    else:
        square_w, feed_w = spread_any(
            squares, feed_in, feed_out, (biases, feed_bias, norm_gain, norm_shift, step_table)
        )
        own = lax.all_to_all(memory, "mem", 0, 1, tiled=True)
        mems = jnp.split(own, X * CORE, axis=1)

    far_a, w_a, near_mix, vecs, fbias, held_a, held_b = self_forward(meta, target, square_w, steps)
    far_b, w_b, after_self, after_cross = cross_forward(meta, target, near_mix, mems, vecs, held_b)
    if quick:
        feed_near, after_cross = fence((feed_near, after_cross))
        feed_w = spread_core(feed_near)
    layer_out, gres_c, sums_c, d_fbias, *d_feed = feed(
        meta, after_cross, cotangent, vecs, fbias, feed_w
    )
    if quick:
        d_feed, gres_c = fence((d_feed, gres_c))
        d_feed[1] = swap(d_feed[1], 1)
    gq_b, gk_b, gv_b, sums_b, *d_cross = cross_back(meta, gres_c, far_b, w_b, held_b)
    if quick:
        d_feed, gq_b, d_cross = fence((d_feed, gq_b, d_cross))
        u_feed = core_sums(*d_feed)
        u_feed, gq_b, d_cross = fence((u_feed, gq_b, d_cross))
        n_feed = near_parts(u_feed)
        d_cross[1] = swap(d_cross[1], 1)
    grad_target, *gmem, d_first, d_second = lower_back(
        meta, gres_c, (gq_b, gk_b, gv_b), after_self, far_a, w_a, target, vecs, (sums_b, sums_c), d_fbias, held_b, held_a, steps
    )
    d_self = [d_first, d_second]
    if quick:
        one = self_query.shape
        n_feed, d_cross, d_self, gmem = fence((n_feed, d_cross, d_self, gmem))
        d_self[1] = swap(d_self[1], 1)
        u_rest = core_sums_joined(*d_cross, *d_self)
        m_feed = chip_sums(meta, n_feed)
        u_rest, m_feed, gmem = fence((u_rest, m_feed, gmem))
        n_rest = near_parts(u_rest)
        gmem[1] = swap(gmem[1], 1)
        m_feed = halved(m_feed[0], swap(m_feed[1], 16))
        g_feed = slice_sums(final_kernel, [m_feed[0], swap(m_feed[1], 8)], (feed_in.shape, feed_out.shape))
        n_rest, gmem, g_feed = fence((n_rest, gmem, g_feed))
        m_rest = sent_z(chip_sums_all(meta, n_rest))
        gmem[2], gmem[3] = swap(gmem[2], 2), swap(gmem[3], 3)
        grad_memory = return_memory(meta, gmem, memory.shape)
        m_rest, grad_memory = fence((m_rest, grad_memory))
        small_shapes = (biases.shape, (2, 128), norm_gain.shape, norm_shift.shape, step_table.shape)
        out = slice_sums(final_small_kernel, m_rest, (one,) * 8 + small_shapes)
        g_cross, g_self, (g_bias, g_fbias, g_gain, g_shift, g_table) = out[:4], out[4:8], out[8:]
        g_fbias = g_fbias.reshape(feed_bias.shape)
    else:
        whole = jnp.concatenate(gmem, axis=1)
        grad_memory = lax.all_to_all(whole, "mem", 1, 0, tiled=True).astype(F32)
        g_feed = reduce_feed_any(d_feed)
        g_cross = reduce_squares_any(d_cross, 4)
        g_self = reduce_squares_any(d_self, 4)
        g_bias, g_fbias, g_gain, g_shift, g_table = reduce_small_any(d_self, steps)
    return (
        layer_out, grad_target, grad_memory, *g_self, *g_cross, *g_feed,
        g_bias, g_fbias, g_gain, g_shift, g_table,
    )


def solution(mesh):
    rows = P(BOTH, None, None)
    piece = P("dp", "mem")
    vector = P(None, "dp")
    mem_rows = P("dp", "mem", None)
    return jax.shard_map(
        shards,
        mesh=mesh,
        in_specs=(rows, mem_rows, P(BOTH), P(BOTH), P("dp"), P("dp"), rows)
        + (piece,) * 10
        + (vector, P("dp"), vector, vector, vector),
        out_specs=(rows, rows, mem_rows) + (piece,) * 10 + (vector, P("dp"), vector, vector, vector),
        check_vma=False,
    )
```

```python
import functools
import math

import jax
import jax.numpy as jnp
from jax import lax
from jax.experimental import pallas as pl
from jax.experimental.pallas import tpu as pltpu
from jax.sharding import PartitionSpec as P

HEADS = 8
DH = 64
GROUP = 4
WIDE = GROUP * DH
EPSILON = 1e-05
SCALE = 1.0 / math.sqrt(DH)
BF = jnp.bfloat16
F32 = jnp.float32
VMEM_LIMIT = 30 * 2**20


def contract(left, right, left_dim, right_dim):
    return lax.dot_general(
        left, right, (((left_dim,), (right_dim,)), ((), ())), preferred_element_type=F32
    )


def mul(left, right):
    return contract(left, right, 1, 0)


def mul_nt(left, right):
    return contract(left, right, 1, 1)


def mul_tn(left, right):
    return contract(left, right, 0, 0)


def normalise(signal):
    centre = signal - jnp.mean(signal, axis=-1, keepdims=True)
    inverse = lax.rsqrt(jnp.mean(centre * centre, axis=-1, keepdims=True) + EPSILON)
    return centre * inverse, inverse


def norm_back(grad, scaled, inverse, gain):
    up = grad * gain
    return inverse * (
        up
        - jnp.mean(up, axis=-1, keepdims=True)
        - scaled * jnp.mean(up * scaled, axis=-1, keepdims=True)
    )


def col_sum(array):
    return jnp.sum(array.astype(F32), axis=0, keepdims=True)


def head_of_lane(rows):
    return lax.broadcasted_iota(jnp.int32, (rows, WIDE), 1) // DH


def stacked(block, lane_head):
    zero = jnp.zeros_like(block)
    return jnp.concatenate([jnp.where(lane_head == h, block, zero) for h in range(GROUP)], axis=0)


def unstacked(result, lane_head, rows):
    picked = result[:rows]
    for h in range(1, GROUP):
        picked = jnp.where(lane_head == h, result[h * rows : (h + 1) * rows], picked)
    return picked


def blocks(pairs):
    return [(p, g, slice(g * WIDE, (g + 1) * WIDE)) for p in range(pairs) for g in range(HEADS // GROUP)]


INPUT, QUERY, KEY, VALUE, MIXED, MEMORY = range(6)


def attend(before, bias_of, kept, w_ref, after):
    pairs, unused, rows, unused2 = kept.shape
    lane_head = head_of_lane(rows)
    every = blocks(pairs)

    def scores_of(p, g, cols):
        return mul_nt(stacked(kept[p, QUERY, :, cols], lane_head), kept[p, KEY, :, cols])

    before(0)
    ahead = scores_of(*every[0])
    for i, (p, g, cols) in enumerate(every):
        scores = ahead + bias_of(p)
        if g == 0 and p + 1 < pairs:
            before(p + 1)
        if i + 1 < len(every):
            ahead = scores_of(*every[i + 1])
        top = jnp.max(scores, axis=-1, keepdims=True)
        raised = jnp.exp(scores - top)
        total = jnp.sum(raised, axis=-1, keepdims=True)
        weights = (raised * (1.0 / total)).astype(BF)
        w_ref[p, g] = weights
        mixed = mul(weights, kept[p, VALUE, :, cols])
        kept[p, MIXED, :, cols] = unstacked(mixed, lane_head, rows).astype(BF)
        if g == HEADS // GROUP - 1:
            after(p)


def attend_back(before, ready, kept, w_ref, grad_ref, gq_ref, gk_ref, gv_ref, after):
    pairs, unused, rows, unused2 = kept.shape
    lane_head = head_of_lane(rows)
    every = blocks(pairs)

    def weight_grads(p, g, cols):
        if g == 0:
            ready(p)
        grads = stacked(grad_ref[p, :, cols], lane_head)
        return grads, mul_nt(grads, kept[p, VALUE, :, cols])

    before(0)
    ahead = weight_grads(*every[0])
    for i, (p, g, cols) in enumerate(every):
        grads, grad_w = ahead
        if g == 0 and p + 1 < pairs:
            before(p + 1)
        if i + 1 < len(every):
            ahead = weight_grads(*every[i + 1])
        weights = w_ref[p, g]
        wide = weights.astype(F32)
        offset = jnp.sum(grad_w * wide, axis=-1, keepdims=True)
        grad_s = (wide * (grad_w - offset)).astype(BF)
        grad_q = unstacked(mul(grad_s, kept[p, KEY, :, cols]), lane_head, rows)
        gq_ref[p, :, cols] = (grad_q * SCALE).astype(BF)
        gk_ref[p, :, cols] = mul_tn(grad_s, stacked(kept[p, QUERY, :, cols], lane_head)).astype(BF)
        gv_ref[p, :, cols] = mul_tn(weights, grads).astype(BF)
        if g == HEADS // GROUP - 1:
            after(p)


def flat(ref):
    value = ref[...]
    return value.reshape(value.shape[0] * value.shape[1], value.shape[2])


Z, Y, X, CORE = 4, 2, 2, 2
SLOTS = [(y, x, c) for y in range(Y) for x in range(X) for c in range(CORE)]
PIECE = 64
FEED_ROWS = 4 * PIECE + 256
SMALL_ROWS = 48
SELF_ROWS = 3 * PIECE + SMALL_ROWS
CROSS_ROWS = 5 * PIECE
FIRST_ROWS = 288
GAIN, SHIFT, TABLE = 7, 10, 16


def places(meta, slot):
    base = meta.shape[0] - 4
    y, x, c = slot
    return y ^ meta[base + 1], (x ^ meta[base + 2]) * CORE + (c ^ meta[base + 3])


def load_copies(meta, sources, held, sems, first=0):
    copies = []
    rows = held.shape[-2]
    for i, slot in enumerate(SLOTS):
        row, panel = places(meta, slot)
        source = sources[i].at[:, pl.ds(first, rows)]
        copies.append(pltpu.make_async_copy(source, held.at[panel, :, row], sems.at[i]))
    return copies


def store_copies(meta, held, targets, sems, first=0):
    copies = []
    rows = targets[0].shape[2]
    for i, slot in enumerate(SLOTS):
        row, panel = places(meta, slot)
        y, x, c = slot
        target = targets[c].at[y * X + x]
        source = held.at[panel, :, row, pl.ds(first, rows)]
        copies.append(pltpu.make_async_copy(source, target, sems.at[i]))
    return copies


def start(copies):
    for copy in copies:
        copy.start()


def wait(copies):
    for copy in copies:
        copy.wait()


def moves(sources, targets, sems):
    return [pltpu.make_async_copy(a, b, sems.at[i]) for i, (a, b) in enumerate(zip(sources, targets))]


def joined(value):
    return value.reshape(-1, value.shape[-1])


def square(held, index):
    span = slice(PIECE * index, PIECE * (index + 1))
    return jnp.concatenate([joined(held[i, :, :, span]) for i in range(X * CORE)], axis=1)


def keep(held, index, value):
    span = slice(PIECE * index, PIECE * (index + 1))
    for i in range(X * CORE):
        part = value[:, i * 128 : (i + 1) * 128].astype(BF)
        held[i, :, :, span] = part.reshape(Z, Y, PIECE, 128)


def all_rows(kept, index):
    value = kept[:, index]
    return value.reshape(value.shape[0] * value.shape[1], value.shape[2])


def each(source, target, sems):
    count = source.shape[0]
    return moves([source.at[p] for p in range(count)], [target.at[p] for p in range(count)], sems)


def self_forward_kernel(meta, target, *refs):
    pieces, refs = refs[:8], refs[8:]
    far, far_w, near_mix, vecs, fbias, held, held_cross = refs[:7]
    kept, w, small, sems, cross_sems, small_sems, far_sems, w_sems = refs[7:]
    base = meta.shape[0] - 4
    small_loads = [
        pltpu.make_async_copy(
            pieces[y * CORE].at[0, :, pl.ds(3 * PIECE, SMALL_ROWS)], small.at[:, y ^ meta[base + 1]], small_sems.at[y]
        )
        for y in range(Y)
    ]
    start(small_loads)
    loads, cross_loads = [], []
    edge = FIRST_ROWS - SELF_ROWS
    for i, slot in enumerate(SLOTS):
        y, x, c = slot
        row, panel = places(meta, slot)
        a_part, b_part = pieces[y * CORE + c].at[x], pieces[Y * CORE + x * CORE + c].at[y]
        own, cross = held.at[panel, :, row], held_cross.at[panel, :, row]
        loads.append(pltpu.make_async_copy(a_part.at[:, pl.ds(0, 3 * PIECE)], own, sems.at[i]))
        cross_loads += moves(
            (a_part.at[:, pl.ds(SELF_ROWS, edge)], b_part),
            (cross.at[:, pl.ds(0, edge)], cross.at[:, pl.ds(edge, CROSS_ROWS - edge)]),
            cross_sems.at[i],
        )
    start(loads)
    start(cross_loads)
    copies, w_copies = each(kept, far, far_sems), each(w, far_w, w_sems)
    pairs, length, width = target.shape
    wait(small_loads)
    every = [small[z, y].astype(F32) for z in range(Z) for y in range(Y)]
    steps = (vecs.shape[0] - TABLE) // 2
    vecs[:TABLE] = jnp.concatenate([one[:TABLE, :64] for one in every], axis=1)
    for i in range(2):
        part = [one[TABLE : TABLE + steps, 64 * i : 64 * (i + 1)] for one in every]
        vecs[TABLE + i * steps : TABLE + (i + 1) * steps] = jnp.concatenate(part, axis=1)
    for d, one in enumerate(every):
        for i in range(2):
            at = TABLE + steps + i
            fbias[:, d * 256 + i * 128 : d * 256 + (i + 1) * 128] = one[at : at + 1]

    def before(p):
        emb = target[p].astype(F32) + vecs[pl.ds(TABLE + meta[pairs + p], 1), :]
        scaled, unused = normalise(emb)
        x = (scaled * vecs[GAIN : GAIN + 1] + vecs[SHIFT : SHIFT + 1]).astype(BF)
        kept[p, INPUT] = x
        if p == 0:
            wait(loads)
        kept[p, QUERY] = (mul(x, square(held, 0)) + vecs[0:1]).astype(BF) * SCALE
        kept[p, KEY] = mul(x, square(held, 1)).astype(BF)
        kept[p, VALUE] = (mul(x, square(held, 2)) + vecs[1:2]).astype(BF)

    def bias_of(p):
        spot = lax.broadcasted_iota(jnp.int32, (1, length), 1)
        return jnp.where(spot < meta[p], 0.0, -1e30)

    def after(p):
        near_mix[p] = kept[p, MIXED]
        copies[p].start()
        w_copies[p].start()

    attend(before, bias_of, kept, w, after)
    wait(cross_loads)
    wait(copies)
    wait(w_copies)


def cross_forward_kernel(meta, target, mix_a, mem_0, mem_1, mem_2, mem_3, vecs, held, *refs):
    far, w, far_after, after_cross = refs[:4]
    kept, after_self, mem_sems, far_sems, after_sems = refs[4:]
    pairs, length, width = target.shape
    source = kept.shape[2]
    base = meta.shape[0] - 4
    mine = meta[base + 2] * CORE + meta[base + 3]
    part = source // (X * CORE)
    mem_loads = [
        pltpu.make_async_copy(
            one,
            kept.at[:, MEMORY, pl.ds(pl.multiple_of((mine ^ i) * part, part), part), :],
            mem_sems.at[i],
        )
        for i, one in enumerate((mem_0, mem_1, mem_2, mem_3))
    ]
    start(mem_loads)
    copies = each(kept, far, far_sems)
    after_copies = each(after_self, far_after, after_sems)

    def before(p):
        row = vecs[pl.ds(TABLE + meta[pairs + p], 1), :]
        total = target[p].astype(F32) + row + mul(mix_a[p], square(held, 0)) + vecs[2:3]
        after_self[p] = total
        after_copies[p].start()
        scaled, unused = normalise(total)
        x = (scaled * vecs[GAIN + 1 : GAIN + 2] + vecs[SHIFT + 1 : SHIFT + 2]).astype(BF)
        kept[p, INPUT] = x
        kept[p, QUERY] = (mul(x, square(held, 1)) + vecs[3:4]).astype(BF) * SCALE
        if p == 0:
            wait(mem_loads)
        m = kept[p, MEMORY]
        kept[p, KEY] = mul(m, square(held, 2)).astype(BF)
        kept[p, VALUE] = (mul(m, square(held, 3)) + vecs[4:5]).astype(BF)

    def bias_of(p):
        spot = lax.broadcasted_iota(jnp.int32, (1, source), 1)
        begin = meta[2 * pairs + p]
        end = begin + meta[3 * pairs + p]
        return jnp.where((spot >= begin) & (spot < end), 0.0, -1e30)

    def after(p):
        copies[p].start()
        after_cross[p] = after_self[p] + mul(kept[p, MIXED], square(held, 4)) + vecs[5:6]

    attend(before, bias_of, kept, w, after)
    wait(after_copies)
    wait(copies)


def gelu_parts(value):
    size = jnp.abs(value) * math.sqrt(0.5)
    t = 1.0 / (1.0 + 0.3275911 * size)
    bell = jnp.exp(-0.5 * value * value)
    tail = (
        t
        * (
            0.5 * 0.254829592
            + t
            * (
                0.5 * -0.284496736
                + t * (0.5 * 1.421413741 + t * (0.5 * -1.453152027 + t * (0.5 * 1.061405429)))
            )
        )
        * bell
    )
    below = jnp.where(value < 0, tail, 1.0 - tail)
    slope = below + value * bell * (1.0 / math.sqrt(2.0 * math.pi))
    return value * below, slope


def feed_kernel(meta, after_cross, cot, vecs, feed_bias, *refs):
    pieces, refs = refs[:8], refs[8:]
    far_out, gres, sums, dbias = refs[:4]
    targets, refs = refs[4:6], refs[6:]
    held, kept, x_c, act, grad_pre, layer_out, sems, out_sems, far_sems = refs
    copies = moves((layer_out,), (far_out,), far_sems)
    loads = load_copies(meta, pieces, held, sems)
    start(loads)
    stores = store_copies(meta, kept, targets, out_sems)
    shape = after_cross.shape
    signal = flat(after_cross)
    scaled, inverse = normalise(signal)
    gain = vecs[GAIN + 2 : GAIN + 3]
    x_c[...] = (scaled * gain + vecs[SHIFT + 2 : SHIFT + 3]).astype(BF)
    wait(loads)
    c = flat(cot)
    x = x_c[...]
    w_in = [
        jnp.concatenate([joined(held[j, :, :, PIECE * i : PIECE * (i + 1)]) for i in range(4)], axis=1)
        for j in range(4)
    ]
    w_out = [jnp.concatenate([joined(held[i, j, :, 4 * PIECE :]) for i in range(4)], axis=1) for j in range(4)]
    w_in = jnp.concatenate(w_in, axis=1)
    w_out = jnp.concatenate(w_out, axis=0)
    block, span = 256, 256
    tiles = [
        (slice(r, r + span), slice(j, j + block))
        for j in range(0, w_in.shape[1], block)
        for r in range(0, x.shape[0], span)
    ]

    def first(rows, cols):
        return mul(x[rows], w_in[:, cols]), mul_nt(c[rows], w_out[cols])

    ready = [first(*tile) for tile in tiles[:1]]
    for j, (rows, cols) in enumerate(tiles):
        if j + 1 < len(tiles):
            ready.append(first(*tiles[j + 1]))
        pre, grad_act = ready[j]
        ready[j] = None
        value, slope = gelu_parts(pre + feed_bias[:, cols])
        act[rows, cols] = value.astype(BF)
        grad = (grad_act * slope).astype(BF)
        grad_pre[rows, cols] = grad
        if rows.start == 0:
            total = col_sum(grad)
        else:
            total = total + col_sum(grad)
        if rows.stop == x.shape[0]:
            dbias[:, cols] = total
    for j in range(4):
        cols = slice(j * 512, (j + 1) * 512)
        d_out = mul_tn(act[:, cols], c)
        for i in range(4):
            part = d_out[:, i * 128 : (i + 1) * 128].astype(BF)
            kept[i, j, :, 4 * PIECE :] = part.reshape(Y, 256, 128)
        d_in = mul_tn(x, grad_pre[:, cols])
        for i in range(4):
            part = d_in[:, i * 128 : (i + 1) * 128].astype(BF)
            kept[j, :, :, PIECE * i : PIECE * (i + 1)] = part.reshape(Z, Y, PIECE, 128)
    start(stores)
    layer_out[...] = (signal + mul(act[...], w_out) + vecs[6:7]).astype(BF).reshape(shape)
    start(copies)
    grad = mul_nt(grad_pre[...], w_in)
    wide_cot = flat(cot).astype(F32)
    sums[0:1] = col_sum(wide_cot)
    sums[1:2] = col_sum(grad * scaled)
    sums[2:3] = col_sum(grad)
    gres[...] = (wide_cot + norm_back(grad, scaled, inverse, gain)).reshape(shape)
    wait(stores)
    wait(copies)


def cross_back_kernel(meta, gres, far, w, held, *refs):
    gq, gk, gv, sums = refs[:4]
    targets, (kept, gmix, grads, out_sems, far_sems) = refs[4:6], refs[6:]
    copies = each(far, kept, far_sems)
    start(copies)
    stores = store_copies(meta, grads, targets, out_sems)

    def before(p):
        gmix[p] = mul_nt(gres[p].astype(BF), square(held, 4)).astype(BF)

    attend_back(before, lambda p: copies[p].wait(), kept, w, gmix, gq, gk, gv, lambda p: None)
    grad = flat(gres).astype(BF)
    m = all_rows(kept, MEMORY)
    keep(grads, 3, mul_tn(all_rows(kept, MIXED), grad))
    keep(grads, 0, mul_tn(all_rows(kept, INPUT), flat(gq)))
    keep(grads, 1, mul_tn(m, flat(gk)))
    keep(grads, 2, mul_tn(m, flat(gv)))
    start(stores)
    sums[0:1] = col_sum(grad)
    sums[1:2] = col_sum(flat(gq))
    sums[2:3] = col_sum(flat(gv))
    wait(stores)


def lower_back_kernel(
    meta, gres, grad_q, grad_k, grad_v, far_after, far, far_w, target, vecs, sums_b, sums_c, dbias, held, held_a, *refs
):
    far_target, gmem_0, gmem_1, gmem_2, gmem_3 = refs[:5]
    targets, refs = refs[5:7], refs[7:]
    kept, w, after_self, gres_a, gmix, gmem, gq, gk, gv, gtarget, gtable, grads = refs[:12]
    mem_sems, far_sems, w_sems, after_sems, target_sems, out_sems = refs[12:]
    copies, w_copies = each(far, kept, far_sems), each(far_w, w, w_sems)
    after_copies = each(far_after, after_self, after_sems)
    for group in zip(after_copies, copies, w_copies):
        start(group)
    target_copies = each(gtarget, far_target, target_sems)
    stores = store_copies(meta, grads, targets, out_sems)
    base = meta.shape[0] - 4
    mine = meta[base + 2] * CORE + meta[base + 3]
    part = gmem.shape[1] // (X * CORE)
    mem_stores = [
        pltpu.make_async_copy(
            gmem.at[:, pl.ds(pl.multiple_of((mine ^ i) * part, part), part), :], one, mem_sems.at[i]
        )
        for i, one in enumerate((gmem_0, gmem_1, gmem_2, gmem_3))
    ]
    pairs, length, width = gres.shape
    totals = [0.0] * 5
    gtable[...] = jnp.zeros_like(gtable)

    def count(first, *parts):
        for i, one in enumerate(parts):
            totals[first + i] = totals[first + i] + col_sum(one)

    def before(p):
        grad_m = mul_nt(grad_k[p], square(held, 2)) + mul_nt(grad_v[p], square(held, 3))
        gmem[p] = grad_m.astype(BF)
        grad_in = mul_nt(grad_q[p], square(held, 1))
        after_copies[p].wait()
        scaled, inverse = normalise(after_self[p])
        total = gres[p] + norm_back(grad_in, scaled, inverse, vecs[GAIN + 1 : GAIN + 2])
        gres_a[p] = total
        grad_a = total.astype(BF)
        gmix[p] = mul_nt(grad_a, square(held, 0)).astype(BF)
        count(0, grad_in * scaled, grad_in, grad_a)
        if p + 1 == pairs:
            start(mem_stores)

    def ready(p):
        copies[p].wait()
        w_copies[p].wait()

    def after(p):
        grad_in = (
            mul_nt(gq[p], square(held_a, 0)) + mul_nt(gk[p], square(held_a, 1)) + mul_nt(gv[p], square(held_a, 2))
        )
        row = pl.ds(TABLE + meta[pairs + p], 1)
        scaled, inverse = normalise(target[p].astype(F32) + vecs[row, :])
        count(3, grad_in * scaled, grad_in)
        total = gres_a[p] + norm_back(grad_in, scaled, inverse, vecs[GAIN : GAIN + 1])
        gtarget[p] = total
        target_copies[p].start()
        gtable[pl.ds(meta[pairs + p], 1), :] += col_sum(total)

    attend_back(before, ready, kept, w, gmix, gq, gk, gv, after)
    x = all_rows(kept, INPUT)
    keep(grads, 3, mul_tn(all_rows(kept, MIXED), flat(gres_a).astype(BF)))
    for i, one in enumerate((gq, gk, gv)):
        keep(grads, i, mul_tn(x, flat(one)))
    rows = [col_sum(flat(gq)), col_sum(flat(gv)), totals[2], sums_b[1:2], sums_b[2:3], sums_b[0:1], sums_c[0:1]]
    rows += [totals[3], totals[0], sums_c[1:2], totals[4], totals[1], sums_c[2:3]]
    vectors = jnp.concatenate(rows + [jnp.zeros((TABLE - len(rows), width), F32)], axis=0)
    steps = gtable.shape[0] // 2
    for d in range(Z * Y):
        lanes = slice(d * 64, (d + 1) * 64)
        top = jnp.concatenate([vectors[:, lanes], jnp.zeros((TABLE, 64), F32)], axis=1)
        low = jnp.concatenate([gtable[:steps, lanes], gtable[steps:, lanes]], axis=1)
        tail = [dbias[:, d * 256 + i * 128 : d * 256 + (i + 1) * 128] for i in range(2)]
        fill = jnp.zeros((SMALL_ROWS - TABLE - steps - 2, 128), F32)
        small = jnp.concatenate([top, low, *tail, fill], axis=0).astype(BF)
        for i in range(X * CORE):
            grads[i, d // Y, d % Y, 4 * PIECE :] = small
    start(stores)
    wait(mem_stores)
    wait(target_copies)
    wait(stores)


HBM = pl.ANY
FAR = pltpu.HBM
VMEM = pltpu.VMEM
SMEM = pltpu.SMEM


def call(kernel, name, args, spaces, outs, scratch, micros=1, limit=VMEM_LIMIT):
    cost = pl.CostEstimate(flops=int(micros * 10**9), bytes_accessed=int(micros * 3 * 10**6), transcendentals=0)
    function = pl.pallas_call(
        kernel,
        out_shape=[FAR(s, d) if m is FAR else jax.ShapeDtypeStruct(s, d) for s, d, m in outs],
        in_specs=[pl.BlockSpec(memory_space=m) for m in spaces],
        out_specs=[pl.BlockSpec(memory_space=m) for unused, unused2, m in outs],
        scratch_shapes=scratch,
        compiler_params=pltpu.CompilerParams(vmem_limit_bytes=limit),
        cost_estimate=cost,
        name=name,
    )
    return list(function(*[pltpu.with_memory_space_constraint(a, m) if m is FAR else a for a, m in zip(args, spaces)]))


def held_shape(rows):
    return (X * CORE, Z, Y, rows, 128)


def held_like(rows):
    return VMEM(held_shape(rows), BF)


def kept_like(slots):
    return VMEM((X * CORE, slots[1], Y, *slots[2:]), BF)


def sems(*shape):
    return pltpu.SemaphoreType.DMA(shape)


def weights_shape(shape, source):
    return (shape[0], HEADS // GROUP, GROUP * shape[1], source)


def slot_shape(count, extra=0):
    return (Y * X, Z, count * PIECE + extra, 128)


def kept_shape(shape, count):
    return (shape[0], count, *shape[1:])


def self_forward(meta, target, pieces, steps):
    shape = target.shape
    kept, w_shape = kept_shape(shape, MIXED + 1), weights_shape(shape, shape[1])
    return call(
        self_forward_kernel,
        "self_forward",
        [meta, target, *pieces],
        [SMEM, VMEM] + [FAR] * 8,
        [(kept, BF, FAR), (w_shape, BF, FAR), (shape, BF, VMEM)]
        + [((TABLE + steps, shape[2]), F32, VMEM), ((1, 4 * shape[2]), F32, VMEM)]
        + [(held_shape(3 * PIECE), BF, VMEM), (held_shape(CROSS_ROWS), BF, VMEM)],
        [VMEM(kept, BF), VMEM(w_shape, BF), VMEM((Z, Y, SMALL_ROWS, 128), BF)]
        + [sems(8), sems(8, 2), sems(2), sems(shape[0]), sems(shape[0])],
        0.1,
    )


def cross_forward(meta, target, mix_a, mems, vecs, held):
    shape = target.shape
    kept, w_shape = kept_shape(shape, MEMORY + 1), weights_shape(shape, shape[1])
    return call(
        cross_forward_kernel,
        "cross_forward",
        [meta, target, mix_a, *mems, vecs, held],
        [SMEM] + [VMEM] * 2 + [HBM] * 4 + [VMEM] * 2,
        [(kept, BF, FAR), (w_shape, BF, VMEM), (shape, F32, FAR), (shape, F32, VMEM)],
        [VMEM(kept, BF), VMEM(shape, F32), sems(4), sems(shape[0]), sems(shape[0])],
        0.1,
    )


def feed(meta, after_cross, cot, vecs, feed_bias, pieces):
    shape = after_cross.shape
    tokens, width = shape[0] * shape[1], shape[2]
    return call(
        feed_kernel,
        "feed",
        [meta, after_cross, cot, vecs, feed_bias, *pieces],
        [SMEM] + [VMEM] * 4 + [FAR] * 8,
        [(shape, BF, FAR), (shape, F32, VMEM), ((3, width), F32, VMEM), (feed_bias.shape, F32, VMEM)]
        + [(slot_shape(4, 256), BF, HBM)] * 2,
        [held_like(FEED_ROWS)] * 2
        + [VMEM((tokens, width), BF)] + [VMEM((tokens, feed_bias.shape[1]), BF)] * 2
        + [VMEM(shape, BF)]
        + [sems(8), sems(8), sems(1)],
        26,
        36 * 2**20,
    )


def cross_back(meta, gres, far, w, held):
    shape = gres.shape
    return call(
        cross_back_kernel,
        "cross_back",
        [meta, gres, far, w, held],
        [SMEM, VMEM, FAR, VMEM, VMEM],
        [(shape, BF, VMEM)] * 3 + [((3, shape[2]), F32, VMEM)] + [(slot_shape(4), BF, HBM)] * 2,
        [VMEM(far.shape, BF), VMEM(shape, BF), kept_like(slot_shape(4)), sems(8), sems(shape[0])],
        15,
    )


def lower_back(meta, gres, grads, after_self, far, far_w, target, vecs, sums, dbias, held, held_a, steps):
    shape = gres.shape
    part = (shape[0], shape[1] // (X * CORE), shape[2])
    slots = slot_shape(4, SMALL_ROWS)
    return call(
        lower_back_kernel,
        "lower_back",
        [meta, gres, *grads, after_self, far, far_w, target, vecs, *sums, dbias, held, held_a],
        [SMEM] + [VMEM] * 4 + [FAR] * 3 + [VMEM] * 7,
        [(shape, F32, FAR)] + [(part, BF, HBM)] * 4 + [(slots, BF, HBM)] * 2,
        [VMEM(far.shape, BF), VMEM(far_w.shape, BF), VMEM(shape, F32), VMEM(shape, F32)]
        + [VMEM(shape, BF)] * 5 + [VMEM(shape, F32), VMEM((steps, shape[2]), F32), kept_like(slots)]
        + [sems(4)] + [sems(shape[0])] * 4 + [sems(8)],
        20,
        38 * 2**20,
    )


BOTH = ("dp", "mem")


def swap(array, mask):
    count = lax.axis_size("dp") * lax.axis_size("mem")
    return lax.ppermute(array, BOTH, [(i, i ^ mask) for i in range(count)])


def pack_kernel(*refs):
    squares, (w_in, w_out, biases, f_bias, gain, shift, table) = refs[:8], refs[8:15]
    square_out, feed_out, stage = refs[15:]
    for i, ref in enumerate(squares):
        if i < 3:
            square_out[PIECE * i : PIECE * (i + 1)] = ref[...]
        else:
            square_out[SELF_ROWS + PIECE * (i - 3) : SELF_ROWS + PIECE * (i - 2)] = ref[...]
    for i in range(4):
        feed_out[PIECE * i : PIECE * (i + 1)] = w_in[:, 128 * i : 128 * (i + 1)]
    feed_out[4 * PIECE :] = w_out[...]
    stage[...] = jnp.zeros_like(stage)
    stage[0:7, :64] = biases[...].astype(F32)
    stage[GAIN : GAIN + 3, :64] = gain[...].astype(F32)
    stage[SHIFT : SHIFT + 3, :64] = shift[...].astype(F32)
    rows = table[...].astype(F32)
    half = rows.shape[0] // 2
    stage[TABLE : TABLE + half] = jnp.concatenate([rows[:half], rows[half:]], axis=1)
    stage[TABLE + half : TABLE + half + 2] = f_bias[...].astype(F32)
    square_out[3 * PIECE : SELF_ROWS] = stage[...].astype(BF)


def pair_kernel(meta, mine, other, out):
    low = meta[meta.shape[0] - 4] % 2
    out[low] = mine[...]
    out[1 - low] = other[...]


def quad_kernel(meta, mine, other, out):
    high = meta[meta.shape[0] - 4] // 2
    for i in range(2):
        out[2 * high + i] = mine[i]
        out[2 * (1 - high) + i] = other[i]


def quarter_kernel(meta, a, b, c, d, first, second):
    mine = meta[meta.shape[0] - 4]
    for i, one in enumerate((a, b, c, d)):
        first[mine ^ i] = one[:FIRST_ROWS]
        second[mine ^ i] = one[FIRST_ROWS:]


def double_kernel(a, a_other, b, b_other, a_out, b_out):
    for out, pair in ((a_out, (a, a_other)), (b_out, (b, b_other))):
        for i, one in enumerate(pair):
            out[i] = one[...]


def doubled(parts):
    outs = [((2, *one.shape), BF, VMEM) for one in parts[::2]]
    return call(double_kernel, "double", parts, [VMEM] * 4, outs, [])


def sent_z(parts):
    return [parts[0], swap(parts[1], 8), swap(parts[2], 16), swap(parts[3], 24)]


def z_halves(meta, parts):
    rows, lanes = parts[0].shape
    return call(
        quarter_kernel,
        "quarter",
        [meta, *parts],
        [SMEM] + [VMEM] * 4,
        [((Z, i, lanes), BF, VMEM) for i in (FIRST_ROWS, rows - FIRST_ROWS)],
        [],
    )


def z_pair(meta, packed):
    return call(
        pair_kernel,
        "pair",
        [meta, packed, swap(packed, 8)],
        [SMEM, VMEM, VMEM],
        [((2, *packed.shape), BF, VMEM)],
        [],
    )[0]


def z_quad(meta, pair, other):
    return call(
        quad_kernel,
        "quad",
        [meta, pair, other],
        [SMEM, VMEM, VMEM],
        [((Z, *pair.shape[1:]), BF, VMEM)],
        [],
    )[0]


fence = lax.optimization_barrier


def spread_near(along_z):
    return [along_z, swap(along_z, 2), swap(along_z, 4), swap(along_z, 6)]


def spread_core(near):
    out = []
    for one in near:
        out += [one, swap(one, 1)]
    return out


def merge_kernel(meta, a, b, c, d, own, sent):
    mine = meta[meta.shape[0] - 4]

    def total(z):
        return (a[z].astype(F32) + b[z].astype(F32)) + (c[z].astype(F32) + d[z].astype(F32))

    for i in range(2):
        own[i] = total(mine ^ i)
        sent[i] = total(mine ^ (2 + i)).astype(BF)


def halve_kernel(pair, other, own, sent):
    own[...] = pair[0] + other[0].astype(F32)
    sent[...] = (pair[1] + other[1].astype(F32)).astype(BF)


def final_parts(refs, outs):
    def total(span):
        value = refs[0][span]
        for ref in refs[1:]:
            value = value + ref[span].astype(F32)
        return value

    at = 0
    for out in outs:
        rows = out.shape[0]
        for i in range(out.shape[1] // 128):
            out[:, 128 * i : 128 * (i + 1)] = total(slice(at, at + rows))
            at += rows
    return total, at


def final_kernel(*refs):
    final_parts(refs[:2], refs[2:])


def final_small_kernel(*refs):
    outs, (biases, f_bias, gain, shift, table) = refs[4:12], refs[12:]
    total, at = final_parts(refs[:4], outs)
    part = total(slice(at, at + SMALL_ROWS))
    biases[...] = part[0:7, :64]
    gain[...] = part[GAIN : GAIN + 3, :64]
    shift[...] = part[SHIFT : SHIFT + 3, :64]
    half = table.shape[0] // 2
    table[:half] = part[TABLE : TABLE + half, :64]
    table[half:] = part[TABLE : TABLE + half, 64:]
    f_bias[...] = part[TABLE + half : TABLE + half + 2]


def add(left, right):
    return (left.astype(F32) + right.astype(F32)).astype(BF)


def core_sums(own, other):
    return [add(own[i], other[i]) for i in range(Y * X)]


def split_kernel(*refs):
    parts, (a_own, a_sent, b_own, b_sent) = refs[:-4], refs[-4:]
    at = 0
    for own, other in zip(parts[::2], parts[1::2]):
        rows = own.shape[2]
        cut = min(max(FIRST_ROWS - at, 0), rows)
        for i in range(Y * X):
            a_out = (a_own, a_sent)[i % X].at[i // X]
            b_out = (b_own, b_sent)[i // X].at[i % X]
            if cut > 0:
                a_out[:, at : at + cut] = add(own[i, :, :cut], other[i, :, :cut])
            if cut < rows:
                first = at + cut - FIRST_ROWS
                b_out[:, first : first + rows - cut] = add(own[i, :, cut:], other[i, :, cut:])
        at += rows


def split_sums(*parts):
    rows = sum(one.shape[2] for one in parts[::2])
    a_shape, b_shape = (2, Z, FIRST_ROWS, 128), (2, Z, rows - FIRST_ROWS, 128)
    return call(
        split_kernel,
        "split",
        list(parts),
        [VMEM] * len(parts),
        [(a_shape, BF, VMEM)] * 2 + [(b_shape, BF, VMEM)] * 2,
        [],
    )


def turn_kernel(a_own, a_other, b_own, b_other, a_kept, a_sent, b_kept, b_sent):
    for own, other, kept, sent in ((a_own, a_other, a_kept, a_sent), (b_own, b_other, b_kept, b_sent)):
        kept[...] = own[0].astype(F32) + other[0].astype(F32)
        sent[...] = add(own[1], other[1])


def turn(parts):
    a_shape, b_shape = parts[0].shape[1:], parts[2].shape[1:]
    return call(
        turn_kernel,
        "turn",
        parts,
        [VMEM] * 4,
        [(a_shape, F32, VMEM), (a_shape, BF, VMEM), (b_shape, F32, VMEM), (b_shape, BF, VMEM)],
        [],
    )


def meet_kernel(meta, a_kept, a_other, b_kept, b_other, *outs):
    mine = meta[meta.shape[0] - 4]
    rows = a_kept.shape[1]
    for i, out in enumerate(outs):
        z = mine ^ i
        out[:rows] = (a_kept[z] + a_other[z].astype(F32)).astype(out.dtype)
        out[rows:] = (b_kept[z] + b_other[z].astype(F32)).astype(out.dtype)


def meet(meta, parts):
    out = (parts[0].shape[1] + parts[2].shape[1], 128)
    return call(
        meet_kernel,
        "meet",
        [meta, *parts],
        [SMEM] + [VMEM] * 4,
        [(out, F32, VMEM)] + [(out, BF, VMEM)] * 3,
        [],
    )


def near_parts(pairs):
    return [pairs[0], swap(pairs[1], 2), swap(pairs[2], 4), swap(pairs[3], 6)]


def chip_sums(meta, near):
    unused, rows, lanes = near[0].shape
    return call(
        merge_kernel,
        "merge",
        [meta, *near],
        [SMEM] + [VMEM] * 4,
        [((2, rows, lanes), F32, VMEM), ((2, rows, lanes), BF, VMEM)],
        [],
    )


def halved(pair, other):
    rows, lanes = pair.shape[1:]
    return call(
        halve_kernel, "halve", [pair, other], [VMEM] * 2, [((rows, lanes), F32, VMEM), ((rows, lanes), BF, VMEM)], []
    )


def slice_sums(kernel, parts, shapes):
    return call(kernel, "final", parts, [VMEM] * len(parts), [(s, F32, VMEM) for s in shapes], [])


def place_kernel(meta, a, b, c, d, out):
    base = meta.shape[0] - 4
    mine = meta[base + 2] * CORE + meta[base + 3]
    pairs = a.shape[0]
    for i, one in enumerate((a, b, c, d)):
        for p in range(pairs):
            out[(mine ^ i) * pairs + p] = one[p].astype(F32)


def swap_memory(memory, pairs):
    mine = lax.axis_index("mem")
    parts = [lax.dynamic_slice_in_dim(memory, (mine ^ i) * pairs, pairs) for i in range(4)]
    return parts


def return_memory(meta, parts, shape):
    return call(place_kernel, "place", [meta, *parts], [SMEM] + [VMEM] * 4, [(shape, F32, VMEM)], [])[0]


def slots_of(wide):
    rows, cols = wide.shape
    cut = wide.reshape(Z, Y, rows // (Z * Y), X, CORE, cols // (X * CORE))
    return [cut[:, y, :, x, c] for y, x, c in SLOTS]


def wide_of(slots):
    z, rows, cols = slots[0].shape
    cut = jnp.stack(slots).reshape(Y, X, CORE, z, rows, cols)
    return cut.transpose(3, 0, 4, 1, 2, 5).reshape(z * Y * rows, X * CORE * cols)


def gather_any(piece):
    return lax.all_gather(lax.all_gather(piece, "mem", axis=1, tiled=True), "dp", axis=0, tiled=True)


def scatter_any(wide):
    part = lax.psum_scatter(wide.astype(F32), "dp", scatter_dimension=0, tiled=True)
    return lax.psum_scatter(part, "mem", scatter_dimension=1, tiled=True)


def narrow_columns(slots):
    return [jnp.concatenate(jnp.split(one, 4, axis=2), axis=1) for one in slots]


def small_pieces(biases, f_bias, gain, shift, table):
    vectors = jnp.concatenate([biases, gain, shift], axis=0)
    vectors = jnp.pad(vectors, ((0, TABLE - vectors.shape[0]), (0, 0)))
    half = table.shape[0] // 2

    def cut(rows):
        return rows.reshape(rows.shape[0], Z, Y, 64).transpose(1, 2, 0, 3)

    top = jnp.pad(cut(vectors), ((0, 0),) * 3 + ((0, 64),))
    low = jnp.concatenate([cut(table[:half]), cut(table[half:])], axis=3)
    whole = jnp.concatenate([top, low, f_bias.reshape(Z, Y, 2, 128)], axis=2)
    return jnp.pad(whole, ((0, 0), (0, 0), (0, SMALL_ROWS - whole.shape[2]), (0, 0)))


def spread_any(squares, w_in, w_out, smalls):
    wide = [slots_of(gather_any(one)) for one in squares]
    small = small_pieces(*[lax.all_gather(one, "dp", axis=one.ndim - 1, tiled=True) for one in smalls])
    ins = narrow_columns(slots_of(gather_any(w_in)))
    outs = slots_of(gather_any(w_out))
    square_w, feed_w = [], []
    for i, (y, unused, unused2) in enumerate(SLOTS):
        parts = [one[i] for one in wide]
        square_w.append(jnp.concatenate([*parts[:3], small[:, y], *parts[3:]], axis=1))
        feed_w.append(jnp.concatenate([ins[i], outs[i]], axis=1))
    return square_w, feed_w


def two_parts(slots):
    at = dict(zip(SLOTS, slots))
    a = [jnp.stack([at[y, x, c][:, :FIRST_ROWS] for x in range(X)]) for y in range(Y) for c in range(CORE)]
    b = [jnp.stack([at[y, x, c][:, FIRST_ROWS:] for y in range(Y)]) for x in range(X) for c in range(CORE)]
    return a + b


def by_slot(halves):
    return [halves[c][y * X + x] for y, x, c in SLOTS]


def reduce_squares_any(halves, count):
    slots = by_slot(halves)
    return [
        scatter_any(wide_of([one[:, PIECE * i : PIECE * (i + 1)] for one in slots]))
        for i in range(count)
    ]


def reduce_feed_any(halves):
    slots = by_slot(halves)
    ins = [
        jnp.concatenate([one[:, PIECE * j : PIECE * (j + 1)] for j in range(4)], axis=2)
        for one in slots
    ]
    return [scatter_any(wide_of(ins)), scatter_any(wide_of([one[:, 4 * PIECE :] for one in slots]))]


def reduce_small_any(halves, count):
    parts = [halves[0][y * X][:, 4 * PIECE :].astype(F32) for y in range(Y)]
    part = jnp.stack(parts, axis=1).reshape(Z * Y, SMALL_ROWS, 128)
    vectors = part[:, :13, :64].transpose(1, 0, 2).reshape(13, -1)
    half = count // 2
    table = part[:, TABLE : TABLE + half]
    table = jnp.concatenate([table[:, :, :64], table[:, :, 64:]], axis=1)
    rows = jnp.concatenate([vectors, table.transpose(1, 0, 2).reshape(count, -1)], axis=0)
    cut = lax.psum_scatter(lax.psum(rows, "mem"), "dp", scatter_dimension=1, tiled=True)
    f_bias = part[:, TABLE + half : TABLE + half + 2].reshape(-1)
    f_bias = lax.psum_scatter(lax.psum(f_bias, "mem"), "dp", scatter_dimension=0, tiled=True)
    return cut[:7], f_bias, cut[7:10], cut[10:13], cut[13:]


def shards(
    target, memory, time_steps, target_len, source_len, source_off, cotangent,
    self_query, self_key, self_value, self_out, cross_query, cross_key, cross_value, cross_out,
    feed_in, feed_out, biases, feed_bias, norm_gain, norm_shift, step_table,
):
    pairs = target.shape[0]
    steps = step_table.shape[0]
    dp, mem = lax.axis_index("dp"), lax.axis_index("mem")
    quick = lax.axis_size("dp") == Z * Y and lax.axis_size("mem") == X * CORE
    here = [dp // 2, dp % 2, mem // 2, mem % 2] if quick else [0, 0, 0, 0]
    meta = jnp.concatenate(
        [
            target_len,
            time_steps,
            lax.dynamic_slice_in_dim(source_off, mem * pairs, pairs),
            lax.dynamic_slice_in_dim(source_len, mem * pairs, pairs),
            jnp.stack([jnp.asarray(i, jnp.int32) for i in here]),
        ]
    )
    squares = (self_query, self_key, self_value, self_out, cross_query, cross_key, cross_value, cross_out)
    if quick:
        packed = call(
            pack_kernel,
            "pack",
            [*squares, feed_in, feed_out, biases, feed_bias.reshape(2, 128)]
            + [norm_gain, norm_shift, step_table],
            [VMEM] * 15,
            [((i, 128), BF, VMEM) for i in (SELF_ROWS + CROSS_ROWS, FEED_ROWS)],
            [VMEM((SMALL_ROWS, 128), F32)],
            1,
            60 * 2**20,
        )
        packed, memory = fence((packed, memory))
        square_p, feed_p = packed
        mems = swap_memory(memory, pairs)
        mems[2], mems[3] = swap(mems[2], 2), swap(mems[3], 3)
        square_z = sent_z([square_p] * 4)
        square_z, mems, feed_p = fence((square_z, mems, feed_p))
        first, second = z_halves(meta, square_z)
        square_near = [first, swap(first, 2), second, swap(second, 4)]
        feed_z = z_pair(meta, feed_p)
        square_near, feed_z = fence((square_near, feed_z))
        first, second = doubled(square_near)
        square_near = [first, swap(first, 4), second, swap(second, 2)]
        feed_z = (feed_z, swap(feed_z, 16))
        mems[1] = swap(mems[1], 1)
        feed_z = z_quad(meta, *feed_z)
        square_near, feed_z, mems = fence((square_near, feed_z, mems))
        square_w = spread_core(square_near)
        feed_near = spread_near(feed_z)
    else:
        square_w, feed_w = spread_any(
            squares, feed_in, feed_out, (biases, feed_bias, norm_gain, norm_shift, step_table)
        )
        square_w = two_parts(square_w)
        own = lax.all_to_all(memory, "mem", 0, 1, tiled=True)
        mems = jnp.split(own, X * CORE, axis=1)

    far_a, w_a, near_mix, vecs, fbias, held_a, held_b = self_forward(meta, target, square_w, steps)
    far_b, w_b, after_self, after_cross = cross_forward(meta, target, near_mix, mems, vecs, held_b)
    if quick:
        feed_near, after_cross = fence((feed_near, after_cross))
        feed_w = spread_core(feed_near)
    layer_out, gres_c, sums_c, d_fbias, *d_feed = feed(
        meta, after_cross, cotangent, vecs, fbias, feed_w
    )
    if quick:
        d_feed, gres_c = fence((d_feed, gres_c))
        d_feed[1] = swap(d_feed[1], 1)
    gq_b, gk_b, gv_b, sums_b, *d_cross = cross_back(meta, gres_c, far_b, w_b, held_b)
    if quick:
        d_feed, gq_b, d_cross = fence((d_feed, gq_b, d_cross))
        u_feed = core_sums(*d_feed)
        u_feed, gq_b, d_cross = fence((u_feed, gq_b, d_cross))
        n_feed = near_parts(u_feed)
        d_cross[1] = swap(d_cross[1], 1)
    grad_target, *gmem, d_first, d_second = lower_back(
        meta, gres_c, (gq_b, gk_b, gv_b), after_self, far_a, w_a, target, vecs, (sums_b, sums_c), d_fbias, held_b, held_a, steps
    )
    d_self = [d_first, d_second]
    if quick:
        one = self_query.shape
        n_feed, d_cross, d_self, gmem = fence((n_feed, d_cross, d_self, gmem))
        d_self[1] = swap(d_self[1], 1)
        rest = split_sums(*d_cross, *d_self)
        m_feed = chip_sums(meta, n_feed)
        rest, m_feed, gmem = fence((rest, m_feed, gmem))
        rest[1], rest[3] = swap(rest[1], 2), swap(rest[3], 4)
        gmem[1] = swap(gmem[1], 1)
        m_feed[1] = swap(m_feed[1], 16)
        rest, m_feed, gmem = fence((rest, m_feed, gmem))
        rest = turn(rest)
        rest[1], rest[3] = swap(rest[1], 4), swap(rest[3], 2)
        m_feed = halved(*m_feed)
        m_feed[1] = swap(m_feed[1], 8)
        rest, gmem, m_feed = fence((rest, gmem, m_feed))
        m_rest = sent_z(meet(meta, rest))
        g_feed = slice_sums(final_kernel, m_feed, (feed_in.shape, feed_out.shape))
        gmem[2], gmem[3] = swap(gmem[2], 2), swap(gmem[3], 3)
        grad_memory = return_memory(meta, gmem, memory.shape)
        m_rest, grad_memory = fence((m_rest, grad_memory))
        small_shapes = (biases.shape, (2, 128), norm_gain.shape, norm_shift.shape, step_table.shape)
        out = slice_sums(final_small_kernel, m_rest, (one,) * 8 + small_shapes)
        g_cross, g_self, (g_bias, g_fbias, g_gain, g_shift, g_table) = out[:4], out[4:8], out[8:]
        g_fbias = g_fbias.reshape(feed_bias.shape)
    else:
        whole = jnp.concatenate(gmem, axis=1)
        grad_memory = lax.all_to_all(whole, "mem", 1, 0, tiled=True).astype(F32)
        g_feed = reduce_feed_any(d_feed)
        g_cross = reduce_squares_any(d_cross, 4)
        g_self = reduce_squares_any(d_self, 4)
        g_bias, g_fbias, g_gain, g_shift, g_table = reduce_small_any(d_self, steps)
    return (
        layer_out, grad_target, grad_memory, *g_self, *g_cross, *g_feed,
        g_bias, g_fbias, g_gain, g_shift, g_table,
    )


def solution(mesh):
    rows = P(BOTH, None, None)
    piece = P("dp", "mem")
    vector = P(None, "dp")
    mem_rows = P("dp", "mem", None)
    return jax.shard_map(
        shards,
        mesh=mesh,
        in_specs=(rows, mem_rows, P(BOTH), P(BOTH), P("dp"), P("dp"), rows)
        + (piece,) * 10
        + (vector, P("dp"), vector, vector, vector),
        out_specs=(rows, rows, mem_rows) + (piece,) * 10 + (vector, P("dp"), vector, vector, vector),
        check_vma=False,
    )
```

```python
import functools
import math

import jax
import jax.numpy as jnp
from jax import lax
from jax.experimental import pallas as pl
from jax.experimental.pallas import tpu as pltpu
from jax.sharding import PartitionSpec as P

HEADS = 8
DH = 64
GROUP = 4
WIDE = GROUP * DH
EPSILON = 1e-05
SCALE = 1.0 / math.sqrt(DH)
BF = jnp.bfloat16
F32 = jnp.float32
VMEM_LIMIT = 30 * 2**20


def contract(left, right, left_dim, right_dim):
    return lax.dot_general(
        left, right, (((left_dim,), (right_dim,)), ((), ())), preferred_element_type=F32
    )


def mul(left, right):
    return contract(left, right, 1, 0)


def mul_nt(left, right):
    return contract(left, right, 1, 1)


def mul_tn(left, right):
    return contract(left, right, 0, 0)


def normalise(signal):
    centre = signal - jnp.mean(signal, axis=-1, keepdims=True)
    inverse = lax.rsqrt(jnp.mean(centre * centre, axis=-1, keepdims=True) + EPSILON)
    return centre * inverse, inverse


def norm_back(grad, scaled, inverse, gain):
    up = grad * gain
    return inverse * (
        up
        - jnp.mean(up, axis=-1, keepdims=True)
        - scaled * jnp.mean(up * scaled, axis=-1, keepdims=True)
    )


def col_sum(array):
    return jnp.sum(array.astype(F32), axis=0, keepdims=True)


def head_of_lane(rows):
    return lax.broadcasted_iota(jnp.int32, (rows, WIDE), 1) // DH


def stacked(block, lane_head):
    zero = jnp.zeros_like(block)
    return jnp.concatenate([jnp.where(lane_head == h, block, zero) for h in range(GROUP)], axis=0)


def unstacked(result, lane_head, rows):
    picked = result[:rows]
    for h in range(1, GROUP):
        picked = jnp.where(lane_head == h, result[h * rows : (h + 1) * rows], picked)
    return picked


def blocks(pairs):
    return [(p, g, slice(g * WIDE, (g + 1) * WIDE)) for p in range(pairs) for g in range(HEADS // GROUP)]


INPUT, QUERY, KEY, VALUE, MIXED, MEMORY = range(6)


def attend(before, bias_of, kept, w_ref, after):
    pairs, unused, rows, unused2 = kept.shape
    lane_head = head_of_lane(rows)
    every = blocks(pairs)

    def scores_of(p, g, cols):
        return mul_nt(stacked(kept[p, QUERY, :, cols], lane_head), kept[p, KEY, :, cols])

    before(0)
    ahead = scores_of(*every[0])
    for i, (p, g, cols) in enumerate(every):
        scores = ahead + bias_of(p)
        if g == 0 and p + 1 < pairs:
            before(p + 1)
        if i + 1 < len(every):
            ahead = scores_of(*every[i + 1])
        top = jnp.max(scores, axis=-1, keepdims=True)
        raised = jnp.exp(scores - top)
        total = jnp.sum(raised, axis=-1, keepdims=True)
        weights = (raised * (1.0 / total)).astype(BF)
        w_ref[p, g] = weights
        mixed = mul(weights, kept[p, VALUE, :, cols])
        kept[p, MIXED, :, cols] = unstacked(mixed, lane_head, rows).astype(BF)
        if g == HEADS // GROUP - 1:
            after(p)


def attend_back(before, ready, kept, w_ref, grad_ref, gq_ref, gk_ref, gv_ref, after):
    pairs, unused, rows, unused2 = kept.shape
    lane_head = head_of_lane(rows)
    every = blocks(pairs)

    def weight_grads(p, g, cols):
        if g == 0:
            ready(p)
        grads = stacked(grad_ref[p, :, cols], lane_head)
        return grads, mul_nt(grads, kept[p, VALUE, :, cols])

    before(0)
    ahead = weight_grads(*every[0])
    for i, (p, g, cols) in enumerate(every):
        grads, grad_w = ahead
        if g == 0 and p + 1 < pairs:
            before(p + 1)
        if i + 1 < len(every):
            ahead = weight_grads(*every[i + 1])
        weights = w_ref[p, g]
        wide = weights.astype(F32)
        offset = jnp.sum(grad_w * wide, axis=-1, keepdims=True)
        grad_s = (wide * (grad_w - offset)).astype(BF)
        grad_q = unstacked(mul(grad_s, kept[p, KEY, :, cols]), lane_head, rows)
        gq_ref[p, :, cols] = (grad_q * SCALE).astype(BF)
        gk_ref[p, :, cols] = mul_tn(grad_s, stacked(kept[p, QUERY, :, cols], lane_head)).astype(BF)
        gv_ref[p, :, cols] = mul_tn(weights, grads).astype(BF)
        if g == HEADS // GROUP - 1:
            after(p)


def flat(ref):
    value = ref[...]
    return value.reshape(value.shape[0] * value.shape[1], value.shape[2])


Z, Y, X, CORE = 4, 2, 2, 2
SLOTS = [(y, x, c) for y in range(Y) for x in range(X) for c in range(CORE)]
PIECE = 64
FEED_ROWS = 4 * PIECE + 256
SMALL_ROWS = 48
SELF_ROWS = 3 * PIECE + SMALL_ROWS
CROSS_ROWS = 5 * PIECE
FIRST_ROWS = 288
GAIN, SHIFT, TABLE = 7, 10, 16


def places(meta, slot):
    base = meta.shape[0] - 4
    y, x, c = slot
    return y ^ meta[base + 1], (x ^ meta[base + 2]) * CORE + (c ^ meta[base + 3])


def load_copies(meta, sources, held, sems, first=0):
    copies = []
    rows = held.shape[-2]
    for i, slot in enumerate(SLOTS):
        row, panel = places(meta, slot)
        source = sources[i].at[:, pl.ds(first, rows)]
        copies.append(pltpu.make_async_copy(source, held.at[panel, :, row], sems.at[i]))
    return copies


def store_copies(meta, held, targets, sems, first=0):
    copies = []
    rows = targets[0].shape[2]
    for i, slot in enumerate(SLOTS):
        row, panel = places(meta, slot)
        y, x, c = slot
        target = targets[c].at[y * X + x]
        source = held.at[panel, :, row, pl.ds(first, rows)]
        copies.append(pltpu.make_async_copy(source, target, sems.at[i]))
    return copies


def start(copies):
    for copy in copies:
        copy.start()


def wait(copies):
    for copy in copies:
        copy.wait()


def moves(sources, targets, sems):
    return [pltpu.make_async_copy(a, b, sems.at[i]) for i, (a, b) in enumerate(zip(sources, targets))]


def joined(value):
    return value.reshape(-1, value.shape[-1])


def square(held, index):
    span = slice(PIECE * index, PIECE * (index + 1))
    return jnp.concatenate([joined(held[i, :, :, span]) for i in range(X * CORE)], axis=1)


def keep(held, index, value):
    span = slice(PIECE * index, PIECE * (index + 1))
    for i in range(X * CORE):
        part = value[:, i * 128 : (i + 1) * 128].astype(BF)
        held[i, :, :, span] = part.reshape(Z, Y, PIECE, 128)


def all_rows(kept, index):
    value = kept[:, index]
    return value.reshape(value.shape[0] * value.shape[1], value.shape[2])


def each(source, target, sems):
    count = source.shape[0]
    return moves([source.at[p] for p in range(count)], [target.at[p] for p in range(count)], sems)


def self_forward_kernel(meta, target, *refs):
    pieces, refs = refs[:8], refs[8:]
    far, far_w, near_mix, vecs, fbias, held, held_cross = refs[:7]
    kept, w, small, sems, cross_sems, small_sems, far_sems, w_sems = refs[7:]
    base = meta.shape[0] - 4
    small_loads = [
        pltpu.make_async_copy(
            pieces[y * CORE].at[0, :, pl.ds(3 * PIECE, SMALL_ROWS)], small.at[:, y ^ meta[base + 1]], small_sems.at[y]
        )
        for y in range(Y)
    ]
    start(small_loads)
    loads, cross_loads = [], []
    edge = FIRST_ROWS - SELF_ROWS
    for i, slot in enumerate(SLOTS):
        y, x, c = slot
        row, panel = places(meta, slot)
        a_part, b_part = pieces[y * CORE + c].at[x], pieces[Y * CORE + x * CORE + c].at[y]
        own, cross = held.at[panel, :, row], held_cross.at[panel, :, row]
        loads.append(pltpu.make_async_copy(a_part.at[:, pl.ds(0, 3 * PIECE)], own, sems.at[i]))
        cross_loads += moves(
            (a_part.at[:, pl.ds(SELF_ROWS, edge)], b_part),
            (cross.at[:, pl.ds(0, edge)], cross.at[:, pl.ds(edge, CROSS_ROWS - edge)]),
            cross_sems.at[i],
        )
    start(loads)
    start(cross_loads)
    copies, w_copies = each(kept, far, far_sems), each(w, far_w, w_sems)
    pairs, length, width = target.shape
    wait(small_loads)
    every = [small[z, y].astype(F32) for z in range(Z) for y in range(Y)]
    steps = (vecs.shape[0] - TABLE) // 2
    vecs[:TABLE] = jnp.concatenate([one[:TABLE, :64] for one in every], axis=1)
    for i in range(2):
        part = [one[TABLE : TABLE + steps, 64 * i : 64 * (i + 1)] for one in every]
        vecs[TABLE + i * steps : TABLE + (i + 1) * steps] = jnp.concatenate(part, axis=1)
    for d, one in enumerate(every):
        for i in range(2):
            at = TABLE + steps + i
            fbias[:, d * 256 + i * 128 : d * 256 + (i + 1) * 128] = one[at : at + 1]

    def before(p):
        emb = target[p].astype(F32) + vecs[pl.ds(TABLE + meta[pairs + p], 1), :]
        scaled, unused = normalise(emb)
        x = (scaled * vecs[GAIN : GAIN + 1] + vecs[SHIFT : SHIFT + 1]).astype(BF)
        kept[p, INPUT] = x
        if p == 0:
            wait(loads)
        kept[p, QUERY] = (mul(x, square(held, 0)) + vecs[0:1]).astype(BF) * SCALE
        kept[p, KEY] = mul(x, square(held, 1)).astype(BF)
        kept[p, VALUE] = (mul(x, square(held, 2)) + vecs[1:2]).astype(BF)

    def bias_of(p):
        spot = lax.broadcasted_iota(jnp.int32, (1, length), 1)
        return jnp.where(spot < meta[p], 0.0, -1e30)

    def after(p):
        near_mix[p] = kept[p, MIXED]
        copies[p].start()
        w_copies[p].start()

    attend(before, bias_of, kept, w, after)
    wait(cross_loads)
    wait(copies)
    wait(w_copies)


def cross_forward_kernel(meta, target, mix_a, mem_0, mem_1, mem_2, mem_3, vecs, held, *refs):
    far, w, far_after, after_cross = refs[:4]
    kept, after_self, mem_sems, far_sems, after_sems = refs[4:]
    pairs, length, width = target.shape
    source = kept.shape[2]
    base = meta.shape[0] - 4
    mine = meta[base + 2] * CORE + meta[base + 3]
    part = source // (X * CORE)
    mem_loads = [
        pltpu.make_async_copy(
            one,
            kept.at[:, MEMORY, pl.ds(pl.multiple_of((mine ^ i) * part, part), part), :],
            mem_sems.at[i],
        )
        for i, one in enumerate((mem_0, mem_1, mem_2, mem_3))
    ]
    start(mem_loads)
    copies = each(kept, far, far_sems)
    after_copies = each(after_self, far_after, after_sems)

    def before(p):
        row = vecs[pl.ds(TABLE + meta[pairs + p], 1), :]
        total = target[p].astype(F32) + row + mul(mix_a[p], square(held, 0)) + vecs[2:3]
        after_self[p] = total
        after_copies[p].start()
        scaled, unused = normalise(total)
        x = (scaled * vecs[GAIN + 1 : GAIN + 2] + vecs[SHIFT + 1 : SHIFT + 2]).astype(BF)
        kept[p, INPUT] = x
        kept[p, QUERY] = (mul(x, square(held, 1)) + vecs[3:4]).astype(BF) * SCALE
        if p == 0:
            wait(mem_loads)
        m = kept[p, MEMORY]
        kept[p, KEY] = mul(m, square(held, 2)).astype(BF)
        kept[p, VALUE] = (mul(m, square(held, 3)) + vecs[4:5]).astype(BF)

    def bias_of(p):
        spot = lax.broadcasted_iota(jnp.int32, (1, source), 1)
        begin = meta[2 * pairs + p]
        end = begin + meta[3 * pairs + p]
        return jnp.where((spot >= begin) & (spot < end), 0.0, -1e30)

    def after(p):
        copies[p].start()
        after_cross[p] = after_self[p] + mul(kept[p, MIXED], square(held, 4)) + vecs[5:6]

    attend(before, bias_of, kept, w, after)
    wait(after_copies)
    wait(copies)


def gelu_parts(value):
    size = jnp.abs(value) * math.sqrt(0.5)
    t = 1.0 / (1.0 + 0.3275911 * size)
    bell = jnp.exp(-0.5 * value * value)
    tail = (
        t
        * (
            0.5 * 0.254829592
            + t
            * (
                0.5 * -0.284496736
                + t * (0.5 * 1.421413741 + t * (0.5 * -1.453152027 + t * (0.5 * 1.061405429)))
            )
        )
        * bell
    )
    below = jnp.where(value < 0, tail, 1.0 - tail)
    slope = below + value * bell * (1.0 / math.sqrt(2.0 * math.pi))
    return value * below, slope


def feed_kernel(meta, after_cross, cot, vecs, feed_bias, *refs):
    pieces, refs = refs[:8], refs[8:]
    far_out, gres, sums, dbias = refs[:4]
    targets, refs = refs[4:6], refs[6:]
    held, kept, x_c, act, grad_pre, layer_out, sems, out_sems, far_sems = refs
    copies = moves((layer_out,), (far_out,), far_sems)
    loads = load_copies(meta, pieces, held, sems)
    start(loads)
    stores = store_copies(meta, kept, targets, out_sems)
    shape = after_cross.shape
    signal = flat(after_cross)
    scaled, inverse = normalise(signal)
    gain = vecs[GAIN + 2 : GAIN + 3]
    x_c[...] = (scaled * gain + vecs[SHIFT + 2 : SHIFT + 3]).astype(BF)
    wait(loads)
    c = flat(cot)
    x = x_c[...]
    w_in = [
        jnp.concatenate([joined(held[j, :, :, PIECE * i : PIECE * (i + 1)]) for i in range(4)], axis=1)
        for j in range(4)
    ]
    w_out = [jnp.concatenate([joined(held[i, j, :, 4 * PIECE :]) for i in range(4)], axis=1) for j in range(4)]
    w_in = jnp.concatenate(w_in, axis=1)
    w_out = jnp.concatenate(w_out, axis=0)
    block, span = 256, 256
    tiles = [
        (slice(r, r + span), slice(j, j + block))
        for j in range(0, w_in.shape[1], block)
        for r in range(0, x.shape[0], span)
    ]

    def first(rows, cols):
        return mul(x[rows], w_in[:, cols]), mul_nt(c[rows], w_out[cols])

    ready = [first(*tile) for tile in tiles[:1]]
    for j, (rows, cols) in enumerate(tiles):
        if j + 1 < len(tiles):
            ready.append(first(*tiles[j + 1]))
        pre, grad_act = ready[j]
        ready[j] = None
        value, slope = gelu_parts(pre + feed_bias[:, cols])
        act[rows, cols] = value.astype(BF)
        grad = (grad_act * slope).astype(BF)
        grad_pre[rows, cols] = grad
        if rows.start == 0:
            total = col_sum(grad)
        else:
            total = total + col_sum(grad)
        if rows.stop == x.shape[0]:
            dbias[:, cols] = total
    for j in range(4):
        cols = slice(j * 512, (j + 1) * 512)
        d_out = mul_tn(act[:, cols], c)
        for i in range(4):
            part = d_out[:, i * 128 : (i + 1) * 128].astype(BF)
            kept[i, j, :, 4 * PIECE :] = part.reshape(Y, 256, 128)
        d_in = mul_tn(x, grad_pre[:, cols])
        for i in range(4):
            part = d_in[:, i * 128 : (i + 1) * 128].astype(BF)
            kept[j, :, :, PIECE * i : PIECE * (i + 1)] = part.reshape(Z, Y, PIECE, 128)
    start(stores)
    layer_out[...] = (signal + mul(act[...], w_out) + vecs[6:7]).astype(BF).reshape(shape)
    start(copies)
    grad = mul_nt(grad_pre[...], w_in)
    wide_cot = flat(cot).astype(F32)
    sums[0:1] = col_sum(wide_cot)
    sums[1:2] = col_sum(grad * scaled)
    sums[2:3] = col_sum(grad)
    gres[...] = (wide_cot + norm_back(grad, scaled, inverse, gain)).reshape(shape)
    wait(stores)
    wait(copies)


def cross_back_kernel(meta, gres, far, w, held, *refs):
    gq, gk, gv, sums = refs[:4]
    targets, (kept, gmix, grads, out_sems, far_sems) = refs[4:6], refs[6:]
    copies = each(far, kept, far_sems)
    start(copies)
    stores = store_copies(meta, grads, targets, out_sems)

    def before(p):
        gmix[p] = mul_nt(gres[p].astype(BF), square(held, 4)).astype(BF)

    attend_back(before, lambda p: copies[p].wait(), kept, w, gmix, gq, gk, gv, lambda p: None)
    grad = flat(gres).astype(BF)
    m = all_rows(kept, MEMORY)
    keep(grads, 3, mul_tn(all_rows(kept, MIXED), grad))
    keep(grads, 0, mul_tn(all_rows(kept, INPUT), flat(gq)))
    keep(grads, 1, mul_tn(m, flat(gk)))
    keep(grads, 2, mul_tn(m, flat(gv)))
    start(stores)
    sums[0:1] = col_sum(grad)
    sums[1:2] = col_sum(flat(gq))
    sums[2:3] = col_sum(flat(gv))
    wait(stores)


def lower_back_kernel(
    meta, gres, grad_q, grad_k, grad_v, far_after, far, far_w, target, vecs, sums_b, sums_c, dbias, held, held_a, *refs
):
    far_target, gmem_0, gmem_1, gmem_2, gmem_3 = refs[:5]
    targets, refs = refs[5:7], refs[7:]
    kept, w, after_self, gres_a, gmix, gmem, gq, gk, gv, gtarget, gtable, grads = refs[:12]
    mem_sems, far_sems, w_sems, after_sems, target_sems, out_sems = refs[12:]
    copies, w_copies = each(far, kept, far_sems), each(far_w, w, w_sems)
    after_copies = each(far_after, after_self, after_sems)
    for group in zip(after_copies, copies, w_copies):
        start(group)
    target_copies = each(gtarget, far_target, target_sems)
    stores = store_copies(meta, grads, targets, out_sems)
    base = meta.shape[0] - 4
    mine = meta[base + 2] * CORE + meta[base + 3]
    part = gmem.shape[1] // (X * CORE)
    mem_stores = [
        pltpu.make_async_copy(
            gmem.at[:, pl.ds(pl.multiple_of((mine ^ i) * part, part), part), :], one, mem_sems.at[i]
        )
        for i, one in enumerate((gmem_0, gmem_1, gmem_2, gmem_3))
    ]
    pairs, length, width = gres.shape
    totals = [0.0] * 5
    gtable[...] = jnp.zeros_like(gtable)

    def count(first, *parts):
        for i, one in enumerate(parts):
            totals[first + i] = totals[first + i] + col_sum(one)

    def before(p):
        grad_m = mul_nt(grad_k[p], square(held, 2)) + mul_nt(grad_v[p], square(held, 3))
        gmem[p] = grad_m.astype(BF)
        grad_in = mul_nt(grad_q[p], square(held, 1))
        after_copies[p].wait()
        scaled, inverse = normalise(after_self[p])
        total = gres[p] + norm_back(grad_in, scaled, inverse, vecs[GAIN + 1 : GAIN + 2])
        gres_a[p] = total
        grad_a = total.astype(BF)
        gmix[p] = mul_nt(grad_a, square(held, 0)).astype(BF)
        count(0, grad_in * scaled, grad_in, grad_a)
        if p + 1 == pairs:
            start(mem_stores)

    def ready(p):
        copies[p].wait()
        w_copies[p].wait()

    def after(p):
        grad_in = (
            mul_nt(gq[p], square(held_a, 0)) + mul_nt(gk[p], square(held_a, 1)) + mul_nt(gv[p], square(held_a, 2))
        )
        row = pl.ds(TABLE + meta[pairs + p], 1)
        scaled, inverse = normalise(target[p].astype(F32) + vecs[row, :])
        count(3, grad_in * scaled, grad_in)
        total = gres_a[p] + norm_back(grad_in, scaled, inverse, vecs[GAIN : GAIN + 1])
        gtarget[p] = total
        target_copies[p].start()
        gtable[pl.ds(meta[pairs + p], 1), :] += col_sum(total)

    attend_back(before, ready, kept, w, gmix, gq, gk, gv, after)
    x = all_rows(kept, INPUT)
    keep(grads, 3, mul_tn(all_rows(kept, MIXED), flat(gres_a).astype(BF)))
    for i, one in enumerate((gq, gk, gv)):
        keep(grads, i, mul_tn(x, flat(one)))
    rows = [col_sum(flat(gq)), col_sum(flat(gv)), totals[2], sums_b[1:2], sums_b[2:3], sums_b[0:1], sums_c[0:1]]
    rows += [totals[3], totals[0], sums_c[1:2], totals[4], totals[1], sums_c[2:3]]
    vectors = jnp.concatenate(rows + [jnp.zeros((TABLE - len(rows), width), F32)], axis=0)
    steps = gtable.shape[0] // 2
    for d in range(Z * Y):
        lanes = slice(d * 64, (d + 1) * 64)
        top = jnp.concatenate([vectors[:, lanes], jnp.zeros((TABLE, 64), F32)], axis=1)
        low = jnp.concatenate([gtable[:steps, lanes], gtable[steps:, lanes]], axis=1)
        tail = [dbias[:, d * 256 + i * 128 : d * 256 + (i + 1) * 128] for i in range(2)]
        fill = jnp.zeros((SMALL_ROWS - TABLE - steps - 2, 128), F32)
        small = jnp.concatenate([top, low, *tail, fill], axis=0).astype(BF)
        for i in range(X * CORE):
            grads[i, d // Y, d % Y, 4 * PIECE :] = small
    start(stores)
    wait(mem_stores)
    wait(target_copies)
    wait(stores)


HBM = pl.ANY
FAR = pltpu.HBM
VMEM = pltpu.VMEM
SMEM = pltpu.SMEM


def call(kernel, name, args, spaces, outs, scratch, micros=1, limit=VMEM_LIMIT):
    cost = pl.CostEstimate(flops=int(micros * 10**9), bytes_accessed=int(micros * 3 * 10**6), transcendentals=0)
    function = pl.pallas_call(
        kernel,
        out_shape=[FAR(s, d) if m is FAR else jax.ShapeDtypeStruct(s, d) for s, d, m in outs],
        in_specs=[pl.BlockSpec(memory_space=m) for m in spaces],
        out_specs=[pl.BlockSpec(memory_space=m) for unused, unused2, m in outs],
        scratch_shapes=scratch,
        compiler_params=pltpu.CompilerParams(vmem_limit_bytes=limit),
        cost_estimate=cost,
        name=name,
    )
    return list(function(*[pltpu.with_memory_space_constraint(a, m) if m is FAR else a for a, m in zip(args, spaces)]))


def held_shape(rows):
    return (X * CORE, Z, Y, rows, 128)


def held_like(rows):
    return VMEM(held_shape(rows), BF)


def kept_like(slots):
    return VMEM((X * CORE, slots[1], Y, *slots[2:]), BF)


def sems(*shape):
    return pltpu.SemaphoreType.DMA(shape)


def weights_shape(shape, source):
    return (shape[0], HEADS // GROUP, GROUP * shape[1], source)


def slot_shape(count, extra=0):
    return (Y * X, Z, count * PIECE + extra, 128)


def kept_shape(shape, count):
    return (shape[0], count, *shape[1:])


def self_forward(meta, target, pieces, steps):
    shape = target.shape
    kept, w_shape = kept_shape(shape, MIXED + 1), weights_shape(shape, shape[1])
    return call(
        self_forward_kernel,
        "self_forward",
        [meta, target, *pieces],
        [SMEM, VMEM] + [HBM] * 8,
        [(kept, BF, FAR), (w_shape, BF, FAR), (shape, BF, VMEM)]
        + [((TABLE + steps, shape[2]), F32, VMEM), ((1, 4 * shape[2]), F32, VMEM)]
        + [(held_shape(3 * PIECE), BF, VMEM), (held_shape(CROSS_ROWS), BF, VMEM)],
        [VMEM(kept, BF), VMEM(w_shape, BF), VMEM((Z, Y, SMALL_ROWS, 128), BF)]
        + [sems(8), sems(8, 2), sems(2), sems(shape[0]), sems(shape[0])],
        0.1,
    )


def cross_forward(meta, target, mix_a, mems, vecs, held):
    shape = target.shape
    kept, w_shape = kept_shape(shape, MEMORY + 1), weights_shape(shape, shape[1])
    return call(
        cross_forward_kernel,
        "cross_forward",
        [meta, target, mix_a, *mems, vecs, held],
        [SMEM] + [VMEM] * 2 + [HBM] * 4 + [VMEM] * 2,
        [(kept, BF, FAR), (w_shape, BF, VMEM), (shape, F32, FAR), (shape, F32, VMEM)],
        [VMEM(kept, BF), VMEM(shape, F32), sems(4), sems(shape[0]), sems(shape[0])],
        0.1,
    )


def feed(meta, after_cross, cot, vecs, feed_bias, pieces):
    shape = after_cross.shape
    tokens, width = shape[0] * shape[1], shape[2]
    return call(
        feed_kernel,
        "feed",
        [meta, after_cross, cot, vecs, feed_bias, *pieces],
        [SMEM] + [VMEM] * 4 + [HBM] * 8,
        [(shape, BF, FAR), (shape, F32, VMEM), ((3, width), F32, VMEM), (feed_bias.shape, F32, VMEM)]
        + [(slot_shape(4, 256), BF, HBM)] * 2,
        [held_like(FEED_ROWS)] * 2
        + [VMEM((tokens, width), BF)] + [VMEM((tokens, feed_bias.shape[1]), BF)] * 2
        + [VMEM(shape, BF)]
        + [sems(8), sems(8), sems(1)],
        26,
        36 * 2**20,
    )


def cross_back(meta, gres, far, w, held):
    shape = gres.shape
    return call(
        cross_back_kernel,
        "cross_back",
        [meta, gres, far, w, held],
        [SMEM, VMEM, FAR, VMEM, VMEM],
        [(shape, BF, VMEM)] * 3 + [((3, shape[2]), F32, VMEM)] + [(slot_shape(4), BF, HBM)] * 2,
        [VMEM(far.shape, BF), VMEM(shape, BF), kept_like(slot_shape(4)), sems(8), sems(shape[0])],
        15,
    )


def lower_back(meta, gres, grads, after_self, far, far_w, target, vecs, sums, dbias, held, held_a, steps):
    shape = gres.shape
    part = (shape[0], shape[1] // (X * CORE), shape[2])
    slots = slot_shape(4, SMALL_ROWS)
    return call(
        lower_back_kernel,
        "lower_back",
        [meta, gres, *grads, after_self, far, far_w, target, vecs, *sums, dbias, held, held_a],
        [SMEM] + [VMEM] * 4 + [FAR] * 3 + [VMEM] * 7,
        [(shape, F32, FAR)] + [(part, BF, HBM)] * 4 + [(slots, BF, HBM)] * 2,
        [VMEM(far.shape, BF), VMEM(far_w.shape, BF), VMEM(shape, F32), VMEM(shape, F32)]
        + [VMEM(shape, BF)] * 5 + [VMEM(shape, F32), VMEM((steps, shape[2]), F32), kept_like(slots)]
        + [sems(4)] + [sems(shape[0])] * 4 + [sems(8)],
        20,
        38 * 2**20,
    )


BOTH = ("dp", "mem")


def swap(array, mask):
    count = lax.axis_size("dp") * lax.axis_size("mem")
    return lax.ppermute(array, BOTH, [(i, i ^ mask) for i in range(count)])


def pack_kernel(*refs):
    squares, (w_in, w_out, biases, f_bias, gain, shift, table) = refs[:8], refs[8:15]
    square_out, feed_out, stage = refs[15:]
    for i, ref in enumerate(squares):
        if i < 3:
            square_out[PIECE * i : PIECE * (i + 1)] = ref[...]
        else:
            square_out[SELF_ROWS + PIECE * (i - 3) : SELF_ROWS + PIECE * (i - 2)] = ref[...]
    for i in range(4):
        feed_out[PIECE * i : PIECE * (i + 1)] = w_in[:, 128 * i : 128 * (i + 1)]
    feed_out[4 * PIECE :] = w_out[...]
    stage[...] = jnp.zeros_like(stage)
    stage[0:7, :64] = biases[...].astype(F32)
    stage[GAIN : GAIN + 3, :64] = gain[...].astype(F32)
    stage[SHIFT : SHIFT + 3, :64] = shift[...].astype(F32)
    rows = table[...].astype(F32)
    half = rows.shape[0] // 2
    stage[TABLE : TABLE + half] = jnp.concatenate([rows[:half], rows[half:]], axis=1)
    stage[TABLE + half : TABLE + half + 2] = f_bias[...].astype(F32)
    square_out[3 * PIECE : SELF_ROWS] = stage[...].astype(BF)


def pair_kernel(meta, mine, other, out):
    low = meta[meta.shape[0] - 4] % 2
    out[low] = mine[...]
    out[1 - low] = other[...]


def quad_kernel(meta, mine, other, out):
    high = meta[meta.shape[0] - 4] // 2
    for i in range(2):
        out[2 * high + i] = mine[i]
        out[2 * (1 - high) + i] = other[i]


def quarter_kernel(meta, a, b, c, d, first, second):
    mine = meta[meta.shape[0] - 4]
    for i, one in enumerate((a, b, c, d)):
        first[mine ^ i] = one[:FIRST_ROWS]
        second[mine ^ i] = one[FIRST_ROWS:]


def double_kernel(a, a_other, b, b_other, a_out, b_out):
    for out, pair in ((a_out, (a, a_other)), (b_out, (b, b_other))):
        for i, one in enumerate(pair):
            out[i] = one[...]


def doubled(parts):
    outs = [((2, *one.shape), BF, VMEM) for one in parts[::2]]
    return call(double_kernel, "double", parts, [VMEM] * 4, outs, [])


def sent_z(parts):
    return [parts[0], swap(parts[1], 8), swap(parts[2], 16), swap(parts[3], 24)]


def z_halves(meta, parts):
    rows, lanes = parts[0].shape
    return call(
        quarter_kernel,
        "quarter",
        [meta, *parts],
        [SMEM] + [VMEM] * 4,
        [((Z, i, lanes), BF, VMEM) for i in (FIRST_ROWS, rows - FIRST_ROWS)],
        [],
    )


def z_pair(meta, packed):
    return call(
        pair_kernel,
        "pair",
        [meta, packed, swap(packed, 8)],
        [SMEM, VMEM, VMEM],
        [((2, *packed.shape), BF, VMEM)],
        [],
    )[0]


def z_quad(meta, pair, other):
    return call(
        quad_kernel,
        "quad",
        [meta, pair, other],
        [SMEM, VMEM, VMEM],
        [((Z, *pair.shape[1:]), BF, VMEM)],
        [],
    )[0]


fence = lax.optimization_barrier


def spread_near(along_z):
    return [along_z, swap(along_z, 2), swap(along_z, 4), swap(along_z, 6)]


def spread_core(near):
    out = []
    for one in near:
        out += [one, swap(one, 1)]
    return out


def merge_kernel(meta, a, b, c, d, own, sent):
    mine = meta[meta.shape[0] - 4]

    def total(z):
        return (a[z].astype(F32) + b[z].astype(F32)) + (c[z].astype(F32) + d[z].astype(F32))

    for i in range(2):
        own[i] = total(mine ^ i)
        sent[i] = total(mine ^ (2 + i)).astype(BF)


def halve_kernel(pair, other, own, sent):
    own[...] = pair[0] + other[0].astype(F32)
    sent[...] = (pair[1] + other[1].astype(F32)).astype(BF)


def final_parts(refs, outs):
    def total(span):
        value = refs[0][span]
        for ref in refs[1:]:
            value = value + ref[span].astype(F32)
        return value

    at = 0
    for out in outs:
        rows = out.shape[0]
        for i in range(out.shape[1] // 128):
            out[:, 128 * i : 128 * (i + 1)] = total(slice(at, at + rows))
            at += rows
    return total, at


def final_kernel(*refs):
    final_parts(refs[:2], refs[2:])


def final_small_kernel(*refs):
    outs, (biases, f_bias, gain, shift, table) = refs[4:12], refs[12:]
    total, at = final_parts(refs[:4], outs)
    part = total(slice(at, at + SMALL_ROWS))
    biases[...] = part[0:7, :64]
    gain[...] = part[GAIN : GAIN + 3, :64]
    shift[...] = part[SHIFT : SHIFT + 3, :64]
    half = table.shape[0] // 2
    table[:half] = part[TABLE : TABLE + half, :64]
    table[half:] = part[TABLE : TABLE + half, 64:]
    f_bias[...] = part[TABLE + half : TABLE + half + 2]


def add(left, right):
    return (left.astype(F32) + right.astype(F32)).astype(BF)


def core_sums(own, other):
    return [add(own[i], other[i]) for i in range(Y * X)]


def split_kernel(*refs):
    parts, (a_own, a_sent, b_own, b_sent) = refs[:-4], refs[-4:]
    at = 0
    for own, other in zip(parts[::2], parts[1::2]):
        rows = own.shape[2]
        cut = min(max(FIRST_ROWS - at, 0), rows)
        for i in range(Y * X):
            a_out = (a_own, a_sent)[i % X].at[i // X]
            b_out = (b_own, b_sent)[i // X].at[i % X]
            if cut > 0:
                a_out[:, at : at + cut] = add(own[i, :, :cut], other[i, :, :cut])
            if cut < rows:
                first = at + cut - FIRST_ROWS
                b_out[:, first : first + rows - cut] = add(own[i, :, cut:], other[i, :, cut:])
        at += rows


def split_sums(*parts):
    rows = sum(one.shape[2] for one in parts[::2])
    a_shape, b_shape = (2, Z, FIRST_ROWS, 128), (2, Z, rows - FIRST_ROWS, 128)
    return call(
        split_kernel,
        "split",
        list(parts),
        [VMEM] * len(parts),
        [(a_shape, BF, VMEM)] * 2 + [(b_shape, BF, VMEM)] * 2,
        [],
    )


def turn_kernel(a_own, a_other, b_own, b_other, a_kept, a_sent, b_kept, b_sent):
    for own, other, kept, sent in ((a_own, a_other, a_kept, a_sent), (b_own, b_other, b_kept, b_sent)):
        kept[...] = own[0].astype(F32) + other[0].astype(F32)
        sent[...] = add(own[1], other[1])


def turn(parts):
    a_shape, b_shape = parts[0].shape[1:], parts[2].shape[1:]
    return call(
        turn_kernel,
        "turn",
        parts,
        [VMEM] * 4,
        [(a_shape, F32, VMEM), (a_shape, BF, VMEM), (b_shape, F32, VMEM), (b_shape, BF, VMEM)],
        [],
    )


def meet_kernel(meta, a_kept, a_other, b_kept, b_other, *outs):
    mine = meta[meta.shape[0] - 4]
    rows = a_kept.shape[1]
    for i, out in enumerate(outs):
        z = mine ^ i
        out[:rows] = (a_kept[z] + a_other[z].astype(F32)).astype(out.dtype)
        out[rows:] = (b_kept[z] + b_other[z].astype(F32)).astype(out.dtype)


def meet(meta, parts):
    out = (parts[0].shape[1] + parts[2].shape[1], 128)
    return call(
        meet_kernel,
        "meet",
        [meta, *parts],
        [SMEM] + [VMEM] * 4,
        [(out, F32, VMEM)] + [(out, BF, VMEM)] * 3,
        [],
    )


def near_parts(pairs):
    return [pairs[0], swap(pairs[1], 2), swap(pairs[2], 4), swap(pairs[3], 6)]


def chip_sums(meta, near):
    unused, rows, lanes = near[0].shape
    return call(
        merge_kernel,
        "merge",
        [meta, *near],
        [SMEM] + [VMEM] * 4,
        [((2, rows, lanes), F32, VMEM), ((2, rows, lanes), BF, VMEM)],
        [],
    )


def halved(pair, other):
    rows, lanes = pair.shape[1:]
    return call(
        halve_kernel, "halve", [pair, other], [VMEM] * 2, [((rows, lanes), F32, VMEM), ((rows, lanes), BF, VMEM)], []
    )


def slice_sums(kernel, parts, shapes):
    return call(kernel, "final", parts, [VMEM] * len(parts), [(s, F32, VMEM) for s in shapes], [])


def place_kernel(meta, a, b, c, d, out):
    base = meta.shape[0] - 4
    mine = meta[base + 2] * CORE + meta[base + 3]
    pairs = a.shape[0]
    for i, one in enumerate((a, b, c, d)):
        for p in range(pairs):
            out[(mine ^ i) * pairs + p] = one[p].astype(F32)


def swap_memory(memory, pairs):
    mine = lax.axis_index("mem")
    parts = [lax.dynamic_slice_in_dim(memory, (mine ^ i) * pairs, pairs) for i in range(4)]
    return parts


def return_memory(meta, parts, shape):
    return call(place_kernel, "place", [meta, *parts], [SMEM] + [VMEM] * 4, [(shape, F32, VMEM)], [])[0]


def slots_of(wide):
    rows, cols = wide.shape
    cut = wide.reshape(Z, Y, rows // (Z * Y), X, CORE, cols // (X * CORE))
    return [cut[:, y, :, x, c] for y, x, c in SLOTS]


def wide_of(slots):
    z, rows, cols = slots[0].shape
    cut = jnp.stack(slots).reshape(Y, X, CORE, z, rows, cols)
    return cut.transpose(3, 0, 4, 1, 2, 5).reshape(z * Y * rows, X * CORE * cols)


def gather_any(piece):
    return lax.all_gather(lax.all_gather(piece, "mem", axis=1, tiled=True), "dp", axis=0, tiled=True)


def scatter_any(wide):
    part = lax.psum_scatter(wide.astype(F32), "dp", scatter_dimension=0, tiled=True)
    return lax.psum_scatter(part, "mem", scatter_dimension=1, tiled=True)


def narrow_columns(slots):
    return [jnp.concatenate(jnp.split(one, 4, axis=2), axis=1) for one in slots]


def small_pieces(biases, f_bias, gain, shift, table):
    vectors = jnp.concatenate([biases, gain, shift], axis=0)
    vectors = jnp.pad(vectors, ((0, TABLE - vectors.shape[0]), (0, 0)))
    half = table.shape[0] // 2

    def cut(rows):
        return rows.reshape(rows.shape[0], Z, Y, 64).transpose(1, 2, 0, 3)

    top = jnp.pad(cut(vectors), ((0, 0),) * 3 + ((0, 64),))
    low = jnp.concatenate([cut(table[:half]), cut(table[half:])], axis=3)
    whole = jnp.concatenate([top, low, f_bias.reshape(Z, Y, 2, 128)], axis=2)
    return jnp.pad(whole, ((0, 0), (0, 0), (0, SMALL_ROWS - whole.shape[2]), (0, 0)))


def spread_any(squares, w_in, w_out, smalls):
    wide = [slots_of(gather_any(one)) for one in squares]
    small = small_pieces(*[lax.all_gather(one, "dp", axis=one.ndim - 1, tiled=True) for one in smalls])
    ins = narrow_columns(slots_of(gather_any(w_in)))
    outs = slots_of(gather_any(w_out))
    square_w, feed_w = [], []
    for i, (y, unused, unused2) in enumerate(SLOTS):
        parts = [one[i] for one in wide]
        square_w.append(jnp.concatenate([*parts[:3], small[:, y], *parts[3:]], axis=1))
        feed_w.append(jnp.concatenate([ins[i], outs[i]], axis=1))
    return square_w, feed_w


def two_parts(slots):
    at = dict(zip(SLOTS, slots))
    a = [jnp.stack([at[y, x, c][:, :FIRST_ROWS] for x in range(X)]) for y in range(Y) for c in range(CORE)]
    b = [jnp.stack([at[y, x, c][:, FIRST_ROWS:] for y in range(Y)]) for x in range(X) for c in range(CORE)]
    return a + b


def by_slot(halves):
    return [halves[c][y * X + x] for y, x, c in SLOTS]


def reduce_squares_any(halves, count):
    slots = by_slot(halves)
    return [
        scatter_any(wide_of([one[:, PIECE * i : PIECE * (i + 1)] for one in slots]))
        for i in range(count)
    ]


def reduce_feed_any(halves):
    slots = by_slot(halves)
    ins = [
        jnp.concatenate([one[:, PIECE * j : PIECE * (j + 1)] for j in range(4)], axis=2)
        for one in slots
    ]
    return [scatter_any(wide_of(ins)), scatter_any(wide_of([one[:, 4 * PIECE :] for one in slots]))]


def reduce_small_any(halves, count):
    parts = [halves[0][y * X][:, 4 * PIECE :].astype(F32) for y in range(Y)]
    part = jnp.stack(parts, axis=1).reshape(Z * Y, SMALL_ROWS, 128)
    vectors = part[:, :13, :64].transpose(1, 0, 2).reshape(13, -1)
    half = count // 2
    table = part[:, TABLE : TABLE + half]
    table = jnp.concatenate([table[:, :, :64], table[:, :, 64:]], axis=1)
    rows = jnp.concatenate([vectors, table.transpose(1, 0, 2).reshape(count, -1)], axis=0)
    cut = lax.psum_scatter(lax.psum(rows, "mem"), "dp", scatter_dimension=1, tiled=True)
    f_bias = part[:, TABLE + half : TABLE + half + 2].reshape(-1)
    f_bias = lax.psum_scatter(lax.psum(f_bias, "mem"), "dp", scatter_dimension=0, tiled=True)
    return cut[:7], f_bias, cut[7:10], cut[10:13], cut[13:]


def shards(
    target, memory, time_steps, target_len, source_len, source_off, cotangent,
    self_query, self_key, self_value, self_out, cross_query, cross_key, cross_value, cross_out,
    feed_in, feed_out, biases, feed_bias, norm_gain, norm_shift, step_table,
):
    pairs = target.shape[0]
    steps = step_table.shape[0]
    dp, mem = lax.axis_index("dp"), lax.axis_index("mem")
    quick = lax.axis_size("dp") == Z * Y and lax.axis_size("mem") == X * CORE
    here = [dp // 2, dp % 2, mem // 2, mem % 2] if quick else [0, 0, 0, 0]
    meta = jnp.concatenate(
        [
            target_len,
            time_steps,
            lax.dynamic_slice_in_dim(source_off, mem * pairs, pairs),
            lax.dynamic_slice_in_dim(source_len, mem * pairs, pairs),
            jnp.stack([jnp.asarray(i, jnp.int32) for i in here]),
        ]
    )
    squares = (self_query, self_key, self_value, self_out, cross_query, cross_key, cross_value, cross_out)
    if quick:
        packed = call(
            pack_kernel,
            "pack",
            [*squares, feed_in, feed_out, biases, feed_bias.reshape(2, 128)]
            + [norm_gain, norm_shift, step_table],
            [VMEM] * 15,
            [((i, 128), BF, VMEM) for i in (SELF_ROWS + CROSS_ROWS, FEED_ROWS)],
            [VMEM((SMALL_ROWS, 128), F32)],
            1,
            60 * 2**20,
        )
        packed, memory = fence((packed, memory))
        square_p, feed_p = packed
        mems = swap_memory(memory, pairs)
        mems[2], mems[3] = swap(mems[2], 2), swap(mems[3], 3)
        square_z = sent_z([square_p] * 4)
        square_z, mems, feed_p = fence((square_z, mems, feed_p))
        first, second = z_halves(meta, square_z)
        square_near = [first, swap(first, 2), second, swap(second, 4)]
        feed_z = z_pair(meta, feed_p)
        square_near, feed_z = fence((square_near, feed_z))
        first, second = doubled(square_near)
        square_near = [first, swap(first, 4), second, swap(second, 2)]
        feed_z = (feed_z, swap(feed_z, 16))
        mems[1] = swap(mems[1], 1)
        feed_z = z_quad(meta, *feed_z)
        square_near, feed_z, mems = fence((square_near, feed_z, mems))
        square_w = spread_core(square_near)
        feed_near = spread_near(feed_z)
    else:
        square_w, feed_w = spread_any(
            squares, feed_in, feed_out, (biases, feed_bias, norm_gain, norm_shift, step_table)
        )
        square_w = two_parts(square_w)
        own = lax.all_to_all(memory, "mem", 0, 1, tiled=True)
        mems = jnp.split(own, X * CORE, axis=1)

    far_a, w_a, near_mix, vecs, fbias, held_a, held_b = self_forward(meta, target, square_w, steps)
    far_b, w_b, after_self, after_cross = cross_forward(meta, target, near_mix, mems, vecs, held_b)
    if quick:
        feed_near, after_cross = fence((feed_near, after_cross))
        feed_w = spread_core(feed_near)
    layer_out, gres_c, sums_c, d_fbias, *d_feed = feed(
        meta, after_cross, cotangent, vecs, fbias, feed_w
    )
    if quick:
        d_feed, gres_c = fence((d_feed, gres_c))
        d_feed[1] = swap(d_feed[1], 1)
    gq_b, gk_b, gv_b, sums_b, *d_cross = cross_back(meta, gres_c, far_b, w_b, held_b)
    if quick:
        d_feed, gq_b, d_cross = fence((d_feed, gq_b, d_cross))
        u_feed = core_sums(*d_feed)
        u_feed, gq_b, d_cross = fence((u_feed, gq_b, d_cross))
        n_feed = near_parts(u_feed)
        d_cross[1] = swap(d_cross[1], 1)
    grad_target, *gmem, d_first, d_second = lower_back(
        meta, gres_c, (gq_b, gk_b, gv_b), after_self, far_a, w_a, target, vecs, (sums_b, sums_c), d_fbias, held_b, held_a, steps
    )
    d_self = [d_first, d_second]
    if quick:
        one = self_query.shape
        n_feed, d_cross, d_self, gmem = fence((n_feed, d_cross, d_self, gmem))
        d_self[1] = swap(d_self[1], 1)
        rest = split_sums(*d_cross, *d_self)
        m_feed = chip_sums(meta, n_feed)
        rest, m_feed, gmem = fence((rest, m_feed, gmem))
        rest[1], rest[3] = swap(rest[1], 2), swap(rest[3], 4)
        gmem[1] = swap(gmem[1], 1)
        m_feed[1] = swap(m_feed[1], 16)
        rest, m_feed, gmem = fence((rest, m_feed, gmem))
        rest = turn(rest)
        rest[1], rest[3] = swap(rest[1], 4), swap(rest[3], 2)
        m_feed = halved(*m_feed)
        m_feed[1] = swap(m_feed[1], 8)
        rest, gmem, m_feed = fence((rest, gmem, m_feed))
        m_rest = sent_z(meet(meta, rest))
        g_feed = slice_sums(final_kernel, m_feed, (feed_in.shape, feed_out.shape))
        gmem[2], gmem[3] = swap(gmem[2], 2), swap(gmem[3], 3)
        grad_memory = return_memory(meta, gmem, memory.shape)
        m_rest, grad_memory = fence((m_rest, grad_memory))
        small_shapes = (biases.shape, (2, 128), norm_gain.shape, norm_shift.shape, step_table.shape)
        out = slice_sums(final_small_kernel, m_rest, (one,) * 8 + small_shapes)
        g_cross, g_self, (g_bias, g_fbias, g_gain, g_shift, g_table) = out[:4], out[4:8], out[8:]
        g_fbias = g_fbias.reshape(feed_bias.shape)
    else:
        whole = jnp.concatenate(gmem, axis=1)
        grad_memory = lax.all_to_all(whole, "mem", 1, 0, tiled=True).astype(F32)
        g_feed = reduce_feed_any(d_feed)
        g_cross = reduce_squares_any(d_cross, 4)
        g_self = reduce_squares_any(d_self, 4)
        g_bias, g_fbias, g_gain, g_shift, g_table = reduce_small_any(d_self, steps)
    return (
        layer_out, grad_target, grad_memory, *g_self, *g_cross, *g_feed,
        g_bias, g_fbias, g_gain, g_shift, g_table,
    )


def solution(mesh):
    rows = P(BOTH, None, None)
    piece = P("dp", "mem")
    vector = P(None, "dp")
    mem_rows = P("dp", "mem", None)
    return jax.shard_map(
        shards,
        mesh=mesh,
        in_specs=(rows, mem_rows, P(BOTH), P(BOTH), P("dp"), P("dp"), rows)
        + (piece,) * 10
        + (vector, P("dp"), vector, vector, vector),
        out_specs=(rows, rows, mem_rows) + (piece,) * 10 + (vector, P("dp"), vector, vector, vector),
        check_vma=False,
    )
```

```python
import functools
import math

import jax
import jax.numpy as jnp
from jax import lax
from jax.experimental import pallas as pl
from jax.experimental.pallas import tpu as pltpu
from jax.sharding import PartitionSpec as P

HEADS = 8
DH = 64
GROUP = 4
WIDE = GROUP * DH
EPSILON = 1e-05
SCALE = 1.0 / math.sqrt(DH)
BF = jnp.bfloat16
F32 = jnp.float32
VMEM_LIMIT = 30 * 2**20


def contract(left, right, left_dim, right_dim):
    return lax.dot_general(
        left, right, (((left_dim,), (right_dim,)), ((), ())), preferred_element_type=F32
    )


def mul(left, right):
    return contract(left, right, 1, 0)


def mul_nt(left, right):
    return contract(left, right, 1, 1)


def mul_tn(left, right):
    return contract(left, right, 0, 0)


def normalise(signal):
    centre = signal - jnp.mean(signal, axis=-1, keepdims=True)
    inverse = lax.rsqrt(jnp.mean(centre * centre, axis=-1, keepdims=True) + EPSILON)
    return centre * inverse, inverse


def norm_back(grad, scaled, inverse, gain):
    up = grad * gain
    return inverse * (
        up
        - jnp.mean(up, axis=-1, keepdims=True)
        - scaled * jnp.mean(up * scaled, axis=-1, keepdims=True)
    )


def col_sum(array):
    return jnp.sum(array.astype(F32), axis=0, keepdims=True)


def head_of_lane(rows):
    return lax.broadcasted_iota(jnp.int32, (rows, WIDE), 1) // DH


def stacked(block, lane_head):
    zero = jnp.zeros_like(block)
    return jnp.concatenate([jnp.where(lane_head == h, block, zero) for h in range(GROUP)], axis=0)


def unstacked(result, lane_head, rows):
    picked = result[:rows]
    for h in range(1, GROUP):
        picked = jnp.where(lane_head == h, result[h * rows : (h + 1) * rows], picked)
    return picked


def blocks(pairs):
    return [(p, g, slice(g * WIDE, (g + 1) * WIDE)) for p in range(pairs) for g in range(HEADS // GROUP)]


INPUT, QUERY, KEY, VALUE, MIXED, MEMORY = range(6)


def attend(before, bias_of, kept, w_ref, after):
    pairs, unused, rows, unused2 = kept.shape
    lane_head = head_of_lane(rows)
    every = blocks(pairs)

    def scores_of(p, g, cols):
        return mul_nt(stacked(kept[p, QUERY, :, cols], lane_head), kept[p, KEY, :, cols])

    before(0)
    ahead = scores_of(*every[0])
    for i, (p, g, cols) in enumerate(every):
        scores = ahead + bias_of(p)
        if g == 0 and p + 1 < pairs:
            before(p + 1)
        if i + 1 < len(every):
            ahead = scores_of(*every[i + 1])
        top = jnp.max(scores, axis=-1, keepdims=True)
        raised = jnp.exp(scores - top)
        total = jnp.sum(raised, axis=-1, keepdims=True)
        weights = (raised * (1.0 / total)).astype(BF)
        w_ref[p, g] = weights
        mixed = mul(weights, kept[p, VALUE, :, cols])
        kept[p, MIXED, :, cols] = unstacked(mixed, lane_head, rows).astype(BF)
        if g == HEADS // GROUP - 1:
            after(p)


def attend_back(before, ready, kept, w_ref, grad_ref, gq_ref, gk_ref, gv_ref, after):
    pairs, unused, rows, unused2 = kept.shape
    lane_head = head_of_lane(rows)
    every = blocks(pairs)

    def weight_grads(p, g, cols):
        if g == 0:
            ready(p)
        grads = stacked(grad_ref[p, :, cols], lane_head)
        return grads, mul_nt(grads, kept[p, VALUE, :, cols])

    before(0)
    ahead = weight_grads(*every[0])
    for i, (p, g, cols) in enumerate(every):
        grads, grad_w = ahead
        if g == 0 and p + 1 < pairs:
            before(p + 1)
        if i + 1 < len(every):
            ahead = weight_grads(*every[i + 1])
        weights = w_ref[p, g]
        wide = weights.astype(F32)
        offset = jnp.sum(grad_w * wide, axis=-1, keepdims=True)
        grad_s = (wide * (grad_w - offset)).astype(BF)
        grad_q = unstacked(mul(grad_s, kept[p, KEY, :, cols]), lane_head, rows)
        gq_ref[p, :, cols] = (grad_q * SCALE).astype(BF)
        gk_ref[p, :, cols] = mul_tn(grad_s, stacked(kept[p, QUERY, :, cols], lane_head)).astype(BF)
        gv_ref[p, :, cols] = mul_tn(weights, grads).astype(BF)
        if g == HEADS // GROUP - 1:
            after(p)


def flat(ref):
    value = ref[...]
    return value.reshape(value.shape[0] * value.shape[1], value.shape[2])


Z, Y, X, CORE = 4, 2, 2, 2
SLOTS = [(y, x, c) for y in range(Y) for x in range(X) for c in range(CORE)]
PIECE = 64
FEED_ROWS = 4 * PIECE + 256
SMALL_ROWS = 48
SELF_ROWS = 3 * PIECE + SMALL_ROWS
CROSS_ROWS = 5 * PIECE
FIRST_ROWS = 288
GAIN, SHIFT, TABLE = 7, 10, 16


def places(meta, slot):
    base = meta.shape[0] - 4
    y, x, c = slot
    return y ^ meta[base + 1], (x ^ meta[base + 2]) * CORE + (c ^ meta[base + 3])


def load_copies(meta, sources, held, sems, first=0):
    copies = []
    rows = held.shape[-2]
    for i, slot in enumerate(SLOTS):
        row, panel = places(meta, slot)
        source = sources[i].at[:, pl.ds(first, rows)]
        copies.append(pltpu.make_async_copy(source, held.at[panel, :, row], sems.at[i]))
    return copies


def store_copies(meta, held, targets, sems, first=0):
    copies = []
    rows = targets[0].shape[2]
    for i, slot in enumerate(SLOTS):
        row, panel = places(meta, slot)
        y, x, c = slot
        target = targets[c].at[y * X + x]
        source = held.at[panel, :, row, pl.ds(first, rows)]
        copies.append(pltpu.make_async_copy(source, target, sems.at[i]))
    return copies


def start(copies):
    for copy in copies:
        copy.start()


def wait(copies):
    for copy in copies:
        copy.wait()


def moves(sources, targets, sems):
    return [pltpu.make_async_copy(a, b, sems.at[i]) for i, (a, b) in enumerate(zip(sources, targets))]


def joined(value):
    return value.reshape(-1, value.shape[-1])


def square(held, index):
    span = slice(PIECE * index, PIECE * (index + 1))
    return jnp.concatenate([joined(held[i, :, :, span]) for i in range(X * CORE)], axis=1)


def keep(held, index, value):
    span = slice(PIECE * index, PIECE * (index + 1))
    for i in range(X * CORE):
        part = value[:, i * 128 : (i + 1) * 128].astype(BF)
        held[i, :, :, span] = part.reshape(Z, Y, PIECE, 128)


def all_rows(kept, index):
    value = kept[:, index]
    return value.reshape(value.shape[0] * value.shape[1], value.shape[2])


def each(source, target, sems):
    count = source.shape[0]
    return moves([source.at[p] for p in range(count)], [target.at[p] for p in range(count)], sems)


def self_forward_kernel(meta, target, *refs):
    pieces, refs = refs[:8], refs[8:]
    far, far_w, near_mix, vecs, fbias, held, held_cross = refs[:7]
    kept, w, small, sems, cross_sems, small_sems, far_sems, w_sems = refs[7:]
    base = meta.shape[0] - 4
    small_loads = [
        pltpu.make_async_copy(
            pieces[y * CORE].at[0, :, pl.ds(3 * PIECE, SMALL_ROWS)], small.at[:, y ^ meta[base + 1]], small_sems.at[y]
        )
        for y in range(Y)
    ]
    start(small_loads)
    loads, cross_loads = [], []
    edge = FIRST_ROWS - SELF_ROWS
    for i, slot in enumerate(SLOTS):
        y, x, c = slot
        row, panel = places(meta, slot)
        a_part, b_part = pieces[y * CORE + c].at[x], pieces[Y * CORE + x * CORE + c].at[y]
        own, cross = held.at[panel, :, row], held_cross.at[panel, :, row]
        loads.append(pltpu.make_async_copy(a_part.at[:, pl.ds(0, 3 * PIECE)], own, sems.at[i]))
        cross_loads += moves(
            (a_part.at[:, pl.ds(SELF_ROWS, edge)], b_part),
            (cross.at[:, pl.ds(0, edge)], cross.at[:, pl.ds(edge, CROSS_ROWS - edge)]),
            cross_sems.at[i],
        )
    start(loads)
    start(cross_loads)
    copies, w_copies = each(kept, far, far_sems), each(w, far_w, w_sems)
    pairs, length, width = target.shape
    wait(small_loads)
    every = [small[z, y].astype(F32) for z in range(Z) for y in range(Y)]
    steps = (vecs.shape[0] - TABLE) // 2
    vecs[:TABLE] = jnp.concatenate([one[:TABLE, :64] for one in every], axis=1)
    for i in range(2):
        part = [one[TABLE : TABLE + steps, 64 * i : 64 * (i + 1)] for one in every]
        vecs[TABLE + i * steps : TABLE + (i + 1) * steps] = jnp.concatenate(part, axis=1)
    for d, one in enumerate(every):
        for i in range(2):
            at = TABLE + steps + i
            fbias[:, d * 256 + i * 128 : d * 256 + (i + 1) * 128] = one[at : at + 1]

    def before(p):
        emb = target[p].astype(F32) + vecs[pl.ds(TABLE + meta[pairs + p], 1), :]
        scaled, unused = normalise(emb)
        x = (scaled * vecs[GAIN : GAIN + 1] + vecs[SHIFT : SHIFT + 1]).astype(BF)
        kept[p, INPUT] = x
        if p == 0:
            wait(loads)
        kept[p, QUERY] = (mul(x, square(held, 0)) + vecs[0:1]).astype(BF) * SCALE
        kept[p, KEY] = mul(x, square(held, 1)).astype(BF)
        kept[p, VALUE] = (mul(x, square(held, 2)) + vecs[1:2]).astype(BF)

    def bias_of(p):
        spot = lax.broadcasted_iota(jnp.int32, (1, length), 1)
        return jnp.where(spot < meta[p], 0.0, -1e30)

    def after(p):
        near_mix[p] = kept[p, MIXED]
        copies[p].start()
        w_copies[p].start()

    attend(before, bias_of, kept, w, after)
    wait(cross_loads)
    wait(copies)
    wait(w_copies)


def cross_forward_kernel(meta, target, mix_a, mem_0, mem_1, mem_2, mem_3, vecs, held, *refs):
    far, w, far_after, after_cross = refs[:4]
    kept, after_self, mem_sems, far_sems, after_sems = refs[4:]
    pairs, length, width = target.shape
    source = kept.shape[2]
    base = meta.shape[0] - 4
    mine = meta[base + 2] * CORE + meta[base + 3]
    part = source // (X * CORE)
    mem_loads = [
        pltpu.make_async_copy(
            one,
            kept.at[:, MEMORY, pl.ds(pl.multiple_of((mine ^ i) * part, part), part), :],
            mem_sems.at[i],
        )
        for i, one in enumerate((mem_0, mem_1, mem_2, mem_3))
    ]
    start(mem_loads)
    copies = each(kept, far, far_sems)
    after_copies = each(after_self, far_after, after_sems)

    def before(p):
        row = vecs[pl.ds(TABLE + meta[pairs + p], 1), :]
        total = target[p].astype(F32) + row + mul(mix_a[p], square(held, 0)) + vecs[2:3]
        after_self[p] = total
        after_copies[p].start()
        scaled, unused = normalise(total)
        x = (scaled * vecs[GAIN + 1 : GAIN + 2] + vecs[SHIFT + 1 : SHIFT + 2]).astype(BF)
        kept[p, INPUT] = x
        kept[p, QUERY] = (mul(x, square(held, 1)) + vecs[3:4]).astype(BF) * SCALE
        if p == 0:
            wait(mem_loads)
        m = kept[p, MEMORY]
        kept[p, KEY] = mul(m, square(held, 2)).astype(BF)
        kept[p, VALUE] = (mul(m, square(held, 3)) + vecs[4:5]).astype(BF)

    def bias_of(p):
        spot = lax.broadcasted_iota(jnp.int32, (1, source), 1)
        begin = meta[2 * pairs + p]
        end = begin + meta[3 * pairs + p]
        return jnp.where((spot >= begin) & (spot < end), 0.0, -1e30)

    def after(p):
        copies[p].start()
        after_cross[p] = after_self[p] + mul(kept[p, MIXED], square(held, 4)) + vecs[5:6]

    attend(before, bias_of, kept, w, after)
    wait(after_copies)
    wait(copies)


def gelu_parts(value):
    size = jnp.abs(value) * math.sqrt(0.5)
    t = 1.0 / (1.0 + 0.3275911 * size)
    bell = jnp.exp(-0.5 * value * value)
    tail = (
        t
        * (
            0.5 * 0.254829592
            + t
            * (
                0.5 * -0.284496736
                + t * (0.5 * 1.421413741 + t * (0.5 * -1.453152027 + t * (0.5 * 1.061405429)))
            )
        )
        * bell
    )
    below = jnp.where(value < 0, tail, 1.0 - tail)
    slope = below + value * bell * (1.0 / math.sqrt(2.0 * math.pi))
    return value * below, slope


def feed_kernel(meta, after_cross, cot, vecs, feed_bias, *refs):
    pieces, refs = refs[:8], refs[8:]
    far_out, gres, sums, dbias = refs[:4]
    targets, refs = refs[4:6], refs[6:]
    held, kept, x_c, act, grad_pre, layer_out, sems, out_sems, far_sems = refs
    copies = moves((layer_out,), (far_out,), far_sems)
    loads = load_copies(meta, pieces, held, sems)
    start(loads)
    stores = store_copies(meta, kept, targets, out_sems)
    shape = after_cross.shape
    signal = flat(after_cross)
    scaled, inverse = normalise(signal)
    gain = vecs[GAIN + 2 : GAIN + 3]
    x_c[...] = (scaled * gain + vecs[SHIFT + 2 : SHIFT + 3]).astype(BF)
    wait(loads)
    c = flat(cot)
    x = x_c[...]
    w_in = [
        jnp.concatenate([joined(held[j, :, :, PIECE * i : PIECE * (i + 1)]) for i in range(4)], axis=1)
        for j in range(4)
    ]
    w_out = [jnp.concatenate([joined(held[i, j, :, 4 * PIECE :]) for i in range(4)], axis=1) for j in range(4)]
    w_in = jnp.concatenate(w_in, axis=1)
    w_out = jnp.concatenate(w_out, axis=0)
    block, span = 256, 256
    tiles = [
        (slice(r, r + span), slice(j, j + block))
        for j in range(0, w_in.shape[1], block)
        for r in range(0, x.shape[0], span)
    ]

    def first(rows, cols):
        return mul(x[rows], w_in[:, cols]), mul_nt(c[rows], w_out[cols])

    ready = [first(*tile) for tile in tiles[:1]]
    for j, (rows, cols) in enumerate(tiles):
        if j + 1 < len(tiles):
            ready.append(first(*tiles[j + 1]))
        pre, grad_act = ready[j]
        ready[j] = None
        value, slope = gelu_parts(pre + feed_bias[:, cols])
        act[rows, cols] = value.astype(BF)
        grad = (grad_act * slope).astype(BF)
        grad_pre[rows, cols] = grad
        if rows.start == 0:
            total = col_sum(grad)
        else:
            total = total + col_sum(grad)
        if rows.stop == x.shape[0]:
            dbias[:, cols] = total
    for j in range(4):
        cols = slice(j * 512, (j + 1) * 512)
        d_out = mul_tn(act[:, cols], c)
        for i in range(4):
            part = d_out[:, i * 128 : (i + 1) * 128].astype(BF)
            kept[i, j, :, 4 * PIECE :] = part.reshape(Y, 256, 128)
        d_in = mul_tn(x, grad_pre[:, cols])
        for i in range(4):
            part = d_in[:, i * 128 : (i + 1) * 128].astype(BF)
            kept[j, :, :, PIECE * i : PIECE * (i + 1)] = part.reshape(Z, Y, PIECE, 128)
    start(stores)
    layer_out[...] = (signal + mul(act[...], w_out) + vecs[6:7]).astype(BF).reshape(shape)
    start(copies)
    grad = mul_nt(grad_pre[...], w_in)
    wide_cot = flat(cot).astype(F32)
    sums[0:1] = col_sum(wide_cot)
    sums[1:2] = col_sum(grad * scaled)
    sums[2:3] = col_sum(grad)
    gres[...] = (wide_cot + norm_back(grad, scaled, inverse, gain)).reshape(shape)
    wait(stores)
    wait(copies)


def cross_back_kernel(meta, gres, far, w, held, *refs):
    gq, gk, gv, sums = refs[:4]
    targets, (kept, gmix, grads, out_sems, far_sems, later_sems) = refs[4:6], refs[6:]
    needed = pl.ds(QUERY, 3)
    copies = [
        pltpu.make_async_copy(far.at[p, needed], kept.at[p, needed], far_sems.at[p]) for p in range(far.shape[0])
    ]
    later = moves(
        (far.at[:, pl.ds(INPUT, 1)], far.at[:, pl.ds(MIXED, 2)]),
        (kept.at[:, pl.ds(INPUT, 1)], kept.at[:, pl.ds(MIXED, 2)]),
        later_sems,
    )
    start(copies)
    start(later)
    stores = store_copies(meta, grads, targets, out_sems)

    def before(p):
        gmix[p] = mul_nt(gres[p].astype(BF), square(held, 4)).astype(BF)

    attend_back(before, lambda p: copies[p].wait(), kept, w, gmix, gq, gk, gv, lambda p: None)
    wait(later)
    grad = flat(gres).astype(BF)
    m = all_rows(kept, MEMORY)
    keep(grads, 3, mul_tn(all_rows(kept, MIXED), grad))
    keep(grads, 0, mul_tn(all_rows(kept, INPUT), flat(gq)))
    keep(grads, 1, mul_tn(m, flat(gk)))
    keep(grads, 2, mul_tn(m, flat(gv)))
    start(stores)
    sums[0:1] = col_sum(grad)
    sums[1:2] = col_sum(flat(gq))
    sums[2:3] = col_sum(flat(gv))
    wait(stores)


def lower_back_kernel(
    meta, gres, grad_q, grad_k, grad_v, far_after, far, far_w, target, vecs, sums_b, sums_c, dbias, held, held_a, *refs
):
    far_target, gmem_0, gmem_1, gmem_2, gmem_3 = refs[:5]
    targets, refs = refs[5:7], refs[7:]
    kept, w, after_self, gres_a, gmix, gmem, gq, gk, gv, gtarget, gtable, grads = refs[:12]
    mem_sems, far_sems, w_sems, after_sems, target_sems, out_sems = refs[12:]
    copies, w_copies = each(far, kept, far_sems), each(far_w, w, w_sems)
    after_copies = each(far_after, after_self, after_sems)
    for group in zip(after_copies, copies, w_copies):
        start(group)
    target_copies = each(gtarget, far_target, target_sems)
    stores = store_copies(meta, grads, targets, out_sems)
    base = meta.shape[0] - 4
    mine = meta[base + 2] * CORE + meta[base + 3]
    part = gmem.shape[1] // (X * CORE)
    mem_stores = [
        pltpu.make_async_copy(
            gmem.at[:, pl.ds(pl.multiple_of((mine ^ i) * part, part), part), :], one, mem_sems.at[i]
        )
        for i, one in enumerate((gmem_0, gmem_1, gmem_2, gmem_3))
    ]
    pairs, length, width = gres.shape
    totals = [0.0] * 5
    gtable[...] = jnp.zeros_like(gtable)

    def count(first, *parts):
        for i, one in enumerate(parts):
            totals[first + i] = totals[first + i] + col_sum(one)

    def before(p):
        grad_m = mul_nt(grad_k[p], square(held, 2)) + mul_nt(grad_v[p], square(held, 3))
        gmem[p] = grad_m.astype(BF)
        grad_in = mul_nt(grad_q[p], square(held, 1))
        after_copies[p].wait()
        scaled, inverse = normalise(after_self[p])
        total = gres[p] + norm_back(grad_in, scaled, inverse, vecs[GAIN + 1 : GAIN + 2])
        gres_a[p] = total
        grad_a = total.astype(BF)
        gmix[p] = mul_nt(grad_a, square(held, 0)).astype(BF)
        count(0, grad_in * scaled, grad_in, grad_a)
        if p + 1 == pairs:
            start(mem_stores)

    def ready(p):
        copies[p].wait()
        w_copies[p].wait()

    def after(p):
        grad_in = (
            mul_nt(gq[p], square(held_a, 0)) + mul_nt(gk[p], square(held_a, 1)) + mul_nt(gv[p], square(held_a, 2))
        )
        row = pl.ds(TABLE + meta[pairs + p], 1)
        scaled, inverse = normalise(target[p].astype(F32) + vecs[row, :])
        count(3, grad_in * scaled, grad_in)
        total = gres_a[p] + norm_back(grad_in, scaled, inverse, vecs[GAIN : GAIN + 1])
        gtarget[p] = total
        target_copies[p].start()
        gtable[pl.ds(meta[pairs + p], 1), :] += col_sum(total)

    attend_back(before, ready, kept, w, gmix, gq, gk, gv, after)
    x = all_rows(kept, INPUT)
    keep(grads, 3, mul_tn(all_rows(kept, MIXED), flat(gres_a).astype(BF)))
    for i, one in enumerate((gq, gk, gv)):
        keep(grads, i, mul_tn(x, flat(one)))
    rows = [col_sum(flat(gq)), col_sum(flat(gv)), totals[2], sums_b[1:2], sums_b[2:3], sums_b[0:1], sums_c[0:1]]
    rows += [totals[3], totals[0], sums_c[1:2], totals[4], totals[1], sums_c[2:3]]
    vectors = jnp.concatenate(rows + [jnp.zeros((TABLE - len(rows), width), F32)], axis=0)
    steps = gtable.shape[0] // 2
    for d in range(Z * Y):
        lanes = slice(d * 64, (d + 1) * 64)
        top = jnp.concatenate([vectors[:, lanes], jnp.zeros((TABLE, 64), F32)], axis=1)
        low = jnp.concatenate([gtable[:steps, lanes], gtable[steps:, lanes]], axis=1)
        tail = [dbias[:, d * 256 + i * 128 : d * 256 + (i + 1) * 128] for i in range(2)]
        fill = jnp.zeros((SMALL_ROWS - TABLE - steps - 2, 128), F32)
        small = jnp.concatenate([top, low, *tail, fill], axis=0).astype(BF)
        for i in range(X * CORE):
            grads[i, d // Y, d % Y, 4 * PIECE :] = small
    start(stores)
    wait(mem_stores)
    wait(target_copies)
    wait(stores)


HBM = pl.ANY
FAR = pltpu.HBM
VMEM = pltpu.VMEM
SMEM = pltpu.SMEM


def call(kernel, name, args, spaces, outs, scratch, micros=1, limit=VMEM_LIMIT):
    cost = pl.CostEstimate(flops=int(micros * 10**9), bytes_accessed=int(micros * 3 * 10**6), transcendentals=0)
    function = pl.pallas_call(
        kernel,
        out_shape=[FAR(s, d) if m is FAR else jax.ShapeDtypeStruct(s, d) for s, d, m in outs],
        in_specs=[pl.BlockSpec(memory_space=m) for m in spaces],
        out_specs=[pl.BlockSpec(memory_space=m) for unused, unused2, m in outs],
        scratch_shapes=scratch,
        compiler_params=pltpu.CompilerParams(vmem_limit_bytes=limit),
        cost_estimate=cost,
        name=name,
    )
    return list(function(*[pltpu.with_memory_space_constraint(a, m) if m is FAR else a for a, m in zip(args, spaces)]))


def held_shape(rows):
    return (X * CORE, Z, Y, rows, 128)


def held_like(rows):
    return VMEM(held_shape(rows), BF)


def kept_like(slots):
    return VMEM((X * CORE, slots[1], Y, *slots[2:]), BF)


def sems(*shape):
    return pltpu.SemaphoreType.DMA(shape)


def weights_shape(shape, source):
    return (shape[0], HEADS // GROUP, GROUP * shape[1], source)


def slot_shape(count, extra=0):
    return (Y * X, Z, count * PIECE + extra, 128)


def kept_shape(shape, count):
    return (shape[0], count, *shape[1:])


def self_forward(meta, target, pieces, steps):
    shape = target.shape
    kept, w_shape = kept_shape(shape, MIXED + 1), weights_shape(shape, shape[1])
    return call(
        self_forward_kernel,
        "self_forward",
        [meta, target, *pieces],
        [SMEM, VMEM] + [HBM] * 8,
        [(kept, BF, FAR), (w_shape, BF, FAR), (shape, BF, VMEM)]
        + [((TABLE + steps, shape[2]), F32, VMEM), ((1, 4 * shape[2]), F32, VMEM)]
        + [(held_shape(3 * PIECE), BF, VMEM), (held_shape(CROSS_ROWS), BF, VMEM)],
        [VMEM(kept, BF), VMEM(w_shape, BF), VMEM((Z, Y, SMALL_ROWS, 128), BF)]
        + [sems(8), sems(8, 2), sems(2), sems(shape[0]), sems(shape[0])],
        0.1,
    )


def cross_forward(meta, target, mix_a, mems, vecs, held):
    shape = target.shape
    kept, w_shape = kept_shape(shape, MEMORY + 1), weights_shape(shape, shape[1])
    return call(
        cross_forward_kernel,
        "cross_forward",
        [meta, target, mix_a, *mems, vecs, held],
        [SMEM] + [VMEM] * 2 + [HBM] * 4 + [VMEM] * 2,
        [(kept, BF, FAR), (w_shape, BF, VMEM), (shape, F32, FAR), (shape, F32, VMEM)],
        [VMEM(kept, BF), VMEM(shape, F32), sems(4), sems(shape[0]), sems(shape[0])],
        0.1,
    )


def feed(meta, after_cross, cot, vecs, feed_bias, pieces):
    shape = after_cross.shape
    tokens, width = shape[0] * shape[1], shape[2]
    return call(
        feed_kernel,
        "feed",
        [meta, after_cross, cot, vecs, feed_bias, *pieces],
        [SMEM] + [VMEM] * 4 + [HBM] * 8,
        [(shape, BF, FAR), (shape, F32, VMEM), ((3, width), F32, VMEM), (feed_bias.shape, F32, VMEM)]
        + [(slot_shape(4, 256), BF, HBM)] * 2,
        [held_like(FEED_ROWS)] * 2
        + [VMEM((tokens, width), BF)] + [VMEM((tokens, feed_bias.shape[1]), BF)] * 2
        + [VMEM(shape, BF)]
        + [sems(8), sems(8), sems(1)],
        26,
        36 * 2**20,
    )


def cross_back(meta, gres, far, w, held):
    shape = gres.shape
    return call(
        cross_back_kernel,
        "cross_back",
        [meta, gres, far, w, held],
        [SMEM, VMEM, FAR, VMEM, VMEM],
        [(shape, BF, VMEM)] * 3 + [((3, shape[2]), F32, VMEM)] + [(slot_shape(4), BF, HBM)] * 2,
        [VMEM(far.shape, BF), VMEM(shape, BF), kept_like(slot_shape(4)), sems(8), sems(shape[0]), sems(2)],
        15,
    )


def lower_back(meta, gres, grads, after_self, far, far_w, target, vecs, sums, dbias, held, held_a, steps):
    shape = gres.shape
    part = (shape[0], shape[1] // (X * CORE), shape[2])
    slots = slot_shape(4, SMALL_ROWS)
    return call(
        lower_back_kernel,
        "lower_back",
        [meta, gres, *grads, after_self, far, far_w, target, vecs, *sums, dbias, held, held_a],
        [SMEM] + [VMEM] * 4 + [FAR] * 3 + [VMEM] * 7,
        [(shape, F32, FAR)] + [(part, BF, HBM)] * 4 + [(slots, BF, HBM)] * 2,
        [VMEM(far.shape, BF), VMEM(far_w.shape, BF), VMEM(shape, F32), VMEM(shape, F32)]
        + [VMEM(shape, BF)] * 5 + [VMEM(shape, F32), VMEM((steps, shape[2]), F32), kept_like(slots)]
        + [sems(4)] + [sems(shape[0])] * 4 + [sems(8)],
        20,
        38 * 2**20,
    )


BOTH = ("dp", "mem")


def swap(array, mask):
    count = lax.axis_size("dp") * lax.axis_size("mem")
    return lax.ppermute(array, BOTH, [(i, i ^ mask) for i in range(count)])


def pack_kernel(*refs):
    squares, (w_in, w_out, biases, f_bias, gain, shift, table) = refs[:8], refs[8:15]
    square_out, feed_out, stage = refs[15:]
    for i, ref in enumerate(squares):
        if i < 3:
            square_out[PIECE * i : PIECE * (i + 1)] = ref[...]
        else:
            square_out[SELF_ROWS + PIECE * (i - 3) : SELF_ROWS + PIECE * (i - 2)] = ref[...]
    for i in range(4):
        feed_out[PIECE * i : PIECE * (i + 1)] = w_in[:, 128 * i : 128 * (i + 1)]
    feed_out[4 * PIECE :] = w_out[...]
    stage[...] = jnp.zeros_like(stage)
    stage[0:7, :64] = biases[...].astype(F32)
    stage[GAIN : GAIN + 3, :64] = gain[...].astype(F32)
    stage[SHIFT : SHIFT + 3, :64] = shift[...].astype(F32)
    rows = table[...].astype(F32)
    half = rows.shape[0] // 2
    stage[TABLE : TABLE + half] = jnp.concatenate([rows[:half], rows[half:]], axis=1)
    stage[TABLE + half : TABLE + half + 2] = f_bias[...].astype(F32)
    square_out[3 * PIECE : SELF_ROWS] = stage[...].astype(BF)


def pair_kernel(meta, mine, other, out):
    low = meta[meta.shape[0] - 4] % 2
    out[low] = mine[...]
    out[1 - low] = other[...]


def quad_kernel(meta, mine, other, out):
    high = meta[meta.shape[0] - 4] // 2
    for i in range(2):
        out[2 * high + i] = mine[i]
        out[2 * (1 - high) + i] = other[i]


def quarter_kernel(meta, a, b, c, d, first, second):
    mine = meta[meta.shape[0] - 4]
    for i, one in enumerate((a, b, c, d)):
        first[mine ^ i] = one[:FIRST_ROWS]
        second[mine ^ i] = one[FIRST_ROWS:]


def double_kernel(a, a_other, b, b_other, a_out, b_out):
    for out, pair in ((a_out, (a, a_other)), (b_out, (b, b_other))):
        for i, one in enumerate(pair):
            out[i] = one[...]


def doubled(parts):
    outs = [((2, *one.shape), BF, VMEM) for one in parts[::2]]
    return call(double_kernel, "double", parts, [VMEM] * 4, outs, [])


def sent_z(parts):
    return [parts[0], swap(parts[1], 8), swap(parts[2], 16), swap(parts[3], 24)]


def z_halves(meta, parts):
    rows, lanes = parts[0].shape
    return call(
        quarter_kernel,
        "quarter",
        [meta, *parts],
        [SMEM] + [VMEM] * 4,
        [((Z, i, lanes), BF, VMEM) for i in (FIRST_ROWS, rows - FIRST_ROWS)],
        [],
    )


def z_pair(meta, packed):
    return call(
        pair_kernel,
        "pair",
        [meta, packed, swap(packed, 8)],
        [SMEM, VMEM, VMEM],
        [((2, *packed.shape), BF, VMEM)],
        [],
    )[0]


def z_quad(meta, pair, other):
    return call(
        quad_kernel,
        "quad",
        [meta, pair, other],
        [SMEM, VMEM, VMEM],
        [((Z, *pair.shape[1:]), BF, VMEM)],
        [],
    )[0]


fence = lax.optimization_barrier


def spread_near(along_z):
    return [along_z, swap(along_z, 2), swap(along_z, 4), swap(along_z, 6)]


def spread_core(near):
    out = []
    for one in near:
        out += [one, swap(one, 1)]
    return out


def merge_kernel(meta, a, b, c, d, own, sent):
    mine = meta[meta.shape[0] - 4]

    def total(z):
        return (a[z].astype(F32) + b[z].astype(F32)) + (c[z].astype(F32) + d[z].astype(F32))

    for i in range(2):
        own[i] = total(mine ^ i)
        sent[i] = total(mine ^ (2 + i)).astype(BF)


def halve_kernel(pair, other, own, sent):
    own[...] = pair[0] + other[0].astype(F32)
    sent[...] = (pair[1] + other[1].astype(F32)).astype(BF)


def final_parts(refs, outs):
    def total(span):
        value = refs[0][span]
        for ref in refs[1:]:
            value = value + ref[span].astype(F32)
        return value

    at = 0
    for out in outs:
        rows = out.shape[0]
        for i in range(out.shape[1] // 128):
            out[:, 128 * i : 128 * (i + 1)] = total(slice(at, at + rows))
            at += rows
    return total, at


def final_kernel(*refs):
    final_parts(refs[:2], refs[2:])


def final_small_kernel(*refs):
    outs, (biases, f_bias, gain, shift, table) = refs[4:12], refs[12:]
    total, at = final_parts(refs[:4], outs)
    part = total(slice(at, at + SMALL_ROWS))
    biases[...] = part[0:7, :64]
    gain[...] = part[GAIN : GAIN + 3, :64]
    shift[...] = part[SHIFT : SHIFT + 3, :64]
    half = table.shape[0] // 2
    table[:half] = part[TABLE : TABLE + half, :64]
    table[half:] = part[TABLE : TABLE + half, 64:]
    f_bias[...] = part[TABLE + half : TABLE + half + 2]


def add(left, right):
    return (left.astype(F32) + right.astype(F32)).astype(BF)


def core_sums(own, other):
    return [add(own[i], other[i]) for i in range(Y * X)]


def split_kernel(*refs):
    parts, (a_own, a_sent, b_own, b_sent) = refs[:-4], refs[-4:]
    at = 0
    for own, other in zip(parts[::2], parts[1::2]):
        rows = own.shape[2]
        cut = min(max(FIRST_ROWS - at, 0), rows)
        for i in range(Y * X):
            a_out = (a_own, a_sent)[i % X].at[i // X]
            b_out = (b_own, b_sent)[i // X].at[i % X]
            if cut > 0:
                a_out[:, at : at + cut] = add(own[i, :, :cut], other[i, :, :cut])
            if cut < rows:
                first = at + cut - FIRST_ROWS
                b_out[:, first : first + rows - cut] = add(own[i, :, cut:], other[i, :, cut:])
        at += rows


def split_sums(*parts):
    rows = sum(one.shape[2] for one in parts[::2])
    a_shape, b_shape = (2, Z, FIRST_ROWS, 128), (2, Z, rows - FIRST_ROWS, 128)
    return call(
        split_kernel,
        "split",
        list(parts),
        [VMEM] * len(parts),
        [(a_shape, BF, VMEM)] * 2 + [(b_shape, BF, VMEM)] * 2,
        [],
    )


def turn_kernel(a_own, a_other, b_own, b_other, a_kept, a_sent, b_kept, b_sent):
    for own, other, kept, sent in ((a_own, a_other, a_kept, a_sent), (b_own, b_other, b_kept, b_sent)):
        kept[...] = own[0].astype(F32) + other[0].astype(F32)
        sent[...] = add(own[1], other[1])


def turn(parts):
    a_shape, b_shape = parts[0].shape[1:], parts[2].shape[1:]
    return call(
        turn_kernel,
        "turn",
        parts,
        [VMEM] * 4,
        [(a_shape, F32, VMEM), (a_shape, BF, VMEM), (b_shape, F32, VMEM), (b_shape, BF, VMEM)],
        [],
    )


def meet_kernel(meta, a_kept, a_other, b_kept, b_other, *outs):
    mine = meta[meta.shape[0] - 4]
    rows = a_kept.shape[1]
    for i, out in enumerate(outs):
        z = mine ^ i
        out[:rows] = (a_kept[z] + a_other[z].astype(F32)).astype(out.dtype)
        out[rows:] = (b_kept[z] + b_other[z].astype(F32)).astype(out.dtype)


def meet(meta, parts):
    out = (parts[0].shape[1] + parts[2].shape[1], 128)
    return call(
        meet_kernel,
        "meet",
        [meta, *parts],
        [SMEM] + [VMEM] * 4,
        [(out, F32, VMEM)] + [(out, BF, VMEM)] * 3,
        [],
    )


def near_parts(pairs):
    return [pairs[0], swap(pairs[1], 2), swap(pairs[2], 4), swap(pairs[3], 6)]


def chip_sums(meta, near):
    unused, rows, lanes = near[0].shape
    return call(
        merge_kernel,
        "merge",
        [meta, *near],
        [SMEM] + [VMEM] * 4,
        [((2, rows, lanes), F32, VMEM), ((2, rows, lanes), BF, VMEM)],
        [],
    )


def halved(pair, other):
    rows, lanes = pair.shape[1:]
    return call(
        halve_kernel, "halve", [pair, other], [VMEM] * 2, [((rows, lanes), F32, VMEM), ((rows, lanes), BF, VMEM)], []
    )


def slice_sums(kernel, parts, shapes):
    return call(kernel, "final", parts, [VMEM] * len(parts), [(s, F32, VMEM) for s in shapes], [])


def place_kernel(meta, a, b, c, d, out):
    base = meta.shape[0] - 4
    mine = meta[base + 2] * CORE + meta[base + 3]
    pairs = a.shape[0]
    for i, one in enumerate((a, b, c, d)):
        for p in range(pairs):
            out[(mine ^ i) * pairs + p] = one[p].astype(F32)


def swap_memory(memory, pairs):
    mine = lax.axis_index("mem")
    parts = [lax.dynamic_slice_in_dim(memory, (mine ^ i) * pairs, pairs) for i in range(4)]
    return parts


def return_memory(meta, parts, shape):
    return call(place_kernel, "place", [meta, *parts], [SMEM] + [VMEM] * 4, [(shape, F32, VMEM)], [])[0]


def slots_of(wide):
    rows, cols = wide.shape
    cut = wide.reshape(Z, Y, rows // (Z * Y), X, CORE, cols // (X * CORE))
    return [cut[:, y, :, x, c] for y, x, c in SLOTS]


def wide_of(slots):
    z, rows, cols = slots[0].shape
    cut = jnp.stack(slots).reshape(Y, X, CORE, z, rows, cols)
    return cut.transpose(3, 0, 4, 1, 2, 5).reshape(z * Y * rows, X * CORE * cols)


def gather_any(piece):
    return lax.all_gather(lax.all_gather(piece, "mem", axis=1, tiled=True), "dp", axis=0, tiled=True)


def scatter_any(wide):
    part = lax.psum_scatter(wide.astype(F32), "dp", scatter_dimension=0, tiled=True)
    return lax.psum_scatter(part, "mem", scatter_dimension=1, tiled=True)


def narrow_columns(slots):
    return [jnp.concatenate(jnp.split(one, 4, axis=2), axis=1) for one in slots]


def small_pieces(biases, f_bias, gain, shift, table):
    vectors = jnp.concatenate([biases, gain, shift], axis=0)
    vectors = jnp.pad(vectors, ((0, TABLE - vectors.shape[0]), (0, 0)))
    half = table.shape[0] // 2

    def cut(rows):
        return rows.reshape(rows.shape[0], Z, Y, 64).transpose(1, 2, 0, 3)

    top = jnp.pad(cut(vectors), ((0, 0),) * 3 + ((0, 64),))
    low = jnp.concatenate([cut(table[:half]), cut(table[half:])], axis=3)
    whole = jnp.concatenate([top, low, f_bias.reshape(Z, Y, 2, 128)], axis=2)
    return jnp.pad(whole, ((0, 0), (0, 0), (0, SMALL_ROWS - whole.shape[2]), (0, 0)))


def spread_any(squares, w_in, w_out, smalls):
    wide = [slots_of(gather_any(one)) for one in squares]
    small = small_pieces(*[lax.all_gather(one, "dp", axis=one.ndim - 1, tiled=True) for one in smalls])
    ins = narrow_columns(slots_of(gather_any(w_in)))
    outs = slots_of(gather_any(w_out))
    square_w, feed_w = [], []
    for i, (y, unused, unused2) in enumerate(SLOTS):
        parts = [one[i] for one in wide]
        square_w.append(jnp.concatenate([*parts[:3], small[:, y], *parts[3:]], axis=1))
        feed_w.append(jnp.concatenate([ins[i], outs[i]], axis=1))
    return square_w, feed_w


def two_parts(slots):
    at = dict(zip(SLOTS, slots))
    a = [jnp.stack([at[y, x, c][:, :FIRST_ROWS] for x in range(X)]) for y in range(Y) for c in range(CORE)]
    b = [jnp.stack([at[y, x, c][:, FIRST_ROWS:] for y in range(Y)]) for x in range(X) for c in range(CORE)]
    return a + b


def by_slot(halves):
    return [halves[c][y * X + x] for y, x, c in SLOTS]


def reduce_squares_any(halves, count):
    slots = by_slot(halves)
    return [
        scatter_any(wide_of([one[:, PIECE * i : PIECE * (i + 1)] for one in slots]))
        for i in range(count)
    ]


def reduce_feed_any(halves):
    slots = by_slot(halves)
    ins = [
        jnp.concatenate([one[:, PIECE * j : PIECE * (j + 1)] for j in range(4)], axis=2)
        for one in slots
    ]
    return [scatter_any(wide_of(ins)), scatter_any(wide_of([one[:, 4 * PIECE :] for one in slots]))]


def reduce_small_any(halves, count):
    parts = [halves[0][y * X][:, 4 * PIECE :].astype(F32) for y in range(Y)]
    part = jnp.stack(parts, axis=1).reshape(Z * Y, SMALL_ROWS, 128)
    vectors = part[:, :13, :64].transpose(1, 0, 2).reshape(13, -1)
    half = count // 2
    table = part[:, TABLE : TABLE + half]
    table = jnp.concatenate([table[:, :, :64], table[:, :, 64:]], axis=1)
    rows = jnp.concatenate([vectors, table.transpose(1, 0, 2).reshape(count, -1)], axis=0)
    cut = lax.psum_scatter(lax.psum(rows, "mem"), "dp", scatter_dimension=1, tiled=True)
    f_bias = part[:, TABLE + half : TABLE + half + 2].reshape(-1)
    f_bias = lax.psum_scatter(lax.psum(f_bias, "mem"), "dp", scatter_dimension=0, tiled=True)
    return cut[:7], f_bias, cut[7:10], cut[10:13], cut[13:]


def shards(
    target, memory, time_steps, target_len, source_len, source_off, cotangent,
    self_query, self_key, self_value, self_out, cross_query, cross_key, cross_value, cross_out,
    feed_in, feed_out, biases, feed_bias, norm_gain, norm_shift, step_table,
):
    pairs = target.shape[0]
    steps = step_table.shape[0]
    dp, mem = lax.axis_index("dp"), lax.axis_index("mem")
    quick = lax.axis_size("dp") == Z * Y and lax.axis_size("mem") == X * CORE
    here = [dp // 2, dp % 2, mem // 2, mem % 2] if quick else [0, 0, 0, 0]
    meta = jnp.concatenate(
        [
            target_len,
            time_steps,
            lax.dynamic_slice_in_dim(source_off, mem * pairs, pairs),
            lax.dynamic_slice_in_dim(source_len, mem * pairs, pairs),
            jnp.stack([jnp.asarray(i, jnp.int32) for i in here]),
        ]
    )
    squares = (self_query, self_key, self_value, self_out, cross_query, cross_key, cross_value, cross_out)
    if quick:
        packed = call(
            pack_kernel,
            "pack",
            [*squares, feed_in, feed_out, biases, feed_bias.reshape(2, 128)]
            + [norm_gain, norm_shift, step_table],
            [VMEM] * 15,
            [((i, 128), BF, VMEM) for i in (SELF_ROWS + CROSS_ROWS, FEED_ROWS)],
            [VMEM((SMALL_ROWS, 128), F32)],
            1,
            60 * 2**20,
        )
        packed, memory = fence((packed, memory))
        square_p, feed_p = packed
        mems = swap_memory(memory, pairs)
        mems[2], mems[3] = swap(mems[2], 2), swap(mems[3], 3)
        square_z = sent_z([square_p] * 4)
        square_z, mems, feed_p = fence((square_z, mems, feed_p))
        first, second = z_halves(meta, square_z)
        square_near = [first, swap(first, 2), second, swap(second, 4)]
        feed_z = z_pair(meta, feed_p)
        square_near, feed_z = fence((square_near, feed_z))
        first, second = doubled(square_near)
        square_near = [first, swap(first, 4), second, swap(second, 2)]
        feed_z = (feed_z, swap(feed_z, 16))
        mems[1] = swap(mems[1], 1)
        feed_z = z_quad(meta, *feed_z)
        square_near, feed_z, mems = fence((square_near, feed_z, mems))
        square_w = spread_core(square_near)
        feed_near = spread_near(feed_z)
    else:
        square_w, feed_w = spread_any(
            squares, feed_in, feed_out, (biases, feed_bias, norm_gain, norm_shift, step_table)
        )
        square_w = two_parts(square_w)
        own = lax.all_to_all(memory, "mem", 0, 1, tiled=True)
        mems = jnp.split(own, X * CORE, axis=1)

    far_a, w_a, near_mix, vecs, fbias, held_a, held_b = self_forward(meta, target, square_w, steps)
    far_b, w_b, after_self, after_cross = cross_forward(meta, target, near_mix, mems, vecs, held_b)
    if quick:
        feed_near, after_cross = fence((feed_near, after_cross))
        feed_w = spread_core(feed_near)
    layer_out, gres_c, sums_c, d_fbias, *d_feed = feed(
        meta, after_cross, cotangent, vecs, fbias, feed_w
    )
    if quick:
        d_feed, gres_c = fence((d_feed, gres_c))
        d_feed[1] = swap(d_feed[1], 1)
    gq_b, gk_b, gv_b, sums_b, *d_cross = cross_back(meta, gres_c, far_b, w_b, held_b)
    if quick:
        d_feed, gq_b, d_cross = fence((d_feed, gq_b, d_cross))
        u_feed = core_sums(*d_feed)
        u_feed, gq_b, d_cross = fence((u_feed, gq_b, d_cross))
        n_feed = near_parts(u_feed)
        d_cross[1] = swap(d_cross[1], 1)
    grad_target, *gmem, d_first, d_second = lower_back(
        meta, gres_c, (gq_b, gk_b, gv_b), after_self, far_a, w_a, target, vecs, (sums_b, sums_c), d_fbias, held_b, held_a, steps
    )
    d_self = [d_first, d_second]
    if quick:
        one = self_query.shape
        n_feed, d_cross, d_self, gmem = fence((n_feed, d_cross, d_self, gmem))
        d_self[1] = swap(d_self[1], 1)
        rest = split_sums(*d_cross, *d_self)
        m_feed = chip_sums(meta, n_feed)
        rest, m_feed, gmem = fence((rest, m_feed, gmem))
        rest[1], rest[3] = swap(rest[1], 2), swap(rest[3], 4)
        gmem[1] = swap(gmem[1], 1)
        m_feed[1] = swap(m_feed[1], 16)
        rest, m_feed, gmem = fence((rest, m_feed, gmem))
        rest = turn(rest)
        rest[1], rest[3] = swap(rest[1], 4), swap(rest[3], 2)
        m_feed = halved(*m_feed)
        m_feed[1] = swap(m_feed[1], 8)
        rest, gmem, m_feed = fence((rest, gmem, m_feed))
        m_rest = sent_z(meet(meta, rest))
        g_feed = slice_sums(final_kernel, m_feed, (feed_in.shape, feed_out.shape))
        gmem[2], gmem[3] = swap(gmem[2], 2), swap(gmem[3], 3)
        grad_memory = return_memory(meta, gmem, memory.shape)
        m_rest, grad_memory = fence((m_rest, grad_memory))
        small_shapes = (biases.shape, (2, 128), norm_gain.shape, norm_shift.shape, step_table.shape)
        out = slice_sums(final_small_kernel, m_rest, (one,) * 8 + small_shapes)
        g_cross, g_self, (g_bias, g_fbias, g_gain, g_shift, g_table) = out[:4], out[4:8], out[8:]
        g_fbias = g_fbias.reshape(feed_bias.shape)
    else:
        whole = jnp.concatenate(gmem, axis=1)
        grad_memory = lax.all_to_all(whole, "mem", 1, 0, tiled=True).astype(F32)
        g_feed = reduce_feed_any(d_feed)
        g_cross = reduce_squares_any(d_cross, 4)
        g_self = reduce_squares_any(d_self, 4)
        g_bias, g_fbias, g_gain, g_shift, g_table = reduce_small_any(d_self, steps)
    return (
        layer_out, grad_target, grad_memory, *g_self, *g_cross, *g_feed,
        g_bias, g_fbias, g_gain, g_shift, g_table,
    )


def solution(mesh):
    rows = P(BOTH, None, None)
    piece = P("dp", "mem")
    vector = P(None, "dp")
    mem_rows = P("dp", "mem", None)
    return jax.shard_map(
        shards,
        mesh=mesh,
        in_specs=(rows, mem_rows, P(BOTH), P(BOTH), P("dp"), P("dp"), rows)
        + (piece,) * 10
        + (vector, P("dp"), vector, vector, vector),
        out_specs=(rows, rows, mem_rows) + (piece,) * 10 + (vector, P("dp"), vector, vector, vector),
        check_vma=False,
    )
```
